32 devices in a mesh: sp: 8 (over z, y), ch: 4 (over x, core).
Axes of the slice: x: 2, y: 2, z: 4, core: 2. Of those that a mesh axis runs over, the one named last changes fastest.
Arguments:
- features: bfloat16 [4, 64, 48, 2048], P('ch', 'sp'), may hold values from -24 to 24
- box_counts: int32 [4], replicated, may hold values from 1 to 32
- b1_w_reduce: bfloat16 [2048, 512], P(None, 'ch'), may hold values from -0.125 to 0.125
- b1_gain1: float32 [512], replicated, may hold values from 0.5 to 1.5
- b1_bias1: float32 [512], replicated, may hold values from -1.2 to 1.2
- b1_w_offset: bfloat16 [9, 512, 18], P(None, 'ch'), may hold values from -0.09375 to 0.09375
- b1_w_deform: bfloat16 [9, 512, 512], P(None, 'ch'), may hold values from -0.09375 to 0.09375
- b1_gain2: float32 [512], replicated, may hold values from 0.5 to 1.5
- b1_bias2: float32 [512], replicated, may hold values from -1.2 to 1.2
- b1_w_expand: bfloat16 [512, 2048], P(None, 'ch'), may hold values from -0.25 to 0.25
- b1_gain3: float32 [2048], replicated, may hold values from 0.5 to 1.5
- b1_bias3: float32 [2048], replicated, may hold values from -1.2 to 1.2
- b2_w_reduce: bfloat16 [2048, 512], P(None, 'ch'), may hold values from -0.125 to 0.125
- b2_gain1: float32 [512], replicated, may hold values from 0.5 to 1.5
- b2_bias1: float32 [512], replicated, may hold values from -1.2 to 1.2
- b2_w_spatial: bfloat16 [9, 512, 512], P(None, 'ch'), may hold values from -0.09375 to 0.09375
- b2_gain2: float32 [512], replicated, may hold values from 0.5 to 1.5
- b2_bias2: float32 [512], replicated, may hold values from -1.2 to 1.2
- b2_w_expand: bfloat16 [512, 2048], P(None, 'ch'), may hold values from -0.25 to 0.25
- b2_gain3: float32 [2048], replicated, may hold values from 0.5 to 1.5
- b2_bias3: float32 [2048], replicated, may hold values from -1.2 to 1.2
- cotangent: bfloat16 [4, 64, 48, 2048], P('ch', 'sp'), may hold values from -24 to 24
Outputs:
- out: bfloat16 [4, 64, 48, 2048], P('ch', 'sp')
- d_features: float32 [4, 64, 48, 2048], P('ch', 'sp')
- grad_b1_w_reduce: float32 [2048, 512], P(None, 'ch')
- grad_b1_gain1: float32 [512], replicated
- grad_b1_bias1: float32 [512], replicated
- grad_b1_w_offset: float32 [9, 512, 18], P(None, 'ch')
- grad_b1_w_deform: float32 [9, 512, 512], P(None, 'ch')
- grad_b1_gain2: float32 [512], replicated
- grad_b1_bias2: float32 [512], replicated
- grad_b1_w_expand: float32 [512, 2048], P(None, 'ch')
- grad_b1_gain3: float32 [2048], replicated
- grad_b1_bias3: float32 [2048], replicated
- grad_b2_w_reduce: float32 [2048, 512], P(None, 'ch')
- grad_b2_gain1: float32 [512], replicated
- grad_b2_bias1: float32 [512], replicated
- grad_b2_w_spatial: float32 [9, 512, 512], P(None, 'ch')
- grad_b2_gain2: float32 [512], replicated
- grad_b2_bias2: float32 [512], replicated
- grad_b2_w_expand: float32 [512, 2048], P(None, 'ch')
- grad_b2_gain3: float32 [2048], replicated
- grad_b2_bias3: float32 [2048], replicated
The draws below stay inside these ranges and needn't reach their ends.
All inputs are finite; a program needn't handle non-finite values.
Results may differ from the reference program's by a relative error of at most 0.025.
The reference program's roundings to bfloat16 on the way (of `first_act`, `extended`, `shifted_cols`, `spatial_cols`, `second_act` and `middle`) count: a program that leaves them out, or rounds other values in their place, can miss the bound.
Values may be sent and summed in bfloat16 or wider, within the bound.
A program may use at most 320 MiB of HBM per device.

```python
import jax
import jax.numpy as jnp
from jax import lax

C_IN = 2048
MID = 512
COLS = 48
HEIGHT = 64
IMAGES = 4


def field_scale(key):
    grid_shape = (IMAGES, HEIGHT, COLS, C_IN)
    rising = 1.0 + 2.0 * lax.broadcasted_iota(jnp.float32, grid_shape, 1) / (HEIGHT - 1)
    channel_scale = jnp.exp(jax.random.uniform(key, (1, 1, 1, C_IN), jnp.float32, -0.69, 0.69))
    return rising * channel_scale


def draw_features(key, part):
    key = jax.random.fold_in(key, 11)
    base_key, scale_key = jax.random.split(key)
    factors = field_scale(scale_key)
    grid_shape = (IMAGES, HEIGHT, COLS, C_IN)
    return (jax.random.truncated_normal(base_key, -4.0, 4.0, grid_shape, jnp.float32) * factors).astype(jnp.bfloat16)


def draw_cotangent(key, part):
    key = jax.random.fold_in(key, 12)
    base_key, scale_key = jax.random.split(key)
    factors = field_scale(scale_key)
    grid_shape = (IMAGES, HEIGHT, COLS, C_IN)
    return (jax.random.truncated_normal(base_key, -4.0, 4.0, grid_shape, jnp.float32) * factors).astype(jnp.bfloat16)


def with_ends(values, key, smallest, top_value):
    spot = [jax.random.randint(jax.random.fold_in(key, axis), (), 0, length) for axis, length in enumerate(values.shape)]
    widest = values.shape.index(max(values.shape))
    neighbour = spot[:widest] + [(spot[widest] + 1) % values.shape[widest]] + spot[widest + 1:]
    return values.at[tuple(spot)].set(smallest).at[tuple(neighbour)].set(top_value)


def block_scale(stream_key, extent, cuts, least, high):
    def one(dim, parts):
        steps = jax.random.uniform(jax.random.fold_in(jax.random.fold_in(stream_key, 6), dim), (parts,), jnp.float32, least / len(cuts), high / len(cuts))
        return jnp.repeat(jnp.exp(steps), extent[dim] // parts).reshape((-1,) + (1,) * (len(extent) - dim - 1))

    level = one(*cuts[0])
    for cut in cuts[1:]:
        level = level * one(*cut)
    return level


def normal_values(rng, shape, scale, limit, cuts=(), kind=jnp.bfloat16):
    gain = block_scale(rng, shape, cuts, -0.22, 0.18) if cuts else 1.0
    entries = jax.random.normal(rng, shape, jnp.float32) * scale * gain
    return jnp.minimum(jnp.maximum(entries, -limit), limit).astype(kind)


def setup_inputs(seed: int = 0) -> dict:
    key_of = jax.random.split(jax.random.key(seed), 23)
    features = draw_features(jax.random.fold_in(key_of[22], 71), 0)
    box_counts = with_ends(jax.random.randint(key_of[1], (IMAGES,), 1, 33), jax.random.fold_in(key_of[1], 1), 1, 32).astype(jnp.int32)
    b1_w_reduce = normal_values(key_of[2], (C_IN, MID), C_IN ** -0.5, 0.125, ((1, 4),))
    b1_gain1 = jnp.clip(1.0 + 0.1 * jax.random.normal(key_of[3], (MID,), jnp.float32), 0.5, 1.5)
    b1_bias1 = normal_values(key_of[4], (MID,), 0.3, 1.2, (), jnp.float32)
    b1_w_offset = normal_values(key_of[5], (9, MID, 18), (9 * MID) ** -0.5, 0.09375, ((1, 4),))
    b1_w_deform = normal_values(key_of[6], (9, MID, MID), (9 * MID) ** -0.5, 0.09375, ((1, 4),))
    b1_gain2 = jnp.clip(1.0 + 0.1 * jax.random.normal(key_of[7], (MID,), jnp.float32), 0.5, 1.5)
    b1_bias2 = normal_values(key_of[8], (MID,), 0.3, 1.2, (), jnp.float32)
    b1_w_expand = normal_values(key_of[9], (MID, C_IN), MID ** -0.5, 0.25, ((1, 4),))
    b1_gain3 = jnp.clip(1.0 + 0.1 * jax.random.normal(key_of[10], (C_IN,), jnp.float32), 0.5, 1.5)
    b1_bias3 = normal_values(key_of[11], (C_IN,), 0.3, 1.2, (), jnp.float32)
    b2_w_reduce = normal_values(key_of[12], (C_IN, MID), C_IN ** -0.5, 0.125, ((1, 4),))
    b2_gain1 = jnp.clip(1.0 + 0.1 * jax.random.normal(key_of[13], (MID,), jnp.float32), 0.5, 1.5)
    b2_bias1 = normal_values(key_of[14], (MID,), 0.3, 1.2, (), jnp.float32)
    b2_w_spatial = normal_values(key_of[15], (9, MID, MID), (9 * MID) ** -0.5, 0.09375, ((1, 4),))
    b2_gain2 = jnp.clip(1.0 + 0.1 * jax.random.normal(key_of[16], (MID,), jnp.float32), 0.5, 1.5)
    b2_bias2 = normal_values(key_of[17], (MID,), 0.3, 1.2, (), jnp.float32)
    b2_w_expand = normal_values(key_of[18], (MID, C_IN), MID ** -0.5, 0.25, ((1, 4),))
    b2_gain3 = jnp.clip(1.0 + 0.1 * jax.random.normal(key_of[19], (C_IN,), jnp.float32), 0.5, 1.5)
    b2_bias3 = normal_values(key_of[20], (C_IN,), 0.3, 1.2, (), jnp.float32)
    cotangent = draw_cotangent(jax.random.fold_in(key_of[22], 71), 0)
    return dict(features=features, box_counts=box_counts, b1_w_reduce=b1_w_reduce, b1_gain1=b1_gain1, b1_bias1=b1_bias1, b1_w_offset=b1_w_offset, b1_w_deform=b1_w_deform, b1_gain2=b1_gain2, b1_bias2=b1_bias2, b1_w_expand=b1_w_expand, b1_gain3=b1_gain3, b1_bias3=b1_bias3, b2_w_reduce=b2_w_reduce, b2_gain1=b2_gain1, b2_bias1=b2_bias1, b2_w_spatial=b2_w_spatial, b2_gain2=b2_gain2, b2_bias2=b2_bias2, b2_w_expand=b2_w_expand, b2_gain3=b2_gain3, b2_bias3=b2_bias3, cotangent=cotangent)


EPS = 1e-05
REACH = 5.5
EXACT = lax.Precision.HIGHEST

@jax.custom_vjp
def low(v):
    return lax.optimization_barrier(v.astype(jnp.bfloat16)).astype(jnp.float32)

@jax.custom_vjp
def low_back(v):
    return v

def low_keep(v):
    return (low(v), None)

def low_pass(kept, grad):
    return (grad,)

def back_keep(v):
    return (v, None)

def back_low(kept, grad):
    return (low(grad),)
low.defvjp(low_keep, low_pass)
low_back.defvjp(back_keep, back_low)

def matmul(left, right):
    return jnp.dot(left, right, precision=EXACT, preferred_element_type=jnp.float32)

def batchnorm(values, gain_vec, bias_vec):
    center = lax.optimization_barrier(jnp.mean(values, axis=0))
    square = lax.optimization_barrier(jnp.mean(values * values, axis=0))
    inverse = lax.rsqrt(square - center * center + EPS)
    return gain_vec * (values - center) * inverse + bias_vec

def smoothstep(fraction):
    return fraction * fraction * (3.0 - 2.0 * fraction)

def shifted(extended):
    images, ext_rows, columns, channels = extended.shape
    height = ext_rows - 16
    padded = jnp.pad(extended, ((0, 0), (0, 0), (2, 2), (0, 0)))
    pieces = []
    for kernel_tap in range(9):
        first_row = 8 + 2 * (kernel_tap // 3) - 2
        first_col = 2 * (kernel_tap % 3)
        pieces.append(padded[:, first_row:first_row + height, first_col:first_col + columns, :].reshape(-1, channels))
    return jnp.concatenate(pieces, axis=1)

def sample(extended, offsets):
    images, ext_rows, columns, channels = extended.shape
    height = ext_rows - 16
    flattened = extended.reshape(-1, channels)
    grid_shape = (images, height, columns)
    image_ids = lax.broadcasted_iota(jnp.int32, grid_shape, 0).reshape(-1)
    row_pos = (lax.broadcasted_iota(jnp.float32, grid_shape, 1) + 8.0).reshape(-1)
    col_pos = lax.broadcasted_iota(jnp.float32, grid_shape, 2).reshape(-1)
    pieces = []
    for kernel_tap in range(9):
        sample_row = row_pos + (2 * (kernel_tap // 3) - 2) + offsets[:, 2 * kernel_tap]
        across = col_pos + (2 * (kernel_tap % 3) - 2) + offsets[:, 2 * kernel_tap + 1]
        row_base = jnp.floor(sample_row)
        col_base = jnp.floor(across)
        row_frac = smoothstep(sample_row - row_base)
        col_frac = smoothstep(across - col_base)
        row_index = row_base.astype(jnp.int32)
        col_index = col_base.astype(jnp.int32)
        summed = jnp.zeros((sample_row.shape[0], channels), flattened.dtype)
        for step_row in range(2):
            row_weight = row_frac if step_row else 1.0 - row_frac
            for step_col in range(2):
                col_weight = col_frac if step_col else 1.0 - col_frac
                column = col_index + step_col
                inside = (column >= 0) & (column < columns)
                weight = jnp.where(inside, row_weight * col_weight, 0.0)
                position = (image_ids * ext_rows + row_index + step_row) * columns + jnp.clip(column, 0, columns - 1)
                summed = summed + jnp.take(flattened, position, axis=0) * weight[:, None]
        pieces.append(summed)
    return jnp.concatenate(pieces, axis=1)

def block(inputs, w_reduce, gain_one, bias_one, w_offset, w_spatial, gain_two, bias_two, w_expand, gain_three, bias_three):
    images, height, columns, channels = inputs.shape
    middle = w_spatial.shape[2]
    flattened = inputs.reshape(-1, channels)
    reduced = low_back(matmul(flattened, w_reduce))
    first_act = low(jax.nn.silu(batchnorm(reduced, gain_one, bias_one)))
    extended = jnp.pad(first_act.reshape(images, height, columns, middle), ((0, 0), (8, 8), (0, 0), (0, 0)))

    def spatial(picture):
        shifted_cols = shifted(picture[None])
        if w_offset is None:
            return matmul(shifted_cols, w_spatial.reshape(-1, middle))
        offset_raw = low_back(matmul(shifted_cols, w_offset.reshape(-1, w_offset.shape[2])))
        spatial_cols = low(sample(picture[None], REACH * jnp.tanh(offset_raw)))
        return matmul(spatial_cols, w_spatial.reshape(-1, middle))
    spread = low_back(lax.map(jax.checkpoint(spatial), extended).reshape(-1, middle))
    second_act = low(jax.nn.silu(batchnorm(spread, gain_two, bias_two)))
    expanded = low_back(matmul(second_act, w_expand))
    joined = batchnorm(expanded, gain_three, bias_three) + flattened
    return jax.nn.silu(joined).reshape(images, height, columns, channels)

def deform_block(inputs, w_reduce, gain_one, bias_one, w_offset, w_deform, gain_two, bias_two, w_expand, gain_three, bias_three):
    return block(inputs, w_reduce, gain_one, bias_one, w_offset, w_deform, gain_two, bias_two, w_expand, gain_three, bias_three)

def plain_block(inputs, w_reduce, gain_one, bias_one, w_spatial, gain_two, bias_two, w_expand, gain_three, bias_three):
    return block(inputs, w_reduce, gain_one, bias_one, None, w_spatial, gain_two, bias_two, w_expand, gain_three, bias_three)

def reference(features, box_counts, b1_w_reduce, b1_gain1, b1_bias1, b1_w_offset, b1_w_deform, b1_gain2, b1_bias2, b1_w_expand, b1_gain3, b1_bias3, b2_w_reduce, b2_gain1, b2_bias1, b2_w_spatial, b2_gain2, b2_bias2, b2_w_expand, b2_gain3, b2_bias3, cotangent):
    arrays = (features, b1_w_reduce, b1_gain1, b1_bias1, b1_w_offset, b1_w_deform, b1_gain2, b1_bias2, b1_w_expand, b1_gain3, b1_bias3, b2_w_reduce, b2_gain1, b2_bias1, b2_w_spatial, b2_gain2, b2_bias2, b2_w_expand, b2_gain3, b2_bias3)
    floats = [member.astype(jnp.float32) for member in arrays]

    def forward(*values):
        first_out = jax.checkpoint(deform_block)(*values[:11])
        return jax.checkpoint(plain_block)(low(first_out), *values[11:])
    result, pullback = jax.vjp(forward, *floats)
    counts = box_counts.astype(jnp.float32)
    box_scale = counts * counts.shape[0] / jnp.sum(counts)
    grads = pullback(cotangent.astype(jnp.float32) * box_scale[:, None, None, None])
    return (result.astype(jnp.bfloat16), grads[0], grads[1], grads[2], grads[3], grads[4], grads[5], grads[6], grads[7], grads[8], grads[9], grads[10], grads[11], grads[12], grads[13], grads[14], grads[15], grads[16], grads[17], grads[18], grads[19])
```

```python
import functools

import jax
import jax.numpy as jnp
from jax import lax
from jax.experimental import pallas as pl
from jax.experimental.pallas import tpu as pltpu
from jax.sharding import PartitionSpec as P

EPS = 1e-05
REACH = 5.5


MESH = pl.DeviceIdType.MESH


def sum_kernel(n_ch, n_sp, x_ref, o_ref, ch_slots, sp_slots, send_sem, ch_sem, sp_sem):
    s, c = lax.axis_index("sp"), lax.axis_index("ch")
    barrier = pltpu.get_barrier_semaphore()
    for d in range(1, n_ch):
        pl.semaphore_signal(barrier, inc=1, device_id=(s, lax.rem(c + d, n_ch)), device_id_type=MESH)
    for d in range(1, n_sp):
        pl.semaphore_signal(barrier, inc=1, device_id=(lax.rem(s + d, n_sp), c), device_id_type=MESH)
    pl.semaphore_wait(barrier, n_ch + n_sp - 2)
    ch_slots[c] = x_ref[...]
    copies = []
    for d in range(1, n_ch):
        copies.append(
            pltpu.make_async_remote_copy(
                src_ref=x_ref,
                dst_ref=ch_slots.at[c],
                send_sem=send_sem.at[d],
                recv_sem=ch_sem.at[c],
                device_id=(s, lax.rem(c + d, n_ch)),
                device_id_type=MESH,
            )
        )
    for copy in copies:
        copy.start()
    for d in range(1, n_ch):
        source = lax.rem(c + d, n_ch)
        pltpu.make_async_remote_copy(
            src_ref=x_ref,
            dst_ref=ch_slots.at[source],
            send_sem=send_sem.at[d],
            recv_sem=ch_sem.at[source],
            device_id=(s, source),
            device_id_type=MESH,
        ).wait_recv()
    total = ch_slots[0]
    for k in range(1, n_ch):
        total = total + ch_slots[k]
    sp_slots[s] = total
    later = []
    for d in range(1, n_sp):
        later.append(
            pltpu.make_async_remote_copy(
                src_ref=sp_slots.at[s],
                dst_ref=sp_slots.at[s],
                send_sem=send_sem.at[n_ch + d],
                recv_sem=sp_sem.at[s],
                device_id=(lax.rem(s + d, n_sp), c),
                device_id_type=MESH,
            )
        )
    for copy in later:
        copy.start()
    for d in range(1, n_sp):
        source = lax.rem(s + d, n_sp)
        pltpu.make_async_remote_copy(
            src_ref=sp_slots.at[source],
            dst_ref=sp_slots.at[source],
            send_sem=send_sem.at[n_ch + d],
            recv_sem=sp_sem.at[source],
            device_id=(source, c),
            device_id_type=MESH,
        ).wait_recv()
    total = sp_slots[0]
    for k in range(1, n_sp):
        total = total + sp_slots[k]
    o_ref[...] = total
    for copy in copies + later:
        copy.wait_send()


def summed(first, second):
    n_ch, n_sp = lax.axis_size("ch"), lax.axis_size("sp")
    x = jnp.stack([first, second])
    rows, lanes = x.shape
    vmem = pl.BlockSpec(memory_space=pltpu.VMEM)
    out = pl.pallas_call(
        functools.partial(sum_kernel, n_ch, n_sp),
        out_shape=jax.ShapeDtypeStruct(x.shape, x.dtype),
        in_specs=[vmem],
        out_specs=vmem,
        scratch_shapes=[
            pltpu.VMEM((n_ch, rows, lanes), jnp.float32),
            pltpu.VMEM((n_sp, rows, lanes), jnp.float32),
            pltpu.SemaphoreType.DMA((n_ch + n_sp,)),
            pltpu.SemaphoreType.DMA((n_ch,)),
            pltpu.SemaphoreType.DMA((n_sp,)),
        ],
        compiler_params=pltpu.CompilerParams(collective_id=lanes // 512, has_side_effects=True),
    )(x)
    return out[0], out[1]


def extended_2(block, sides, width):
    for axis, dim in sides:
        count = lax.axis_size(axis)
        forward = [(i, i + 1) for i in range(count - 1)]
        backward = [(target, source) for source, target in forward]
        low = lax.ppermute(
            lax.slice_in_dim(block, block.shape[dim] - width, None, axis=dim), axis, forward
        )
        high = lax.ppermute(lax.slice_in_dim(block, 0, width, axis=dim), axis, backward)
        block = jnp.concatenate([low, block, high], axis=dim)
    return block


def smoothstep(fraction):
    return fraction * fraction * (3.0 - 2.0 * fraction)


def shifted(extended):
    images, ext_rows, columns, channels = extended.shape
    height = ext_rows - 16
    padded = jnp.pad(extended, ((0, 0), (0, 0), (2, 2), (0, 0)))
    pieces = []
    for kernel_tap in range(9):
        first_row = 8 + 2 * (kernel_tap // 3) - 2
        first_col = 2 * (kernel_tap % 3)
        pieces.append(
            padded[:, first_row : first_row + height, first_col : first_col + columns, :].reshape(
                -1, channels
            )
        )
    return jnp.concatenate(pieces, axis=1)


def tent(position, count):
    base = jnp.floor(position)
    fraction = position - base
    upper = smoothstep(fraction)
    slope = 6.0 * fraction * (1.0 - fraction)
    cells = lax.broadcasted_iota(jnp.float32, position.shape + (count,), position.ndim)
    at = cells == base[..., None]
    after = cells == base[..., None] + 1.0
    weight = jnp.where(at, (1.0 - upper)[..., None], jnp.where(after, upper[..., None], 0.0))
    rate = jnp.where(at, -slope[..., None], jnp.where(after, slope[..., None], 0.0))
    return weight, rate


def sample_weights(offsets, height, columns):
    pixels = offsets.shape[0]
    taps = offsets.reshape(pixels, 9, 2)
    tap = lax.broadcasted_iota(jnp.int32, (pixels, 9), 1)
    pixel = lax.broadcasted_iota(jnp.int32, (pixels, 9), 0)
    row = (pixel // columns + 8 + 2 * (tap // 3) - 2).astype(jnp.float32) + taps[:, :, 0]
    col = (pixel % columns + 2 * (tap % 3) - 2).astype(jnp.float32) + taps[:, :, 1]
    rows = tent(row, height + 16)
    cols = tent(col, columns)
    return rows, cols


def outer(rows, cols):
    pixels = rows.shape[0]
    return (rows[:, :, :, None] * cols[:, :, None, :]).reshape(pixels * 9, -1)


def contract_rows(left, right):
    return lax.dot_general(
        left, right, (((0,), (0,)), ((), ())), preferred_element_type=jnp.float32
    )


def contract_cols(left, right):
    return lax.dot_general(
        left, right, (((1,), (1,)), ((), ())), preferred_element_type=jnp.float32
    )


def silu_slope(values):
    sigma = jax.nn.sigmoid(values)
    return sigma * (1.0 + values * (1.0 - sigma))


def norm_forward(values, gain_vec, bias_vec, pixel_total):
    totals = summed(jnp.sum(values, axis=0), jnp.sum(values * values, axis=0))
    center = totals[0] / pixel_total
    inverse = lax.rsqrt(totals[1] / pixel_total - center * center + EPS)
    normed = (values - center) * inverse
    return (gain_vec * normed + bias_vec, (normed, inverse))


def norm_backward(upstream, saved, gain_vec, pixel_total):
    normed, inverse = saved
    totals = summed(jnp.sum(upstream, axis=0), jnp.sum(upstream * normed, axis=0))
    inner = upstream - totals[0] / pixel_total - normed * (totals[1] / pixel_total)
    return (gain_vec * inverse * inner, totals[1], totals[0])


def gather_deform(reduce_w, offset_w, deform_w, expand_w):
    return (
        lax.all_gather(reduce_w, "ch", axis=1, tiled=True),
        lax.all_gather(offset_w, "ch", axis=1, tiled=True),
        lax.all_gather(deform_w, "ch", axis=1, tiled=True),
        lax.all_gather(expand_w, "ch", axis=1, tiled=True),
    )


def gather_plain(reduce_w, spatial_w, expand_w):
    return (
        lax.all_gather(reduce_w, "ch", axis=1, tiled=True),
        lax.all_gather(spatial_w, "ch", axis=1, tiled=True),
        lax.all_gather(expand_w, "ch", axis=1, tiled=True),
    )


def borrow_rows(first_act, images, height, columns):
    tiles = first_act.reshape(images, height, columns, first_act.shape[1])
    return extended_2(tiles, (("sp", 1),), 8)


def fold_rims(grad_ext, height):
    edges = jnp.concatenate([grad_ext[:, :8], grad_ext[:, height + 8 :]], axis=1)
    returned = extended_2(edges.astype(jnp.bfloat16), (("sp", 1),), 8).astype(edges.dtype)
    core = grad_ext[:, 8 : height + 8]
    above = returned[:, :8]
    below = returned[:, 24:]
    summed = core + above + below
    return summed.reshape(-1, summed.shape[3])


def forward_block(
    inputs, w_reduce, w_offset, w_spatial, w_expand, norms, images, height, columns, pixel_total
):
    middle = w_spatial.shape[2]
    memory = {}
    reduced = jnp.dot(inputs, w_reduce, preferred_element_type=jnp.float32)
    first_pre, memory["first_norm"] = norm_forward(reduced, norms[0], norms[1], pixel_total)
    first_act = jax.nn.silu(first_pre).astype(jnp.bfloat16)
    extended = borrow_rows(first_act, images, height, columns)
    shifted_cols = shifted(extended)
    if w_offset is None:
        spatial_cols = shifted_cols
    else:
        offset_raw = jnp.dot(
            shifted_cols,
            w_offset.reshape(-1, w_offset.shape[2]),
            preferred_element_type=jnp.float32,
        )
        offset_tanh = jnp.tanh(offset_raw)
        sides = sample_weights(REACH * offset_tanh, height, columns)
        weights = outer(sides[0][0], sides[1][0]).astype(jnp.bfloat16)
        cells = extended.reshape(-1, middle)
        sampled = jnp.dot(weights, cells, preferred_element_type=jnp.float32)
        spatial_cols = sampled.astype(jnp.bfloat16).reshape(-1, 9 * middle)
        memory["sides"] = sides
        memory["offset_tanh"] = offset_tanh
    spread = jnp.dot(
        spatial_cols, w_spatial.reshape(-1, middle), preferred_element_type=jnp.float32
    )
    second_pre, memory["second_norm"] = norm_forward(spread, norms[2], norms[3], pixel_total)
    second_act = jax.nn.silu(second_pre).astype(jnp.bfloat16)
    expanded = jnp.dot(second_act, w_expand, preferred_element_type=jnp.float32)
    third_pre, memory["third_norm"] = norm_forward(expanded, norms[4], norms[5], pixel_total)
    joined = third_pre + inputs.astype(jnp.float32)
    memory["first_pre"] = first_pre
    memory["extended"] = extended
    memory["shifted_cols"] = shifted_cols
    memory["spatial_cols"] = spatial_cols
    memory["second_pre"] = second_pre
    memory["second_act"] = second_act
    memory["joined"] = joined
    return (jax.nn.silu(joined), memory)


def backward_block(
    upstream, inputs, w_reduce, w_offset, w_spatial, w_expand, norms, memory, height, pixel_total
):
    middle = w_spatial.shape[2]
    joined_grad = upstream * silu_slope(memory["joined"])
    third_grad, gain_three, bias_three = norm_backward(
        joined_grad, memory["third_norm"], norms[4], pixel_total
    )
    third_low = third_grad.astype(jnp.bfloat16)
    expand_grad = contract_rows(memory["second_act"], third_low)
    second_act_grad = contract_cols(third_low, w_expand)
    second_grad, gain_two, bias_two = norm_backward(
        second_act_grad * silu_slope(memory["second_pre"]),
        memory["second_norm"],
        norms[2],
        pixel_total,
    )
    second_low = second_grad.astype(jnp.bfloat16)
    spatial_grad = contract_rows(memory["spatial_cols"], second_low).reshape(9, -1, middle)
    cols_grad = contract_cols(second_low, w_spatial.reshape(-1, middle))
    shift_back = jax.vjp(shifted, memory["extended"].astype(jnp.float32))[1]
    if w_offset is None:
        ext_grad = shift_back(cols_grad)[0]
    else:
        rows, cols = memory["sides"]
        weights = outer(rows[0], cols[0]).astype(jnp.bfloat16)
        extended = memory["extended"]
        cells = extended.reshape(-1, middle)
        low_cols = cols_grad.reshape(-1, middle).astype(jnp.bfloat16)
        ext_grad = contract_rows(weights, low_cols).reshape(extended.shape)
        matches = contract_cols(low_cols, cells).reshape(-1, 9, rows[0].shape[2], cols[0].shape[2])
        down = jnp.sum(matches * rows[1][:, :, :, None] * cols[0][:, :, None, :], axis=(2, 3))
        across = jnp.sum(matches * rows[0][:, :, :, None] * cols[1][:, :, None, :], axis=(2, 3))
        offset_grad = jnp.stack([down, across], axis=2).reshape(-1, 18)
        offset_tanh = memory["offset_tanh"]
        raw_low = (offset_grad * REACH * (1.0 - offset_tanh * offset_tanh)).astype(jnp.bfloat16)
        offset_flat = w_offset.reshape(-1, w_offset.shape[2])
        offset_weight_grad = contract_rows(memory["shifted_cols"], raw_low).reshape(
            9, -1, w_offset.shape[2]
        )
        ext_grad = ext_grad + shift_back(contract_cols(raw_low, offset_flat))[0]
    first_act_grad = fold_rims(ext_grad, height)
    first_grad, gain_one, bias_one = norm_backward(
        first_act_grad * silu_slope(memory["first_pre"]),
        memory["first_norm"],
        norms[0],
        pixel_total,
    )
    first_low = first_grad.astype(jnp.bfloat16)
    reduce_grad = contract_rows(inputs, first_low)
    input_grad = joined_grad + contract_cols(first_low, w_reduce)
    norm_grads = (gain_one, bias_one, gain_two, bias_two, gain_three, bias_three)
    if w_offset is None:
        weight_grads = (reduce_grad, spatial_grad, expand_grad)
    else:
        weight_grads = (reduce_grad, offset_weight_grad, spatial_grad, expand_grad)
    return (input_grad, weight_grads, norm_grads)


def per_device(
    features,
    box_counts,
    b1_w_reduce,
    b1_gain1,
    b1_bias1,
    b1_w_offset,
    b1_w_deform,
    b1_gain2,
    b1_bias2,
    b1_w_expand,
    b1_gain3,
    b1_bias3,
    b2_w_reduce,
    b2_gain1,
    b2_bias1,
    b2_w_spatial,
    b2_gain2,
    b2_bias2,
    b2_w_expand,
    b2_gain3,
    b2_bias3,
    cotangent,
):
    images, height, columns, channels = features.shape
    pixel_total = images * height * columns * lax.axis_size("sp") * lax.axis_size("ch")
    first_norms = (b1_gain1, b1_bias1, b1_gain2, b1_bias2, b1_gain3, b1_bias3)
    second_norms = (b2_gain1, b2_bias1, b2_gain2, b2_bias2, b2_gain3, b2_bias3)
    first_full = gather_deform(b1_w_reduce, b1_w_offset, b1_w_deform, b1_w_expand)
    second_full = gather_plain(b2_w_reduce, b2_w_spatial, b2_w_expand)
    entry_rows = features.reshape(-1, channels)
    first_out, first_memory = forward_block(
        entry_rows,
        first_full[0],
        first_full[1],
        first_full[2],
        first_full[3],
        first_norms,
        images,
        height,
        columns,
        pixel_total,
    )
    middle_rows = first_out.astype(jnp.bfloat16)
    final_out, second_memory = forward_block(
        middle_rows,
        second_full[0],
        None,
        second_full[1],
        second_full[2],
        second_norms,
        images,
        height,
        columns,
        pixel_total,
    )
    counts = box_counts.astype(jnp.float32)
    local_counts = lax.dynamic_slice_in_dim(counts, lax.axis_index("ch") * images, images)
    image_scale = local_counts * counts.shape[0] / jnp.sum(counts)
    upstream = (cotangent.astype(jnp.float32) * image_scale[:, None, None, None]).reshape(
        -1, channels
    )
    second_back = gather_plain(b2_w_reduce, b2_w_spatial, b2_w_expand)
    first_back = gather_deform(b1_w_reduce, b1_w_offset, b1_w_deform, b1_w_expand)
    middle_grad, second_grads, second_norm_grads = backward_block(
        upstream,
        middle_rows,
        second_back[0],
        None,
        second_back[1],
        second_back[2],
        second_norms,
        second_memory,
        height,
        pixel_total,
    )
    second_shares = (
        lax.psum_scatter(
            second_grads[0].astype(jnp.bfloat16), "ch", scatter_dimension=1, tiled=True
        ).astype(jnp.float32),
        lax.psum_scatter(
            second_grads[1].astype(jnp.bfloat16), "ch", scatter_dimension=1, tiled=True
        ).astype(jnp.float32),
        lax.psum_scatter(
            second_grads[2].astype(jnp.bfloat16), "ch", scatter_dimension=1, tiled=True
        ).astype(jnp.float32),
    )
    second_final = (
        lax.psum(second_shares[0].astype(jnp.bfloat16), "sp").astype(jnp.float32),
        lax.psum(second_shares[1].astype(jnp.bfloat16), "sp").astype(jnp.float32),
        lax.psum(second_shares[2].astype(jnp.bfloat16), "sp").astype(jnp.float32),
    )
    entry_grad, first_grads, first_norm_grads = backward_block(
        middle_grad,
        entry_rows,
        first_back[0],
        first_back[1],
        first_back[2],
        first_back[3],
        first_norms,
        first_memory,
        height,
        pixel_total,
    )
    first_shares = (
        lax.psum_scatter(
            first_grads[0].astype(jnp.bfloat16), "ch", scatter_dimension=1, tiled=True
        ).astype(jnp.float32),
        lax.psum_scatter(
            first_grads[1].astype(jnp.bfloat16), "ch", scatter_dimension=1, tiled=True
        ).astype(jnp.float32),
        lax.psum_scatter(
            first_grads[2].astype(jnp.bfloat16), "ch", scatter_dimension=1, tiled=True
        ).astype(jnp.float32),
        lax.psum_scatter(
            first_grads[3].astype(jnp.bfloat16), "ch", scatter_dimension=1, tiled=True
        ).astype(jnp.float32),
    )
    first_final = (
        lax.psum(first_shares[0].astype(jnp.bfloat16), "sp").astype(jnp.float32),
        lax.psum(first_shares[1].astype(jnp.bfloat16), "sp").astype(jnp.float32),
        lax.psum(first_shares[2].astype(jnp.bfloat16), "sp").astype(jnp.float32),
        lax.psum(first_shares[3].astype(jnp.bfloat16), "sp").astype(jnp.float32),
    )
    return (
        final_out.astype(jnp.bfloat16).reshape(images, height, columns, channels),
        entry_grad.reshape(images, height, columns, channels),
        first_final[0],
        first_norm_grads[0],
        first_norm_grads[1],
        first_final[1],
        first_final[2],
        first_norm_grads[2],
        first_norm_grads[3],
        first_final[3],
        first_norm_grads[4],
        first_norm_grads[5],
        second_final[0],
        second_norm_grads[0],
        second_norm_grads[1],
        second_final[1],
        second_norm_grads[2],
        second_norm_grads[3],
        second_final[2],
        second_norm_grads[4],
        second_norm_grads[5],
    )


def solution(mesh):
    return jax.shard_map(
        per_device,
        mesh=mesh,
        in_specs=(
            P("ch", "sp", None, None),
            P(),
            P(None, "ch"),
            P(),
            P(),
            P(None, "ch", None),
            P(None, "ch", None),
            P(),
            P(),
            P(None, "ch"),
            P(),
            P(),
            P(None, "ch"),
            P(),
            P(),
            P(None, "ch", None),
            P(),
            P(),
            P(None, "ch"),
            P(),
            P(),
            P("ch", "sp", None, None),
        ),
        out_specs=(
            P("ch", "sp", None, None),
            P("ch", "sp", None, None),
            P(None, "ch"),
            P(),
            P(),
            P(None, "ch", None),
            P(None, "ch", None),
            P(),
            P(),
            P(None, "ch"),
            P(),
            P(),
            P(None, "ch"),
            P(),
            P(),
            P(None, "ch", None),
            P(),
            P(),
            P(None, "ch"),
            P(),
            P(),
        ),
        check_vma=False,
    )
```

```python
import functools
import types

import jax
import jax.numpy as jnp
from jax import lax
from jax.experimental import pallas as pl
from jax.experimental.pallas import tpu as pltpu
from jax.sharding import PartitionSpec as P

EPS = 1e-05
REACH = 5.5
MESH = pl.DeviceIdType.MESH
MIB = 2**20


def mm(left, right):
    return jnp.dot(left, right, preferred_element_type=jnp.float32)


def mm_nt(left, right):
    return lax.dot_general(
        left, right, (((1,), (1,)), ((), ())), preferred_element_type=jnp.float32
    )


def smooth_rise(fraction):
    return fraction * fraction * (3.0 - 2.0 * fraction)


def sigmoid(v):
    return 1.0 / (1.0 + jnp.exp(-v))


class Place:
    def __init__(self, n_sp, n_ch):
        self.n_sp, self.n_ch, self.n_x = n_sp, n_ch, n_ch // 2
        self.s, self.c = lax.axis_index("sp"), lax.axis_index("ch")
        self.x, self.k = lax.div(self.c, 2), lax.rem(self.c, 2)
        self.y = lax.rem(self.s, 2)
        self.sib = self.c + 1 - 2 * self.k
        self.sibling = (self.s, self.sib)

    def other_x(self, d):
        return 2 * lax.rem(self.x + d, self.n_x) + self.k

    def near(self, d):
        q = lax.rem(self.y * self.n_ch + self.c + d, 2 * self.n_ch)
        return self.s - self.y + lax.div(q, self.n_ch), lax.rem(q, self.n_ch)

    def far(self, d):
        return lax.rem(self.s + 2 * d, self.n_sp), self.c

    def barrier(self):
        sem = pltpu.get_barrier_semaphore()

        def tell(device):
            pl.semaphore_signal(sem, inc=1, device_id=device, device_id_type=MESH)

        for d in range(1, 2 * self.n_ch):
            tell(self.near(d))
        for d in range(1, self.n_sp // 2):
            tell(self.far(d))
        diagonal = lax.rem(self.s + self.n_sp - 1 + 2 * self.y, self.n_sp)
        tell((diagonal, self.c))
        pl.semaphore_wait(sem, 2 * self.n_ch + self.n_sp // 2 - 1)


def remote(src, dst, send, recv, device):
    return pltpu.make_async_remote_copy(
        src_ref=src,
        dst_ref=dst,
        send_sem=send,
        recv_sem=recv,
        device_id=device,
        device_id_type=MESH,
    )


class AllSum:
    def __init__(self, place, first, second, send, recv_one, recv_two):
        self.p, self.first, self.second = place, first, second
        self.send, self.one, self.two = send, recv_one, recv_two
        self.me = place.y * place.n_ch + place.c
        self.row = lax.div(place.s, 2)

    def put(self, lanes, sums, squares):
        self.first[self.me, 0:1, lanes] = sums
        self.first[self.me, 1:2, lanes] = squares

    def _near(self, d):
        return remote(self.first.at[self.me], self.first.at[self.me], self.send.at[d], self.one.at[self.me], self.p.near(d))

    def _far(self, d):
        n = 2 * self.p.n_ch
        return remote(self.second.at[self.row], self.second.at[self.row], self.send.at[n + d], self.two.at[self.row], self.p.far(d))

    def start(self):
        for d in range(1, 2 * self.p.n_ch):
            self._near(d).start()

    def relay(self):
        n = 2 * self.p.n_ch
        for d in range(1, n):
            other = lax.rem(self.me + d, n)
            slot = self.first.at[other]
            remote(slot, slot, self.send.at[d], self.one.at[other], self.p.near(d)).wait_recv()
        total = self.first[0]
        for q in range(1, n):
            total = total + self.first[q]
        self.second[self.row] = total
        for d in range(1, self.p.n_sp // 2):
            self._far(d).start()

    def finish(self):
        n = self.p.n_sp // 2
        for d in range(1, n):
            other = lax.rem(self.row + d, n)
            slot = self.second.at[other]
            remote(slot, slot, self.send.at[d], self.two.at[other], self.p.far(d)).wait_recv()
        total = self.second[0]
        for q in range(1, n):
            total = total + self.second[q]
        return total

    def drain(self):
        for d in range(1, 2 * self.p.n_ch):
            self._near(d).wait_send()
        for d in range(1, self.p.n_sp // 2):
            self._far(d).wait_send()


class Gather:
    def __init__(self, place, src, slot, send, recv):
        self.p, self.src, self.slot, self.send, self.recv = place, src, slot, send, recv

    def _own(self):
        return pltpu.make_async_copy(self.src, self.slot(self.p.c), self.recv.at[self.p.c])

    def _sibling(self):
        c = self.p.c
        return remote(self.src, self.slot(c), self.send.at[0], self.recv.at[c], self.p.sibling)

    def _direct(self, d):
        c = self.p.c
        return remote(self.src, self.slot(c), self.send.at[d], self.recv.at[c], (self.p.s, self.p.other_x(d)))

    def _forward(self, d):
        o = self.p.other_x(d)
        return remote(self.slot(o), self.slot(o), self.send.at[self.p.n_x + d - 1], self.recv.at[o], self.p.sibling)

    def _arrived(self, o):
        remote(self.slot(o), self.slot(o), self.send.at[0], self.recv.at[o], self.p.sibling).wait_recv()

    def start(self):
        for d in range(1, self.p.n_x):
            self._direct(d).start()
        self._sibling().start()
        self._own().start()

    def pump(self):
        for d in range(1, self.p.n_x):
            self._arrived(self.p.other_x(d))
            self._forward(d).start()

    def finish(self):
        self._own().wait()
        self._arrived(self.p.sib)
        for d in range(1, self.p.n_x):
            self._arrived(self.p.other_x(d) + 1 - 2 * self.p.k)

    def drain(self):
        self._sibling().wait_send()
        for d in range(1, self.p.n_x):
            self._direct(d).wait_send()
            self._forward(d).wait_send()


class Halo:
    def __init__(self, place, up, down, sems):
        self.p, self.up, self.down, self.sems = place, up, down, sems

    def _up(self):
        return remote(*self.up, self.sems.at[0], self.sems.at[1], (self.p.s - 1, self.p.c))

    def _down(self):
        return remote(*self.down, self.sems.at[2], self.sems.at[3], (self.p.s + 1, self.p.c))

    def _each(self, act_up, act_down):
        pl.when(self.p.s > 0)(act_up)
        pl.when(self.p.s < self.p.n_sp - 1)(act_down)

    def start(self):
        self._each(lambda: self._up().start(), lambda: self._down().start())

    def finish(self):
        self._each(lambda: self._down().wait_recv(), lambda: self._up().wait_recv())

    def drain(self):
        self._each(lambda: self._up().wait_send(), lambda: self._down().wait_send())


def over_rows(rows, step, body, init):
    def one(i, carry):
        return body(pl.ds(pl.multiple_of(i * step, step), step), carry)

    return lax.fori_loop(0, rows // step, one, init, unroll=2)


def fold(v):
    return jnp.sum(v.reshape(-1, 8, v.shape[1]), axis=0)


def moments(ref, lanes, rows):
    width = lanes.size

    def body(at, carry):
        v = ref[at, lanes]
        return carry[0] + fold(v), carry[1] + fold(v * v)

    zero = jnp.zeros((8, width), jnp.float32)
    a, b = over_rows(rows, 16, body, (zero, zero))
    return jnp.sum(a, axis=0, keepdims=True), jnp.sum(b, axis=0, keepdims=True)


def center_inverse(sums, squares, pixel_total):
    center = sums / pixel_total
    return center, lax.rsqrt(squares / pixel_total - center * center + EPS)


def cell_weights(position, cells):
    base = jnp.floor(position)
    upper = smooth_rise(position - base)
    return jnp.where(cells == base, 1.0 - upper, jnp.where(cells == base + 1.0, upper, 0.0))


def iota(shape, axis):
    return lax.broadcasted_iota(jnp.int32, shape, axis)


def set_identity(ref):
    n = ref.shape[0]
    for r in range(0, n, 128):
        same = iota((128, n), 0) + r == iota((128, n), 1)
        ref[r : r + 128, :] = jnp.where(same, 1.0, 0.0).astype(jnp.bfloat16)


def column_shift(v, j, columns):
    if j == 1:
        return v
    col = lax.rem(iota(v.shape, 0), columns)
    if j == 0:
        return jnp.where(col < 2, 0.0, pltpu.roll(v, 2, 0))
    return jnp.where(col >= columns - 2, 0.0, pltpu.roll(v, v.shape[0] - 2, 0))


def forward_kernel(geo, names, *refs):
    k = types.SimpleNamespace(**dict(zip(names, refs, strict=True)))
    p = Place(geo.n_sp, geo.n_ch)
    s, pixels, columns, mid = p.s, geo.pixels, geo.columns, geo.mid
    n_ch, wr, we, total = p.n_ch, geo.wr, geo.we, geo.pixel_total
    bf, f32 = jnp.bfloat16, jnp.float32

    def rows_of(ref, width):
        return lambda c: ref.at[:, pl.ds(pl.multiple_of(c * width, width), width), :]

    def slots_of(ref):
        return lambda c: ref.at[c]

    def gather(i, src, slot):
        return Gather(p, src, slot, k.gather_send.at[i], k.gather_recv.at[i])

    r1 = gather(0, k.r1, slots_of(k.r1_all))
    o1 = gather(1, k.o1, slots_of(k.o1_all))
    d1 = gather(2, k.d1, rows_of(k.d1_all, wr))
    e1 = gather(3, k.e1, slots_of(k.e1_all))
    r2 = gather(4, k.r2, slots_of(k.r2_all))
    d2 = gather(5, k.d2, rows_of(k.d2_all, wr))
    e2 = gather(6, k.e2, slots_of(k.e2_all))

    def all_sum(wide, i):
        if wide:
            parts = (k.wide_one, k.wide_two, k.wide_send, k.wide_recv_one, k.wide_recv_two)
        else:
            parts = (k.slim_one, k.slim_two, k.slim_send, k.slim_recv_one, k.slim_recv_two)
        return AllSum(p, *[part.at[i] for part in parts])

    saves = []

    def save(src, dst):
        copy = pltpu.make_async_copy(src, dst, k.save_sem.at[len(saves)])
        copy.start()
        saves.append(copy)

    def run_sum(task, totals, between=None):
        task.start()
        task.relay()
        if between is not None:
            between()
        totals[...] = task.finish()

    def reduce_matmul(x, weights, out):
        for c in range(n_ch):
            out[:, c * wr : (c + 1) * wr] = mm(x[...], weights[c])

    def activate(values, totals, gain, bias, out, first_row):
        center, inverse = center_inverse(totals[0:1, :], totals[1:2, :], total)
        scale = gain[...] * inverse
        shift = bias[...]

        def body(at, carry):
            v = (values[at, :] - center) * scale + shift
            row = pl.ds(pl.multiple_of(at.start + first_row, 16), at.size)
            out[row, :] = (v * sigmoid(v)).astype(bf)
            return carry

        over_rows(pixels, 16, body, 0)

    def expand(x, weights, out, task):
        for c in range(n_ch):
            lanes = pl.ds(c * we, we)
            out[:, lanes] = mm(x[...], weights[c])
            task.put(lanes, *moments(out, lanes, pixels))

    def leave(values, totals, gain, bias, residual, out):
        for start in range(0, geo.c_in, 512):
            lanes = pl.ds(start, 512)
            center, inverse = center_inverse(totals[0:1, lanes], totals[1:2, lanes], total)
            scale = gain[:, lanes] * inverse
            shift = bias[:, lanes]

            def body(at, carry):
                v = (values[at, lanes] - center) * scale + shift + residual[at, lanes].astype(f32)
                out[at, lanes] = (v * sigmoid(v)).astype(bf)
                return carry

            over_rows(pixels, 16, body, 0)

    slim = pl.ds(0, mid)

    p.barrier()
    r1.start()
    o1.start()
    set_identity(k.ident)
    r1.pump()
    d1.start()
    o1.pump()
    r1.finish()
    reduce_matmul(k.x, k.r1_all, k.reduced1)
    task1 = all_sum(False, 0)
    task1.put(slim, *moments(k.reduced1, slim, pixels))
    run_sum(task1, k.totals1a)
    activate(k.reduced1, k.totals1a, k.gain1a, k.bias1a, k.ext1, pixels)
    own = k.ext1.at[pixels : 2 * pixels]
    halo1 = Halo(p, (own, k.ext1.at[2 * pixels :]), (own, k.ext1.at[:pixels]), k.halo_sem.at[0])
    halo1.start()
    save(k.reduced1, k.reduced1_out)

    @pl.when(s == 0)
    def _():
        k.ext1[:pixels, :] = jnp.zeros((pixels, mid), bf)

    @pl.when(s == p.n_sp - 1)
    def _():
        k.ext1[2 * pixels :, :] = jnp.zeros((pixels, mid), bf)

    o1.finish()
    k.ext1_t[:, pixels : 2 * pixels] = mm_nt(k.ident[...], k.ext1[pixels : 2 * pixels, :]).astype(bf)
    halo1.finish()
    d1.pump()
    e1.start()
    r2.start()
    for part in (0, 2):
        at = slice(part * pixels, (part + 1) * pixels)
        k.ext1_t[:, at] = mm_nt(k.ident[...], k.ext1[at, :]).astype(bf)
    save(k.ext1, k.ext1_out)

    window = slice(4 * columns, 20 * columns)
    raw_all = jnp.zeros((9 * 32, 16 * columns), f32)
    for c in range(n_ch):
        raw_all += mm_nt(k.o1_all[c], k.ext1[window, c * wr : (c + 1) * wr])
    k.raw_all[...] = raw_all
    lane = iota((32, pixels), 1)
    col = lax.rem(lane, columns)
    raw = jnp.zeros((32, pixels), f32)
    for tap in range(9):
        i, j = tap // 3, tap % 3
        offset = (2 + 2 * i) * columns + 2 * (j - 1)
        part = k.raw_all[32 * tap : 32 * tap + 32, :]
        part = pltpu.roll(part, 16 * columns - offset, 1)[:, :pixels]
        if j == 0:
            part = jnp.where(col < 2, 0.0, part)
        if j == 2:
            part = jnp.where(col >= columns - 2, 0.0, part)
        raw += part
    k.bend[...] = jnp.tanh(raw)
    save(k.bend, k.bend_out)

    d1.finish()
    d2.start()
    save(k.d1_all, k.d1_all_out)
    k.spread1[...] = jnp.zeros((pixels, mid), f32)

    def tap_step(tap, carry):
        i, j = lax.div(tap, 3), lax.rem(tap, 3)
        lane = iota((1, pixels), 1)
        row = (lax.div(lane, columns) + 6 + 2 * i).astype(f32) + REACH * k.bend[pl.ds(tap, 1), :]
        across = (lax.rem(lane, columns) - 2 + 2 * j).astype(f32) + REACH * k.bend[pl.ds(tap + 16, 1), :]
        k.col_weight[...] = cell_weights(across, iota((columns, pixels), 0).astype(f32))
        base = jnp.floor(row)
        upper = smooth_rise(row - base)
        for r in range(3 * geo.height):
            weight = jnp.where(base == r, 1.0 - upper, jnp.where(base == r - 1, upper, 0.0))
            k.cells[r * columns : (r + 1) * columns, :] = (k.col_weight[...] * weight).astype(bf)
        k.cols1_t[tap] = mm(k.ext1_t[...], k.cells[...]).astype(bf)
        cols = mm_nt(k.ident[:pixels, :pixels], k.cols1_t[tap]).astype(bf)
        k.spread1[...] += mm(cols, k.d1_all[tap])
        return carry

    lax.fori_loop(0, 9, tap_step, 0)
    save(k.cols1_t, k.cols1_t_out)
    task2 = all_sum(False, 1)
    task2.put(slim, *moments(k.spread1, slim, pixels))
    run_sum(task2, k.totals1b, e1.pump)
    save(k.spread1, k.spread1_out)
    activate(k.spread1, k.totals1b, k.gain1b, k.bias1b, k.act, 0)
    e1.finish()
    save(k.e1_all, k.e1_all_out)
    task3 = all_sum(True, 0)
    expand(k.act, k.e1_all, k.expanded1, task3)
    run_sum(task3, k.totals1c, r2.pump)
    save(k.expanded1, k.expanded1_out)
    leave(k.expanded1, k.totals1c, k.gain1c, k.bias1c, k.x, k.middle)
    save(k.middle, k.middle_out)

    r2.finish()
    e2.start()
    save(k.r1_all, k.r1_all_out)
    save(k.r2_all, k.r2_all_out)
    save(k.o1_all, k.o1_all_out)
    reduce_matmul(k.middle, k.r2_all, k.reduced2)
    task4 = all_sum(False, 2)
    task4.put(slim, *moments(k.reduced2, slim, pixels))
    run_sum(task4, k.totals2a, d2.pump)
    save(k.reduced2, k.reduced2_out)
    rim = 2 * columns
    activate(k.reduced2, k.totals2a, k.gain2a, k.bias2a, k.ext2, rim)
    halo2 = Halo(
        p,
        (k.ext2.at[rim : 2 * rim], k.ext2.at[pixels + rim :]),
        (k.ext2.at[pixels : pixels + rim], k.ext2.at[:rim]),
        k.halo_sem.at[1],
    )
    halo2.start()

    @pl.when(s == 0)
    def _():
        k.ext2[:rim, :] = jnp.zeros((rim, mid), bf)

    @pl.when(s == p.n_sp - 1)
    def _():
        k.ext2[pixels + rim :, :] = jnp.zeros((rim, mid), bf)

    d2.finish()
    save(k.d2_all, k.d2_all_out)
    halo2.finish()

    def shift_row(r, carry):
        at = pl.ds(pl.multiple_of(r * columns, columns), columns)
        v = k.ext2[at, :].astype(f32)
        k.moved[0, at, :] = column_shift(v, 0, columns).astype(bf)
        k.moved[1, at, :] = v.astype(bf)
        k.moved[2, at, :] = column_shift(v, 2, columns).astype(bf)
        return carry

    lax.fori_loop(0, geo.height + 4, shift_row, 0)
    save(k.moved, k.moved_out)
    k.spread2[...] = jnp.zeros((pixels, mid), f32)

    def plain_step(tap, carry):
        i, j = lax.div(tap, 3), lax.rem(tap, 3)
        cols = k.moved[j, pl.ds(pl.multiple_of(i * rim, rim), pixels), :]
        k.spread2[...] += mm(cols, k.d2_all[tap])
        return carry

    lax.fori_loop(0, 9, plain_step, 0)
    task5 = all_sum(False, 3)
    task5.put(slim, *moments(k.spread2, slim, pixels))
    run_sum(task5, k.totals2b, e2.pump)
    save(k.spread2, k.spread2_out)
    activate(k.spread2, k.totals2b, k.gain2b, k.bias2b, k.act, 0)
    e2.finish()
    save(k.e2_all, k.e2_all_out)
    task6 = all_sum(True, 1)
    expand(k.act, k.e2_all, k.expanded2, task6)
    run_sum(task6, k.totals2c)
    save(k.expanded2, k.expanded2_out)
    leave(k.expanded2, k.totals2c, k.gain2c, k.bias2c, k.middle, k.last)
    save(k.last, k.last_out)

    for task in (r1, o1, d1, e1, r2, d2, e2, task1, task2, task3, task4, task5, task6, halo1, halo2):
        task.drain()
    for copy in saves:
        copy.wait()


def run_forward(geo, features, shards, norms):
    bf, f32 = jnp.bfloat16, jnp.float32
    n_ch, n_sp, mid, pixels, wr, we = geo.n_ch, geo.n_sp, geo.mid, geo.pixels, geo.wr, geo.we
    ext_rows = 3 * pixels
    rim_rows = pixels + 4 * geo.columns
    near, far = 2 * n_ch, n_sp // 2
    vmem = pl.BlockSpec(memory_space=pltpu.VMEM)
    anywhere = pl.BlockSpec(memory_space=pl.ANY)
    dma = pltpu.SemaphoreType.DMA
    v = pltpu.VMEM
    close = dict(x=features, **norms)
    kept = dict(
        r1_all=((n_ch, geo.c_in, wr), bf),
        o1_all=((n_ch, 9 * 32, wr), bf),
        d1_all=((9, mid, mid), bf),
        e1_all=((n_ch, mid, we), bf),
        r2_all=((n_ch, geo.c_in, wr), bf),
        d2_all=((9, mid, mid), bf),
        e2_all=((n_ch, mid, we), bf),
        reduced1=((pixels, mid), f32),
        ext1=((ext_rows, mid), bf),
        bend=((32, pixels), f32),
        cols1_t=((9, mid, pixels), bf),
        spread1=((pixels, mid), f32),
        expanded1=((pixels, geo.c_in), f32),
        middle=((pixels, geo.c_in), bf),
        reduced2=((pixels, mid), f32),
        moved=((3, rim_rows, mid), bf),
        spread2=((pixels, mid), f32),
        expanded2=((pixels, geo.c_in), f32),
        last=((pixels, geo.c_in), bf),
    )
    totals = dict(
        totals1a=(2, mid),
        totals1b=(2, mid),
        totals1c=(2, geo.c_in),
        totals2a=(2, mid),
        totals2b=(2, mid),
        totals2c=(2, geo.c_in),
    )
    scratch = dict(
        ident=v((mid, mid), bf),
        ext1_t=v((mid, ext_rows), bf),
        raw_all=v((9 * 32, 16 * geo.columns), f32),
        col_weight=v((geo.columns, pixels), f32),
        cells=v((ext_rows, pixels), bf),
        act=v((pixels, mid), bf),
        ext2=v((rim_rows, mid), bf),
        slim_one=v((4, near, 2, mid), f32),
        slim_two=v((4, far, 2, mid), f32),
        slim_send=dma((4, near + far)),
        slim_recv_one=dma((4, near)),
        slim_recv_two=dma((4, far)),
        wide_one=v((2, near, 2, geo.c_in), f32),
        wide_two=v((2, far, 2, geo.c_in), f32),
        wide_send=dma((2, near + far)),
        wide_recv_one=dma((2, near)),
        wide_recv_two=dma((2, far)),
        gather_send=dma((7, n_ch)),
        gather_recv=dma((7, n_ch)),
        halo_sem=dma((2, 4)),
        save_sem=dma((len(kept),)),
    )
    scratch |= {name: v(*what) for name, what in kept.items()}
    out_names = [f"{name}_out" for name in kept]
    results = pl.pallas_call(
        functools.partial(forward_kernel, geo, [*close, *shards, *out_names, *totals, *scratch]),
        out_shape=[jax.ShapeDtypeStruct(*what) for what in kept.values()]
        + [jax.ShapeDtypeStruct(shape, f32) for shape in totals.values()],
        in_specs=[vmem] * len(close) + [anywhere] * len(shards),
        out_specs=[anywhere] * len(kept) + [vmem] * len(totals),
        scratch_shapes=list(scratch.values()),
        compiler_params=pltpu.CompilerParams(
            collective_id=0, has_side_effects=True, vmem_limit_bytes=60 * MIB
        ),
    )(*close.values(), *shards.values())
    return types.SimpleNamespace(**dict(zip([*kept, *totals], results, strict=True)))


class Reduce:
    def __init__(self, place, stage, one, two, three, four, done, send, recv):
        self.p, self.stage, self.one, self.two, self.three, self.four = place, stage, one, two, three, four
        self.done = done
        self.send, self.recv = send, recv
        self.n_far = place.n_sp // 2
        self.half = stage.shape[2] // 2
        self.chunk = self.half // self.n_far
        self.row = lax.div(place.s, 2)
        self.pair = (place.s + 1 - 2 * place.y, place.c)
        self.mine = stage.at[place.k, place.x]
        self.at_x, self.at_out = 3, 3 + place.n_x
        self.at_back = self.at_out + self.n_far

    @staticmethod
    def sems(n_sp, n_ch):
        return 3 + n_ch // 2 + n_sp

    def _half(self, ref, y):
        return ref.at[pl.ds(pl.multiple_of(y * self.half, 16), self.half)]

    def _chunk(self, ref, z):
        return ref.at[pl.ds(pl.multiple_of(self.p.y * self.half + z * self.chunk, 16), self.chunk)]

    def _to_sibling(self):
        return remote(self.stage.at[1 - self.p.k], self.one, self.send.at[0], self.recv.at[0], self.p.sibling)

    def _to_x(self, d):
        other = lax.rem(self.p.x + d, self.p.n_x)
        return remote(
            self.stage.at[self.p.k, other],
            self.two.at[self.p.n_x - d - 1],
            self.send.at[self.at_x + d],
            self.recv.at[self.at_x + self.p.n_x - d],
            (self.p.s, 2 * other + self.p.k),
        )

    def _to_pair(self):
        return remote(self._half(self.mine, 1 - self.p.y), self.three, self.send.at[1], self.recv.at[1], self.pair)

    def _out(self, d):
        other = lax.rem(self.row + d, self.n_far)
        return remote(
            self._chunk(self.mine, other), self.four.at[self.row], self.send.at[self.at_out + d], self.recv.at[self.at_out + self.row], self.p.far(d)
        )

    def _back(self, d):
        return remote(
            self._chunk(self.done, self.row), self._chunk(self.done, self.row), self.send.at[self.at_back + d], self.recv.at[self.at_back + self.row], self.p.far(d)
        )

    def _pair_back(self, y):
        return remote(self._half(self.done, y), self._half(self.done, y), self.send.at[2], self.recv.at[2], self.pair)

    def _await(self, ref, sem):
        remote(ref, ref, self.send.at[0], sem, self.p.sibling).wait_recv()

    def _add(self, start, rows, pieces, out):
        step = max(n for n in (16, 32, 48, 64) if rows % n == 0)

        def one(i, carry):
            at = pl.ds(pl.multiple_of(start + i * step, 16), step)
            there = pl.ds(pl.multiple_of(i * step, 16), step)
            total = self.mine[at, :].astype(jnp.float32)
            for piece in pieces:
                total = total + piece[there, :].astype(jnp.float32)
            out[at, :] = total.astype(jnp.bfloat16)
            return carry

        lax.fori_loop(0, rows // step, one, 0)

    def s1(self):
        self._to_sibling().start()

    def s2(self):
        self._await(self.one, self.recv.at[0])
        rows = self.stage.shape[2]
        step = max(n for n in (16, 32, 48, 64) if rows % n == 0)
        for x in range(self.p.n_x):

            def one(i, carry):
                at = pl.ds(pl.multiple_of(i * step, 16), step)
                total = self.stage[self.p.k, x, at, :].astype(jnp.float32) + self.one[x, at, :].astype(jnp.float32)
                self.stage[self.p.k, x, at, :] = total.astype(jnp.bfloat16)
                return carry

            lax.fori_loop(0, rows // step, one, 0)
        for d in range(1, self.p.n_x):
            self._to_x(d).start()

    def s3(self):
        for d in range(1, self.p.n_x):
            self._await(self.two.at[d - 1], self.recv.at[self.at_x + d])
        self._add(0, self.stage.shape[2], [self.two.at[d - 1] for d in range(1, self.p.n_x)], self.mine)
        self._to_pair().start()

    def s4(self):
        self._await(self.three, self.recv.at[1])
        self._add(self.p.y * self.half, self.half, [self.three], self.mine)
        for d in range(1, self.n_far):
            self._out(d).start()

    def s5(self):
        others = [lax.rem(self.row + d, self.n_far) for d in range(1, self.n_far)]
        for other in others:
            self._await(self.four.at[other], self.recv.at[self.at_out + other])
        self._add(self.p.y * self.half + self.row * self.chunk, self.chunk, [self.four.at[other] for other in others], self.done)
        for d in range(1, self.n_far):
            self._back(d).start()

    def s6(self):
        for d in range(1, self.n_far):
            other = lax.rem(self.row + d, self.n_far)
            self._await(self._chunk(self.done, other), self.recv.at[self.at_back + other])
        self._pair_back(self.p.y).start()

    def s7(self):
        self._await(self._half(self.done, 1 - self.p.y), self.recv.at[2])
        self._to_sibling().wait_send()
        self._to_pair().wait_send()
        self._pair_back(self.p.y).wait_send()
        for d in range(1, self.p.n_x):
            self._to_x(d).wait_send()
        for d in range(1, self.n_far):
            self._out(d).wait_send()
            self._back(d).wait_send()


def slope_of(v):
    sigma = sigmoid(v)
    return sigma, sigma * (1.0 + v * (1.0 - sigma))


def backward_kernel(geo, names, *refs):
    k = types.SimpleNamespace(**dict(zip(names, refs, strict=True)))
    p = Place(geo.n_sp, geo.n_ch)
    s, pixels, columns, mid = p.s, geo.pixels, geo.columns, geo.mid
    n_ch, wr, we, total = p.n_ch, geo.wr, geo.we, geo.pixel_total
    bf, f32 = jnp.bfloat16, jnp.float32
    rim = 2 * columns
    slim = pl.ds(0, mid)
    count = [0, 0, 0]

    def load(src, dst):
        copy = pltpu.make_async_copy(src, dst, k.load_sem.at[count[0]])
        count[0] += 1
        copy.start()
        return copy

    def write_out(src, dst):
        copy = pltpu.make_async_copy(src, dst, k.out_sem.at[count[1]])
        count[1] += 1
        copy.start()
        return copy

    def reduction(*buffers):
        i = count[2]
        count[2] += 1
        return Reduce(p, *buffers, k.reduce_send.at[i], k.reduce_recv.at[i])

    def for_e():
        return reduction(k.stage_e, k.one_e, k.two_e, k.three_e, k.four_e, k.done_e)

    def for_d():
        return reduction(k.stage_d, k.one_d, k.two_d, k.three_d, k.four_d, k.done_d)

    def for_r():
        return reduction(k.stage_r, k.one_r, k.two_r, k.three_r, k.four_r, k.done_r)

    def all_sum(wide, i):
        if wide:
            parts = (k.wide_one, k.wide_two, k.wide_send, k.wide_recv_one, k.wide_recv_two)
        else:
            parts = (k.slim_one, k.slim_two, k.slim_send, k.slim_recv_one, k.slim_recv_two)
        return AllSum(p, *[part.at[i] for part in parts])

    def place_of(c):
        return c % 2, c // 2

    def norm_of(totals, lanes):
        return center_inverse(totals[0:1, lanes], totals[1:2, lanes], total)

    def block_end(upstream, totals, gain, bias, task):
        for start in range(0, geo.c_in, 512):
            lanes = pl.ds(start, 512)
            center, inverse = norm_of(totals, lanes)
            gain_row, bias_row = gain[:, lanes], bias[:, lanes]

            def body(at, carry):
                normed = (k.expanded[at, lanes] - center) * inverse
                joined = gain_row * normed + bias_row + k.inputs[at, lanes].astype(f32)
                grad = upstream(at, lanes) * slope_of(joined)[1]
                k.grad[at, lanes] = grad
                return carry[0] + fold(grad), carry[1] + fold(grad * normed)

            zero = jnp.zeros((8, 512), f32)
            a, b = over_rows(pixels, 16, body, (zero, zero))
            task.put(lanes, jnp.sum(a, axis=0, keepdims=True), jnp.sum(b, axis=0, keepdims=True))

    def third_norm(totals, grads, gain):
        for start in range(0, geo.c_in, 512):
            lanes = pl.ds(start, 512)
            center, inverse = norm_of(totals, lanes)
            scale = gain[:, lanes] * inverse
            bias_mean = grads[0:1, lanes] / total
            gain_mean = grads[1:2, lanes] / total

            def body(at, carry):
                normed = (k.expanded[at, lanes] - center) * inverse
                inner = k.grad[at, lanes] - bias_mean - normed * gain_mean
                k.third[at, lanes] = (scale * inner).astype(bf)
                return carry

            over_rows(pixels, 16, body, 0)

    def act_grad(values, totals, gain, bias, act, task):
        center, inverse = norm_of(totals, slim)
        gain_row, bias_row = gain[...], bias[...]

        def body(at, carry):
            normed = (values[at, :] - center) * inverse
            pre = gain_row * normed + bias_row
            sigma, slope = slope_of(pre)
            if act is not None:
                act[at, :] = (pre * sigma).astype(bf)
            grad = k.flow[at, :] * slope
            k.flow[at, :] = grad
            return carry[0] + fold(grad), carry[1] + fold(grad * normed)

        zero = jnp.zeros((8, mid), f32)
        a, b = over_rows(pixels, 16, body, (zero, zero))
        task.put(slim, jnp.sum(a, axis=0, keepdims=True), jnp.sum(b, axis=0, keepdims=True))

    def norm_grad(values, totals, grads, gain, out):
        center, inverse = norm_of(totals, slim)
        scale = gain[...] * inverse
        bias_mean = grads[0:1, :] / total
        gain_mean = grads[1:2, :] / total

        def body(at, carry):
            normed = (values[at, :] - center) * inverse
            out[at, :] = (scale * (k.flow[at, :] - bias_mean - normed * gain_mean)).astype(bf)
            return carry

        over_rows(pixels, 16, body, 0)

    def through_expand():
        for c in range(n_ch):
            part = mm_nt(k.third[:, c * we : (c + 1) * we], k.e[c])
            if c == 0:
                k.flow[...] = part
            else:
                k.flow[...] += part

    def expand_weights():
        k.act_t[...] = mm_nt(k.ident[...], k.act[...]).astype(bf)
        for c in range(n_ch):
            k.stage_e[place_of(c)] = mm(k.act_t[...], k.third[:, c * we : (c + 1) * we]).astype(bf)

    def stage_tap(tap, cols_t):
        product = mm(cols_t, k.low2[...])
        for c in range(n_ch):
            for q in range(mid // 128):
                at = pl.ds(pl.multiple_of(tap * wr + q * 9 * wr, 16), wr)
                piece = product[c * wr : (c + 1) * wr, q * 128 : (q + 1) * 128]
                k.stage_d[(*place_of(c), at)] = piece.astype(bf)

    def through_reduce():
        for start in range(0, geo.c_in, 512):
            rows = pl.ds(start, 512)
            for c in range(n_ch):
                k.grad[:, start : start + 512] += mm_nt(k.low1[:, c * wr : (c + 1) * wr], k.r[c, rows, :])

    def reduce_weights():
        for start in range(0, geo.c_in, 512):
            inputs_t = mm_nt(k.ident[...], k.inputs[:, start : start + 512]).astype(bf)
            product = mm(inputs_t, k.low1[...])
            for c in range(n_ch):
                k.stage_r[(*place_of(c), pl.ds(start, 512))] = product[:, c * wr : (c + 1) * wr].astype(bf)

    def deliver(task, buffer, out, piece):
        rows = out.shape[0]
        for start in range(0, rows, piece):
            buffer[...] = task.done[pl.ds(start, piece), :].astype(f32)
            write_out(buffer, out.at[pl.ds(start, piece)]).wait()

    def deliver_d(task, out):
        piece = 3 * wr
        for start in range(0, 9 * wr, piece):
            for q in range(mid // 128):
                at = pl.ds(q * 9 * wr + start, piece)
                k.out_d[:, q * 128 : (q + 1) * 128] = task.done[at, :].astype(f32)
            write_out(k.out_d, out.at[pl.ds(start, piece)]).wait()

    def rims_of(top, bottom, rows):
        halo = Halo(
            p,
            (k.rim_send.at[0, pl.ds(0, rows)], k.rim_recv.at[1, pl.ds(0, rows)]),
            (k.rim_send.at[1, pl.ds(0, rows)], k.rim_recv.at[0, pl.ds(0, rows)]),
            k.halo_sem.at[0 if rows == rim else 1],
        )
        k.rim_send[0, :rows, :] = k.spread_grad[top : top + rows, :].astype(bf)
        k.rim_send[1, :rows, :] = k.spread_grad[bottom : bottom + rows, :].astype(bf)
        return halo

    def add_rims(rows):
        @pl.when(s > 0)
        def _():
            k.flow[:rows, :] += k.rim_recv[0, :rows, :].astype(f32)

        @pl.when(s < p.n_sp - 1)
        def _():
            k.flow[pixels - rows :, :] += k.rim_recv[1, :rows, :].astype(f32)

    expanded2 = load(k.expanded2, k.expanded)
    middle = load(k.middle, k.inputs)
    cotangent = load(k.cotangent, k.third)
    e2 = load(k.e2, k.e)
    spread2 = load(k.spread2, k.spread)
    d2 = load(k.d2, k.d)
    moved2 = load(k.moved_in, k.moved)
    reduced2 = load(k.reduced2, k.reduced)
    r2 = load(k.r2, k.r)
    ext1 = load(k.ext1_in, k.ext1)
    o1 = load(k.o1_in, k.o1)
    p.barrier()
    set_identity(k.ident)
    for stage, rows in ((k.stage_o, 9 * 32), (k.stage_d, 9 * wr * mid // 128)):
        if stage.shape[2] > rows:
            for q in range(n_ch):
                spare = (stage.shape[2] - rows, stage.shape[3])
                stage[(*place_of(q), pl.ds(rows, spare[0]))] = jnp.zeros(spare, bf)

    expanded2.wait()
    middle.wait()
    cotangent.wait()
    sum2c = all_sum(True, 0)
    box = k.box[0:1, 0:1]
    block_end(lambda at, lanes: k.third[at, lanes].astype(f32) * box, k.totals2c, k.gain2c, k.bias2c, sum2c)
    sum2c.start()
    e2.wait()
    spread2.wait()
    d2.wait()
    moved2.wait()
    reduced2.wait()
    r2.wait()
    sum2c.relay()
    k.grads2c[...] = sum2c.finish()
    third_norm(k.totals2c, k.grads2c, k.gain2c)
    expanded1 = load(k.expanded1, k.expanded)
    through_expand()
    e1 = load(k.e1, k.e)
    sum2b = all_sum(False, 0)
    act_grad(k.spread, k.totals2b, k.gain2b, k.bias2b, k.act, sum2b)
    sum2b.start()
    expand_weights()
    work_e2 = for_e()
    work_e2.s1()
    sum2b.relay()
    k.grads2b[...] = sum2b.finish()
    norm_grad(k.spread, k.totals2b, k.grads2b, k.gain2b, k.low2)
    spread1 = load(k.spread1, k.spread)
    work_e2.s2()

    area = pixels + 2 * rim
    k.spread_grad[:area, :] = jnp.zeros((area, mid), f32)
    for j in range(3):
        k.spread_grad[area : 2 * area, :] = jnp.zeros((area, mid), f32)

        def row_step(i, carry):
            at = pl.ds(pl.multiple_of(area + i * rim, 16), pixels)
            k.spread_grad[at, :] += mm_nt(k.low2[...], k.d[3 * i + j])
            return carry

        lax.fori_loop(0, 3, row_step, 0)

        def shift_back(r, carry):
            at = pl.ds(pl.multiple_of(r * columns, 16), columns)
            there = pl.ds(pl.multiple_of(area + r * columns, 16), columns)
            k.spread_grad[at, :] += column_shift(k.spread_grad[there, :], 2 - j, columns)
            return carry

        lax.fori_loop(0, geo.height + 4, shift_back, 0)
    d1 = load(k.d1, k.d)
    halo2 = rims_of(0, pixels + rim, rim)
    halo2.start()
    k.flow[...] = k.spread_grad[rim : pixels + rim, :]

    def plain_tap(tap, carry):
        cols = k.moved[lax.rem(tap, 3), pl.ds(pl.multiple_of(lax.div(tap, 3) * rim, 16), pixels), :]
        stage_tap(tap, mm_nt(k.ident[...], cols).astype(bf))
        return carry

    lax.fori_loop(0, 9, plain_tap, 0)
    work_e2.s3()
    work_d2 = for_d()
    work_d2.s1()
    halo2.finish()
    add_rims(rim)
    sum2a = all_sum(False, 1)
    act_grad(k.reduced, k.totals2a, k.gain2a, k.bias2a, None, sum2a)
    sum2a.start()
    work_d2.s2()
    work_e2.s4()
    sum2a.relay()
    work_e2.s5()
    k.grads2a[...] = sum2a.finish()
    norm_grad(k.reduced, k.totals2a, k.grads2a, k.gain2a, k.low1)
    reduced1 = load(k.reduced1, k.reduced)
    through_reduce()
    r1 = load(k.r1, k.r)
    reduce_weights()
    features = load(k.features, k.inputs)
    work_r2 = for_r()
    work_r2.s1()
    work_e2.s6()

    expanded1.wait()
    features.wait()
    sum1c = all_sum(True, 1)
    block_end(lambda at, lanes: k.grad[at, lanes], k.totals1c, k.gain1c, k.bias1c, sum1c)
    sum1c.start()
    work_r2.s2()
    work_e2.s7()
    deliver(work_e2, k.out_e, k.grad_e2, geo.mid)
    sum1c.relay()
    e1.wait()
    spread1.wait()
    d1.wait()
    reduced1.wait()
    r1.wait()
    ext1.wait()
    o1.wait()
    k.grads1c[...] = sum1c.finish()
    third_norm(k.totals1c, k.grads1c, k.gain1c)
    through_expand()
    sum1b = all_sum(False, 2)
    act_grad(k.spread, k.totals1b, k.gain1b, k.bias1b, k.act, sum1b)
    sum1b.start()
    expand_weights()
    work_e1 = for_e()
    work_e1.s1()
    work_d2.s3()
    sum1b.relay()
    work_r2.s3()
    k.grads1b[...] = sum1b.finish()
    norm_grad(k.spread, k.totals1b, k.grads1b, k.gain1b, k.low2)
    work_d2.s4()
    work_e1.s2()

    k.spread_grad[...] = jnp.zeros((3 * pixels, mid), f32)
    k.raw_grad[...] = jnp.zeros((32, pixels), f32)

    def tap_step(tap, carry):
        @pl.when(tap == 5)
        def _():
            work_d2.s5()
            work_r2.s4()
            work_e1.s3()

        i, j = lax.div(tap, 3), lax.rem(tap, 3)
        lane = iota((1, pixels), 1)
        row = (lax.div(lane, columns) + 6 + 2 * i).astype(f32) + REACH * k.bend[pl.ds(tap, 1), :]
        across = (lax.rem(lane, columns) - 2 + 2 * j).astype(f32) + REACH * k.bend[pl.ds(tap + 16, 1), :]
        cell = iota((columns, pixels), 0).astype(f32)
        k.col_weight[...] = cell_weights(across, cell)
        row_base = jnp.floor(row)
        row_part = row - row_base
        row_upper = smooth_rise(row_part)
        row_rate = 6.0 * row_part * (1.0 - row_part)
        for r in range(3 * geo.height):
            weight = jnp.where(row_base == r, 1.0 - row_upper, jnp.where(row_base == r - 1, row_upper, 0.0))
            k.cells[r * columns : (r + 1) * columns, :] = (k.col_weight[...] * weight).astype(bf)
        k.cols_grad_t[...] = mm_nt(k.d[tap], k.low2[...]).astype(bf)
        k.spread_grad[...] += mm_nt(k.cells[...], k.cols_grad_t[...])
        k.matches[...] = mm(k.ext1[...], k.cols_grad_t[...])
        for start in range(0, pixels, 128):
            lanes = slice(start, start + 128)
            base, upper, rate = row_base[:, lanes], row_upper[:, lanes], row_rate[:, lanes]
            along = jnp.zeros((columns, 128), f32)
            down = jnp.zeros((columns, 128), f32)
            for r in range(3 * geo.height):
                match = k.matches[r * columns : (r + 1) * columns, lanes]
                at, after = base == r, base == r - 1
                along += match * jnp.where(at, 1.0 - upper, jnp.where(after, upper, 0.0))
                down += match * jnp.where(at, -rate, jnp.where(after, rate, 0.0))
            place = across[:, lanes]
            col_base = jnp.floor(place)
            col_part = place - col_base
            col_rate = 6.0 * col_part * (1.0 - col_part)
            cell_at = cell[:, lanes]
            col_slope = jnp.where(cell_at == col_base, -col_rate, jnp.where(cell_at == col_base + 1.0, col_rate, 0.0))
            here = iota((16, 128), 0) == tap
            by_row = jnp.sum(down * k.col_weight[:, lanes], axis=0, keepdims=True)
            by_col = jnp.sum(along * col_slope, axis=0, keepdims=True)
            k.raw_grad[:16, lanes] = jnp.where(here, by_row, k.raw_grad[:16, lanes])
            k.raw_grad[16:, lanes] = jnp.where(here, by_col, k.raw_grad[16:, lanes])
        return carry

    lax.fori_loop(0, 9, tap_step, 0)
    work_d2.s6()
    work_r2.s5()
    work_e1.s4()

    window = slice(4 * columns, 20 * columns)
    bend = k.bend[...]
    raw = k.raw_grad[...] * (REACH * (1.0 - bend * bend))
    col = lax.rem(iota((32, pixels), 1), columns)
    for tap in range(9):
        i, j = tap // 3, tap % 3
        offset = (2 + 2 * i) * columns + 2 * (j - 1)
        part = raw
        if j == 0:
            part = jnp.where(col < 2, 0.0, part)
        if j == 2:
            part = jnp.where(col >= columns - 2, 0.0, part)
        part = jnp.concatenate([part, jnp.zeros((32, 16 * columns - pixels), f32)], axis=1)
        k.placed[32 * tap : 32 * tap + 32, :] = pltpu.roll(part, offset, 1).astype(bf)
    for start in range(0, 16 * columns, 256):
        k.placed_t[start : start + 256, :] = mm_nt(k.ident[:256, :256], k.placed[:, start : start + 256]).astype(bf)
    for c in range(n_ch):
        k.spread_grad[window, c * wr : (c + 1) * wr] += mm(k.placed_t[...], k.o1[c])
    halo2.drain()
    halo1 = rims_of(0, 2 * pixels, pixels)
    halo1.start()
    k.flow[...] = k.spread_grad[pixels : 2 * pixels, :]
    product = mm(k.placed[...], k.ext1[window, :])
    for c in range(n_ch):
        k.stage_o[(*place_of(c), pl.ds(0, 9 * 32))] = product[:, c * wr : (c + 1) * wr].astype(bf)
    work_o1 = reduction(k.stage_o, k.one_o, k.two_o, k.three_o, k.four_o, k.done_o)
    work_o1.s1()
    work_d2.s7()
    deliver_d(work_d2, k.grad_d2)

    def fetch(tap, slot):
        return pltpu.make_async_copy(k.cols1.at[tap], k.cols_t.at[slot], k.fetch_sem.at[slot])

    fetch(0, 0).start()

    def sampled_tap(tap, carry):
        slot = lax.rem(tap, 2)

        @pl.when(tap < 8)
        def _():
            fetch(tap + 1, 1 - slot).start()

        fetch(tap, slot).wait()
        stage_tap(tap, k.cols_t[slot])
        return carry

    lax.fori_loop(0, 9, sampled_tap, 0)
    work_d1 = for_d()
    work_d1.s1()
    work_o1.s2()
    work_r2.s6()
    work_e1.s5()
    halo1.finish()
    add_rims(pixels)
    sum1a = all_sum(False, 3)
    act_grad(k.reduced, k.totals1a, k.gain1a, k.bias1a, None, sum1a)
    sum1a.start()
    work_d1.s2()
    work_o1.s3()
    work_e1.s6()
    sum1a.relay()
    work_r2.s7()
    deliver(work_r2, k.out_r, k.grad_r2, geo.c_in)
    k.grads1a[...] = sum1a.finish()
    norm_grad(k.reduced, k.totals1a, k.grads1a, k.gain1a, k.low1)
    reduce_weights()
    work_r1 = for_r()
    work_r1.s1()
    through_reduce()
    d_features = write_out(k.grad, k.d_features)
    work_r1.s2()
    work_o1.s4()
    work_e1.s7()
    deliver(work_e1, k.out_e, k.grad_e1, geo.mid)
    work_d1.s3()
    work_o1.s5()
    work_r1.s3()
    work_d1.s4()
    work_o1.s6()
    work_r1.s4()
    work_d1.s5()
    work_r1.s5()
    work_o1.s7()
    deliver(work_o1, k.out_o, k.grad_o1, 9 * 32)
    work_d1.s6()
    work_r1.s6()
    work_d1.s7()
    deliver_d(work_d1, k.grad_d1)
    work_r1.s7()
    deliver(work_r1, k.out_r, k.grad_r1, geo.c_in)
    for task in (sum2c, sum2b, sum2a, sum1c, sum1b, sum1a, halo1):
        task.drain()
    d_features.wait()


def run_backward(geo, kept, features, cotangent, box, norms):
    bf, f32 = jnp.bfloat16, jnp.float32
    n_ch, n_sp, mid, pixels, wr, we = geo.n_ch, geo.n_sp, geo.mid, geo.pixels, geo.wr, geo.we
    n_x, near, far = n_ch // 2, 2 * n_ch, n_sp // 2
    columns, c_in = geo.columns, geo.c_in
    rim = 2 * columns
    vmem = pl.BlockSpec(memory_space=pltpu.VMEM)
    anywhere = pl.BlockSpec(memory_space=pl.ANY)
    far_away = dict(
        features=features,
        cotangent=cotangent,
        expanded2=kept.expanded2,
        middle=kept.middle,
        e2=kept.e2_all,
        spread2=kept.spread2,
        d2=kept.d2_all,
        moved_in=kept.moved,
        reduced2=kept.reduced2,
        r2=kept.r2_all,
        expanded1=kept.expanded1,
        e1=kept.e1_all,
        spread1=kept.spread1,
        d1=kept.d1_all,
        cols1=kept.cols1_t,
        ext1_in=kept.ext1,
        reduced1=kept.reduced1,
        r1=kept.r1_all,
        o1_in=kept.o1_all,
    )
    close = dict(
        bend=kept.bend,
        box=box,
        totals1a=kept.totals1a,
        totals1b=kept.totals1b,
        totals1c=kept.totals1c,
        totals2a=kept.totals2a,
        totals2b=kept.totals2b,
        totals2c=kept.totals2c,
        **norms,
    )
    d_rows = -(-9 * wr * mid // 128 // (32 * far)) * 32 * far
    grads = dict(
        grad_e2=((mid, we), anywhere),
        grad_d2=((9 * wr, mid), anywhere),
        grad_r2=((c_in, wr), anywhere),
        grad_e1=((mid, we), anywhere),
        grad_d1=((9 * wr, mid), anywhere),
        grad_r1=((c_in, wr), anywhere),
        grad_o1=((9 * 32, wr), anywhere),
        d_features=((pixels, c_in), anywhere),
        grads2c=((2, c_in), vmem),
        grads2b=((2, mid), vmem),
        grads2a=((2, mid), vmem),
        grads1c=((2, c_in), vmem),
        grads1b=((2, mid), vmem),
        grads1a=((2, mid), vmem),
    )
    dma = pltpu.SemaphoreType.DMA
    v = pltpu.VMEM
    scratch = dict(
        e=v((n_ch, mid, we), bf),
        d=v((9, mid, mid), bf),
        r=v((n_ch, c_in, wr), bf),
        o1=v((n_ch, 9 * 32, wr), bf),
        expanded=v((pixels, c_in), f32),
        grad=v((pixels, c_in), f32),
        inputs=v((pixels, c_in), bf),
        third=v((pixels, c_in), bf),
        spread=v((pixels, mid), f32),
        reduced=v((pixels, mid), f32),
        flow=v((pixels, mid), f32),
        act=v((pixels, mid), bf),
        act_t=v((mid, pixels), bf),
        low1=v((pixels, mid), bf),
        low2=v((pixels, mid), bf),
        moved=v((3, pixels + 2 * rim, mid), bf),
        ext1=v((3 * pixels, mid), bf),
        cols_t=v((2, mid, pixels), bf),
        col_weight=v((columns, pixels), f32),
        cells=v((3 * pixels, pixels), bf),
        cols_grad_t=v((mid, pixels), bf),
        matches=v((3 * pixels, pixels), f32),
        spread_grad=v((3 * pixels, mid), f32),
        raw_grad=v((32, pixels), f32),
        placed=v((9 * 32, 16 * columns), bf),
        placed_t=v((16 * columns, 9 * 32), bf),
        ident=v((mid, mid), bf),
        rim_send=v((2, pixels, mid), bf),
        rim_recv=v((2, pixels, mid), bf),
        out_e=v((mid, we), f32),
        out_d=v((3 * wr, mid), f32),
        out_r=v((c_in, wr), f32),
        out_o=v((9 * 32, wr), f32),
        slim_one=v((4, near, 2, mid), f32),
        slim_two=v((4, far, 2, mid), f32),
        slim_send=dma((4, near + far)),
        slim_recv_one=dma((4, near)),
        slim_recv_two=dma((4, far)),
        wide_one=v((2, near, 2, c_in), f32),
        wide_two=v((2, far, 2, c_in), f32),
        wide_send=dma((2, near + far)),
        wide_recv_one=dma((2, near)),
        wide_recv_two=dma((2, far)),
        halo_sem=dma((2, 4)),
        load_sem=dma((20,)),
        out_sem=dma((16,)),
        fetch_sem=dma((2,)),
        reduce_send=dma((7, Reduce.sems(n_sp, n_ch))),
        reduce_recv=dma((7, Reduce.sems(n_sp, n_ch))),
    )

    def staging(rows, lanes):
        return (
            v((2, n_x, rows, lanes), bf),
            v((n_x, rows, lanes), bf),
            v((n_x - 1, rows, lanes), bf),
            v((rows // 2, lanes), bf),
            v((far, rows // n_sp, lanes), bf),
            v((rows, lanes), bf),
        )

    o_rows = -(-9 * 32 // (32 * far)) * 32 * far
    scratch["stage_e"], scratch["one_e"], scratch["two_e"], scratch["three_e"], scratch["four_e"], scratch["done_e"] = staging(mid, we)
    scratch["stage_d"], scratch["one_d"], scratch["two_d"], scratch["three_d"], scratch["four_d"], scratch["done_d"] = staging(d_rows, 128)
    scratch["stage_r"], scratch["one_r"], scratch["two_r"], scratch["three_r"], scratch["four_r"], scratch["done_r"] = staging(c_in, wr)
    scratch["stage_o"], scratch["one_o"], scratch["two_o"], scratch["three_o"], scratch["four_o"], scratch["done_o"] = staging(o_rows, wr)
    results = pl.pallas_call(
        functools.partial(backward_kernel, geo, [*far_away, *close, *grads, *scratch]),
        out_shape=[jax.ShapeDtypeStruct(shape, f32) for shape, _ in grads.values()],
        in_specs=[anywhere] * len(far_away) + [vmem] * len(close),
        out_specs=[spec for _, spec in grads.values()],
        scratch_shapes=list(scratch.values()),
        compiler_params=pltpu.CompilerParams(
            collective_id=1, has_side_effects=True, vmem_limit_bytes=63 * MIB
        ),
    )(*far_away.values(), *close.values())
    return types.SimpleNamespace(**dict(zip(grads, results, strict=True)))


def per_device(
    features,
    box_counts,
    b1_w_reduce,
    b1_gain1,
    b1_bias1,
    b1_w_offset,
    b1_w_deform,
    b1_gain2,
    b1_bias2,
    b1_w_expand,
    b1_gain3,
    b1_bias3,
    b2_w_reduce,
    b2_gain1,
    b2_bias1,
    b2_w_spatial,
    b2_gain2,
    b2_bias2,
    b2_w_expand,
    b2_gain3,
    b2_bias3,
    cotangent,
):
    images, height, columns, channels = features.shape
    n_sp, n_ch = lax.axis_size("sp"), lax.axis_size("ch")
    pixels = images * height * columns
    mid, wr = b1_w_deform.shape[2], b1_w_reduce.shape[1]
    geo = types.SimpleNamespace(
        n_sp=n_sp,
        n_ch=n_ch,
        pixels=pixels,
        height=height,
        columns=columns,
        mid=mid,
        c_in=channels,
        wr=wr,
        we=b1_w_expand.shape[1],
        pixel_total=pixels * n_sp * n_ch,
    )
    offset_w = jnp.moveaxis(b1_w_offset.reshape(9, wr, 9, 2), 1, 3)
    offset_w = jnp.pad(offset_w, ((0, 0), (0, 7), (0, 0), (0, 0)))
    offset_w = jnp.moveaxis(offset_w, 2, 1).reshape(9 * 32, wr)
    shards = dict(
        r1=b1_w_reduce,
        o1=offset_w,
        d1=b1_w_deform,
        e1=b1_w_expand,
        r2=b2_w_reduce,
        d2=b2_w_spatial,
        e2=b2_w_expand,
    )
    norms = dict(
        gain1a=b1_gain1,
        bias1a=b1_bias1,
        gain1b=b1_gain2,
        bias1b=b1_bias2,
        gain1c=b1_gain3,
        bias1c=b1_bias3,
        gain2a=b2_gain1,
        bias2a=b2_bias1,
        gain2b=b2_gain2,
        bias2b=b2_bias2,
        gain2c=b2_gain3,
        bias2c=b2_bias3,
    )
    norms = {name: vector.reshape(1, -1) for name, vector in norms.items()}
    entry = features.reshape(pixels, channels)
    kept = run_forward(geo, entry, shards, norms)
    counts = box_counts.astype(jnp.float32)
    local_counts = lax.dynamic_slice_in_dim(counts, lax.axis_index("ch") * images, images)
    image_scale = local_counts * counts.shape[0] / jnp.sum(counts)
    box = jnp.broadcast_to(image_scale.reshape(1, 1), (1, 128))
    g = run_backward(geo, kept, entry, cotangent.reshape(pixels, channels), box, norms)
    grad_offset = g.grad_o1.reshape(9, 2, 16, wr)[:, :, :9]
    grad_offset = jnp.transpose(grad_offset, (0, 3, 2, 1)).reshape(9, wr, 18)
    return (
        kept.last.reshape(features.shape),
        g.d_features.reshape(features.shape),
        g.grad_r1,
        g.grads1a[1],
        g.grads1a[0],
        grad_offset,
        g.grad_d1.reshape(9, wr, mid),
        g.grads1b[1],
        g.grads1b[0],
        g.grad_e1,
        g.grads1c[1],
        g.grads1c[0],
        g.grad_r2,
        g.grads2a[1],
        g.grads2a[0],
        g.grad_d2.reshape(9, wr, mid),
        g.grads2b[1],
        g.grads2b[0],
        g.grad_e2,
        g.grads2c[1],
        g.grads2c[0],
    )


def solution(mesh):
    return jax.shard_map(
        per_device,
        mesh=mesh,
        in_specs=(
            P("ch", "sp", None, None),
            P(),
            P(None, "ch"),
            P(),
            P(),
            P(None, "ch", None),
            P(None, "ch", None),
            P(),
            P(),
            P(None, "ch"),
            P(),
            P(),
            P(None, "ch"),
            P(),
            P(),
            P(None, "ch", None),
            P(),
            P(),
            P(None, "ch"),
            P(),
            P(),
            P("ch", "sp", None, None),
        ),
        out_specs=(
            P("ch", "sp", None, None),
            P("ch", "sp", None, None),
            P(None, "ch"),
            P(),
            P(),
            P(None, "ch", None),
            P(None, "ch", None),
            P(),
            P(),
            P(None, "ch"),
            P(),
            P(),
            P(None, "ch"),
            P(),
            P(),
            P(None, "ch", None),
            P(),
            P(),
            P(None, "ch"),
            P(),
            P(),
        ),
        check_vma=False,
    )
```

```python
import functools
import types

import jax
import jax.numpy as jnp
from jax import lax
from jax.experimental import pallas as pl
from jax.experimental.pallas import tpu as pltpu
from jax.sharding import PartitionSpec as P

EPS = 1e-05
REACH = 5.5
MESH = pl.DeviceIdType.MESH
MIB = 2**20


def mm(left, right):
    return jnp.dot(left, right, preferred_element_type=jnp.float32)


def mm_nt(left, right):
    return lax.dot_general(
        left, right, (((1,), (1,)), ((), ())), preferred_element_type=jnp.float32
    )


def smooth_rise(fraction):
    return fraction * fraction * (3.0 - 2.0 * fraction)


def sigmoid(v):
    return 1.0 / (1.0 + jnp.exp(-v))


class Place:
    def __init__(self, n_sp, n_ch):
        self.n_sp, self.n_ch, self.n_x = n_sp, n_ch, n_ch // 2
        self.s, self.c = lax.axis_index("sp"), lax.axis_index("ch")
        self.x, self.k = lax.div(self.c, 2), lax.rem(self.c, 2)
        self.y = lax.rem(self.s, 2)
        self.sib = self.c + 1 - 2 * self.k
        self.sibling = (self.s, self.sib)

    def other_x(self, d):
        return 2 * lax.rem(self.x + d, self.n_x) + self.k

    def near(self, d):
        q = lax.rem(self.y * self.n_ch + self.c + d, 2 * self.n_ch)
        return self.s - self.y + lax.div(q, self.n_ch), lax.rem(q, self.n_ch)

    def far(self, d):
        return lax.rem(self.s + 2 * d, self.n_sp), self.c

    def barrier(self):
        sem = pltpu.get_barrier_semaphore()

        def tell(device):
            pl.semaphore_signal(sem, inc=1, device_id=device, device_id_type=MESH)

        for d in range(1, 2 * self.n_ch):
            tell(self.near(d))
        for d in range(1, self.n_sp // 2):
            tell(self.far(d))
        diagonal = lax.rem(self.s + self.n_sp - 1 + 2 * self.y, self.n_sp)
        tell((diagonal, self.c))
        pl.semaphore_wait(sem, 2 * self.n_ch + self.n_sp // 2 - 1)


def remote(src, dst, send, recv, device):
    return pltpu.make_async_remote_copy(
        src_ref=src,
        dst_ref=dst,
        send_sem=send,
        recv_sem=recv,
        device_id=device,
        device_id_type=MESH,
    )


class AllSum:
    def __init__(self, place, first, second, send, recv_one, recv_two):
        self.p, self.first, self.second = place, first, second
        self.send, self.one, self.two = send, recv_one, recv_two
        self.me = place.y * place.n_ch + place.c
        self.row = lax.div(place.s, 2)

    def put(self, lanes, sums, squares):
        self.first[self.me, 0:1, lanes] = sums
        self.first[self.me, 1:2, lanes] = squares

    def _near(self, d):
        return remote(self.first.at[self.me], self.first.at[self.me], self.send.at[d], self.one.at[self.me], self.p.near(d))

    def _far(self, d):
        n = 2 * self.p.n_ch
        return remote(self.second.at[self.row], self.second.at[self.row], self.send.at[n + d], self.two.at[self.row], self.p.far(d))

    def start(self):
        for d in range(1, 2 * self.p.n_ch):
            self._near(d).start()

    def relay(self):
        n = 2 * self.p.n_ch
        for d in range(1, n):
            other = lax.rem(self.me + d, n)
            slot = self.first.at[other]
            remote(slot, slot, self.send.at[d], self.one.at[other], self.p.near(d)).wait_recv()
        total = self.first[0]
        for q in range(1, n):
            total = total + self.first[q]
        self.second[self.row] = total
        for d in range(1, self.p.n_sp // 2):
            self._far(d).start()

    def finish(self):
        n = self.p.n_sp // 2
        for d in range(1, n):
            other = lax.rem(self.row + d, n)
            slot = self.second.at[other]
            remote(slot, slot, self.send.at[d], self.two.at[other], self.p.far(d)).wait_recv()
        total = self.second[0]
        for q in range(1, n):
            total = total + self.second[q]
        return total

    def drain(self):
        for d in range(1, 2 * self.p.n_ch):
            self._near(d).wait_send()
        for d in range(1, self.p.n_sp // 2):
            self._far(d).wait_send()


class Gather:
    def __init__(self, place, src, slot, send, recv):
        self.p, self.src, self.slot, self.send, self.recv = place, src, slot, send, recv

    def _own(self):
        return pltpu.make_async_copy(self.src, self.slot(self.p.c), self.recv.at[self.p.c])

    def _sibling(self):
        c = self.p.c
        return remote(self.src, self.slot(c), self.send.at[0], self.recv.at[c], self.p.sibling)

    def _direct(self, d):
        c = self.p.c
        return remote(self.src, self.slot(c), self.send.at[d], self.recv.at[c], (self.p.s, self.p.other_x(d)))

    def _forward(self, d):
        o = self.p.other_x(d)
        return remote(self.slot(o), self.slot(o), self.send.at[self.p.n_x + d - 1], self.recv.at[o], self.p.sibling)

    def _arrived(self, o):
        remote(self.slot(o), self.slot(o), self.send.at[0], self.recv.at[o], self.p.sibling).wait_recv()

    def start(self):
        for d in range(1, self.p.n_x):
            self._direct(d).start()
        self._sibling().start()
        self._own().start()

    def pump(self):
        for d in range(1, self.p.n_x):
            self._arrived(self.p.other_x(d))
            self._forward(d).start()

    def finish(self):
        self._own().wait()
        self._arrived(self.p.sib)
        for d in range(1, self.p.n_x):
            self._arrived(self.p.other_x(d) + 1 - 2 * self.p.k)

    def drain(self):
        self._sibling().wait_send()
        for d in range(1, self.p.n_x):
            self._direct(d).wait_send()
            self._forward(d).wait_send()


class Halo:
    def __init__(self, place, up, down, sems):
        self.p, self.up, self.down, self.sems = place, up, down, sems

    def _up(self):
        return remote(*self.up, self.sems.at[0], self.sems.at[1], (self.p.s - 1, self.p.c))

    def _down(self):
        return remote(*self.down, self.sems.at[2], self.sems.at[3], (self.p.s + 1, self.p.c))

    def _each(self, act_up, act_down):
        pl.when(self.p.s > 0)(act_up)
        pl.when(self.p.s < self.p.n_sp - 1)(act_down)

    def start(self):
        self._each(lambda: self._up().start(), lambda: self._down().start())

    def finish(self):
        self._each(lambda: self._down().wait_recv(), lambda: self._up().wait_recv())

    def drain(self):
        self._each(lambda: self._up().wait_send(), lambda: self._down().wait_send())


def over_rows(rows, step, body, init):
    def one(i, carry):
        return body(pl.ds(pl.multiple_of(i * step, step), step), carry)

    return lax.fori_loop(0, rows // step, one, init, unroll=2)


def fold(v):
    return jnp.sum(v.reshape(-1, 8, v.shape[1]), axis=0)


def moments(ref, lanes, rows):
    width = lanes.size

    def body(at, carry):
        v = ref[at, lanes]
        return carry[0] + fold(v), carry[1] + fold(v * v)

    zero = jnp.zeros((8, width), jnp.float32)
    a, b = over_rows(rows, 16, body, (zero, zero))
    return jnp.sum(a, axis=0, keepdims=True), jnp.sum(b, axis=0, keepdims=True)


def center_inverse(sums, squares, pixel_total):
    center = sums / pixel_total
    return center, lax.rsqrt(squares / pixel_total - center * center + EPS)


def cell_weights(position, cells):
    base = jnp.floor(position)
    upper = smooth_rise(position - base)
    return jnp.where(cells == base, 1.0 - upper, jnp.where(cells == base + 1.0, upper, 0.0))


def iota(shape, axis):
    return lax.broadcasted_iota(jnp.int32, shape, axis)


def set_identity(ref):
    n = ref.shape[0]
    for r in range(0, n, 128):
        same = iota((128, n), 0) + r == iota((128, n), 1)
        ref[r : r + 128, :] = jnp.where(same, 1.0, 0.0).astype(jnp.bfloat16)


def column_shift(v, j, columns):
    if j == 1:
        return v
    col = lax.rem(iota(v.shape, 0), columns)
    if j == 0:
        return jnp.where(col < 2, 0.0, pltpu.roll(v, 2, 0))
    return jnp.where(col >= columns - 2, 0.0, pltpu.roll(v, v.shape[0] - 2, 0))


def forward_kernel(geo, names, *refs):
    k = types.SimpleNamespace(**dict(zip(names, refs, strict=True)))
    p = Place(geo.n_sp, geo.n_ch)
    s, pixels, columns, mid = p.s, geo.pixels, geo.columns, geo.mid
    n_ch, wr, we, total = p.n_ch, geo.wr, geo.we, geo.pixel_total
    bf, f32 = jnp.bfloat16, jnp.float32

    def rows_of(ref, width, first, taps):
        at = pl.ds(first, taps)
        return lambda c: ref.at[at, pl.ds(pl.multiple_of(c * width, width), width), :]

    def slots_of(ref):
        return lambda c: ref.at[c]

    def gather(i, src, slot):
        return Gather(p, src, slot, k.gather_send.at[i], k.gather_recv.at[i])

    r1 = gather(0, k.r1, slots_of(k.r1_all))
    o1 = gather(1, k.o1, slots_of(k.o1_all))
    d1a = gather(2, k.d1.at[pl.ds(0, 2)], rows_of(k.d1_all, wr, 0, 2))
    d1b = gather(3, k.d1.at[pl.ds(2, 7)], rows_of(k.d1_all, wr, 2, 7))
    e1 = gather(4, k.e1, slots_of(k.e1_all))
    r2 = gather(5, k.r2, slots_of(k.r2_all))
    d2a = gather(6, k.d2.at[pl.ds(0, 4)], rows_of(k.d2_all, wr, 0, 4))
    d2b = gather(7, k.d2.at[pl.ds(4, 5)], rows_of(k.d2_all, wr, 4, 5))
    e2 = gather(8, k.e2, slots_of(k.e2_all))

    def all_sum(wide, i):
        if wide:
            parts = (k.wide_one, k.wide_two, k.wide_send, k.wide_recv_one, k.wide_recv_two)
        else:
            parts = (k.slim_one, k.slim_two, k.slim_send, k.slim_recv_one, k.slim_recv_two)
        return AllSum(p, *[part.at[i] for part in parts])

    saves = []

    def save(src, dst):
        copy = pltpu.make_async_copy(src, dst, k.save_sem.at[len(saves)])
        copy.start()
        saves.append(copy)

    def run_sum(task, totals, *between):
        task.start()
        for one in between:
            one()
        task.relay()
        totals[...] = task.finish()

    def reduce_matmul(x, weights, out):
        for c in range(n_ch):
            out[:, c * wr : (c + 1) * wr] = mm(x[...], weights[c])

    def activate(values, totals, gain, bias, out, first_row):
        center, inverse = center_inverse(totals[0:1, :], totals[1:2, :], total)
        scale = gain[...] * inverse
        shift = bias[...]

        def body(at, carry):
            v = (values[at, :] - center) * scale + shift
            row = pl.ds(pl.multiple_of(at.start + first_row, 16), at.size)
            out[row, :] = (v * sigmoid(v)).astype(bf)
            return carry

        over_rows(pixels, 16, body, 0)

    def expand(x, weights, out, task):
        for c in range(n_ch):
            lanes = pl.ds(c * we, we)
            out[:, lanes] = mm(x[...], weights[c])
            task.put(lanes, *moments(out, lanes, pixels))

    def leave(values, totals, gain, bias, residual, out):
        for start in range(0, geo.c_in, 512):
            lanes = pl.ds(start, 512)
            center, inverse = center_inverse(totals[0:1, lanes], totals[1:2, lanes], total)
            scale = gain[:, lanes] * inverse
            shift = bias[:, lanes]

            def body(at, carry):
                v = (values[at, lanes] - center) * scale + shift + residual[at, lanes].astype(f32)
                out[at, lanes] = (v * sigmoid(v)).astype(bf)
                return carry

            over_rows(pixels, 16, body, 0)

    slim = pl.ds(0, mid)

    p.barrier()
    r1.start()
    o1.start()
    d1a.start()
    set_identity(k.ident)
    r1.pump()
    r1.finish()
    reduce_matmul(k.x, k.r1_all, k.reduced1)
    task1 = all_sum(False, 0)
    task1.put(slim, *moments(k.reduced1, slim, pixels))
    run_sum(task1, k.totals1a, d1b.start)
    o1.pump()
    activate(k.reduced1, k.totals1a, k.gain1a, k.bias1a, k.ext1, pixels)
    own = k.ext1.at[pixels : 2 * pixels]
    halo1 = Halo(p, (own, k.ext1.at[2 * pixels :]), (own, k.ext1.at[:pixels]), k.halo_sem.at[0])
    halo1.start()
    save(k.reduced1, k.reduced1_out)

    @pl.when(s == 0)
    def _():
        k.ext1[:pixels, :] = jnp.zeros((pixels, mid), bf)

    @pl.when(s == p.n_sp - 1)
    def _():
        k.ext1[2 * pixels :, :] = jnp.zeros((pixels, mid), bf)

    d1a.pump()
    o1.finish()
    k.ext1_t[:, pixels : 2 * pixels] = mm_nt(k.ident[...], k.ext1[pixels : 2 * pixels, :]).astype(bf)
    halo1.finish()
    e1.start()
    r2.start()
    d1b.pump()
    for part in (0, 2):
        at = slice(part * pixels, (part + 1) * pixels)
        k.ext1_t[:, at] = mm_nt(k.ident[...], k.ext1[at, :]).astype(bf)
    save(k.ext1, k.ext1_out)

    window = slice(4 * columns, 20 * columns)
    raw_all = jnp.zeros((9 * 32, 16 * columns), f32)
    for c in range(n_ch):
        raw_all += mm_nt(k.o1_all[c], k.ext1[window, c * wr : (c + 1) * wr])
    k.raw_all[...] = raw_all
    lane = iota((32, pixels), 1)
    col = lax.rem(lane, columns)
    raw = jnp.zeros((32, pixels), f32)
    for tap in range(9):
        i, j = tap // 3, tap % 3
        offset = (2 + 2 * i) * columns + 2 * (j - 1)
        part = k.raw_all[32 * tap : 32 * tap + 32, :]
        part = pltpu.roll(part, 16 * columns - offset, 1)[:, :pixels]
        if j == 0:
            part = jnp.where(col < 2, 0.0, part)
        if j == 2:
            part = jnp.where(col >= columns - 2, 0.0, part)
        raw += part
    k.bend[...] = jnp.tanh(raw)
    save(k.bend, k.bend_out)

    d1a.finish()
    d1b.finish()
    save(k.d1_all, k.d1_all_out)
    k.spread1[...] = jnp.zeros((pixels, mid), f32)

    def tap_step(tap, carry):
        i, j = lax.div(tap, 3), lax.rem(tap, 3)
        lane = iota((1, pixels), 1)
        row = (lax.div(lane, columns) + 6 + 2 * i).astype(f32) + REACH * k.bend[pl.ds(tap, 1), :]
        across = (lax.rem(lane, columns) - 2 + 2 * j).astype(f32) + REACH * k.bend[pl.ds(tap + 16, 1), :]
        k.col_weight[...] = cell_weights(across, iota((columns, pixels), 0).astype(f32))
        base = jnp.floor(row)
        upper = smooth_rise(row - base)
        for r in range(3 * geo.height):
            weight = jnp.where(base == r, 1.0 - upper, jnp.where(base == r - 1, upper, 0.0))
            k.cells[r * columns : (r + 1) * columns, :] = (k.col_weight[...] * weight).astype(bf)
        k.cols1_t[tap] = mm(k.ext1_t[...], k.cells[...]).astype(bf)
        cols = mm_nt(k.ident[:pixels, :pixels], k.cols1_t[tap]).astype(bf)
        k.spread1[...] += mm(cols, k.d1_all[tap])
        return carry

    lax.fori_loop(0, 9, tap_step, 0)
    save(k.cols1_t, k.cols1_t_out)
    task2 = all_sum(False, 1)
    task2.put(slim, *moments(k.spread1, slim, pixels))
    run_sum(task2, k.totals1b, d2a.start, e1.pump)
    save(k.spread1, k.spread1_out)
    activate(k.spread1, k.totals1b, k.gain1b, k.bias1b, k.act, 0)
    e1.finish()
    save(k.e1_all, k.e1_all_out)
    task3 = all_sum(True, 0)
    expand(k.act, k.e1_all, k.expanded1, task3)
    run_sum(task3, k.totals1c, d2b.start, r2.pump)
    save(k.expanded1, k.expanded1_out)
    leave(k.expanded1, k.totals1c, k.gain1c, k.bias1c, k.x, k.middle)
    save(k.middle, k.middle_out)

    r2.finish()
    save(k.r1_all, k.r1_all_out)
    save(k.r2_all, k.r2_all_out)
    save(k.o1_all, k.o1_all_out)
    reduce_matmul(k.middle, k.r2_all, k.reduced2)
    task4 = all_sum(False, 2)
    task4.put(slim, *moments(k.reduced2, slim, pixels))
    run_sum(task4, k.totals2a, e2.start, d2a.pump)
    save(k.reduced2, k.reduced2_out)
    rim = 2 * columns
    activate(k.reduced2, k.totals2a, k.gain2a, k.bias2a, k.ext2, rim)
    halo2 = Halo(
        p,
        (k.ext2.at[rim : 2 * rim], k.ext2.at[pixels + rim :]),
        (k.ext2.at[pixels : pixels + rim], k.ext2.at[:rim]),
        k.halo_sem.at[1],
    )
    halo2.start()

    @pl.when(s == 0)
    def _():
        k.ext2[:rim, :] = jnp.zeros((rim, mid), bf)

    @pl.when(s == p.n_sp - 1)
    def _():
        k.ext2[pixels + rim :, :] = jnp.zeros((rim, mid), bf)

    d2b.pump()
    d2a.finish()
    d2b.finish()
    save(k.d2_all, k.d2_all_out)
    halo2.finish()

    def shift_row(r, carry):
        at = pl.ds(pl.multiple_of(r * columns, columns), columns)
        v = k.ext2[at, :].astype(f32)
        k.moved[0, at, :] = column_shift(v, 0, columns).astype(bf)
        k.moved[1, at, :] = v.astype(bf)
        k.moved[2, at, :] = column_shift(v, 2, columns).astype(bf)
        return carry

    lax.fori_loop(0, geo.height + 4, shift_row, 0)
    save(k.moved, k.moved_out)
    k.spread2[...] = jnp.zeros((pixels, mid), f32)

    def plain_step(tap, carry):
        i, j = lax.div(tap, 3), lax.rem(tap, 3)
        cols = k.moved[j, pl.ds(pl.multiple_of(i * rim, rim), pixels), :]
        k.spread2[...] += mm(cols, k.d2_all[tap])
        return carry

    lax.fori_loop(0, 9, plain_step, 0)
    task5 = all_sum(False, 3)
    task5.put(slim, *moments(k.spread2, slim, pixels))
    run_sum(task5, k.totals2b, e2.pump)
    save(k.spread2, k.spread2_out)
    activate(k.spread2, k.totals2b, k.gain2b, k.bias2b, k.act, 0)
    e2.finish()
    save(k.e2_all, k.e2_all_out)
    task6 = all_sum(True, 1)
    expand(k.act, k.e2_all, k.expanded2, task6)
    run_sum(task6, k.totals2c)
    save(k.expanded2, k.expanded2_out)
    leave(k.expanded2, k.totals2c, k.gain2c, k.bias2c, k.middle, k.last)
    save(k.last, k.last_out)

    for task in (r1, o1, d1a, d1b, e1, r2, d2a, d2b, e2, task1, task2, task3, task4, task5, task6, halo1, halo2):
        task.drain()
    for copy in saves:
        copy.wait()


def run_forward(geo, features, shards, norms):
    bf, f32 = jnp.bfloat16, jnp.float32
    n_ch, n_sp, mid, pixels, wr, we = geo.n_ch, geo.n_sp, geo.mid, geo.pixels, geo.wr, geo.we
    ext_rows = 3 * pixels
    rim_rows = pixels + 4 * geo.columns
    near, far = 2 * n_ch, n_sp // 2
    vmem = pl.BlockSpec(memory_space=pltpu.VMEM)
    anywhere = pl.BlockSpec(memory_space=pl.ANY)
    dma = pltpu.SemaphoreType.DMA
    v = pltpu.VMEM
    close = dict(x=features, **norms)
    kept = dict(
        r1_all=((n_ch, geo.c_in, wr), bf),
        o1_all=((n_ch, 9 * 32, wr), bf),
        d1_all=((9, mid, mid), bf),
        e1_all=((n_ch, mid, we), bf),
        r2_all=((n_ch, geo.c_in, wr), bf),
        d2_all=((9, mid, mid), bf),
        e2_all=((n_ch, mid, we), bf),
        reduced1=((pixels, mid), f32),
        ext1=((ext_rows, mid), bf),
        bend=((32, pixels), f32),
        cols1_t=((9, mid, pixels), bf),
        spread1=((pixels, mid), f32),
        expanded1=((pixels, geo.c_in), f32),
        middle=((pixels, geo.c_in), bf),
        reduced2=((pixels, mid), f32),
        moved=((3, rim_rows, mid), bf),
        spread2=((pixels, mid), f32),
        expanded2=((pixels, geo.c_in), f32),
        last=((pixels, geo.c_in), bf),
    )
    totals = dict(
        totals1a=(2, mid),
        totals1b=(2, mid),
        totals1c=(2, geo.c_in),
        totals2a=(2, mid),
        totals2b=(2, mid),
        totals2c=(2, geo.c_in),
    )
    scratch = dict(
        ident=v((mid, mid), bf),
        ext1_t=v((mid, ext_rows), bf),
        raw_all=v((9 * 32, 16 * geo.columns), f32),
        col_weight=v((geo.columns, pixels), f32),
        cells=v((ext_rows, pixels), bf),
        act=v((pixels, mid), bf),
        ext2=v((rim_rows, mid), bf),
        slim_one=v((4, near, 2, mid), f32),
        slim_two=v((4, far, 2, mid), f32),
        slim_send=dma((4, near + far)),
        slim_recv_one=dma((4, near)),
        slim_recv_two=dma((4, far)),
        wide_one=v((2, near, 2, geo.c_in), f32),
        wide_two=v((2, far, 2, geo.c_in), f32),
        wide_send=dma((2, near + far)),
        wide_recv_one=dma((2, near)),
        wide_recv_two=dma((2, far)),
        gather_send=dma((9, n_ch)),
        gather_recv=dma((9, n_ch)),
        halo_sem=dma((2, 4)),
        save_sem=dma((len(kept),)),
    )
    scratch |= {name: v(*what) for name, what in kept.items()}
    out_names = [f"{name}_out" for name in kept]
    results = pl.pallas_call(
        functools.partial(forward_kernel, geo, [*close, *shards, *out_names, *totals, *scratch]),
        out_shape=[jax.ShapeDtypeStruct(*what) for what in kept.values()]
        + [jax.ShapeDtypeStruct(shape, f32) for shape in totals.values()],
        in_specs=[vmem] * len(close) + [anywhere] * len(shards),
        out_specs=[anywhere] * len(kept) + [vmem] * len(totals),
        scratch_shapes=list(scratch.values()),
        compiler_params=pltpu.CompilerParams(
            collective_id=0, has_side_effects=True, vmem_limit_bytes=60 * MIB
        ),
    )(*close.values(), *shards.values())
    return types.SimpleNamespace(**dict(zip([*kept, *totals], results, strict=True)))


class Reduce:
    def __init__(self, place, stage, one, two, three, four, total, done, send, recv):
        self.p, self.stage, self.one, self.two, self.three, self.four = place, stage, one, two, three, four
        self.total, self.done = total, done
        self.send, self.recv = send, recv
        self.n_far = place.n_sp // 2
        self.half = stage.shape[2] // 2
        self.chunk = self.half // self.n_far
        self.row = lax.div(place.s, 2)
        self.pair = (place.s + 1 - 2 * place.y, place.c)
        self.mine = stage.at[place.k, place.x]
        self.at_x, self.at_out = 3, 3 + place.n_x
        self.at_back = self.at_out + self.n_far

    nothing = types.SimpleNamespace(**dict.fromkeys(["s1", "s2", "s3", "s3_add", "s3_send", "s4", "s5", "s6", "s7"], lambda: None))

    @staticmethod
    def sems(n_sp, n_ch):
        return 3 + n_ch // 2 + n_sp

    def _half(self, ref, y):
        return ref.at[pl.ds(pl.multiple_of(y * self.half, 16), self.half)]

    def _chunk(self, ref, z):
        return ref.at[pl.ds(pl.multiple_of(self.p.y * self.half + z * self.chunk, 16), self.chunk)]

    def _to_sibling(self):
        return remote(self.stage.at[1 - self.p.k], self.one, self.send.at[0], self.recv.at[0], self.p.sibling)

    def _to_x(self, d):
        other = lax.rem(self.p.x + d, self.p.n_x)
        return remote(
            self.stage.at[self.p.k, other],
            self.two.at[self.p.n_x - d - 1],
            self.send.at[self.at_x + d],
            self.recv.at[self.at_x + self.p.n_x - d],
            (self.p.s, 2 * other + self.p.k),
        )

    def _to_pair(self):
        return remote(self._half(self.total, 1 - self.p.y), self.three, self.send.at[1], self.recv.at[1], self.pair)

    def _out(self, d):
        other = lax.rem(self.row + d, self.n_far)
        return remote(
            self._chunk(self.total, other), self.four.at[self.row], self.send.at[self.at_out + d], self.recv.at[self.at_out + self.row], self.p.far(d)
        )

    def _back(self, d):
        return remote(
            self._chunk(self.done, self.row), self._chunk(self.done, self.row), self.send.at[self.at_back + d], self.recv.at[self.at_back + self.row], self.p.far(d)
        )

    def _pair_back(self, y):
        return remote(self._half(self.done, y), self._half(self.done, y), self.send.at[2], self.recv.at[2], self.pair)

    def _await(self, ref, sem):
        remote(ref, ref, self.send.at[0], sem, self.p.sibling).wait_recv()

    def _add(self, source, start, rows, pieces, out):
        step = max(n for n in (16, 32, 48, 64) if rows % n == 0)

        def one(i, carry):
            at = pl.ds(pl.multiple_of(start + i * step, 16), step)
            there = pl.ds(pl.multiple_of(i * step, 16), step)
            total = source[at, :].astype(jnp.float32)
            for piece in pieces:
                total = total + piece[there, :].astype(jnp.float32)
            out[at, :] = total.astype(jnp.bfloat16)
            return carry

        lax.fori_loop(0, rows // step, one, 0)

    def s1(self):
        self._to_sibling().start()

    def s2(self):
        self._await(self.one, self.recv.at[0])
        rows = self.stage.shape[2]
        step = max(n for n in (16, 32, 48, 64) if rows % n == 0)
        for x in range(self.p.n_x):

            def one(i, carry):
                at = pl.ds(pl.multiple_of(i * step, 16), step)
                total = self.stage[self.p.k, x, at, :].astype(jnp.float32) + self.one[x, at, :].astype(jnp.float32)
                self.stage[self.p.k, x, at, :] = total.astype(jnp.bfloat16)
                return carry

            lax.fori_loop(0, rows // step, one, 0)
        for d in range(1, self.p.n_x):
            self._to_x(d).start()

    def s3_add(self):
        for d in range(1, self.p.n_x):
            self._await(self.two.at[d - 1], self.recv.at[self.at_x + d])
        pieces = [self.two.at[d - 1] for d in range(1, self.p.n_x)]
        self._add(self.mine, 0, self.stage.shape[2], pieces, self.total)
        self._to_sibling().wait_send()
        for d in range(1, self.p.n_x):
            self._to_x(d).wait_send()

    def s3_send(self):
        self._to_pair().start()

    def s3(self):
        self.s3_add()
        self.s3_send()

    def s4(self):
        self._await(self.three, self.recv.at[1])
        self._add(self.total, self.p.y * self.half, self.half, [self.three], self.total)
        for d in range(1, self.n_far):
            self._out(d).start()

    def s5(self):
        others = [lax.rem(self.row + d, self.n_far) for d in range(1, self.n_far)]
        for other in others:
            self._await(self.four.at[other], self.recv.at[self.at_out + other])
        start = self.p.y * self.half + self.row * self.chunk
        self._add(self.total, start, self.chunk, [self.four.at[other] for other in others], self.done)
        for d in range(1, self.n_far):
            self._back(d).start()

    def s6(self):
        for d in range(1, self.n_far):
            other = lax.rem(self.row + d, self.n_far)
            self._await(self._chunk(self.done, other), self.recv.at[self.at_back + other])
        self._pair_back(self.p.y).start()

    def s7(self):
        self._await(self._half(self.done, 1 - self.p.y), self.recv.at[2])
        self._to_pair().wait_send()
        self._pair_back(self.p.y).wait_send()
        for d in range(1, self.n_far):
            self._out(d).wait_send()
            self._back(d).wait_send()


def slope_of(v):
    sigma = sigmoid(v)
    return sigma, sigma * (1.0 + v * (1.0 - sigma))


def backward_kernel(geo, names, *refs):
    k = types.SimpleNamespace(**dict(zip(names, refs, strict=True)))
    p = Place(geo.n_sp, geo.n_ch)
    s, pixels, columns, mid = p.s, geo.pixels, geo.columns, geo.mid
    n_ch, wr, we, total = p.n_ch, geo.wr, geo.we, geo.pixel_total
    bf, f32 = jnp.bfloat16, jnp.float32
    rim = 2 * columns
    slim = pl.ds(0, mid)
    count = [0, 0, 0]

    cells = k.moved.at[pl.ds(0, 3 * pixels), pl.ds(0, pixels)]
    placed = k.third.at[pl.ds(0, 9 * 32), pl.ds(2 * mid, 16 * columns)]
    placed_t = k.moved.at[pl.ds(0, 16 * columns)]
    cols_grad_t = k.moved.at[pl.ds(3 * pixels, mid), pl.ds(0, pixels)]

    def load(src, dst):
        copy = pltpu.make_async_copy(src, dst, k.load_sem.at[count[0]])
        count[0] += 1
        copy.start()
        return copy

    def write_out(src, dst):
        copy = pltpu.make_async_copy(src, dst, k.out_sem.at[count[1]])
        count[1] += 1
        copy.start()
        return copy

    def reduction(*buffers):
        i = count[2]
        count[2] += 1
        return Reduce(p, *buffers, k.reduce_send.at[i], k.reduce_recv.at[i])

    def for_e():
        return reduction(k.stage_e, k.one_e, k.two_e, k.three_e, k.four_e, k.total_e, k.done_e)

    d_parts, tap_count = geo.d_parts, 9 // geo.d_parts

    def for_d():
        buffers = (k.stage_d, k.one_d, k.two_d, k.three_d, k.four_d, k.total_d, k.done_d)
        parts = [reduction(*[buffer.at[i] for buffer in buffers]) for i in range(d_parts)]
        return parts if d_parts == 3 else [Reduce.nothing, Reduce.nothing, parts[0]]

    def for_r():
        buffers = (k.stage_r, k.one_r, k.two_r, k.three_r, k.four_r, k.total_r, k.done_r)
        return [reduction(*[buffer.at[i] for buffer in buffers]) for i in range(4)]

    def all_sum(wide, i):
        if wide:
            parts = (k.wide_one, k.wide_two, k.wide_send, k.wide_recv_one, k.wide_recv_two)
        else:
            parts = (k.slim_one, k.slim_two, k.slim_send, k.slim_recv_one, k.slim_recv_two)
        return AllSum(p, *[part.at[i] for part in parts])

    def place_of(c):
        return c % 2, c // 2

    def norm_of(totals, lanes):
        return center_inverse(totals[0:1, lanes], totals[1:2, lanes], total)

    def block_end(upstream, totals, gain, bias, task):
        for start in range(0, geo.c_in, 512):
            lanes = pl.ds(start, 512)
            center, inverse = norm_of(totals, lanes)
            gain_row, bias_row = gain[:, lanes], bias[:, lanes]

            def body(at, carry):
                normed = (k.expanded[at, lanes] - center) * inverse
                joined = gain_row * normed + bias_row + k.inputs[at, lanes].astype(f32)
                grad = upstream(at, lanes) * slope_of(joined)[1]
                k.grad[at, lanes] = grad
                return carry[0] + fold(grad), carry[1] + fold(grad * normed)

            zero = jnp.zeros((8, 512), f32)
            a, b = over_rows(pixels, 16, body, (zero, zero))
            task.put(lanes, jnp.sum(a, axis=0, keepdims=True), jnp.sum(b, axis=0, keepdims=True))

    def third_norm(totals, grads, gain):
        for start in range(0, geo.c_in, 512):
            lanes = pl.ds(start, 512)
            center, inverse = norm_of(totals, lanes)
            scale = gain[:, lanes] * inverse
            bias_mean = grads[0:1, lanes] / total
            gain_mean = grads[1:2, lanes] / total

            def body(at, carry):
                normed = (k.expanded[at, lanes] - center) * inverse
                inner = k.grad[at, lanes] - bias_mean - normed * gain_mean
                k.third[at, lanes] = (scale * inner).astype(bf)
                return carry

            over_rows(pixels, 16, body, 0)

    def act_grad(values, totals, gain, bias, act, task):
        center, inverse = norm_of(totals, slim)
        gain_row, bias_row = gain[...], bias[...]

        def body(at, carry):
            normed = (values[at, :] - center) * inverse
            pre = gain_row * normed + bias_row
            sigma, slope = slope_of(pre)
            if act is not None:
                act[at, :] = (pre * sigma).astype(bf)
            grad = k.flow[at, :] * slope
            k.flow[at, :] = grad
            return carry[0] + fold(grad), carry[1] + fold(grad * normed)

        zero = jnp.zeros((8, mid), f32)
        a, b = over_rows(pixels, 16, body, (zero, zero))
        task.put(slim, jnp.sum(a, axis=0, keepdims=True), jnp.sum(b, axis=0, keepdims=True))

    def norm_grad(values, totals, grads, gain, out):
        center, inverse = norm_of(totals, slim)
        scale = gain[...] * inverse
        bias_mean = grads[0:1, :] / total
        gain_mean = grads[1:2, :] / total

        def body(at, carry):
            normed = (values[at, :] - center) * inverse
            out[at, :] = (scale * (k.flow[at, :] - bias_mean - normed * gain_mean)).astype(bf)
            return carry

        over_rows(pixels, 16, body, 0)

    def through_expand():
        for c in range(n_ch):
            part = mm_nt(k.third[:, c * we : (c + 1) * we], k.e[c])
            if c == 0:
                k.flow[...] = part
            else:
                k.flow[...] += part

    def expand_weights():
        k.act_t[...] = mm_nt(k.ident[...], k.low1[...]).astype(bf)
        for c in range(n_ch):
            k.stage_e[place_of(c)] = mm(k.act_t[...], k.third[:, c * we : (c + 1) * we]).astype(bf)

    def stage_tap(tap, cols_t):
        product = mm(cols_t, k.low2[...])
        part, inner = lax.div(tap, tap_count), lax.rem(tap, tap_count)
        for c in range(n_ch):
            for q in range(mid // 128):
                at = pl.ds(pl.multiple_of(inner * wr + q * tap_count * wr, 16), wr)
                piece = product[c * wr : (c + 1) * wr, q * 128 : (q + 1) * 128]
                k.stage_d[(part, *place_of(c), at)] = piece.astype(bf)

    def through_reduce():
        for start in range(0, geo.c_in, 512):
            rows = pl.ds(start, 512)
            for c in range(n_ch):
                k.grad[:, start : start + 512] += mm_nt(k.low1[:, c * wr : (c + 1) * wr], k.r[c, rows, :])

    def reduce_weights(work):
        for i, start in enumerate(range(0, geo.c_in, 512)):
            inputs_t = mm_nt(k.ident[...], k.inputs[:, start : start + 512]).astype(bf)
            product = mm(inputs_t, k.low1[...])
            for c in range(n_ch):
                k.stage_r[(i, *place_of(c))] = product[:, c * wr : (c + 1) * wr].astype(bf)
            work[i].s1()

    def deliver(task, buffer, out):
        buffer[...] = task.done[pl.ds(0, out.shape[0]), :].astype(f32)
        return write_out(buffer, out)

    def deliver_d(parts, out):
        piece = 3 * wr
        copies = []
        for i, task in enumerate(parts[-d_parts:]):
            for start in range(0, tap_count * wr, piece):
                turn = len(copies) % 2
                if len(copies) > 1:
                    copies[-2].wait()
                for q in range(mid // 128):
                    at = pl.ds(q * tap_count * wr + start, piece)
                    k.out_d[turn, :, q * 128 : (q + 1) * 128] = task.done[at, :].astype(f32)
                copies.append(write_out(k.out_d.at[turn], out.at[pl.ds(i * tap_count * wr + start, piece)]))

        return copies[-2:]

    def deliver_r(parts, out):
        return [deliver(task, k.out_r.at[i], out.at[pl.ds(512 * i, 512)]) for i, task in enumerate(parts)]

    def wait_all(copies):
        for copy in copies:
            copy.wait()

    def fetch(tap, slot):
        return pltpu.make_async_copy(k.cols1.at[tap], k.cols_t.at[slot], k.fetch_sem.at[slot])

    def sampled_tap(tap, carry):
        slot = lax.rem(tap, 2)

        @pl.when(tap < 8)
        def _():
            fetch(tap + 1, 1 - slot).start()

        fetch(tap, slot).wait()
        stage_tap(tap, k.cols_t[slot])
        return carry

    def rims_of(top, bottom, rows):
        halo = Halo(
            p,
            (k.third.at[pl.ds(0, rows), pl.ds(0, mid)], k.rim_recv.at[1, pl.ds(0, rows)]),
            (k.third.at[pl.ds(0, rows), pl.ds(mid, mid)], k.rim_recv.at[0, pl.ds(0, rows)]),
            k.halo_sem.at[0 if rows == rim else 1],
        )
        k.third[:rows, :mid] = k.spread_grad[top : top + rows, :].astype(bf)
        k.third[:rows, mid : 2 * mid] = k.spread_grad[bottom : bottom + rows, :].astype(bf)
        return halo

    def add_rims(rows):
        @pl.when(s > 0)
        def _():
            k.flow[:rows, :] += k.rim_recv[0, :rows, :].astype(f32)

        @pl.when(s < p.n_sp - 1)
        def _():
            k.flow[pixels - rows :, :] += k.rim_recv[1, :rows, :].astype(f32)

    expanded2 = load(k.expanded2, k.expanded)
    middle = load(k.middle, k.inputs)
    cotangent = load(k.cotangent, k.third)
    e2 = load(k.e2, k.e)
    spread2 = load(k.spread2, k.spread)
    d2 = load(k.d2, k.d)
    moved2 = load(k.moved_in, k.moved)
    reduced2 = load(k.reduced2, k.reduced)
    r2 = load(k.r2, k.r)
    ext1 = load(k.ext1_in, k.ext1)
    o1 = load(k.o1_in, k.o1)
    p.barrier()
    set_identity(k.ident)
    stages = [(k.stage_o, 9 * 32)] + [(k.stage_d.at[i], tap_count * wr * mid // 128) for i in range(d_parts)]
    for stage, rows in stages:
        if stage.shape[2] > rows:
            for q in range(n_ch):
                spare = (stage.shape[2] - rows, stage.shape[3])
                stage[(*place_of(q), pl.ds(rows, spare[0]))] = jnp.zeros(spare, bf)

    expanded2.wait()
    middle.wait()
    cotangent.wait()
    sum2c = all_sum(True, 0)
    box = k.box[0:1, 0:1]
    block_end(lambda at, lanes: k.third[at, lanes].astype(f32) * box, k.totals2c, k.gain2c, k.bias2c, sum2c)
    sum2c.start()
    e2.wait()
    spread2.wait()
    d2.wait()
    moved2.wait()
    reduced2.wait()
    r2.wait()
    sum2c.relay()
    k.grads2c[...] = sum2c.finish()
    third_norm(k.totals2c, k.grads2c, k.gain2c)
    expanded1 = load(k.expanded1, k.expanded)
    through_expand()
    e1 = load(k.e1, k.e)
    sum2b = all_sum(False, 0)
    act_grad(k.spread, k.totals2b, k.gain2b, k.bias2b, k.low1, sum2b)
    sum2b.start()
    expand_weights()
    work_e2 = for_e()
    work_e2.s1()
    sum2b.relay()
    k.grads2b[...] = sum2b.finish()
    norm_grad(k.spread, k.totals2b, k.grads2b, k.gain2b, k.low2)
    spread1 = load(k.spread1, k.spread)
    work_e2.s2()

    area = pixels + 2 * rim
    k.spread_grad[:area, :] = jnp.zeros((area, mid), f32)
    for j in range(3):
        k.spread_grad[area : 2 * area, :] = jnp.zeros((area, mid), f32)

        def row_step(i, carry):
            at = pl.ds(pl.multiple_of(area + i * rim, 16), pixels)
            k.spread_grad[at, :] += mm_nt(k.low2[...], k.d[3 * i + j])
            return carry

        lax.fori_loop(0, 3, row_step, 0)

        def shift_back(r, carry):
            at = pl.ds(pl.multiple_of(r * columns, 16), columns)
            there = pl.ds(pl.multiple_of(area + r * columns, 16), columns)
            k.spread_grad[at, :] += column_shift(k.spread_grad[there, :], 2 - j, columns)
            return carry

        lax.fori_loop(0, geo.height + 4, shift_back, 0)
    d1 = load(k.d1, k.d)
    halo2 = rims_of(0, pixels + rim, rim)
    halo2.start()
    k.flow[...] = k.spread_grad[rim : pixels + rim, :]

    def plain_tap(tap, carry):
        first = lax.rem(tap, 3) * (pixels + 2 * rim) + lax.div(tap, 3) * rim
        cols = k.moved[pl.ds(pl.multiple_of(first, 16), pixels), :]
        stage_tap(tap, mm_nt(k.ident[...], cols).astype(bf))
        return carry

    work_d2 = for_d()
    for i in range(3):
        lax.fori_loop(3 * i, 3 * i + 3, plain_tap, 0)
        work_d2[i].s1()
    halo2.finish()
    add_rims(rim)
    sum2a = all_sum(False, 1)
    act_grad(k.reduced, k.totals2a, k.gain2a, k.bias2a, None, sum2a)
    sum2a.start()
    work_d2[0].s2()
    work_e2.s3()
    work_d2[1].s2()
    sum2a.relay()
    k.grads2a[...] = sum2a.finish()
    norm_grad(k.reduced, k.totals2a, k.grads2a, k.gain2a, k.low1)
    reduced1 = load(k.reduced1, k.reduced)
    through_reduce()
    r1 = load(k.r1, k.r)
    work_e2.s4()
    work_r2 = for_r()
    reduce_weights(work_r2)
    features = load(k.features, k.inputs)

    expanded1.wait()
    features.wait()
    sum1c = all_sum(True, 1)
    block_end(lambda at, lanes: k.grad[at, lanes], k.totals1c, k.gain1c, k.bias1c, sum1c)
    sum1c.start()
    work_d2[2].s2()
    work_d2[0].s3()
    work_d2[1].s3()
    e1.wait()
    spread1.wait()
    d1.wait()
    reduced1.wait()
    r1.wait()
    ext1.wait()
    o1.wait()
    sum1c.relay()
    work_e2.s5()
    k.grads1c[...] = sum1c.finish()
    work_d2[0].s4()
    halo2.drain()
    third_norm(k.totals1c, k.grads1c, k.gain1c)
    through_expand()
    sum1b = all_sum(False, 2)
    act_grad(k.spread, k.totals1b, k.gain1b, k.bias1b, k.low1, sum1b)
    work_d2[2].s3_add()
    sum1b.start()
    for part in work_r2:
        part.s2()
    work_e2.s6()
    work_d2[2].s3_send()
    expand_weights()
    work_e1 = for_e()
    sum1b.relay()
    work_d2[1].s4()
    work_d2[0].s5()
    work_e1.s1()
    work_e2.s7()
    e2_copy = deliver(work_e2, k.out_e, k.grad_e2)
    fetch(0, 0).start()
    k.grads1b[...] = sum1b.finish()
    norm_grad(k.spread, k.totals1b, k.grads1b, k.gain1b, k.low2)
    work_e1.s2()
    work_d1 = for_d()
    for i in range(3):
        lax.fori_loop(3 * i, 3 * i + 3, sampled_tap, 0)
        work_d1[i].s1()

    k.spread_grad[...] = jnp.zeros((3 * pixels, mid), f32)
    k.raw_grad[...] = jnp.zeros((32, pixels), f32)

    def tap_step(tap, carry):
        @pl.when(tap == 0)
        def _():
            work_d1[0].s2()
            work_d2[2].s4()
            work_d2[1].s5()
            work_d2[0].s6()

        @pl.when(tap == 3)
        def _():
            for part in work_r2:
                part.s3()
            work_d2[2].s5()
            work_d2[1].s6()

        @pl.when(tap == 6)
        def _():
            for part in work_r2:
                part.s4()
            work_d2[2].s6()
            work_d1[1].s2()
            work_e1.s3()

        i, j = lax.div(tap, 3), lax.rem(tap, 3)
        lane = iota((1, pixels), 1)
        row = (lax.div(lane, columns) + 6 + 2 * i).astype(f32) + REACH * k.bend[pl.ds(tap, 1), :]
        across = (lax.rem(lane, columns) - 2 + 2 * j).astype(f32) + REACH * k.bend[pl.ds(tap + 16, 1), :]
        cell = iota((columns, pixels), 0).astype(f32)
        k.col_weight[...] = cell_weights(across, cell)
        row_base = jnp.floor(row)
        row_part = row - row_base
        row_upper = smooth_rise(row_part)
        row_rate = 6.0 * row_part * (1.0 - row_part)
        for r in range(3 * geo.height):
            weight = jnp.where(row_base == r, 1.0 - row_upper, jnp.where(row_base == r - 1, row_upper, 0.0))
            cells[r * columns : (r + 1) * columns, :] = (k.col_weight[...] * weight).astype(bf)
        cols_grad_t[...] = mm_nt(k.d[tap], k.low2[...]).astype(bf)
        k.spread_grad[...] += mm_nt(cells[...], cols_grad_t[...])
        for part in range(3):
            rows_at = slice(part * pixels, (part + 1) * pixels)
            k.expanded[:, 512 * part : 512 * part + pixels] = mm(k.ext1[rows_at, :], cols_grad_t[...])
        for start in range(0, pixels, 128):
            lanes = slice(start, start + 128)
            base, upper, rate = row_base[:, lanes], row_upper[:, lanes], row_rate[:, lanes]
            along = jnp.zeros((columns, 128), f32)
            down = jnp.zeros((columns, 128), f32)
            for r in range(3 * geo.height):
                row_at, col_at = r % geo.height * columns, r // geo.height * 512 + start
                match = k.expanded[row_at : row_at + columns, col_at : col_at + 128]
                at, after = base == r, base == r - 1
                along += match * jnp.where(at, 1.0 - upper, jnp.where(after, upper, 0.0))
                down += match * jnp.where(at, -rate, jnp.where(after, rate, 0.0))
            place = across[:, lanes]
            col_base = jnp.floor(place)
            col_part = place - col_base
            col_rate = 6.0 * col_part * (1.0 - col_part)
            cell_at = cell[:, lanes]
            col_slope = jnp.where(cell_at == col_base, -col_rate, jnp.where(cell_at == col_base + 1.0, col_rate, 0.0))
            here = iota((16, 128), 0) == tap
            by_row = jnp.sum(down * k.col_weight[:, lanes], axis=0, keepdims=True)
            by_col = jnp.sum(along * col_slope, axis=0, keepdims=True)
            k.raw_grad[:16, lanes] = jnp.where(here, by_row, k.raw_grad[:16, lanes])
            k.raw_grad[16:, lanes] = jnp.where(here, by_col, k.raw_grad[16:, lanes])
        return carry

    lax.fori_loop(0, 9, tap_step, 0)
    for part in work_r2:
        part.s5()
    for part in work_d2:
        part.s7()
    d2_copies = deliver_d(work_d2, k.grad_d2)

    window = slice(4 * columns, 20 * columns)
    bend = k.bend[...]
    raw = k.raw_grad[...] * (REACH * (1.0 - bend * bend))
    col = lax.rem(iota((32, pixels), 1), columns)
    for tap in range(9):
        i, j = tap // 3, tap % 3
        offset = (2 + 2 * i) * columns + 2 * (j - 1)
        part = raw
        if j == 0:
            part = jnp.where(col < 2, 0.0, part)
        if j == 2:
            part = jnp.where(col >= columns - 2, 0.0, part)
        part = jnp.concatenate([part, jnp.zeros((32, 16 * columns - pixels), f32)], axis=1)
        placed[32 * tap : 32 * tap + 32, :] = pltpu.roll(part, offset, 1).astype(bf)
    for start in range(0, 16 * columns, 256):
        placed_t[start : start + 256, : 9 * 32] = mm_nt(k.ident[:256, :256], placed[:, start : start + 256]).astype(bf)
    for c in range(n_ch):
        k.spread_grad[window, c * wr : (c + 1) * wr] += mm(placed_t[:, : 9 * 32], k.o1[c])
    halo1 = rims_of(0, 2 * pixels, pixels)
    halo1.start()
    k.flow[...] = k.spread_grad[pixels : 2 * pixels, :]
    product = mm(placed[...], k.ext1[window, :])
    for c in range(n_ch):
        k.stage_o[(*place_of(c), pl.ds(0, 9 * 32))] = product[:, c * wr : (c + 1) * wr].astype(bf)
    work_o1 = reduction(k.stage_o, k.one_o, k.two_o, k.three_o, k.four_o, k.total_o, k.done_o)
    work_o1.s1()

    work_e1.s4()
    work_d1[2].s2()
    halo1.finish()
    add_rims(pixels)
    sum1a = all_sum(False, 3)
    act_grad(k.reduced, k.totals1a, k.gain1a, k.bias1a, None, sum1a)
    sum1a.start()
    work_d1[0].s3()
    work_o1.s2()
    for part in work_r2:
        part.s6()
    sum1a.relay()
    work_e1.s5()
    k.grads1a[...] = sum1a.finish()
    norm_grad(k.reduced, k.totals1a, k.grads1a, k.gain1a, k.low1)
    work_r1 = for_r()
    reduce_weights(work_r1)
    work_d1[1].s3()
    through_reduce()
    for part in work_r1:
        part.s2()
    d_features = write_out(k.grad, k.d_features)
    for part in work_r2:
        part.s7()
    r2_copies = deliver_r(work_r2, k.grad_r2)
    work_e1.s6()
    work_d1[0].s4()
    work_o1.s3()
    work_d1[1].s4()
    work_d1[0].s5()
    work_o1.s4()
    work_d1[2].s3()
    work_d1[1].s5()
    work_d1[2].s4()
    work_r1[0].s3()
    work_d1[0].s6()
    work_o1.s5()
    work_r1[0].s4()
    work_r1[1].s3()
    work_d1[2].s5()
    work_d1[1].s6()
    work_e1.s7()
    e2_copy.wait()
    e1_copy = deliver(work_e1, k.out_e, k.grad_e1)
    work_r1[0].s5()
    work_r1[1].s4()
    work_r1[2].s3()
    work_o1.s6()
    work_d1[2].s6()
    work_r1[0].s6()
    work_r1[1].s5()
    work_r1[2].s4()
    work_r1[3].s3()
    work_r1[1].s6()
    work_r1[2].s5()
    work_r1[3].s4()
    for part in work_d1:
        part.s7()
    wait_all(d2_copies)
    d1_copies = deliver_d(work_d1, k.grad_d1)
    work_r1[2].s6()
    work_r1[3].s5()
    work_o1.s7()
    o1_copy = deliver(work_o1, k.out_o, k.grad_o1)
    work_r1[3].s6()
    for part in work_r1:
        part.s7()
    wait_all(r2_copies)
    wait_all(deliver_r(work_r1, k.grad_r1) + d1_copies)
    e1_copy.wait()
    o1_copy.wait()
    for task in (sum2c, sum2b, sum2a, sum1c, sum1b, sum1a, halo1):
        task.drain()
    d_features.wait()


def run_backward(geo, kept, features, cotangent, box, norms):
    bf, f32 = jnp.bfloat16, jnp.float32
    n_ch, n_sp, mid, pixels, wr, we = geo.n_ch, geo.n_sp, geo.mid, geo.pixels, geo.wr, geo.we
    n_x, near, far = n_ch // 2, 2 * n_ch, n_sp // 2
    columns, c_in = geo.columns, geo.c_in
    rim = 2 * columns
    vmem = pl.BlockSpec(memory_space=pltpu.VMEM)
    anywhere = pl.BlockSpec(memory_space=pl.ANY)
    far_away = dict(
        features=features,
        cotangent=cotangent,
        expanded2=kept.expanded2,
        middle=kept.middle,
        e2=kept.e2_all,
        spread2=kept.spread2,
        d2=kept.d2_all,
        moved_in=kept.moved.reshape(-1, mid),
        reduced2=kept.reduced2,
        r2=kept.r2_all,
        expanded1=kept.expanded1,
        e1=kept.e1_all,
        spread1=kept.spread1,
        d1=kept.d1_all,
        cols1=kept.cols1_t,
        ext1_in=kept.ext1,
        reduced1=kept.reduced1,
        r1=kept.r1_all,
        o1_in=kept.o1_all,
    )
    close = dict(
        bend=kept.bend,
        box=box,
        totals1a=kept.totals1a,
        totals1b=kept.totals1b,
        totals1c=kept.totals1c,
        totals2a=kept.totals2a,
        totals2b=kept.totals2b,
        totals2c=kept.totals2c,
        **norms,
    )
    grads = dict(
        grad_e2=((mid, we), anywhere),
        grad_d2=((9 * wr, mid), anywhere),
        grad_r2=((c_in, wr), anywhere),
        grad_e1=((mid, we), anywhere),
        grad_d1=((9 * wr, mid), anywhere),
        grad_r1=((c_in, wr), anywhere),
        grad_o1=((9 * 32, wr), anywhere),
        d_features=((pixels, c_in), anywhere),
        grads2c=((2, c_in), vmem),
        grads2b=((2, mid), vmem),
        grads2a=((2, mid), vmem),
        grads1c=((2, c_in), vmem),
        grads1b=((2, mid), vmem),
        grads1a=((2, mid), vmem),
    )
    dma = pltpu.SemaphoreType.DMA
    v = pltpu.VMEM
    scratch = dict(
        e=v((n_ch, mid, we), bf),
        d=v((9, mid, mid), bf),
        r=v((n_ch, c_in, wr), bf),
        o1=v((n_ch, 9 * 32, wr), bf),
        expanded=v((pixels, c_in), f32),
        grad=v((pixels, c_in), f32),
        inputs=v((pixels, c_in), bf),
        third=v((pixels, c_in), bf),
        spread=v((pixels, mid), f32),
        reduced=v((pixels, mid), f32),
        flow=v((pixels, mid), f32),
        act_t=v((mid, pixels), bf),
        low1=v((pixels, mid), bf),
        low2=v((pixels, mid), bf),
        moved=v((3 * (pixels + 2 * rim), mid), bf),
        ext1=v((3 * pixels, mid), bf),
        cols_t=v((2, mid, pixels), bf),
        col_weight=v((columns, pixels), f32),
        spread_grad=v((3 * pixels, mid), f32),
        raw_grad=v((32, pixels), f32),
        ident=v((mid, mid), bf),
        rim_recv=v((2, pixels, mid), bf),
        out_e=v((mid, we), f32),
        out_d=v((2, 3 * wr, mid), f32),
        out_r=v((4, 512, wr), f32),
        out_o=v((9 * 32, wr), f32),
        slim_one=v((4, near, 2, mid), f32),
        slim_two=v((4, far, 2, mid), f32),
        slim_send=dma((4, near + far)),
        slim_recv_one=dma((4, near)),
        slim_recv_two=dma((4, far)),
        wide_one=v((2, near, 2, c_in), f32),
        wide_two=v((2, far, 2, c_in), f32),
        wide_send=dma((2, near + far)),
        wide_recv_one=dma((2, near)),
        wide_recv_two=dma((2, far)),
        halo_sem=dma((2, 4)),
        load_sem=dma((20,)),
        out_sem=dma((24,)),
        fetch_sem=dma((2,)),
        reduce_send=dma((17, Reduce.sems(n_sp, n_ch))),
        reduce_recv=dma((17, Reduce.sems(n_sp, n_ch))),
    )

    def staging(rows, lanes, *parts):
        return (
            v((*parts, 2, n_x, rows, lanes), bf),
            v((*parts, n_x, rows, lanes), bf),
            v((*parts, n_x - 1, rows, lanes), bf),
            v((*parts, rows // 2, lanes), bf),
            v((*parts, far, rows // n_sp, lanes), bf),
            v((*parts, rows, lanes), bf),
            v((*parts, rows, lanes), bf),
        )

    def padded(rows):
        return -(-rows // (32 * far)) * 32 * far

    d_rows = padded(9 // geo.d_parts * wr * mid // 128)
    e, d, r, o = staging(mid, we), staging(d_rows, 128, geo.d_parts), staging(512, wr, 4), staging(padded(9 * 32), wr)
    scratch |= dict(stage_e=e[0], one_e=e[1], two_e=e[2], three_e=e[3], four_e=e[4], total_e=e[5], done_e=e[6])
    scratch |= dict(stage_d=d[0], one_d=d[1], two_d=d[2], three_d=d[3], four_d=d[4], total_d=d[5], done_d=d[6])
    scratch |= dict(stage_r=r[0], one_r=r[1], two_r=r[2], three_r=r[3], four_r=r[4], total_r=r[5], done_r=r[6])
    scratch |= dict(stage_o=o[0], one_o=o[1], two_o=o[2], three_o=o[3], four_o=o[4], total_o=o[5], done_o=o[6])
    results = pl.pallas_call(
        functools.partial(backward_kernel, geo, [*far_away, *close, *grads, *scratch]),
        out_shape=[jax.ShapeDtypeStruct(shape, f32) for shape, _ in grads.values()],
        in_specs=[anywhere] * len(far_away) + [vmem] * len(close),
        out_specs=[spec for _, spec in grads.values()],
        scratch_shapes=list(scratch.values()),
        compiler_params=pltpu.CompilerParams(
            collective_id=1, has_side_effects=True, vmem_limit_bytes=63 * MIB
        ),
    )(*far_away.values(), *close.values())
    return types.SimpleNamespace(**dict(zip(grads, results, strict=True)))


def per_device(
    features,
    box_counts,
    b1_w_reduce,
    b1_gain1,
    b1_bias1,
    b1_w_offset,
    b1_w_deform,
    b1_gain2,
    b1_bias2,
    b1_w_expand,
    b1_gain3,
    b1_bias3,
    b2_w_reduce,
    b2_gain1,
    b2_bias1,
    b2_w_spatial,
    b2_gain2,
    b2_bias2,
    b2_w_expand,
    b2_gain3,
    b2_bias3,
    cotangent,
):
    images, height, columns, channels = features.shape
    n_sp, n_ch = lax.axis_size("sp"), lax.axis_size("ch")
    pixels = images * height * columns
    mid, wr = b1_w_deform.shape[2], b1_w_reduce.shape[1]
    geo = types.SimpleNamespace(
        n_sp=n_sp,
        n_ch=n_ch,
        pixels=pixels,
        height=height,
        columns=columns,
        mid=mid,
        c_in=channels,
        wr=wr,
        we=b1_w_expand.shape[1],
        pixel_total=pixels * n_sp * n_ch,
        d_parts=3 if 3 * wr * mid // 128 % (16 * n_sp) == 0 else 1,
    )
    offset_w = jnp.moveaxis(b1_w_offset.reshape(9, wr, 9, 2), 1, 3)
    offset_w = jnp.pad(offset_w, ((0, 0), (0, 7), (0, 0), (0, 0)))
    offset_w = jnp.moveaxis(offset_w, 2, 1).reshape(9 * 32, wr)
    shards = dict(
        r1=b1_w_reduce,
        o1=offset_w,
        d1=b1_w_deform,
        e1=b1_w_expand,
        r2=b2_w_reduce,
        d2=b2_w_spatial,
        e2=b2_w_expand,
    )
    norms = dict(
        gain1a=b1_gain1,
        bias1a=b1_bias1,
        gain1b=b1_gain2,
        bias1b=b1_bias2,
        gain1c=b1_gain3,
        bias1c=b1_bias3,
        gain2a=b2_gain1,
        bias2a=b2_bias1,
        gain2b=b2_gain2,
        bias2b=b2_bias2,
        gain2c=b2_gain3,
        bias2c=b2_bias3,
    )
    norms = {name: vector.reshape(1, -1) for name, vector in norms.items()}
    entry = features.reshape(pixels, channels)
    kept = run_forward(geo, entry, shards, norms)
    counts = box_counts.astype(jnp.float32)
    local_counts = lax.dynamic_slice_in_dim(counts, lax.axis_index("ch") * images, images)
    image_scale = local_counts * counts.shape[0] / jnp.sum(counts)
    box = jnp.broadcast_to(image_scale.reshape(1, 1), (1, 128))
    g = run_backward(geo, kept, entry, cotangent.reshape(pixels, channels), box, norms)
    grad_offset = g.grad_o1.reshape(9, 2, 16, wr)[:, :, :9]
    grad_offset = jnp.transpose(grad_offset, (0, 3, 2, 1)).reshape(9, wr, 18)
    return (
        kept.last.reshape(features.shape),
        g.d_features.reshape(features.shape),
        g.grad_r1,
        g.grads1a[1],
        g.grads1a[0],
        grad_offset,
        g.grad_d1.reshape(9, wr, mid),
        g.grads1b[1],
        g.grads1b[0],
        g.grad_e1,
        g.grads1c[1],
        g.grads1c[0],
        g.grad_r2,
        g.grads2a[1],
        g.grads2a[0],
        g.grad_d2.reshape(9, wr, mid),
        g.grads2b[1],
        g.grads2b[0],
        g.grad_e2,
        g.grads2c[1],
        g.grads2c[0],
    )


def solution(mesh):
    return jax.shard_map(
        per_device,
        mesh=mesh,
        in_specs=(
            P("ch", "sp", None, None),
            P(),
            P(None, "ch"),
            P(),
            P(),
            P(None, "ch", None),
            P(None, "ch", None),
            P(),
            P(),
            P(None, "ch"),
            P(),
            P(),
            P(None, "ch"),
            P(),
            P(),
            P(None, "ch", None),
            P(),
            P(),
            P(None, "ch"),
            P(),
            P(),
            P("ch", "sp", None, None),
        ),
        out_specs=(
            P("ch", "sp", None, None),
            P("ch", "sp", None, None),
            P(None, "ch"),
            P(),
            P(),
            P(None, "ch", None),
            P(None, "ch", None),
            P(),
            P(),
            P(None, "ch"),
            P(),
            P(),
            P(None, "ch"),
            P(),
            P(),
            P(None, "ch", None),
            P(),
            P(),
            P(None, "ch"),
            P(),
            P(),
        ),
        check_vma=False,
    )
```

```python
import functools
import types

import jax
import jax.numpy as jnp
from jax import lax
from jax.experimental import pallas as pl
from jax.experimental.pallas import tpu as pltpu
from jax.sharding import PartitionSpec as P

EPS = 1e-05
REACH = 5.5
MESH = pl.DeviceIdType.MESH
MIB = 2**20


def mm(left, right):
    return jnp.dot(left, right, preferred_element_type=jnp.float32)


def mm_nt(left, right):
    return lax.dot_general(
        left, right, (((1,), (1,)), ((), ())), preferred_element_type=jnp.float32
    )


def smooth_rise(fraction):
    return fraction * fraction * (3.0 - 2.0 * fraction)


def sigmoid(v):
    return 1.0 / (1.0 + jnp.exp(-v))


class Place:
    def __init__(self, n_sp, n_ch):
        self.n_sp, self.n_ch, self.n_x = n_sp, n_ch, n_ch // 2
        self.s, self.c = lax.axis_index("sp"), lax.axis_index("ch")
        self.x, self.k = lax.div(self.c, 2), lax.rem(self.c, 2)
        self.y = lax.rem(self.s, 2)
        self.sib = self.c + 1 - 2 * self.k
        self.sibling = (self.s, self.sib)

    def other_x(self, d):
        return 2 * lax.rem(self.x + d, self.n_x) + self.k

    def near(self, d):
        q = lax.rem(self.y * self.n_ch + self.c + d, 2 * self.n_ch)
        return self.s - self.y + lax.div(q, self.n_ch), lax.rem(q, self.n_ch)

    def far(self, d):
        return lax.rem(self.s + 2 * d, self.n_sp), self.c

    def barrier(self):
        sem = pltpu.get_barrier_semaphore()

        def tell(device):
            pl.semaphore_signal(sem, inc=1, device_id=device, device_id_type=MESH)

        for d in range(1, 2 * self.n_ch):
            tell(self.near(d))
        for d in range(1, self.n_sp // 2):
            tell(self.far(d))
        diagonal = lax.rem(self.s + self.n_sp - 1 + 2 * self.y, self.n_sp)
        tell((diagonal, self.c))
        pl.semaphore_wait(sem, 2 * self.n_ch + self.n_sp // 2 - 1)


def remote(src, dst, send, recv, device):
    return pltpu.make_async_remote_copy(
        src_ref=src,
        dst_ref=dst,
        send_sem=send,
        recv_sem=recv,
        device_id=device,
        device_id_type=MESH,
    )


class AllSum:
    def __init__(self, place, first, second, send, recv_one, recv_two):
        self.p, self.first, self.second = place, first, second
        self.send, self.one, self.two = send, recv_one, recv_two
        self.me = place.y * place.n_ch + place.c
        self.row = lax.div(place.s, 2)

    def put(self, lanes, sums, squares):
        self.first[self.me, 0:1, lanes] = sums
        self.first[self.me, 1:2, lanes] = squares

    def _near(self, d):
        return remote(self.first.at[self.me], self.first.at[self.me], self.send.at[d], self.one.at[self.me], self.p.near(d))

    def _far(self, d):
        n = 2 * self.p.n_ch
        return remote(self.second.at[self.row], self.second.at[self.row], self.send.at[n + d], self.two.at[self.row], self.p.far(d))

    def start(self):
        for d in range(1, 2 * self.p.n_ch):
            self._near(d).start()

    def relay(self):
        n = 2 * self.p.n_ch
        for d in range(1, n):
            other = lax.rem(self.me + d, n)
            slot = self.first.at[other]
            remote(slot, slot, self.send.at[d], self.one.at[other], self.p.near(d)).wait_recv()
        total = self.first[0]
        for q in range(1, n):
            total = total + self.first[q]
        self.second[self.row] = total
        for d in range(1, self.p.n_sp // 2):
            self._far(d).start()

    def finish(self):
        n = self.p.n_sp // 2
        for d in range(1, n):
            other = lax.rem(self.row + d, n)
            slot = self.second.at[other]
            remote(slot, slot, self.send.at[d], self.two.at[other], self.p.far(d)).wait_recv()
        total = self.second[0]
        for q in range(1, n):
            total = total + self.second[q]
        return total

    def drain(self):
        for d in range(1, 2 * self.p.n_ch):
            self._near(d).wait_send()
        for d in range(1, self.p.n_sp // 2):
            self._far(d).wait_send()


class Gather:
    def __init__(self, place, src, slot, send, recv):
        self.p, self.src, self.slot, self.send, self.recv = place, src, slot, send, recv

    def _own(self):
        return pltpu.make_async_copy(self.src, self.slot(self.p.c), self.recv.at[self.p.c])

    def _sibling(self):
        c = self.p.c
        return remote(self.src, self.slot(c), self.send.at[0], self.recv.at[c], self.p.sibling)

    def _direct(self, d):
        c = self.p.c
        return remote(self.src, self.slot(c), self.send.at[d], self.recv.at[c], (self.p.s, self.p.other_x(d)))

    def _forward(self, d):
        o = self.p.other_x(d)
        return remote(self.slot(o), self.slot(o), self.send.at[self.p.n_x + d - 1], self.recv.at[o], self.p.sibling)

    def _arrived(self, o):
        remote(self.slot(o), self.slot(o), self.send.at[0], self.recv.at[o], self.p.sibling).wait_recv()

    def start(self):
        for d in range(1, self.p.n_x):
            self._direct(d).start()
        self._sibling().start()
        self._own().start()

    def pump(self):
        for d in range(1, self.p.n_x):
            self._arrived(self.p.other_x(d))
            self._forward(d).start()

    def finish(self):
        self._own().wait()
        self._arrived(self.p.sib)
        for d in range(1, self.p.n_x):
            self._arrived(self.p.other_x(d) + 1 - 2 * self.p.k)

    def drain(self):
        self._sibling().wait_send()
        for d in range(1, self.p.n_x):
            self._direct(d).wait_send()
            self._forward(d).wait_send()


class HalfGather:
    def __init__(self, place, src, slot, send, recv):
        self.p, self.src, self.slot, self.send, self.recv = place, src, slot, send, recv
        z = lax.div(place.s, 2)
        self.h = lax.rem(z, 2)
        self.beside = (place.s + 2 - 4 * self.h, place.c)

    def _own(self, h):
        c = self.p.c
        return pltpu.make_async_copy(self.src(h), self.slot(c, h), self.recv.at[2 * c + h])

    def _sibling(self, h):
        c = self.p.c
        return remote(self.src(h), self.slot(c, h), self.send.at[h], self.recv.at[2 * c + h], self.p.sibling)

    def _direct(self, d):
        c, h = self.p.c, self.h
        there = (self.p.s, self.p.other_x(d))
        return remote(self.src(h), self.slot(c, h), self.send.at[1 + d], self.recv.at[2 * c + h], there)

    def _pass(self, d, kind, h, device):
        o = self.p.other_x(d)
        sem = self.send.at[2 + (kind + 1) * (self.p.n_x - 1) + d - 1]
        return remote(self.slot(o, h), self.slot(o, h), sem, self.recv.at[2 * o + h], device)

    def _beside(self, d):
        return self._pass(d, 0, self.h, self.beside)

    def _forward(self, d):
        return self._pass(d, 1, self.h, self.p.sibling)

    def _second(self, d):
        return self._pass(d, 2, 1 - self.h, self.p.sibling)

    def _arrived(self, o, h):
        remote(self.slot(o, h), self.slot(o, h), self.send.at[0], self.recv.at[2 * o + h], self.p.sibling).wait_recv()

    def start(self):
        for d in range(1, self.p.n_x):
            self._direct(d).start()
        for h in range(2):
            self._sibling(h).start()
            self._own(h).start()

    def pump(self):
        for d in range(1, self.p.n_x):
            self._arrived(self.p.other_x(d), self.h)
            self._beside(d).start()
            self._forward(d).start()

    def pump_again(self):
        for d in range(1, self.p.n_x):
            self._arrived(self.p.other_x(d), 1 - self.h)
            self._second(d).start()

    def finish(self):
        for h in range(2):
            self._own(h).wait()
            self._arrived(self.p.sib, h)
            for d in range(1, self.p.n_x):
                self._arrived(self.p.other_x(d) + 1 - 2 * self.p.k, h)

    def drain(self):
        for h in range(2):
            self._sibling(h).wait_send()
        for d in range(1, self.p.n_x):
            for copy in (self._direct(d), self._beside(d), self._forward(d), self._second(d)):
                copy.wait_send()


class Halo:
    def __init__(self, place, up, down, sems):
        self.p, self.up, self.down, self.sems = place, up, down, sems

    def _up(self):
        return remote(*self.up, self.sems.at[0], self.sems.at[1], (self.p.s - 1, self.p.c))

    def _down(self):
        return remote(*self.down, self.sems.at[2], self.sems.at[3], (self.p.s + 1, self.p.c))

    def _each(self, act_up, act_down):
        pl.when(self.p.s > 0)(act_up)
        pl.when(self.p.s < self.p.n_sp - 1)(act_down)

    def start(self):
        self._each(lambda: self._up().start(), lambda: self._down().start())

    def finish(self):
        self._each(lambda: self._down().wait_recv(), lambda: self._up().wait_recv())

    def drain(self):
        self._each(lambda: self._up().wait_send(), lambda: self._down().wait_send())


def over_rows(rows, step, body, init):
    def one(i, carry):
        return body(pl.ds(pl.multiple_of(i * step, step), step), carry)

    return lax.fori_loop(0, rows // step, one, init, unroll=2)


def fold(v):
    return jnp.sum(v.reshape(-1, 8, v.shape[1]), axis=0)


def moments(ref, lanes, rows):
    width = lanes.size

    def body(at, carry):
        v = ref[at, lanes]
        return carry[0] + fold(v), carry[1] + fold(v * v)

    zero = jnp.zeros((8, width), jnp.float32)
    a, b = over_rows(rows, 16, body, (zero, zero))
    return jnp.sum(a, axis=0, keepdims=True), jnp.sum(b, axis=0, keepdims=True)


def center_inverse(sums, squares, pixel_total):
    center = sums / pixel_total
    return center, lax.rsqrt(squares / pixel_total - center * center + EPS)


def cell_weights(position, cells):
    base = jnp.floor(position)
    upper = smooth_rise(position - base)
    return jnp.where(cells == base, 1.0 - upper, jnp.where(cells == base + 1.0, upper, 0.0))


def iota(shape, axis):
    return lax.broadcasted_iota(jnp.int32, shape, axis)


def set_identity(ref):
    n = ref.shape[0]
    for r in range(0, n, 128):
        same = iota((128, n), 0) + r == iota((128, n), 1)
        ref[r : r + 128, :] = jnp.where(same, 1.0, 0.0).astype(jnp.bfloat16)


def column_shift(v, j, columns):
    if j == 1:
        return v
    col = lax.rem(iota(v.shape, 0), columns)
    if j == 0:
        return jnp.where(col < 2, 0.0, pltpu.roll(v, 2, 0))
    return jnp.where(col >= columns - 2, 0.0, pltpu.roll(v, v.shape[0] - 2, 0))


def forward_kernel(geo, names, *refs):
    k = types.SimpleNamespace(**dict(zip(names, refs, strict=True)))
    p = Place(geo.n_sp, geo.n_ch)
    s, pixels, columns, mid = p.s, geo.pixels, geo.columns, geo.mid
    n_ch, wr, we, total = p.n_ch, geo.wr, geo.we, geo.pixel_total
    bf, f32 = jnp.bfloat16, jnp.float32

    def rows_of(ref, width, first, taps):
        at = pl.ds(first, taps)
        return lambda c: ref.at[at, pl.ds(pl.multiple_of(c * width, width), width), :]

    def slots_of(ref):
        return lambda c: ref.at[c]

    def gather(i, src, slot):
        return Gather(p, src, slot, k.gather_send.at[i], k.gather_recv.at[i])

    r1 = gather(0, k.r1, slots_of(k.r1_all))
    o1 = gather(1, k.o1, slots_of(k.o1_all))
    d1a = gather(2, k.d1.at[pl.ds(0, 2)], rows_of(k.d1_all, wr, 0, 2))
    d1b = gather(3, k.d1.at[pl.ds(2, 7)], rows_of(k.d1_all, wr, 2, 7))
    e1 = gather(4, k.e1, slots_of(k.e1_all))

    def half_gather(i, src, slot):
        return HalfGather(p, src, slot, k.half_send.at[i], k.half_recv.at[i])

    def half_rows(ref, rows):
        return lambda h: ref.at[pl.ds(pl.multiple_of(h * rows, 16), rows)]

    def half_slots(ref, rows):
        return lambda c, h: ref.at[c, pl.ds(pl.multiple_of(h * rows, 16), rows)]

    r2 = half_gather(0, half_rows(k.r2, geo.c_in // 2), half_slots(k.r2_all, geo.c_in // 2))
    d2 = half_gather(
        1,
        lambda h: k.d2.at[:, pl.ds(pl.multiple_of(h * (wr // 2), 16), wr // 2), :],
        lambda c, h: k.d2_all.at[:, pl.ds(pl.multiple_of(c * wr + h * (wr // 2), 16), wr // 2), :],
    )
    e2 = half_gather(2, half_rows(k.e2, mid // 2), half_slots(k.e2_all, mid // 2))

    def all_sum(wide, i):
        if wide:
            parts = (k.wide_one, k.wide_two, k.wide_send, k.wide_recv_one, k.wide_recv_two)
        else:
            parts = (k.slim_one, k.slim_two, k.slim_send, k.slim_recv_one, k.slim_recv_two)
        return AllSum(p, *[part.at[i] for part in parts])

    saves = []

    def save(src, dst):
        copy = pltpu.make_async_copy(src, dst, k.save_sem.at[len(saves)])
        copy.start()
        saves.append(copy)

    def run_sum(task, totals, *between):
        task.start()
        for one in between:
            one()
        task.relay()
        totals[...] = task.finish()

    def reduce_matmul(x, weights, out):
        for c in range(n_ch):
            out[:, c * wr : (c + 1) * wr] = mm(x[...], weights[c])

    def activate(values, totals, gain, bias, out, first_row):
        center, inverse = center_inverse(totals[0:1, :], totals[1:2, :], total)
        scale = gain[...] * inverse
        shift = bias[...]

        def body(at, carry):
            v = (values[at, :] - center) * scale + shift
            row = pl.ds(pl.multiple_of(at.start + first_row, 16), at.size)
            out[row, :] = (v * sigmoid(v)).astype(bf)
            return carry

        over_rows(pixels, 16, body, 0)

    def expand(x, weights, out, task):
        for c in range(n_ch):
            lanes = pl.ds(c * we, we)
            out[:, lanes] = mm(x[...], weights[c])
            task.put(lanes, *moments(out, lanes, pixels))

    def leave(values, totals, gain, bias, residual, out):
        for start in range(0, geo.c_in, 512):
            lanes = pl.ds(start, 512)
            center, inverse = center_inverse(totals[0:1, lanes], totals[1:2, lanes], total)
            scale = gain[:, lanes] * inverse
            shift = bias[:, lanes]

            def body(at, carry):
                v = (values[at, lanes] - center) * scale + shift + residual[at, lanes].astype(f32)
                out[at, lanes] = (v * sigmoid(v)).astype(bf)
                return carry

            over_rows(pixels, 16, body, 0)

    slim = pl.ds(0, mid)

    p.barrier()
    r1.start()
    o1.start()
    d1a.start()
    set_identity(k.ident)
    r1.pump()
    r1.finish()
    reduce_matmul(k.x, k.r1_all, k.reduced1)
    task1 = all_sum(False, 0)
    task1.put(slim, *moments(k.reduced1, slim, pixels))
    run_sum(task1, k.totals1a, d1b.start, e1.start)
    o1.pump()
    activate(k.reduced1, k.totals1a, k.gain1a, k.bias1a, k.ext1, pixels)
    own = k.ext1.at[pixels : 2 * pixels]
    rim, rest = 2 * columns, pixels - 2 * columns

    def strip(start, size):
        return k.ext1.at[pl.ds(start, size)]

    halo1 = Halo(
        p,
        (strip(pixels, rim), strip(2 * pixels, rim)),
        (strip(2 * pixels - rim, rim), strip(rest, rim)),
        k.halo_sem.at[0],
    )
    halo1_far = Halo(
        p,
        (strip(pixels + rim, rest), strip(2 * pixels + rim, rest)),
        (strip(pixels, rest), strip(0, rest)),
        k.halo_sem.at[2],
    )
    halo1.start()
    halo1_far.start()
    save(k.reduced1, k.reduced1_out)

    @pl.when(s == 0)
    def _():
        k.ext1[:pixels, :] = jnp.zeros((pixels, mid), bf)

    @pl.when(s == p.n_sp - 1)
    def _():
        k.ext1[2 * pixels :, :] = jnp.zeros((pixels, mid), bf)

    d1a.pump()
    o1.finish()
    k.ext1_t[:, pixels : 2 * pixels] = mm_nt(k.ident[...], k.ext1[pixels : 2 * pixels, :]).astype(bf)
    edge = jnp.zeros((rim, mid), bf)
    k.window[:rim, :] = edge
    k.window[14 * columns :, :] = edge
    halo1.finish()
    k.window[rim : 14 * columns, :] = k.ext1[6 * columns : 18 * columns, :]
    raw_all = jnp.zeros((9 * 32, 16 * columns), f32)
    for c in range(n_ch):
        raw_all += mm_nt(k.o1_all[c], k.window[:, c * wr : (c + 1) * wr])
    k.raw_all[...] = raw_all
    lane = iota((32, pixels), 1)
    col = lax.rem(lane, columns)
    raw = jnp.zeros((32, pixels), f32)
    for tap in range(9):
        i, j = tap // 3, tap % 3
        offset = (2 + 2 * i) * columns + 2 * (j - 1)
        part = k.raw_all[32 * tap : 32 * tap + 32, :]
        part = pltpu.roll(part, 16 * columns - offset, 1)[:, :pixels]
        if j == 0:
            part = jnp.where(col < 2, 0.0, part)
        if j == 2:
            part = jnp.where(col >= columns - 2, 0.0, part)
        raw += part
    k.bend[...] = jnp.tanh(raw)
    save(k.bend, k.bend_out)

    halo1_far.finish()
    r2.start()
    d1b.pump()
    for part in (0, 2):
        at = slice(part * pixels, (part + 1) * pixels)
        k.ext1_t[:, at] = mm_nt(k.ident[...], k.ext1[at, :]).astype(bf)
    save(k.ext1, k.ext1_out)
    d1a.finish()
    d1b.finish()
    save(k.d1_all, k.d1_all_out)
    k.spread1[...] = jnp.zeros((pixels, mid), f32)

    def tap_step(tap, carry):
        i, j = lax.div(tap, 3), lax.rem(tap, 3)
        lane = iota((1, pixels), 1)
        row = (lax.div(lane, columns) + 6 + 2 * i).astype(f32) + REACH * k.bend[pl.ds(tap, 1), :]
        across = (lax.rem(lane, columns) - 2 + 2 * j).astype(f32) + REACH * k.bend[pl.ds(tap + 16, 1), :]
        k.col_weight[...] = cell_weights(across, iota((columns, pixels), 0).astype(f32))
        base = jnp.floor(row)
        upper = smooth_rise(row - base)
        for r in range(3 * geo.height):
            weight = jnp.where(base == r, 1.0 - upper, jnp.where(base == r - 1, upper, 0.0))
            k.cells[r * columns : (r + 1) * columns, :] = (k.col_weight[...] * weight).astype(bf)
        k.cols1_t[tap] = mm(k.ext1_t[...], k.cells[...]).astype(bf)
        cols = mm_nt(k.ident[:pixels, :pixels], k.cols1_t[tap]).astype(bf)
        k.spread1[...] += mm(cols, k.d1_all[tap])
        return carry

    lax.fori_loop(0, 9, tap_step, 0)
    save(k.cols1_t, k.cols1_t_out)
    task2 = all_sum(False, 1)
    task2.put(slim, *moments(k.spread1, slim, pixels))
    task2.start()
    d2.start()
    e1.pump()
    task2.relay()
    r2.pump()
    k.totals1b[...] = task2.finish()
    save(k.spread1, k.spread1_out)
    activate(k.spread1, k.totals1b, k.gain1b, k.bias1b, k.act, 0)
    e1.finish()
    save(k.e1_all, k.e1_all_out)
    task3 = all_sum(True, 0)
    expand(k.act, k.e1_all, k.expanded1, task3)
    task3.start()
    r2.pump_again()
    task3.relay()
    d2.pump()
    k.totals1c[...] = task3.finish()
    save(k.expanded1, k.expanded1_out)
    leave(k.expanded1, k.totals1c, k.gain1c, k.bias1c, k.x, k.middle)
    save(k.middle, k.middle_out)

    r2.finish()
    save(k.r1_all, k.r1_all_out)
    save(k.r2_all, k.r2_all_out)
    save(k.o1_all, k.o1_all_out)
    reduce_matmul(k.middle, k.r2_all, k.reduced2)
    task4 = all_sum(False, 2)
    task4.put(slim, *moments(k.reduced2, slim, pixels))
    task4.start()
    e2.start()
    task4.relay()
    k.totals2a[...] = task4.finish()
    d2.pump_again()
    save(k.reduced2, k.reduced2_out)
    activate(k.reduced2, k.totals2a, k.gain2a, k.bias2a, k.ext2, rim)
    halo2 = Halo(
        p,
        (k.ext2.at[rim : 2 * rim], k.ext2.at[pixels + rim :]),
        (k.ext2.at[pixels : pixels + rim], k.ext2.at[:rim]),
        k.halo_sem.at[1],
    )
    halo2.start()

    @pl.when(s == 0)
    def _():
        k.ext2[:rim, :] = jnp.zeros((rim, mid), bf)

    @pl.when(s == p.n_sp - 1)
    def _():
        k.ext2[pixels + rim :, :] = jnp.zeros((rim, mid), bf)

    e2.pump()
    d2.finish()
    save(k.d2_all, k.d2_all_out)
    halo2.finish()

    def shift_row(r, carry):
        at = pl.ds(pl.multiple_of(r * columns, columns), columns)
        v = k.ext2[at, :].astype(f32)
        k.moved[0, at, :] = column_shift(v, 0, columns).astype(bf)
        k.moved[1, at, :] = v.astype(bf)
        k.moved[2, at, :] = column_shift(v, 2, columns).astype(bf)
        return carry

    lax.fori_loop(0, geo.height + 4, shift_row, 0)
    save(k.moved, k.moved_out)
    k.spread2[...] = jnp.zeros((pixels, mid), f32)

    def plain_step(tap, carry):
        i, j = lax.div(tap, 3), lax.rem(tap, 3)
        cols = k.moved[j, pl.ds(pl.multiple_of(i * rim, rim), pixels), :]
        k.spread2[...] += mm(cols, k.d2_all[tap])
        return carry

    lax.fori_loop(0, 9, plain_step, 0)
    task5 = all_sum(False, 3)
    task5.put(slim, *moments(k.spread2, slim, pixels))
    run_sum(task5, k.totals2b, e2.pump_again)
    save(k.spread2, k.spread2_out)
    activate(k.spread2, k.totals2b, k.gain2b, k.bias2b, k.act, 0)
    e2.finish()
    save(k.e2_all, k.e2_all_out)
    task6 = all_sum(True, 1)
    expand(k.act, k.e2_all, k.expanded2, task6)
    run_sum(task6, k.totals2c)
    save(k.expanded2, k.expanded2_out)
    leave(k.expanded2, k.totals2c, k.gain2c, k.bias2c, k.middle, k.last)
    save(k.last, k.last_out)

    for task in (r1, o1, d1a, d1b, e1, r2, d2, e2, task1, task2, task3, task4, task5, task6, halo1, halo1_far, halo2):
        task.drain()
    for copy in saves:
        copy.wait()


def run_forward(geo, features, shards, norms):
    bf, f32 = jnp.bfloat16, jnp.float32
    n_ch, n_sp, mid, pixels, wr, we = geo.n_ch, geo.n_sp, geo.mid, geo.pixels, geo.wr, geo.we
    ext_rows = 3 * pixels
    rim_rows = pixels + 4 * geo.columns
    near, far = 2 * n_ch, n_sp // 2
    vmem = pl.BlockSpec(memory_space=pltpu.VMEM)
    anywhere = pl.BlockSpec(memory_space=pl.ANY)
    dma = pltpu.SemaphoreType.DMA
    v = pltpu.VMEM
    close = dict(x=features, **norms)
    kept = dict(
        r1_all=((n_ch, geo.c_in, wr), bf),
        o1_all=((n_ch, 9 * 32, wr), bf),
        d1_all=((9, mid, mid), bf),
        e1_all=((n_ch, mid, we), bf),
        r2_all=((n_ch, geo.c_in, wr), bf),
        d2_all=((9, mid, mid), bf),
        e2_all=((n_ch, mid, we), bf),
        reduced1=((pixels, mid), f32),
        ext1=((ext_rows, mid), bf),
        bend=((32, pixels), f32),
        cols1_t=((9, mid, pixels), bf),
        spread1=((pixels, mid), f32),
        expanded1=((pixels, geo.c_in), f32),
        middle=((pixels, geo.c_in), bf),
        reduced2=((pixels, mid), f32),
        moved=((3, rim_rows, mid), bf),
        spread2=((pixels, mid), f32),
        expanded2=((pixels, geo.c_in), f32),
        last=((pixels, geo.c_in), bf),
    )
    totals = dict(
        totals1a=(2, mid),
        totals1b=(2, mid),
        totals1c=(2, geo.c_in),
        totals2a=(2, mid),
        totals2b=(2, mid),
        totals2c=(2, geo.c_in),
    )
    scratch = dict(
        ident=v((mid, mid), bf),
        ext1_t=v((mid, ext_rows), bf),
        raw_all=v((9 * 32, 16 * geo.columns), f32),
        col_weight=v((geo.columns, pixels), f32),
        cells=v((ext_rows, pixels), bf),
        act=v((pixels, mid), bf),
        ext2=v((rim_rows, mid), bf),
        slim_one=v((4, near, 2, mid), f32),
        slim_two=v((4, far, 2, mid), f32),
        slim_send=dma((4, near + far)),
        slim_recv_one=dma((4, near)),
        slim_recv_two=dma((4, far)),
        wide_one=v((2, near, 2, geo.c_in), f32),
        wide_two=v((2, far, 2, geo.c_in), f32),
        wide_send=dma((2, near + far)),
        wide_recv_one=dma((2, near)),
        wide_recv_two=dma((2, far)),
        gather_send=dma((5, n_ch)),
        gather_recv=dma((5, n_ch)),
        half_send=dma((3, 2 + 4 * (n_ch // 2 - 1))),
        half_recv=dma((3, 2 * n_ch)),
        window=v((16 * geo.columns, mid), bf),
        halo_sem=dma((3, 4)),
        save_sem=dma((len(kept),)),
    )
    scratch |= {name: v(*what) for name, what in kept.items()}
    out_names = [f"{name}_out" for name in kept]
    results = pl.pallas_call(
        functools.partial(forward_kernel, geo, [*close, *shards, *out_names, *totals, *scratch]),
        out_shape=[jax.ShapeDtypeStruct(*what) for what in kept.values()]
        + [jax.ShapeDtypeStruct(shape, f32) for shape in totals.values()],
        in_specs=[vmem] * len(close) + [anywhere] * len(shards),
        out_specs=[anywhere] * len(kept) + [vmem] * len(totals),
        scratch_shapes=list(scratch.values()),
        compiler_params=pltpu.CompilerParams(
            collective_id=0, has_side_effects=True, vmem_limit_bytes=60 * MIB
        ),
    )(*close.values(), *shards.values())
    return types.SimpleNamespace(**dict(zip([*kept, *totals], results, strict=True)))


class Reduce:
    def __init__(self, place, stage, one, two, three, four, total, done, send, recv, z_first=False):
        self.z_first = z_first
        self.p, self.stage, self.one, self.two, self.three, self.four = place, stage, one, two, three, four
        self.total, self.done = total, done
        self.send, self.recv = send, recv
        self.n_far = place.n_sp // 2
        self.half = stage.shape[2] // 2
        self.chunk = self.half // self.n_far
        self.row = lax.div(place.s, 2)
        self.pair = (place.s + 1 - 2 * place.y, place.c)
        self.mine = stage.at[place.k, place.x]
        self.at_x, self.at_out = 3, 3 + place.n_x
        self.at_back = self.at_out + 2 * self.n_far

    nothing = types.SimpleNamespace(**dict.fromkeys(["s1", "s2", "s3", "s3_add", "s3_send", "s4", "s5", "s6", "s7"], lambda: None))

    @staticmethod
    def sems(n_sp, n_ch):
        return 3 + n_ch // 2 + 3 * (n_sp // 2)

    def _half(self, ref, y):
        return ref.at[pl.ds(pl.multiple_of(y * self.half, 16), self.half)]

    def _chunk(self, ref, z, y=None):
        y = self.p.y if y is None else y
        return ref.at[pl.ds(pl.multiple_of(y * self.half + z * self.chunk, 16), self.chunk)]

    def _to_sibling(self):
        return remote(self.stage.at[1 - self.p.k], self.one, self.send.at[0], self.recv.at[0], self.p.sibling)

    def _to_x(self, d):
        other = lax.rem(self.p.x + d, self.p.n_x)
        return remote(
            self.stage.at[self.p.k, other],
            self.two.at[self.p.n_x - d - 1],
            self.send.at[self.at_x + d],
            self.recv.at[self.at_x + self.p.n_x - d],
            (self.p.s, 2 * other + self.p.k),
        )

    def _to_pair(self):
        if self.z_first:
            source, there = self._chunk(self.total, self.row, 1 - self.p.y), self.three.at[pl.ds(0, self.chunk)]
        else:
            source, there = self._half(self.total, 1 - self.p.y), self.three
        return remote(source, there, self.send.at[1], self.recv.at[1], self.pair)

    def _from(self, z, h):
        return self.four.at[z, pl.ds(h * self.chunk, self.chunk)]

    def _out(self, d, h):
        other = lax.rem(self.row + d, self.n_far)
        source = self._chunk(self.total, other, h if self.z_first else None)
        n = self.at_out + h * self.n_far
        return remote(source, self._from(self.row, h), self.send.at[n + d], self.recv.at[n + self.row], self.p.far(d))

    def _back(self, d):
        return remote(
            self._chunk(self.done, self.row), self._chunk(self.done, self.row), self.send.at[self.at_back + d], self.recv.at[self.at_back + self.row], self.p.far(d)
        )

    def _pair_back(self, y):
        return remote(self._half(self.done, y), self._half(self.done, y), self.send.at[2], self.recv.at[2], self.pair)

    def _await(self, ref, sem):
        remote(ref, ref, self.send.at[0], sem, self.p.sibling).wait_recv()

    def _add(self, source, start, rows, pieces, out):
        step = max(n for n in (16, 32, 48, 64) if rows % n == 0)

        def one(i, carry):
            at = pl.ds(pl.multiple_of(start + i * step, 16), step)
            there = pl.ds(pl.multiple_of(i * step, 16), step)
            total = source[at, :].astype(jnp.float32)
            for piece in pieces:
                total = total + piece[there, :].astype(jnp.float32)
            out[at, :] = total.astype(jnp.bfloat16)
            return carry

        lax.fori_loop(0, rows // step, one, 0)

    def s1(self):
        self._to_sibling().start()

    def s2(self):
        self._await(self.one, self.recv.at[0])
        rows = self.stage.shape[2]
        step = max(n for n in (16, 32, 48, 64) if rows % n == 0)
        for x in range(self.p.n_x):

            def one(i, carry):
                at = pl.ds(pl.multiple_of(i * step, 16), step)
                total = self.stage[self.p.k, x, at, :].astype(jnp.float32) + self.one[x, at, :].astype(jnp.float32)
                self.stage[self.p.k, x, at, :] = total.astype(jnp.bfloat16)
                return carry

            lax.fori_loop(0, rows // step, one, 0)
        for d in range(1, self.p.n_x):
            self._to_x(d).start()

    def s3_add(self):
        for d in range(1, self.p.n_x):
            self._await(self.two.at[d - 1], self.recv.at[self.at_x + d])
        pieces = [self.two.at[d - 1] for d in range(1, self.p.n_x)]
        self._add(self.mine, 0, self.stage.shape[2], pieces, self.total)
        self._to_sibling().wait_send()
        for d in range(1, self.p.n_x):
            self._to_x(d).wait_send()

    def _start_out(self):
        for d in range(1, self.n_far):
            for h in range(1 + self.z_first):
                self._out(d, h).start()

    def _add_far(self, h, y, out):
        others = [lax.rem(self.row + d, self.n_far) for d in range(1, self.n_far)]
        for other in others:
            self._await(self._from(other, h), self.recv.at[self.at_out + h * self.n_far + other])
        start = y * self.half + self.row * self.chunk
        self._add(self.total, start, self.chunk, [self._from(other, h) for other in others], out)

    def s3_send(self):
        if self.z_first:
            self._start_out()
        else:
            self._to_pair().start()

    def s3(self):
        self.s3_add()
        self.s3_send()

    def s4(self):
        if self.z_first:
            for h in range(2):
                self._add_far(h, h, self.total)
            self._to_pair().start()
        else:
            self._await(self.three, self.recv.at[1])
            self._add(self.total, self.p.y * self.half, self.half, [self.three], self.total)
            self._start_out()

    def s5(self):
        if self.z_first:
            there = self.three.at[pl.ds(0, self.chunk)]
            self._await(there, self.recv.at[1])
            start = self.p.y * self.half + self.row * self.chunk
            self._add(self.total, start, self.chunk, [there], self.done)
        else:
            self._add_far(0, self.p.y, self.done)
        for d in range(1, self.n_far):
            self._back(d).start()

    def s6(self):
        for d in range(1, self.n_far):
            other = lax.rem(self.row + d, self.n_far)
            self._await(self._chunk(self.done, other), self.recv.at[self.at_back + other])
        self._pair_back(self.p.y).start()

    def s7(self):
        self._await(self._half(self.done, 1 - self.p.y), self.recv.at[2])
        self._to_pair().wait_send()
        self._pair_back(self.p.y).wait_send()
        for d in range(1, self.n_far):
            for h in range(1 + self.z_first):
                self._out(d, h).wait_send()
            self._back(d).wait_send()


def slope_of(v):
    sigma = sigmoid(v)
    return sigma, sigma * (1.0 + v * (1.0 - sigma))


def backward_kernel(geo, names, *refs):
    k = types.SimpleNamespace(**dict(zip(names, refs, strict=True)))
    p = Place(geo.n_sp, geo.n_ch)
    s, pixels, columns, mid = p.s, geo.pixels, geo.columns, geo.mid
    n_ch, wr, we, total = p.n_ch, geo.wr, geo.we, geo.pixel_total
    bf, f32 = jnp.bfloat16, jnp.float32
    rim = 2 * columns
    slim = pl.ds(0, mid)
    count = [0, 0, 0]

    cells = k.moved.at[pl.ds(0, 3 * pixels), pl.ds(0, pixels)]
    placed = k.third.at[pl.ds(0, 9 * 32), pl.ds(2 * mid, 16 * columns)]
    placed_t = k.moved.at[pl.ds(0, 16 * columns)]
    cols_grad_t = k.moved.at[pl.ds(3 * pixels, mid), pl.ds(0, pixels)]

    def load(src, dst):
        copy = pltpu.make_async_copy(src, dst, k.load_sem.at[count[0]])
        count[0] += 1
        copy.start()
        return copy

    def write_out(src, dst):
        copy = pltpu.make_async_copy(src, dst, k.out_sem.at[count[1]])
        count[1] += 1
        copy.start()
        return copy

    def reduction(*buffers, z_first=False):
        i = count[2]
        count[2] += 1
        return Reduce(p, *buffers, k.reduce_send.at[i], k.reduce_recv.at[i], z_first)

    def for_e():
        return reduction(k.stage_e, k.one_e, k.two_e, k.three_e, k.four_e, k.total_e, k.done_e)

    d_parts, tap_count = geo.d_parts, 9 // geo.d_parts

    def for_d(*z_first):
        buffers = (k.stage_d, k.one_d, k.two_d, k.three_d, k.four_d, k.total_d, k.done_d)
        parts = [reduction(*[b.at[i] for b in buffers], z_first=i in z_first and d_parts == 3) for i in range(d_parts)]
        return parts if d_parts == 3 else [Reduce.nothing, Reduce.nothing, parts[0]]

    def for_r():
        buffers = (k.stage_r, k.one_r, k.two_r, k.three_r, k.four_r, k.total_r, k.done_r)
        return [reduction(*[buffer.at[i] for buffer in buffers]) for i in range(4)]

    def all_sum(wide, i):
        if wide:
            parts = (k.wide_one, k.wide_two, k.wide_send, k.wide_recv_one, k.wide_recv_two)
        else:
            parts = (k.slim_one, k.slim_two, k.slim_send, k.slim_recv_one, k.slim_recv_two)
        return AllSum(p, *[part.at[i] for part in parts])

    def place_of(c):
        return c % 2, c // 2

    def norm_of(totals, lanes):
        return center_inverse(totals[0:1, lanes], totals[1:2, lanes], total)

    def block_end(upstream, totals, gain, bias, task):
        for start in range(0, geo.c_in, 512):
            lanes = pl.ds(start, 512)
            center, inverse = norm_of(totals, lanes)
            gain_row, bias_row = gain[:, lanes], bias[:, lanes]

            def body(at, carry):
                normed = (k.expanded[at, lanes] - center) * inverse
                joined = gain_row * normed + bias_row + k.inputs[at, lanes].astype(f32)
                grad = upstream(at, lanes) * slope_of(joined)[1]
                k.grad[at, lanes] = grad
                return carry[0] + fold(grad), carry[1] + fold(grad * normed)

            zero = jnp.zeros((8, 512), f32)
            a, b = over_rows(pixels, 16, body, (zero, zero))
            task.put(lanes, jnp.sum(a, axis=0, keepdims=True), jnp.sum(b, axis=0, keepdims=True))

    def third_norm(totals, grads, gain):
        for start in range(0, geo.c_in, 512):
            lanes = pl.ds(start, 512)
            center, inverse = norm_of(totals, lanes)
            scale = gain[:, lanes] * inverse
            bias_mean = grads[0:1, lanes] / total
            gain_mean = grads[1:2, lanes] / total

            def body(at, carry):
                normed = (k.expanded[at, lanes] - center) * inverse
                inner = k.grad[at, lanes] - bias_mean - normed * gain_mean
                k.third[at, lanes] = (scale * inner).astype(bf)
                return carry

            over_rows(pixels, 16, body, 0)

    def act_grad(values, totals, gain, bias, act, task):
        center, inverse = norm_of(totals, slim)
        gain_row, bias_row = gain[...], bias[...]

        def body(at, carry):
            normed = (values[at, :] - center) * inverse
            pre = gain_row * normed + bias_row
            sigma, slope = slope_of(pre)
            if act is not None:
                act[at, :] = (pre * sigma).astype(bf)
            grad = k.flow[at, :] * slope
            k.flow[at, :] = grad
            return carry[0] + fold(grad), carry[1] + fold(grad * normed)

        zero = jnp.zeros((8, mid), f32)
        a, b = over_rows(pixels, 16, body, (zero, zero))
        task.put(slim, jnp.sum(a, axis=0, keepdims=True), jnp.sum(b, axis=0, keepdims=True))

    def norm_grad(values, totals, grads, gain, out):
        center, inverse = norm_of(totals, slim)
        scale = gain[...] * inverse
        bias_mean = grads[0:1, :] / total
        gain_mean = grads[1:2, :] / total

        def body(at, carry):
            normed = (values[at, :] - center) * inverse
            out[at, :] = (scale * (k.flow[at, :] - bias_mean - normed * gain_mean)).astype(bf)
            return carry

        over_rows(pixels, 16, body, 0)

    def through_expand():
        for c in range(n_ch):
            part = mm_nt(k.third[:, c * we : (c + 1) * we], k.e[c])
            if c == 0:
                k.flow[...] = part
            else:
                k.flow[...] += part

    def expand_weights():
        k.act_t[...] = mm_nt(k.ident[...], k.low1[...]).astype(bf)
        for c in range(n_ch):
            k.stage_e[place_of(c)] = mm(k.act_t[...], k.third[:, c * we : (c + 1) * we]).astype(bf)

    def stage_tap(tap, cols_t):
        product = mm(cols_t, k.low2[...])
        part, inner = lax.div(tap, tap_count), lax.rem(tap, tap_count)
        for c in range(n_ch):
            for q in range(mid // 128):
                at = pl.ds(pl.multiple_of(inner * wr + q * tap_count * wr, 16), wr)
                piece = product[c * wr : (c + 1) * wr, q * 128 : (q + 1) * 128]
                k.stage_d[(part, *place_of(c), at)] = piece.astype(bf)

    def through_reduce():
        for start in range(0, geo.c_in, 512):
            rows = pl.ds(start, 512)
            for c in range(n_ch):
                k.grad[:, start : start + 512] += mm_nt(k.low1[:, c * wr : (c + 1) * wr], k.r[c, rows, :])

    def reduce_weights(work):
        for i, start in enumerate(range(0, geo.c_in, 512)):
            inputs_t = mm_nt(k.ident[...], k.inputs[:, start : start + 512]).astype(bf)
            product = mm(inputs_t, k.low1[...])
            for c in range(n_ch):
                k.stage_r[(i, *place_of(c))] = product[:, c * wr : (c + 1) * wr].astype(bf)
            work[i].s1()

    def deliver(task, out):
        return write_out(task.done.at[pl.ds(0, out.shape[0])], out)

    def deliver_d(parts, out):
        return [deliver(task, out.at[i]) for i, task in enumerate(parts[-d_parts:])]

    def deliver_r(parts, out):
        return [deliver(task, out.at[i]) for i, task in enumerate(parts)]

    def wait_all(copies):
        for copy in copies:
            copy.wait()

    def fetch(tap, slot):
        return pltpu.make_async_copy(k.cols1.at[tap], k.cols_t.at[slot], k.fetch_sem.at[slot])

    def sampled_tap(tap, carry):
        slot = lax.rem(tap, 2)

        @pl.when(tap < 8)
        def _():
            fetch(tap + 1, 1 - slot).start()

        fetch(tap, slot).wait()
        stage_tap(tap, k.cols_t[slot])
        return carry

    def rims_of(up, up_at, down, down_at, rows, sems):
        up_to, down_to = pl.ds(up_at, rows), pl.ds(down_at, rows)
        halo = Halo(
            p,
            (k.third.at[up_to, pl.ds(0, mid)], k.rim_recv.at[1, up_to]),
            (k.third.at[down_to, pl.ds(mid, mid)], k.rim_recv.at[0, down_to]),
            sems,
        )
        k.third[up_at : up_at + rows, :mid] = k.spread_grad[up : up + rows, :].astype(bf)
        k.third[down_at : down_at + rows, mid : 2 * mid] = k.spread_grad[down : down + rows, :].astype(bf)
        return halo

    def add_rims(rows):
        @pl.when(s > 0)
        def _():
            k.flow[:rows, :] += k.rim_recv[0, :rows, :].astype(f32)

        @pl.when(s < p.n_sp - 1)
        def _():
            k.flow[pixels - rows :, :] += k.rim_recv[1, :rows, :].astype(f32)

    expanded2 = load(k.expanded2, k.expanded)
    middle = load(k.middle, k.inputs)
    cotangent = load(k.cotangent, k.third)
    e2 = load(k.e2, k.e)
    spread2 = load(k.spread2, k.spread)
    d2 = load(k.d2, k.d)
    moved2 = load(k.moved_in, k.moved)
    reduced2 = load(k.reduced2, k.reduced)
    r2 = load(k.r2, k.r)
    ext1 = load(k.ext1_in, k.ext1)
    o1 = load(k.o1_in, k.o1)
    p.barrier()
    set_identity(k.ident)
    stages = [(k.stage_o, 9 * 32)] + [(k.stage_d.at[i], tap_count * wr * mid // 128) for i in range(d_parts)]
    for stage, rows in stages:
        if stage.shape[2] > rows:
            for q in range(n_ch):
                spare = (stage.shape[2] - rows, stage.shape[3])
                stage[(*place_of(q), pl.ds(rows, spare[0]))] = jnp.zeros(spare, bf)

    expanded2.wait()
    middle.wait()
    cotangent.wait()
    sum2c = all_sum(True, 0)
    counts = k.counts[...].astype(f32)
    mine = jnp.where(iota(counts.shape, 1) == p.c, counts, 0.0)
    box = jnp.sum(mine, axis=1, keepdims=True) * counts.shape[1] / jnp.sum(counts, axis=1, keepdims=True)
    block_end(lambda at, lanes: k.third[at, lanes].astype(f32) * box, k.totals2c, k.gain2c, k.bias2c, sum2c)
    sum2c.start()
    e2.wait()
    spread2.wait()
    d2.wait()
    moved2.wait()
    reduced2.wait()
    r2.wait()
    sum2c.relay()
    k.grads2c[...] = sum2c.finish()
    third_norm(k.totals2c, k.grads2c, k.gain2c)
    expanded1 = load(k.expanded1, k.expanded)
    through_expand()
    e1 = load(k.e1, k.e)
    sum2b = all_sum(False, 0)
    act_grad(k.spread, k.totals2b, k.gain2b, k.bias2b, k.low1, sum2b)
    sum2b.start()
    expand_weights()
    work_e2 = for_e()
    work_e2.s1()
    sum2b.relay()
    k.grads2b[...] = sum2b.finish()
    norm_grad(k.spread, k.totals2b, k.grads2b, k.gain2b, k.low2)
    spread1 = load(k.spread1, k.spread)
    work_e2.s2()

    area = pixels + 2 * rim
    k.spread_grad[:area, :] = jnp.zeros((area, mid), f32)
    for j in range(3):
        k.spread_grad[area : 2 * area, :] = jnp.zeros((area, mid), f32)

        def row_step(i, carry):
            at = pl.ds(pl.multiple_of(area + i * rim, 16), pixels)
            k.spread_grad[at, :] += mm_nt(k.low2[...], k.d[3 * i + j])
            return carry

        lax.fori_loop(0, 3, row_step, 0)

        def shift_back(r, carry):
            at = pl.ds(pl.multiple_of(r * columns, 16), columns)
            there = pl.ds(pl.multiple_of(area + r * columns, 16), columns)
            k.spread_grad[at, :] += column_shift(k.spread_grad[there, :], 2 - j, columns)
            return carry

        lax.fori_loop(0, geo.height + 4, shift_back, 0)
    d1 = load(k.d1, k.d)
    halo2 = rims_of(0, 0, pixels + rim, 0, rim, k.halo_sem.at[0])
    halo2.start()
    k.flow[...] = k.spread_grad[rim : pixels + rim, :]

    def plain_tap(tap, carry):
        first = lax.rem(tap, 3) * (pixels + 2 * rim) + lax.div(tap, 3) * rim
        cols = k.moved[pl.ds(pl.multiple_of(first, 16), pixels), :]
        stage_tap(tap, mm_nt(k.ident[...], cols).astype(bf))
        return carry

    work_d2 = for_d()
    for i in range(3):
        lax.fori_loop(3 * i, 3 * i + 3, plain_tap, 0)
        work_d2[i].s1()
    halo2.finish()
    add_rims(rim)
    sum2a = all_sum(False, 1)
    act_grad(k.reduced, k.totals2a, k.gain2a, k.bias2a, None, sum2a)
    sum2a.start()
    work_d2[0].s2()
    work_e2.s3()
    work_d2[1].s2()
    sum2a.relay()
    k.grads2a[...] = sum2a.finish()
    norm_grad(k.reduced, k.totals2a, k.grads2a, k.gain2a, k.low1)
    reduced1 = load(k.reduced1, k.reduced)
    through_reduce()
    r1 = load(k.r1, k.r)
    work_e2.s4()
    work_r2 = for_r()
    reduce_weights(work_r2)
    features = load(k.features, k.inputs)

    expanded1.wait()
    features.wait()
    sum1c = all_sum(True, 1)
    block_end(lambda at, lanes: k.grad[at, lanes], k.totals1c, k.gain1c, k.bias1c, sum1c)
    sum1c.start()
    work_d2[2].s2()
    work_d2[0].s3()
    work_d2[1].s3()
    e1.wait()
    spread1.wait()
    d1.wait()
    reduced1.wait()
    r1.wait()
    ext1.wait()
    o1.wait()
    sum1c.relay()
    work_e2.s5()
    k.grads1c[...] = sum1c.finish()
    work_d2[0].s4()
    halo2.drain()
    third_norm(k.totals1c, k.grads1c, k.gain1c)
    through_expand()
    sum1b = all_sum(False, 2)
    act_grad(k.spread, k.totals1b, k.gain1b, k.bias1b, k.low1, sum1b)
    work_d2[2].s3_add()
    sum1b.start()
    for part in work_r2:
        part.s2()
    work_e2.s6()
    work_d2[2].s3_send()
    expand_weights()
    work_e1 = for_e()
    sum1b.relay()
    work_d2[1].s4()
    work_d2[0].s5()
    work_e1.s1()
    work_e2.s7()
    e2_copy = deliver(work_e2, k.grad_e2)
    fetch(0, 0).start()
    k.grads1b[...] = sum1b.finish()
    norm_grad(k.spread, k.totals1b, k.grads1b, k.gain1b, k.low2)
    work_e1.s2()
    work_d1 = for_d(0, 1)
    for i in range(3):
        lax.fori_loop(3 * i, 3 * i + 3, sampled_tap, 0)
        work_d1[i].s1()

    k.spread_grad[...] = jnp.zeros((3 * pixels, mid), f32)
    k.raw_grad[...] = jnp.zeros((32, pixels), f32)

    def tap_step(tap, carry):
        @pl.when(tap == 0)
        def _():
            work_d1[0].s2()
            work_d2[2].s4()
            work_d2[1].s5()
            work_d2[0].s6()

        @pl.when(tap == 3)
        def _():
            for part in work_r2:
                part.s3()
            work_d2[2].s5()
            work_d2[1].s6()

        @pl.when(tap == 6)
        def _():
            for part in work_r2:
                part.s4()
            work_d2[2].s6()
            work_d1[1].s2()
            work_e1.s3()

        i, j = lax.div(tap, 3), lax.rem(tap, 3)
        lane = iota((1, pixels), 1)
        row = (lax.div(lane, columns) + 6 + 2 * i).astype(f32) + REACH * k.bend[pl.ds(tap, 1), :]
        across = (lax.rem(lane, columns) - 2 + 2 * j).astype(f32) + REACH * k.bend[pl.ds(tap + 16, 1), :]
        cell = iota((columns, pixels), 0).astype(f32)
        k.col_weight[...] = cell_weights(across, cell)
        row_base = jnp.floor(row)
        row_part = row - row_base
        row_upper = smooth_rise(row_part)
        row_rate = 6.0 * row_part * (1.0 - row_part)
        for r in range(3 * geo.height):
            weight = jnp.where(row_base == r, 1.0 - row_upper, jnp.where(row_base == r - 1, row_upper, 0.0))
            cells[r * columns : (r + 1) * columns, :] = (k.col_weight[...] * weight).astype(bf)
        cols_grad_t[...] = mm_nt(k.d[tap], k.low2[...]).astype(bf)
        k.spread_grad[...] += mm_nt(cells[...], cols_grad_t[...])
        for part in range(3):
            rows_at = slice(part * pixels, (part + 1) * pixels)
            k.expanded[:, 512 * part : 512 * part + pixels] = mm(k.ext1[rows_at, :], cols_grad_t[...])
        for start in range(0, pixels, 128):
            lanes = slice(start, start + 128)
            base, upper, rate = row_base[:, lanes], row_upper[:, lanes], row_rate[:, lanes]
            along = jnp.zeros((columns, 128), f32)
            down = jnp.zeros((columns, 128), f32)
            for r in range(3 * geo.height):
                row_at, col_at = r % geo.height * columns, r // geo.height * 512 + start
                match = k.expanded[row_at : row_at + columns, col_at : col_at + 128]
                at, after = base == r, base == r - 1
                along += match * jnp.where(at, 1.0 - upper, jnp.where(after, upper, 0.0))
                down += match * jnp.where(at, -rate, jnp.where(after, rate, 0.0))
            place = across[:, lanes]
            col_base = jnp.floor(place)
            col_part = place - col_base
            col_rate = 6.0 * col_part * (1.0 - col_part)
            cell_at = cell[:, lanes]
            col_slope = jnp.where(cell_at == col_base, -col_rate, jnp.where(cell_at == col_base + 1.0, col_rate, 0.0))
            here = iota((16, 128), 0) == tap
            by_row = jnp.sum(down * k.col_weight[:, lanes], axis=0, keepdims=True)
            by_col = jnp.sum(along * col_slope, axis=0, keepdims=True)
            k.raw_grad[:16, lanes] = jnp.where(here, by_row, k.raw_grad[:16, lanes])
            k.raw_grad[16:, lanes] = jnp.where(here, by_col, k.raw_grad[16:, lanes])
        return carry

    lax.fori_loop(0, 9, tap_step, 0)
    for part in work_r2:
        part.s5()
    for part in work_d2:
        part.s7()
    d2_copies = deliver_d(work_d2, k.grad_d2)

    rest = pixels - rim
    halo1_far = rims_of(0, 0, 2 * pixels + rim, rim, rest, k.halo_sem.at[2])
    halo1_far.start()

    window = slice(6 * columns, 18 * columns)
    inner = slice(2 * columns, 14 * columns)
    bend = k.bend[...]
    raw = k.raw_grad[...] * (REACH * (1.0 - bend * bend))
    col = lax.rem(iota((32, pixels), 1), columns)
    for tap in range(9):
        i, j = tap // 3, tap % 3
        offset = (2 + 2 * i) * columns + 2 * (j - 1)
        part = raw
        if j == 0:
            part = jnp.where(col < 2, 0.0, part)
        if j == 2:
            part = jnp.where(col >= columns - 2, 0.0, part)
        part = jnp.concatenate([part, jnp.zeros((32, 16 * columns - pixels), f32)], axis=1)
        placed[32 * tap : 32 * tap + 32, :] = pltpu.roll(part, offset, 1).astype(bf)
    for start in range(0, 16 * columns, 256):
        placed_t[start : start + 256, : 9 * 32] = mm_nt(k.ident[:256, :256], placed[:, start : start + 256]).astype(bf)
    for c in range(n_ch):
        k.spread_grad[window, c * wr : (c + 1) * wr] += mm(placed_t[inner, : 9 * 32], k.o1[c])
    halo1 = rims_of(rest, rest, 2 * pixels, 0, rim, k.halo_sem.at[1])
    halo1.start()
    k.flow[...] = k.spread_grad[pixels : 2 * pixels, :]
    product = mm(placed[...], k.ext1[4 * columns : 20 * columns, :])
    for c in range(n_ch):
        k.stage_o[(*place_of(c), pl.ds(0, 9 * 32))] = product[:, c * wr : (c + 1) * wr].astype(bf)
    work_o1 = reduction(k.stage_o, k.one_o, k.two_o, k.three_o, k.four_o, k.total_o, k.done_o)
    work_o1.s1()

    e2_copy.wait()
    work_e1.s4()
    work_d1[2].s2()
    wait_all(d2_copies)
    work_d1[0].s3()
    work_d1[1].s3()
    halo1_far.finish()
    halo1.finish()
    add_rims(pixels)
    sum1a = all_sum(False, 3)
    act_grad(k.reduced, k.totals1a, k.gain1a, k.bias1a, None, sum1a)
    work_d1[0].s4()
    sum1a.start()
    work_o1.s2()
    for part in work_r2:
        part.s6()
    sum1a.relay()
    work_e1.s5()
    work_d1[1].s4()
    k.grads1a[...] = sum1a.finish()
    norm_grad(k.reduced, k.totals1a, k.grads1a, k.gain1a, k.low1)
    work_r1 = for_r()
    reduce_weights(work_r1)
    for part in work_r1:
        part.s2()
    work_d1[2].s3()
    through_reduce()
    d_features = write_out(k.grad, k.d_features)
    work_e1.s6()
    for part in work_r2:
        part.s7()
    r2_copies = deliver_r(work_r2, k.grad_r2)
    work_d1[0].s5()
    work_d1[1].s5()
    work_o1.s3()
    wait_all(r2_copies)
    work_r1[0].s3()
    work_d1[2].s4()
    work_r1[1].s3()
    work_r1[0].s4()
    work_d1[0].s6()
    work_r1[2].s3()
    work_r1[1].s4()
    work_r1[0].s5()
    work_o1.s4()
    work_d1[2].s5()
    work_r1[3].s3()
    work_r1[2].s4()
    work_r1[1].s5()
    work_r1[0].s6()
    work_d1[1].s6()
    work_o1.s5()
    work_e1.s7()
    e1_copy = deliver(work_e1, k.grad_e1)
    work_r1[3].s4()
    work_r1[2].s5()
    work_r1[1].s6()
    work_r1[3].s5()
    work_r1[2].s6()
    work_d1[2].s6()
    work_o1.s6()
    work_r1[3].s6()
    for part in work_d1:
        part.s7()
    d1_copies = deliver_d(work_d1, k.grad_d1)
    work_o1.s7()
    o1_copy = deliver(work_o1, k.grad_o1)
    for part in work_r1:
        part.s7()
    wait_all(deliver_r(work_r1, k.grad_r1) + d1_copies)
    e1_copy.wait()
    o1_copy.wait()
    for task in (sum2c, sum2b, sum2a, sum1c, sum1b, sum1a, halo1, halo1_far):
        task.drain()
    d_features.wait()


def run_backward(geo, kept, features, cotangent, counts, norms):
    bf, f32 = jnp.bfloat16, jnp.float32
    n_ch, n_sp, mid, pixels, wr, we = geo.n_ch, geo.n_sp, geo.mid, geo.pixels, geo.wr, geo.we
    n_x, near, far = n_ch // 2, 2 * n_ch, n_sp // 2
    columns, c_in = geo.columns, geo.c_in
    rim = 2 * columns
    vmem = pl.BlockSpec(memory_space=pltpu.VMEM)
    anywhere = pl.BlockSpec(memory_space=pl.ANY)
    far_away = dict(
        features=features,
        cotangent=cotangent,
        expanded2=kept.expanded2,
        middle=kept.middle,
        e2=kept.e2_all,
        spread2=kept.spread2,
        d2=kept.d2_all,
        moved_in=kept.moved.reshape(-1, mid),
        reduced2=kept.reduced2,
        r2=kept.r2_all,
        expanded1=kept.expanded1,
        e1=kept.e1_all,
        spread1=kept.spread1,
        d1=kept.d1_all,
        cols1=kept.cols1_t,
        ext1_in=kept.ext1,
        reduced1=kept.reduced1,
        r1=kept.r1_all,
        o1_in=kept.o1_all,
    )
    close = dict(
        bend=kept.bend,
        counts=counts,
        totals1a=kept.totals1a,
        totals1b=kept.totals1b,
        totals1c=kept.totals1c,
        totals2a=kept.totals2a,
        totals2b=kept.totals2b,
        totals2c=kept.totals2c,
        **norms,
    )
    grads = dict(
        grad_e2=((mid, we), bf, anywhere),
        grad_d2=((geo.d_parts, 9 // geo.d_parts * wr * 4, 128), bf, anywhere),
        grad_r2=((4, 512, wr), bf, anywhere),
        grad_e1=((mid, we), bf, anywhere),
        grad_d1=((geo.d_parts, 9 // geo.d_parts * wr * 4, 128), bf, anywhere),
        grad_r1=((4, 512, wr), bf, anywhere),
        grad_o1=((9 * 32, wr), bf, anywhere),
        d_features=((pixels, c_in), f32, anywhere),
        grads2c=((2, c_in), f32, vmem),
        grads2b=((2, mid), f32, vmem),
        grads2a=((2, mid), f32, vmem),
        grads1c=((2, c_in), f32, vmem),
        grads1b=((2, mid), f32, vmem),
        grads1a=((2, mid), f32, vmem),
    )
    dma = pltpu.SemaphoreType.DMA
    v = pltpu.VMEM
    scratch = dict(
        e=v((n_ch, mid, we), bf),
        d=v((9, mid, mid), bf),
        r=v((n_ch, c_in, wr), bf),
        o1=v((n_ch, 9 * 32, wr), bf),
        expanded=v((pixels, c_in), f32),
        grad=v((pixels, c_in), f32),
        inputs=v((pixels, c_in), bf),
        third=v((pixels, c_in), bf),
        spread=v((pixels, mid), f32),
        reduced=v((pixels, mid), f32),
        flow=v((pixels, mid), f32),
        act_t=v((mid, pixels), bf),
        low1=v((pixels, mid), bf),
        low2=v((pixels, mid), bf),
        moved=v((3 * (pixels + 2 * rim), mid), bf),
        ext1=v((3 * pixels, mid), bf),
        cols_t=v((2, mid, pixels), bf),
        col_weight=v((columns, pixels), f32),
        spread_grad=v((3 * pixels, mid), f32),
        raw_grad=v((32, pixels), f32),
        ident=v((mid, mid), bf),
        rim_recv=v((2, pixels, mid), bf),
        slim_one=v((4, near, 2, mid), f32),
        slim_two=v((4, far, 2, mid), f32),
        slim_send=dma((4, near + far)),
        slim_recv_one=dma((4, near)),
        slim_recv_two=dma((4, far)),
        wide_one=v((2, near, 2, c_in), f32),
        wide_two=v((2, far, 2, c_in), f32),
        wide_send=dma((2, near + far)),
        wide_recv_one=dma((2, near)),
        wide_recv_two=dma((2, far)),
        halo_sem=dma((3, 4)),
        load_sem=dma((20,)),
        out_sem=dma((24,)),
        fetch_sem=dma((2,)),
        reduce_send=dma((17, Reduce.sems(n_sp, n_ch))),
        reduce_recv=dma((17, Reduce.sems(n_sp, n_ch))),
    )

    def staging(rows, lanes, *parts, both=1):
        return (
            v((*parts, 2, n_x, rows, lanes), bf),
            v((*parts, n_x, rows, lanes), bf),
            v((*parts, n_x - 1, rows, lanes), bf),
            v((*parts, rows // 2, lanes), bf),
            v((*parts, far, both * rows // n_sp, lanes), bf),
            v((*parts, rows, lanes), bf),
            v((*parts, rows, lanes), bf),
        )

    def padded(rows):
        return -(-rows // (32 * far)) * 32 * far

    d_rows = padded(9 // geo.d_parts * wr * mid // 128)
    e, d, r, o = staging(mid, we), staging(d_rows, 128, geo.d_parts, both=2 if geo.d_parts == 3 else 1), staging(512, wr, 4), staging(padded(9 * 32), wr)
    scratch |= dict(stage_e=e[0], one_e=e[1], two_e=e[2], three_e=e[3], four_e=e[4], total_e=e[5], done_e=e[6])
    scratch |= dict(stage_d=d[0], one_d=d[1], two_d=d[2], three_d=d[3], four_d=d[4], total_d=d[5], done_d=d[6])
    scratch |= dict(stage_r=r[0], one_r=r[1], two_r=r[2], three_r=r[3], four_r=r[4], total_r=r[5], done_r=r[6])
    scratch |= dict(stage_o=o[0], one_o=o[1], two_o=o[2], three_o=o[3], four_o=o[4], total_o=o[5], done_o=o[6])
    results = pl.pallas_call(
        functools.partial(backward_kernel, geo, [*far_away, *close, *grads, *scratch]),
        out_shape=[jax.ShapeDtypeStruct(shape, dtype) for shape, dtype, _ in grads.values()],
        in_specs=[anywhere] * len(far_away) + [vmem] * len(close),
        out_specs=[spec for _, _, spec in grads.values()],
        scratch_shapes=list(scratch.values()),
        compiler_params=pltpu.CompilerParams(
            collective_id=1, has_side_effects=True, vmem_limit_bytes=63 * MIB
        ),
    )(*far_away.values(), *close.values())
    return types.SimpleNamespace(**dict(zip(grads, results, strict=True)))


def finish_kernel(geo, names, *refs):
    k = types.SimpleNamespace(**dict(zip(names, refs, strict=True)))
    f32 = jnp.float32
    wr = geo.wr
    for source, out in ((k.e2, k.e2_out), (k.e1, k.e1_out), (k.d_features, k.d_features_out), (k.last, k.last_out)):
        out[...] = source[...].astype(out.dtype)
    for source, out in ((k.r2, k.r2_out), (k.r1, k.r1_out)):
        out[...] = source[0].astype(f32)
    for source, out in ((k.d2, k.d2_out), (k.d1, k.d1_out)):
        rows = source.shape[2]
        for part in range(source.shape[0]):
            out[part * rows : (part + 1) * rows, :] = source[part, 0].astype(f32)

    @pl.when(pl.program_id(0) == 0)
    def _():
        row, offset = iota((32, 18), 0), iota((32, 18), 1)
        chosen = (lax.rem(row, 16) == lax.div(offset, 2)) & (lax.div(row, 16) == lax.rem(offset, 2))
        chosen = jnp.where(chosen, 1.0, 0.0).astype(jnp.bfloat16)
        for tap in range(9):
            part = k.o1[32 * tap : 32 * tap + 32, :]
            k.o1_out[tap] = lax.dot_general(part, chosen, (((0,), (0,)), ((), ())), preferred_element_type=f32)
        vectors = (
            (k.sums1a, k.gain1a, k.bias1a),
            (k.sums1b, k.gain1b, k.bias1b),
            (k.sums1c, k.gain1c, k.bias1c),
            (k.sums2a, k.gain2a, k.bias2a),
            (k.sums2b, k.gain2b, k.bias2b),
            (k.sums2c, k.gain2c, k.bias2c),
        )
        for sums, gain, bias in vectors:
            gain[...] = sums[1:2, :]
            bias[...] = sums[0:1, :]


def run_finish(geo, g, last):
    f32 = jnp.float32
    steps, wr, we, mid, c_in, pixels = 4, geo.wr, geo.we, geo.mid, geo.c_in, geo.pixels
    d_rows = 9 // geo.d_parts * wr

    def rows(height, width):
        return pl.BlockSpec((height // steps, width), lambda i: (i, 0))

    def whole(*shape):
        return pl.BlockSpec(shape, lambda i: (0,) * len(shape))

    d_in = pl.BlockSpec((geo.d_parts, 1, d_rows, 128), lambda i: (0, i, 0, 0))
    r_in = pl.BlockSpec((1, 512, wr), lambda i: (i, 0, 0))
    d_shape = (geo.d_parts, 4, d_rows, 128)
    ins = dict(
        e2=(g.grad_e2, rows(mid, we)),
        d2=(g.grad_d2.reshape(d_shape), d_in),
        r2=(g.grad_r2, r_in),
        e1=(g.grad_e1, rows(mid, we)),
        d1=(g.grad_d1.reshape(d_shape), d_in),
        r1=(g.grad_r1, r_in),
        o1=(g.grad_o1, whole(9 * 32, wr)),
        d_features=(g.d_features, rows(pixels, c_in)),
        last=(last, rows(pixels, c_in)),
        sums1a=(g.grads1a, whole(2, mid)),
        sums1b=(g.grads1b, whole(2, mid)),
        sums1c=(g.grads1c, whole(2, c_in)),
        sums2a=(g.grads2a, whole(2, mid)),
        sums2b=(g.grads2b, whole(2, mid)),
        sums2c=(g.grads2c, whole(2, c_in)),
    )
    slim, wide = ((1, mid), whole(1, mid)), ((1, c_in), whole(1, c_in))
    d_out = ((9 * wr, mid), pl.BlockSpec((9 * wr, 128), lambda i: (0, i)))
    outs = dict(
        e2_out=((mid, we), rows(mid, we)),
        d2_out=d_out,
        r2_out=((c_in, wr), rows(c_in, wr)),
        e1_out=((mid, we), rows(mid, we)),
        d1_out=d_out,
        r1_out=((c_in, wr), rows(c_in, wr)),
        o1_out=((9, wr, 18), whole(9, wr, 18)),
        d_features_out=((pixels, c_in), rows(pixels, c_in)),
        last_out=((pixels, c_in), rows(pixels, c_in)),
        gain1a=slim,
        bias1a=slim,
        gain1b=slim,
        bias1b=slim,
        gain1c=wide,
        bias1c=wide,
        gain2a=slim,
        bias2a=slim,
        gain2b=slim,
        bias2b=slim,
        gain2c=wide,
        bias2c=wide,
    )
    results = pl.pallas_call(
        functools.partial(finish_kernel, geo, [*ins, *outs]),
        grid=(steps,),
        out_shape=[
            jax.ShapeDtypeStruct(shape, last.dtype if name == "last_out" else f32) for name, (shape, _) in outs.items()
        ],
        in_specs=[spec for _, spec in ins.values()],
        out_specs=[spec for _, spec in outs.values()],
        compiler_params=pltpu.CompilerParams(vmem_limit_bytes=60 * MIB),
    )(*[array for array, _ in ins.values()])
    return types.SimpleNamespace(**dict(zip(outs, results, strict=True)))


def per_device(
    features,
    box_counts,
    b1_w_reduce,
    b1_gain1,
    b1_bias1,
    b1_w_offset,
    b1_w_deform,
    b1_gain2,
    b1_bias2,
    b1_w_expand,
    b1_gain3,
    b1_bias3,
    b2_w_reduce,
    b2_gain1,
    b2_bias1,
    b2_w_spatial,
    b2_gain2,
    b2_bias2,
    b2_w_expand,
    b2_gain3,
    b2_bias3,
    cotangent,
):
    images, height, columns, channels = features.shape
    n_sp, n_ch = lax.axis_size("sp"), lax.axis_size("ch")
    pixels = images * height * columns
    mid, wr = b1_w_deform.shape[2], b1_w_reduce.shape[1]
    geo = types.SimpleNamespace(
        n_sp=n_sp,
        n_ch=n_ch,
        pixels=pixels,
        height=height,
        columns=columns,
        mid=mid,
        c_in=channels,
        wr=wr,
        we=b1_w_expand.shape[1],
        pixel_total=pixels * n_sp * n_ch,
        d_parts=3 if 3 * wr * mid // 128 % (16 * n_sp) == 0 else 1,
    )
    offset_w = jnp.moveaxis(b1_w_offset.reshape(9, wr, 9, 2), 1, 3)
    offset_w = jnp.pad(offset_w, ((0, 0), (0, 7), (0, 0), (0, 0)))
    offset_w = jnp.moveaxis(offset_w, 2, 1).reshape(9 * 32, wr)
    shards = dict(
        r1=b1_w_reduce,
        o1=offset_w,
        d1=b1_w_deform,
        e1=b1_w_expand,
        r2=b2_w_reduce,
        d2=b2_w_spatial,
        e2=b2_w_expand,
    )
    norms = dict(
        gain1a=b1_gain1,
        bias1a=b1_bias1,
        gain1b=b1_gain2,
        bias1b=b1_bias2,
        gain1c=b1_gain3,
        bias1c=b1_bias3,
        gain2a=b2_gain1,
        bias2a=b2_bias1,
        gain2b=b2_gain2,
        bias2b=b2_bias2,
        gain2c=b2_gain3,
        bias2c=b2_bias3,
    )
    norms = {name: vector.reshape(1, -1) for name, vector in norms.items()}
    entry = features.reshape(pixels, channels)
    kept = run_forward(geo, entry, shards, norms)
    g = run_backward(geo, kept, entry, cotangent.reshape(pixels, channels), box_counts.reshape(1, -1), norms)
    done = run_finish(geo, g, kept.last)
    return (
        done.last_out.reshape(features.shape),
        done.d_features_out.reshape(features.shape),
        done.r1_out,
        done.gain1a.reshape(mid),
        done.bias1a.reshape(mid),
        done.o1_out,
        done.d1_out.reshape(9, wr, mid),
        done.gain1b.reshape(mid),
        done.bias1b.reshape(mid),
        done.e1_out,
        done.gain1c.reshape(channels),
        done.bias1c.reshape(channels),
        done.r2_out,
        done.gain2a.reshape(mid),
        done.bias2a.reshape(mid),
        done.d2_out.reshape(9, wr, mid),
        done.gain2b.reshape(mid),
        done.bias2b.reshape(mid),
        done.e2_out,
        done.gain2c.reshape(channels),
        done.bias2c.reshape(channels),
    )


def solution(mesh):
    return jax.shard_map(
        per_device,
        mesh=mesh,
        in_specs=(
            P("ch", "sp", None, None),
            P(),
            P(None, "ch"),
            P(),
            P(),
            P(None, "ch", None),
            P(None, "ch", None),
            P(),
            P(),
            P(None, "ch"),
            P(),
            P(),
            P(None, "ch"),
            P(),
            P(),
            P(None, "ch", None),
            P(),
            P(),
            P(None, "ch"),
            P(),
            P(),
            P("ch", "sp", None, None),
        ),
        out_specs=(
            P("ch", "sp", None, None),
            P("ch", "sp", None, None),
            P(None, "ch"),
            P(),
            P(),
            P(None, "ch", None),
            P(None, "ch", None),
            P(),
            P(),
            P(None, "ch"),
            P(),
            P(),
            P(None, "ch"),
            P(),
            P(),
            P(None, "ch", None),
            P(),
            P(),
            P(None, "ch"),
            P(),
            P(),
        ),
        check_vma=False,
    )
```

```python
import functools
import types

import jax
import jax.numpy as jnp
from jax import lax
from jax.experimental import pallas as pl
from jax.experimental.pallas import tpu as pltpu
from jax.sharding import PartitionSpec as P

EPS = 1e-05
REACH = 5.5
MESH = pl.DeviceIdType.MESH
MIB = 2**20


def mm(left, right):
    return jnp.dot(left, right, preferred_element_type=jnp.float32)


def mm_nt(left, right):
    return lax.dot_general(
        left, right, (((1,), (1,)), ((), ())), preferred_element_type=jnp.float32
    )


def smooth_rise(fraction):
    return fraction * fraction * (3.0 - 2.0 * fraction)


def sigmoid(v):
    return 1.0 / (1.0 + jnp.exp(-v))


class Place:
    def __init__(self, n_sp, n_ch):
        self.n_sp, self.n_ch, self.n_x = n_sp, n_ch, n_ch // 2
        self.s, self.c = lax.axis_index("sp"), lax.axis_index("ch")
        self.x, self.k = lax.div(self.c, 2), lax.rem(self.c, 2)
        self.y = lax.rem(self.s, 2)
        self.sib = self.c + 1 - 2 * self.k
        self.sibling = (self.s, self.sib)

    def other_x(self, d):
        return 2 * lax.rem(self.x + d, self.n_x) + self.k

    def near(self, d):
        q = lax.rem(self.y * self.n_ch + self.c + d, 2 * self.n_ch)
        return self.s - self.y + lax.div(q, self.n_ch), lax.rem(q, self.n_ch)

    def far(self, d):
        return lax.rem(self.s + 2 * d, self.n_sp), self.c

    def barrier(self):
        sem = pltpu.get_barrier_semaphore()

        def tell(device):
            pl.semaphore_signal(sem, inc=1, device_id=device, device_id_type=MESH)

        for d in range(1, 2 * self.n_ch):
            tell(self.near(d))
        for d in range(1, self.n_sp // 2):
            tell(self.far(d))
        diagonal = lax.rem(self.s + self.n_sp - 1 + 2 * self.y, self.n_sp)
        tell((diagonal, self.c))
        pl.semaphore_wait(sem, 2 * self.n_ch + self.n_sp // 2 - 1)


def remote(src, dst, send, recv, device):
    return pltpu.make_async_remote_copy(
        src_ref=src,
        dst_ref=dst,
        send_sem=send,
        recv_sem=recv,
        device_id=device,
        device_id_type=MESH,
    )


class AllSum:
    def __init__(self, place, first, second, send, recv_one, recv_two):
        self.p, self.first, self.second = place, first, second
        self.send, self.one, self.two = send, recv_one, recv_two
        self.me = place.y * place.n_ch + place.c
        self.row = lax.div(place.s, 2)

    def put(self, lanes, sums, squares):
        self.first[self.me, 0:1, lanes] = sums
        self.first[self.me, 1:2, lanes] = squares

    def _near(self, d):
        return remote(self.first.at[self.me], self.first.at[self.me], self.send.at[d], self.one.at[self.me], self.p.near(d))

    def _far(self, d):
        n = 2 * self.p.n_ch
        return remote(self.second.at[self.row], self.second.at[self.row], self.send.at[n + d], self.two.at[self.row], self.p.far(d))

    def start(self):
        for d in range(1, 2 * self.p.n_ch):
            self._near(d).start()

    def relay(self):
        n = 2 * self.p.n_ch
        for d in range(1, n):
            other = lax.rem(self.me + d, n)
            slot = self.first.at[other]
            remote(slot, slot, self.send.at[d], self.one.at[other], self.p.near(d)).wait_recv()
        total = self.first[0]
        for q in range(1, n):
            total = total + self.first[q]
        self.second[self.row] = total
        for d in range(1, self.p.n_sp // 2):
            self._far(d).start()

    def finish(self):
        n = self.p.n_sp // 2
        for d in range(1, n):
            other = lax.rem(self.row + d, n)
            slot = self.second.at[other]
            remote(slot, slot, self.send.at[d], self.two.at[other], self.p.far(d)).wait_recv()
        total = self.second[0]
        for q in range(1, n):
            total = total + self.second[q]
        return total

    def drain(self):
        for d in range(1, 2 * self.p.n_ch):
            self._near(d).wait_send()
        for d in range(1, self.p.n_sp // 2):
            self._far(d).wait_send()


class Gather:
    def __init__(self, place, src, slot, send, recv):
        self.p, self.src, self.slot, self.send, self.recv = place, src, slot, send, recv

    def _own(self):
        return pltpu.make_async_copy(self.src, self.slot(self.p.c), self.recv.at[self.p.c])

    def _sibling(self):
        c = self.p.c
        return remote(self.src, self.slot(c), self.send.at[0], self.recv.at[c], self.p.sibling)

    def _direct(self, d):
        c = self.p.c
        return remote(self.src, self.slot(c), self.send.at[d], self.recv.at[c], (self.p.s, self.p.other_x(d)))

    def _forward(self, d):
        o = self.p.other_x(d)
        return remote(self.slot(o), self.slot(o), self.send.at[self.p.n_x + d - 1], self.recv.at[o], self.p.sibling)

    def _arrived(self, o):
        remote(self.slot(o), self.slot(o), self.send.at[0], self.recv.at[o], self.p.sibling).wait_recv()

    def start(self):
        for d in range(1, self.p.n_x):
            self._direct(d).start()
        self._sibling().start()
        self._own().start()

    def pump(self):
        for d in range(1, self.p.n_x):
            self._arrived(self.p.other_x(d))
            self._forward(d).start()

    def finish(self):
        self._own().wait()
        self._arrived(self.p.sib)
        for d in range(1, self.p.n_x):
            self._arrived(self.p.other_x(d) + 1 - 2 * self.p.k)

    def drain(self):
        self._sibling().wait_send()
        for d in range(1, self.p.n_x):
            self._direct(d).wait_send()
            self._forward(d).wait_send()


class HalfGather:
    def __init__(self, place, src, slot, send, recv):
        self.p, self.src, self.slot, self.send, self.recv = place, src, slot, send, recv
        z = lax.div(place.s, 2)
        self.h = lax.rem(z, 2)
        self.beside = (place.s + 2 - 4 * self.h, place.c)

    def _own(self, h):
        c = self.p.c
        return pltpu.make_async_copy(self.src(h), self.slot(c, h), self.recv.at[2 * c + h])

    def _sibling(self, h):
        c = self.p.c
        return remote(self.src(h), self.slot(c, h), self.send.at[h], self.recv.at[2 * c + h], self.p.sibling)

    def _direct(self, d):
        c, h = self.p.c, self.h
        there = (self.p.s, self.p.other_x(d))
        return remote(self.src(h), self.slot(c, h), self.send.at[1 + d], self.recv.at[2 * c + h], there)

    def _pass(self, d, kind, h, device):
        o = self.p.other_x(d)
        sem = self.send.at[2 + (kind + 1) * (self.p.n_x - 1) + d - 1]
        return remote(self.slot(o, h), self.slot(o, h), sem, self.recv.at[2 * o + h], device)

    def _beside(self, d):
        return self._pass(d, 0, self.h, self.beside)

    def _forward(self, d):
        return self._pass(d, 1, self.h, self.p.sibling)

    def _second(self, d):
        return self._pass(d, 2, 1 - self.h, self.p.sibling)

    def _arrived(self, o, h):
        remote(self.slot(o, h), self.slot(o, h), self.send.at[0], self.recv.at[2 * o + h], self.p.sibling).wait_recv()

    def start(self):
        for d in range(1, self.p.n_x):
            self._direct(d).start()
        for h in range(2):
            self._sibling(h).start()
            self._own(h).start()

    def pump(self):
        for d in range(1, self.p.n_x):
            self._arrived(self.p.other_x(d), self.h)
            self._beside(d).start()
            self._forward(d).start()

    def pump_again(self):
        for d in range(1, self.p.n_x):
            self._arrived(self.p.other_x(d), 1 - self.h)
            self._second(d).start()

    def finish(self):
        for h in range(2):
            self._own(h).wait()
            self._arrived(self.p.sib, h)
            for d in range(1, self.p.n_x):
                self._arrived(self.p.other_x(d) + 1 - 2 * self.p.k, h)

    def drain(self):
        for h in range(2):
            self._sibling(h).wait_send()
        for d in range(1, self.p.n_x):
            for copy in (self._direct(d), self._beside(d), self._forward(d), self._second(d)):
                copy.wait_send()


class Halo:
    def __init__(self, place, up, down, sems):
        self.p, self.up, self.down, self.sems = place, up, down, sems

    def _up(self):
        return remote(*self.up, self.sems.at[0], self.sems.at[1], (self.p.s - 1, self.p.c))

    def _down(self):
        return remote(*self.down, self.sems.at[2], self.sems.at[3], (self.p.s + 1, self.p.c))

    def _each(self, act_up, act_down):
        pl.when(self.p.s > 0)(act_up)
        pl.when(self.p.s < self.p.n_sp - 1)(act_down)

    def start(self):
        self._each(lambda: self._up().start(), lambda: self._down().start())

    def finish(self):
        self._each(lambda: self._down().wait_recv(), lambda: self._up().wait_recv())

    def drain(self):
        self._each(lambda: self._up().wait_send(), lambda: self._down().wait_send())


def over_rows(rows, step, body, init):
    def one(i, carry):
        return body(pl.ds(pl.multiple_of(i * step, step), step), carry)

    return lax.fori_loop(0, rows // step, one, init, unroll=2)


def fold(v):
    return jnp.sum(v.reshape(-1, 8, v.shape[1]), axis=0)


def moments(ref, lanes, rows):
    width = lanes.size

    def body(at, carry):
        v = ref[at, lanes]
        return carry[0] + fold(v), carry[1] + fold(v * v)

    zero = jnp.zeros((8, width), jnp.float32)
    a, b = over_rows(rows, 16, body, (zero, zero))
    return jnp.sum(a, axis=0, keepdims=True), jnp.sum(b, axis=0, keepdims=True)


def center_inverse(sums, squares, pixel_total):
    center = sums / pixel_total
    return center, lax.rsqrt(squares / pixel_total - center * center + EPS)


def cell_weights(position, cells):
    base = jnp.floor(position)
    upper = smooth_rise(position - base)
    return jnp.where(cells == base, 1.0 - upper, jnp.where(cells == base + 1.0, upper, 0.0))


def iota(shape, axis):
    return lax.broadcasted_iota(jnp.int32, shape, axis)


def set_identity(ref):
    n = ref.shape[0]
    for r in range(0, n, 128):
        same = iota((128, n), 0) + r == iota((128, n), 1)
        ref[r : r + 128, :] = jnp.where(same, 1.0, 0.0).astype(jnp.bfloat16)


def column_shift(v, j, columns):
    if j == 1:
        return v
    col = lax.rem(iota(v.shape, 0), columns)
    if j == 0:
        return jnp.where(col < 2, 0.0, pltpu.roll(v, 2, 0))
    return jnp.where(col >= columns - 2, 0.0, pltpu.roll(v, v.shape[0] - 2, 0))


def forward_kernel(geo, names, *refs):
    k = types.SimpleNamespace(**dict(zip(names, refs, strict=True)))
    p = Place(geo.n_sp, geo.n_ch)
    s, pixels, columns, mid = p.s, geo.pixels, geo.columns, geo.mid
    n_ch, wr, we, total = p.n_ch, geo.wr, geo.we, geo.pixel_total
    bf, f32 = jnp.bfloat16, jnp.float32

    def rows_of(ref, width, first, taps):
        at = pl.ds(first, taps)
        return lambda c: ref.at[at, pl.ds(pl.multiple_of(c * width, width), width), :]

    def slots_of(ref):
        return lambda c: ref.at[c]

    def gather(i, src, slot):
        return Gather(p, src, slot, k.gather_send.at[i], k.gather_recv.at[i])

    o1 = gather(1, k.o1_own, slots_of(k.o1_all))
    d1a = gather(2, k.d1.at[pl.ds(0, 2)], rows_of(k.d1_all, wr, 0, 2))
    d1b = gather(3, k.d1.at[pl.ds(2, 7)], rows_of(k.d1_all, wr, 2, 7))
    e1 = gather(4, k.e1, slots_of(k.e1_all))

    def half_gather(i, src, slot):
        return HalfGather(p, src, slot, k.half_send.at[i], k.half_recv.at[i])

    def half_rows(ref, rows):
        return lambda h: ref.at[pl.ds(pl.multiple_of(h * rows, 16), rows)]

    def half_slots(ref, rows):
        return lambda c, h: ref.at[c, pl.ds(pl.multiple_of(h * rows, 16), rows)]

    def quarter(i):
        rows = geo.c_in // 8

        def at(h):
            return pl.ds(pl.multiple_of(2 * i * rows + h * rows, 16), rows)

        return half_gather(3 + i, lambda h: k.r1.at[at(h)], lambda c, h: k.r1_all.at[c, at(h)])

    r1 = [quarter(i) for i in range(4)]
    r2 = half_gather(0, half_rows(k.r2, geo.c_in // 2), half_slots(k.r2_all, geo.c_in // 2))
    d2 = half_gather(
        1,
        lambda h: k.d2.at[:, pl.ds(pl.multiple_of(h * (wr // 2), 16), wr // 2), :],
        lambda c, h: k.d2_all.at[:, pl.ds(pl.multiple_of(c * wr + h * (wr // 2), 16), wr // 2), :],
    )
    e2 = half_gather(2, half_rows(k.e2, mid // 2), half_slots(k.e2_all, mid // 2))

    def all_sum(wide, i):
        if wide:
            parts = (k.wide_one, k.wide_two, k.wide_send, k.wide_recv_one, k.wide_recv_two)
        else:
            parts = (k.slim_one, k.slim_two, k.slim_send, k.slim_recv_one, k.slim_recv_two)
        return AllSum(p, *[part.at[i] for part in parts])

    saves = []

    def save(src, dst):
        copy = pltpu.make_async_copy(src, dst, k.save_sem.at[len(saves)])
        copy.start()
        saves.append(copy)

    def run_sum(task, totals, *between):
        task.start()
        for one in between:
            one()
        task.relay()
        totals[...] = task.finish()

    def reduce_matmul(x, weights, out):
        for c in range(n_ch):
            out[:, c * wr : (c + 1) * wr] = mm(x[...], weights[c])

    def activate(values, totals, gain, bias, out, first_row):
        center, inverse = center_inverse(totals[0:1, :], totals[1:2, :], total)
        scale = gain[...] * inverse
        shift = bias[...]

        def body(at, carry):
            v = (values[at, :] - center) * scale + shift
            row = pl.ds(pl.multiple_of(at.start + first_row, 16), at.size)
            out[row, :] = (v * sigmoid(v)).astype(bf)
            return carry

        over_rows(pixels, 16, body, 0)

    def expand(x, weights, out, task):
        for c in range(n_ch):
            lanes = pl.ds(c * we, we)
            out[:, lanes] = mm(x[...], weights[c])
            task.put(lanes, *moments(out, lanes, pixels))

    def leave(values, totals, gain, bias, residual, out):
        for start in range(0, geo.c_in, 512):
            lanes = pl.ds(start, 512)
            center, inverse = center_inverse(totals[0:1, lanes], totals[1:2, lanes], total)
            scale = gain[:, lanes] * inverse
            shift = bias[:, lanes]

            def body(at, carry):
                v = (values[at, lanes] - center) * scale + shift + residual[at, lanes].astype(f32)
                out[at, lanes] = (v * sigmoid(v)).astype(bf)
                return carry

            over_rows(pixels, 16, body, 0)

    slim = pl.ds(0, mid)

    p.barrier()
    for part in r1:
        part.start()
    row, offset = iota((32, 18), 0), iota((32, 18), 1)
    chosen = (lax.rem(row, 16) == lax.div(offset, 2)) & (lax.div(row, 16) == lax.rem(offset, 2))
    chosen = jnp.where(chosen, 1.0, 0.0).astype(bf)
    for tap in range(9):
        k.o1_own[32 * tap : 32 * tap + 32, :] = mm(chosen, k.o1[tap]).astype(bf)
    o1.start()
    d1a.start()
    set_identity(k.ident)

    def reduce_quarter(i):
        r1[i].finish()
        at = slice(i * (geo.c_in // 4), (i + 1) * (geo.c_in // 4))
        for c in range(n_ch):
            part = mm(k.x[:, at], k.r1_all[c, at, :])
            if i == 0:
                k.reduced1[:, c * wr : (c + 1) * wr] = part
            else:
                k.reduced1[:, c * wr : (c + 1) * wr] += part

    r1[0].pump()
    r1[1].pump()
    r1[0].pump_again()
    r1[2].pump()
    r1[1].pump_again()
    r1[3].pump()
    reduce_quarter(0)
    r1[2].pump_again()
    reduce_quarter(1)
    r1[3].pump_again()
    reduce_quarter(2)
    reduce_quarter(3)
    task1 = all_sum(False, 0)
    task1.put(slim, *moments(k.reduced1, slim, pixels))
    run_sum(task1, k.totals1a, d1b.start, e1.start)
    o1.pump()
    activate(k.reduced1, k.totals1a, k.gain1a, k.bias1a, k.ext1, pixels)
    own = k.ext1.at[pixels : 2 * pixels]
    rim, rest = 2 * columns, pixels - 2 * columns

    def strip(start, size):
        return k.ext1.at[pl.ds(start, size)]

    halo1 = Halo(
        p,
        (strip(pixels, rim), strip(2 * pixels, rim)),
        (strip(2 * pixels - rim, rim), strip(rest, rim)),
        k.halo_sem.at[0],
    )
    halo1_far = Halo(
        p,
        (strip(pixels + rim, rest), strip(2 * pixels + rim, rest)),
        (strip(pixels, rest), strip(0, rest)),
        k.halo_sem.at[2],
    )
    halo1.start()
    halo1_far.start()
    save(k.reduced1, k.reduced1_out)

    @pl.when(s == 0)
    def _():
        k.ext1[:pixels, :] = jnp.zeros((pixels, mid), bf)

    @pl.when(s == p.n_sp - 1)
    def _():
        k.ext1[2 * pixels :, :] = jnp.zeros((pixels, mid), bf)

    d1a.pump()
    o1.finish()
    k.ext1_t[:, pixels : 2 * pixels] = mm_nt(k.ident[...], k.ext1[pixels : 2 * pixels, :]).astype(bf)
    edge = jnp.zeros((rim, mid), bf)
    k.window[:rim, :] = edge
    k.window[14 * columns :, :] = edge
    halo1.finish()
    k.window[rim : 14 * columns, :] = k.ext1[6 * columns : 18 * columns, :]
    raw_all = jnp.zeros((9 * 32, 16 * columns), f32)
    for c in range(n_ch):
        raw_all += mm_nt(k.o1_all[c], k.window[:, c * wr : (c + 1) * wr])
    k.raw_all[...] = raw_all
    lane = iota((32, pixels), 1)
    col = lax.rem(lane, columns)
    raw = jnp.zeros((32, pixels), f32)
    for tap in range(9):
        i, j = tap // 3, tap % 3
        offset = (2 + 2 * i) * columns + 2 * (j - 1)
        part = k.raw_all[32 * tap : 32 * tap + 32, :]
        part = pltpu.roll(part, 16 * columns - offset, 1)[:, :pixels]
        if j == 0:
            part = jnp.where(col < 2, 0.0, part)
        if j == 2:
            part = jnp.where(col >= columns - 2, 0.0, part)
        raw += part
    k.bend[...] = jnp.tanh(raw)
    save(k.bend, k.bend_out)

    halo1_far.finish()
    r2.start()
    d1b.pump()
    for part in (0, 2):
        at = slice(part * pixels, (part + 1) * pixels)
        k.ext1_t[:, at] = mm_nt(k.ident[...], k.ext1[at, :]).astype(bf)
    save(k.ext1, k.ext1_out)
    d1a.finish()
    d1b.finish()
    save(k.d1_all, k.d1_all_out)
    k.spread1[...] = jnp.zeros((pixels, mid), f32)

    def tap_step(tap, carry):
        i, j = lax.div(tap, 3), lax.rem(tap, 3)
        lane = iota((1, pixels), 1)
        row = (lax.div(lane, columns) + 6 + 2 * i).astype(f32) + REACH * k.bend[pl.ds(tap, 1), :]
        across = (lax.rem(lane, columns) - 2 + 2 * j).astype(f32) + REACH * k.bend[pl.ds(tap + 16, 1), :]
        k.col_weight[...] = cell_weights(across, iota((columns, pixels), 0).astype(f32))
        base = jnp.floor(row)
        upper = smooth_rise(row - base)
        for r in range(3 * geo.height):
            weight = jnp.where(base == r, 1.0 - upper, jnp.where(base == r - 1, upper, 0.0))
            k.cells[r * columns : (r + 1) * columns, :] = (k.col_weight[...] * weight).astype(bf)
        k.cols1_t[tap] = mm(k.ext1_t[...], k.cells[...]).astype(bf)
        cols = mm_nt(k.ident[:pixels, :pixels], k.cols1_t[tap]).astype(bf)
        k.spread1[...] += mm(cols, k.d1_all[tap])
        return carry

    lax.fori_loop(0, 9, tap_step, 0)
    save(k.cols1_t, k.cols1_t_out)
    task2 = all_sum(False, 1)
    task2.put(slim, *moments(k.spread1, slim, pixels))
    task2.start()
    d2.start()
    e1.pump()
    task2.relay()
    r2.pump()
    k.totals1b[...] = task2.finish()
    save(k.spread1, k.spread1_out)
    activate(k.spread1, k.totals1b, k.gain1b, k.bias1b, k.act, 0)
    e1.finish()
    save(k.e1_all, k.e1_all_out)
    task3 = all_sum(True, 0)
    expand(k.act, k.e1_all, k.expanded1, task3)
    task3.start()
    r2.pump_again()
    task3.relay()
    d2.pump()
    k.totals1c[...] = task3.finish()
    save(k.expanded1, k.expanded1_out)
    leave(k.expanded1, k.totals1c, k.gain1c, k.bias1c, k.x, k.middle)
    save(k.middle, k.middle_out)

    r2.finish()
    save(k.r1_all, k.r1_all_out)
    save(k.r2_all, k.r2_all_out)
    save(k.o1_all, k.o1_all_out)
    reduce_matmul(k.middle, k.r2_all, k.reduced2)
    task4 = all_sum(False, 2)
    task4.put(slim, *moments(k.reduced2, slim, pixels))
    task4.start()
    e2.start()
    task4.relay()
    k.totals2a[...] = task4.finish()
    d2.pump_again()
    save(k.reduced2, k.reduced2_out)
    activate(k.reduced2, k.totals2a, k.gain2a, k.bias2a, k.ext2, rim)
    halo2 = Halo(
        p,
        (k.ext2.at[rim : 2 * rim], k.ext2.at[pixels + rim :]),
        (k.ext2.at[pixels : pixels + rim], k.ext2.at[:rim]),
        k.halo_sem.at[1],
    )
    halo2.start()

    @pl.when(s == 0)
    def _():
        k.ext2[:rim, :] = jnp.zeros((rim, mid), bf)

    @pl.when(s == p.n_sp - 1)
    def _():
        k.ext2[pixels + rim :, :] = jnp.zeros((rim, mid), bf)

    e2.pump()
    d2.finish()
    save(k.d2_all, k.d2_all_out)
    halo2.finish()

    def shift_row(r, carry):
        at = pl.ds(pl.multiple_of(r * columns, columns), columns)
        v = k.ext2[at, :].astype(f32)
        k.moved[0, at, :] = column_shift(v, 0, columns).astype(bf)
        k.moved[1, at, :] = v.astype(bf)
        k.moved[2, at, :] = column_shift(v, 2, columns).astype(bf)
        return carry

    lax.fori_loop(0, geo.height + 4, shift_row, 0)
    save(k.moved, k.moved_out)
    k.spread2[...] = jnp.zeros((pixels, mid), f32)

    def plain_step(tap, carry):
        i, j = lax.div(tap, 3), lax.rem(tap, 3)
        cols = k.moved[j, pl.ds(pl.multiple_of(i * rim, rim), pixels), :]
        k.spread2[...] += mm(cols, k.d2_all[tap])
        return carry

    lax.fori_loop(0, 9, plain_step, 0)
    task5 = all_sum(False, 3)
    task5.put(slim, *moments(k.spread2, slim, pixels))
    run_sum(task5, k.totals2b, e2.pump_again)
    save(k.spread2, k.spread2_out)
    activate(k.spread2, k.totals2b, k.gain2b, k.bias2b, k.act, 0)
    e2.finish()
    save(k.e2_all, k.e2_all_out)
    task6 = all_sum(True, 1)
    expand(k.act, k.e2_all, k.expanded2, task6)
    run_sum(task6, k.totals2c)
    save(k.expanded2, k.expanded2_out)
    leave(k.expanded2, k.totals2c, k.gain2c, k.bias2c, k.middle, k.last)
    save(k.last, k.last_out)

    for task in (*r1, o1, d1a, d1b, e1, r2, d2, e2, task1, task2, task3, task4, task5, task6, halo1, halo1_far, halo2):
        task.drain()
    for copy in saves:
        copy.wait()


def run_forward(geo, features, offset_w, shards, norms):
    bf, f32 = jnp.bfloat16, jnp.float32
    n_ch, n_sp, mid, pixels, wr, we = geo.n_ch, geo.n_sp, geo.mid, geo.pixels, geo.wr, geo.we
    ext_rows = 3 * pixels
    rim_rows = pixels + 4 * geo.columns
    near, far = 2 * n_ch, n_sp // 2
    vmem = pl.BlockSpec(memory_space=pltpu.VMEM)
    anywhere = pl.BlockSpec(memory_space=pl.ANY)
    dma = pltpu.SemaphoreType.DMA
    v = pltpu.VMEM
    close = dict(x=features, o1=offset_w, **norms)
    kept = dict(
        r1_all=((n_ch, geo.c_in, wr), bf),
        o1_all=((n_ch, 9 * 32, wr), bf),
        d1_all=((9, mid, mid), bf),
        e1_all=((n_ch, mid, we), bf),
        r2_all=((n_ch, geo.c_in, wr), bf),
        d2_all=((9, mid, mid), bf),
        e2_all=((n_ch, mid, we), bf),
        reduced1=((pixels, mid), f32),
        ext1=((ext_rows, mid), bf),
        bend=((32, pixels), f32),
        cols1_t=((9, mid, pixels), bf),
        spread1=((pixels, mid), f32),
        expanded1=((pixels, geo.c_in), f32),
        middle=((pixels, geo.c_in), bf),
        reduced2=((pixels, mid), f32),
        moved=((3, rim_rows, mid), bf),
        spread2=((pixels, mid), f32),
        expanded2=((pixels, geo.c_in), f32),
        last=((pixels, geo.c_in), bf),
    )
    totals = dict(
        totals1a=(2, mid),
        totals1b=(2, mid),
        totals1c=(2, geo.c_in),
        totals2a=(2, mid),
        totals2b=(2, mid),
        totals2c=(2, geo.c_in),
    )
    scratch = dict(
        ident=v((mid, mid), bf),
        ext1_t=v((mid, ext_rows), bf),
        raw_all=v((9 * 32, 16 * geo.columns), f32),
        col_weight=v((geo.columns, pixels), f32),
        cells=v((ext_rows, pixels), bf),
        act=v((pixels, mid), bf),
        ext2=v((rim_rows, mid), bf),
        slim_one=v((4, near, 2, mid), f32),
        slim_two=v((4, far, 2, mid), f32),
        slim_send=dma((4, near + far)),
        slim_recv_one=dma((4, near)),
        slim_recv_two=dma((4, far)),
        wide_one=v((2, near, 2, geo.c_in), f32),
        wide_two=v((2, far, 2, geo.c_in), f32),
        wide_send=dma((2, near + far)),
        wide_recv_one=dma((2, near)),
        wide_recv_two=dma((2, far)),
        gather_send=dma((5, n_ch)),
        gather_recv=dma((5, n_ch)),
        half_send=dma((7, 2 + 4 * (n_ch // 2 - 1))),
        half_recv=dma((7, 2 * n_ch)),
        o1_own=v((9 * 32, wr), bf),
        window=v((16 * geo.columns, mid), bf),
        halo_sem=dma((3, 4)),
        save_sem=dma((len(kept),)),
    )
    scratch |= {name: v(*what) for name, what in kept.items()}
    out_names = [f"{name}_out" for name in kept]
    results = pl.pallas_call(
        functools.partial(forward_kernel, geo, [*close, *shards, *out_names, *totals, *scratch]),
        out_shape=[jax.ShapeDtypeStruct(*what) for what in kept.values()]
        + [jax.ShapeDtypeStruct(shape, f32) for shape in totals.values()],
        in_specs=[vmem] * len(close) + [anywhere] * len(shards),
        out_specs=[anywhere] * len(kept) + [vmem] * len(totals),
        scratch_shapes=list(scratch.values()),
        compiler_params=pltpu.CompilerParams(
            collective_id=0, has_side_effects=True, vmem_limit_bytes=60 * MIB
        ),
    )(*close.values(), *shards.values())
    return types.SimpleNamespace(**dict(zip([*kept, *totals], results, strict=True)))


class Reduce:
    def __init__(self, place, stage, one, two, three, four, total, done, send, recv, z_first=False):
        self.z_first = z_first
        self.p, self.stage, self.one, self.two, self.three, self.four = place, stage, one, two, three, four
        self.total, self.done = total, done
        self.send, self.recv = send, recv
        self.n_far = place.n_sp // 2
        self.half = stage.shape[2] // 2
        self.chunk = self.half // self.n_far
        self.row = lax.div(place.s, 2)
        self.pair = (place.s + 1 - 2 * place.y, place.c)
        self.mine = stage.at[place.k, place.x]
        self.at_x, self.at_out = 3, 3 + place.n_x
        self.at_back = self.at_out + 2 * self.n_far

    nothing = types.SimpleNamespace(**dict.fromkeys(["s1", "s2", "s3", "s3_add", "s3_send", "s4", "s5", "s6", "freed", "s7_end", "s7"], lambda: None))

    @staticmethod
    def sems(n_sp, n_ch):
        return 3 + n_ch // 2 + 3 * (n_sp // 2)

    def _half(self, ref, y):
        return ref.at[pl.ds(pl.multiple_of(y * self.half, 16), self.half)]

    def _chunk(self, ref, z, y=None):
        y = self.p.y if y is None else y
        return ref.at[pl.ds(pl.multiple_of(y * self.half + z * self.chunk, 16), self.chunk)]

    def _to_sibling(self):
        return remote(self.stage.at[1 - self.p.k], self.one, self.send.at[0], self.recv.at[0], self.p.sibling)

    def _to_x(self, d):
        other = lax.rem(self.p.x + d, self.p.n_x)
        return remote(
            self.stage.at[self.p.k, other],
            self.two.at[self.p.n_x - d - 1],
            self.send.at[self.at_x + d],
            self.recv.at[self.at_x + self.p.n_x - d],
            (self.p.s, 2 * other + self.p.k),
        )

    def _to_pair(self):
        if self.z_first:
            source, there = self._chunk(self.total, self.row, 1 - self.p.y), self.three.at[pl.ds(0, self.chunk)]
        else:
            source, there = self._half(self.total, 1 - self.p.y), self.three
        return remote(source, there, self.send.at[1], self.recv.at[1], self.pair)

    def _from(self, z, h):
        return self.four.at[z, pl.ds(h * self.chunk, self.chunk)]

    def _out(self, d, h):
        other = lax.rem(self.row + d, self.n_far)
        source = self._chunk(self.total, other, h if self.z_first else None)
        n = self.at_out + h * self.n_far
        return remote(source, self._from(self.row, h), self.send.at[n + d], self.recv.at[n + self.row], self.p.far(d))

    def _back(self, d):
        return remote(
            self._chunk(self.done, self.row), self._chunk(self.done, self.row), self.send.at[self.at_back + d], self.recv.at[self.at_back + self.row], self.p.far(d)
        )

    def _pair_back(self, y):
        return remote(self._half(self.done, y), self._half(self.done, y), self.send.at[2], self.recv.at[2], self.pair)

    def _await(self, ref, sem):
        remote(ref, ref, self.send.at[0], sem, self.p.sibling).wait_recv()

    def _add(self, source, start, rows, pieces, out):
        step = max(n for n in (16, 32, 48, 64) if rows % n == 0)

        def one(i, carry):
            at = pl.ds(pl.multiple_of(start + i * step, 16), step)
            there = pl.ds(pl.multiple_of(i * step, 16), step)
            total = source[at, :].astype(jnp.float32)
            for piece in pieces:
                total = total + piece[there, :].astype(jnp.float32)
            out[at, :] = total.astype(jnp.bfloat16)
            return carry

        lax.fori_loop(0, rows // step, one, 0)

    def s1(self):
        self._to_sibling().start()

    def s2(self):
        self._await(self.one, self.recv.at[0])
        rows = self.stage.shape[2]
        step = max(n for n in (16, 32, 48, 64) if rows % n == 0)
        for x in range(self.p.n_x):

            def one(i, carry):
                at = pl.ds(pl.multiple_of(i * step, 16), step)
                total = self.stage[self.p.k, x, at, :].astype(jnp.float32) + self.one[x, at, :].astype(jnp.float32)
                self.stage[self.p.k, x, at, :] = total.astype(jnp.bfloat16)
                return carry

            lax.fori_loop(0, rows // step, one, 0)
        for d in range(1, self.p.n_x):
            self._to_x(d).start()

    def s3_add(self):
        for d in range(1, self.p.n_x):
            self._await(self.two.at[d - 1], self.recv.at[self.at_x + d])
        pieces = [self.two.at[d - 1] for d in range(1, self.p.n_x)]
        self._add(self.mine, 0, self.stage.shape[2], pieces, self.total)
        self._to_sibling().wait_send()
        for d in range(1, self.p.n_x):
            self._to_x(d).wait_send()

    def _start_out(self):
        for d in range(1, self.n_far):
            for h in range(1 + self.z_first):
                self._out(d, h).start()

    def _add_far(self, h, y, out):
        others = [lax.rem(self.row + d, self.n_far) for d in range(1, self.n_far)]
        for other in others:
            self._await(self._from(other, h), self.recv.at[self.at_out + h * self.n_far + other])
        start = y * self.half + self.row * self.chunk
        self._add(self.total, start, self.chunk, [self._from(other, h) for other in others], out)

    def s3_send(self):
        if self.z_first:
            self._start_out()
        else:
            self._to_pair().start()

    def s3(self):
        self.s3_add()
        self.s3_send()

    def s4(self):
        if self.z_first:
            for h in range(2):
                self._add_far(h, h, self.total)
            self._to_pair().start()
        else:
            self._await(self.three, self.recv.at[1])
            self._add(self.total, self.p.y * self.half, self.half, [self.three], self.total)
            self._start_out()

    def s5(self):
        if self.z_first:
            there = self.three.at[pl.ds(0, self.chunk)]
            self._await(there, self.recv.at[1])
            start = self.p.y * self.half + self.row * self.chunk
            self._add(self.total, start, self.chunk, [there], self.done)
        else:
            self._add_far(0, self.p.y, self.done)
        for d in range(1, self.n_far):
            self._back(d).start()

    def s6(self):
        for d in range(1, self.n_far):
            other = lax.rem(self.row + d, self.n_far)
            self._await(self._chunk(self.done, other), self.recv.at[self.at_back + other])
        self._pair_back(self.p.y).start()

    def freed(self):
        self._to_pair().wait_send()
        for d in range(1, self.n_far):
            for h in range(1 + self.z_first):
                self._out(d, h).wait_send()

    def s7_end(self):
        self._await(self._half(self.done, 1 - self.p.y), self.recv.at[2])
        self._pair_back(self.p.y).wait_send()
        for d in range(1, self.n_far):
            self._back(d).wait_send()

    def s7(self):
        self.freed()
        self.s7_end()


def slope_of(v):
    sigma = sigmoid(v)
    return sigma, sigma * (1.0 + v * (1.0 - sigma))


def backward_kernel(geo, names, *refs):
    k = types.SimpleNamespace(**dict(zip(names, refs, strict=True)))
    p = Place(geo.n_sp, geo.n_ch)
    s, pixels, columns, mid = p.s, geo.pixels, geo.columns, geo.mid
    n_ch, wr, we, total = p.n_ch, geo.wr, geo.we, geo.pixel_total
    bf, f32 = jnp.bfloat16, jnp.float32
    rim = 2 * columns
    slim = pl.ds(0, mid)
    count = [0, 0, 0]

    cells = k.moved.at[pl.ds(0, 3 * pixels), pl.ds(0, pixels)]
    placed = k.third.at[pl.ds(0, 9 * 32), pl.ds(2 * mid, 16 * columns)]
    placed_t = k.moved.at[pl.ds(0, 16 * columns)]
    cols_grad_t = k.moved.at[pl.ds(3 * pixels, mid), pl.ds(0, pixels)]

    def load(src, dst):
        copy = pltpu.make_async_copy(src, dst, k.load_sem.at[count[0]])
        count[0] += 1
        copy.start()
        return copy

    def write_out(src, dst):
        copy = pltpu.make_async_copy(src, dst, k.out_sem.at[count[1]])
        count[1] += 1
        copy.start()
        return copy

    def reduction(*buffers, z_first=False):
        i = count[2]
        count[2] += 1
        return Reduce(p, *buffers, k.reduce_send.at[i], k.reduce_recv.at[i], z_first)

    def for_e():
        return reduction(k.stage_e, k.one_e, k.two_e, k.three_e, k.four_e, k.total_e, k.done_e)

    d_parts, tap_count = geo.d_parts, 9 // geo.d_parts

    def for_d(four, done, *z_first):
        buffers = (k.stage_d, k.one_d, k.two_d, k.three_d, four, k.total_d, done)
        parts = [reduction(*[b.at[i] for b in buffers], z_first=i in z_first and d_parts == 3) for i in range(d_parts)]
        return parts if d_parts == 3 else [Reduce.nothing, Reduce.nothing, parts[0]]

    def for_r(done):
        buffers = (k.stage_r, k.one_r, k.two_r, k.three_r, k.four_r, k.total_r, done)
        return [reduction(*[buffer.at[i] for buffer in buffers]) for i in range(4)]

    def all_sum(wide, i):
        if wide:
            parts = (k.wide_one, k.wide_two, k.wide_send, k.wide_recv_one, k.wide_recv_two)
        else:
            parts = (k.slim_one, k.slim_two, k.slim_send, k.slim_recv_one, k.slim_recv_two)
        return AllSum(p, *[part.at[i] for part in parts])

    def place_of(c):
        return c % 2, c // 2

    def norm_of(totals, lanes):
        return center_inverse(totals[0:1, lanes], totals[1:2, lanes], total)

    def block_end(upstream, totals, gain, bias, task):
        for start in range(0, geo.c_in, 512):
            lanes = pl.ds(start, 512)
            center, inverse = norm_of(totals, lanes)
            gain_row, bias_row = gain[:, lanes], bias[:, lanes]

            def body(at, carry):
                normed = (k.expanded[at, lanes] - center) * inverse
                joined = gain_row * normed + bias_row + k.inputs[at, lanes].astype(f32)
                grad = upstream(at, lanes) * slope_of(joined)[1]
                k.grad[at, lanes] = grad
                return carry[0] + fold(grad), carry[1] + fold(grad * normed)

            zero = jnp.zeros((8, 512), f32)
            a, b = over_rows(pixels, 16, body, (zero, zero))
            task.put(lanes, jnp.sum(a, axis=0, keepdims=True), jnp.sum(b, axis=0, keepdims=True))

    def third_norm(totals, grads, gain):
        for start in range(0, geo.c_in, 512):
            lanes = pl.ds(start, 512)
            center, inverse = norm_of(totals, lanes)
            scale = gain[:, lanes] * inverse
            bias_mean = grads[0:1, lanes] / total
            gain_mean = grads[1:2, lanes] / total

            def body(at, carry):
                normed = (k.expanded[at, lanes] - center) * inverse
                inner = k.grad[at, lanes] - bias_mean - normed * gain_mean
                k.third[at, lanes] = (scale * inner).astype(bf)
                return carry

            over_rows(pixels, 16, body, 0)

    def act_grad(values, totals, gain, bias, act, task):
        center, inverse = norm_of(totals, slim)
        gain_row, bias_row = gain[...], bias[...]

        def body(at, carry):
            normed = (values[at, :] - center) * inverse
            pre = gain_row * normed + bias_row
            sigma, slope = slope_of(pre)
            if act is not None:
                act[at, :] = (pre * sigma).astype(bf)
            grad = k.flow[at, :] * slope
            k.flow[at, :] = grad
            return carry[0] + fold(grad), carry[1] + fold(grad * normed)

        zero = jnp.zeros((8, mid), f32)
        a, b = over_rows(pixels, 16, body, (zero, zero))
        task.put(slim, jnp.sum(a, axis=0, keepdims=True), jnp.sum(b, axis=0, keepdims=True))

    def norm_grad(values, totals, grads, gain, out):
        center, inverse = norm_of(totals, slim)
        scale = gain[...] * inverse
        bias_mean = grads[0:1, :] / total
        gain_mean = grads[1:2, :] / total

        def body(at, carry):
            normed = (values[at, :] - center) * inverse
            out[at, :] = (scale * (k.flow[at, :] - bias_mean - normed * gain_mean)).astype(bf)
            return carry

        over_rows(pixels, 16, body, 0)

    def through_expand():
        for c in range(n_ch):
            part = mm_nt(k.third[:, c * we : (c + 1) * we], k.e[c])
            if c == 0:
                k.flow[...] = part
            else:
                k.flow[...] += part

    def expand_weights():
        k.act_t[...] = mm_nt(k.ident[...], k.low1[...]).astype(bf)
        for c in range(n_ch):
            k.stage_e[place_of(c)] = mm(k.act_t[...], k.third[:, c * we : (c + 1) * we]).astype(bf)

    def stage_tap(tap, cols_t):
        product = mm(cols_t, k.low2[...])
        part, inner = lax.div(tap, tap_count), lax.rem(tap, tap_count)
        for c in range(n_ch):
            for q in range(mid // 128):
                at = pl.ds(pl.multiple_of(inner * wr + q * tap_count * wr, 16), wr)
                piece = product[c * wr : (c + 1) * wr, q * 128 : (q + 1) * 128]
                k.stage_d[(part, *place_of(c), at)] = piece.astype(bf)

    def through_reduce():
        for start in range(0, geo.c_in, 512):
            rows = pl.ds(start, 512)
            for c in range(n_ch):
                k.grad[:, start : start + 512] += mm_nt(k.low1[:, c * wr : (c + 1) * wr], k.r[c, rows, :])

    def reduce_weights(work):
        for i, start in enumerate(range(0, geo.c_in, 512)):
            inputs_t = mm_nt(k.ident[...], k.inputs[:, start : start + 512]).astype(bf)
            product = mm(inputs_t, k.low1[...])
            for c in range(n_ch):
                k.stage_r[(i, *place_of(c))] = product[:, c * wr : (c + 1) * wr].astype(bf)
            work[i].s1()

    def deliver(task, out):
        return write_out(task.done.at[pl.ds(0, out.shape[0])], out)

    def deliver_d(parts, out):
        return [deliver(task, out.at[i]) for i, task in enumerate(parts[-d_parts:])]

    def deliver_r(parts, out):
        return [deliver(task, out.at[i]) for i, task in enumerate(parts)]

    def wait_all(copies):
        for copy in copies:
            copy.wait()

    def fetch(tap, slot):
        return pltpu.make_async_copy(k.cols1.at[tap], k.cols_t.at[slot], k.fetch_sem.at[slot])

    def sampled_tap(tap, carry):
        slot = lax.rem(tap, 2)

        @pl.when(tap < 8)
        def _():
            fetch(tap + 1, 1 - slot).start()

        fetch(tap, slot).wait()
        stage_tap(tap, k.cols_t[slot])
        return carry

    def rims_of(up, up_at, down, down_at, rows, sems):
        up_to, down_to = pl.ds(up_at, rows), pl.ds(down_at, rows)
        halo = Halo(
            p,
            (k.third.at[up_to, pl.ds(0, mid)], k.rim_recv.at[1, up_to]),
            (k.third.at[down_to, pl.ds(mid, mid)], k.rim_recv.at[0, down_to]),
            sems,
        )
        k.third[up_at : up_at + rows, :mid] = k.spread_grad[up : up + rows, :].astype(bf)
        k.third[down_at : down_at + rows, mid : 2 * mid] = k.spread_grad[down : down + rows, :].astype(bf)
        return halo

    def add_rims(rows):
        @pl.when(s > 0)
        def _():
            k.flow[:rows, :] += k.rim_recv[0, :rows, :].astype(f32)

        @pl.when(s < p.n_sp - 1)
        def _():
            k.flow[pixels - rows :, :] += k.rim_recv[1, :rows, :].astype(f32)

    expanded2 = load(k.expanded2, k.expanded)
    middle = load(k.middle, k.inputs)
    cotangent = load(k.cotangent, k.third)
    e2 = load(k.e2, k.e)
    spread2 = load(k.spread2, k.spread)
    d2 = load(k.d2, k.d)
    moved2 = load(k.moved_in, k.moved)
    reduced2 = load(k.reduced2, k.reduced)
    r2 = load(k.r2, k.r)
    ext1 = load(k.ext1_in, k.ext1)
    o1 = load(k.o1_in, k.o1)
    p.barrier()
    set_identity(k.ident)
    stages = [(k.stage_o, 9 * 32)] + [(k.stage_d.at[i], tap_count * wr * mid // 128) for i in range(d_parts)]
    for stage, rows in stages:
        if stage.shape[2] > rows:
            for q in range(n_ch):
                spare = (stage.shape[2] - rows, stage.shape[3])
                stage[(*place_of(q), pl.ds(rows, spare[0]))] = jnp.zeros(spare, bf)

    expanded2.wait()
    middle.wait()
    cotangent.wait()
    sum2c = all_sum(True, 0)
    counts = k.counts[...].astype(f32)
    mine = jnp.where(iota(counts.shape, 1) == p.c, counts, 0.0)
    box = jnp.sum(mine, axis=1, keepdims=True) * counts.shape[1] / jnp.sum(counts, axis=1, keepdims=True)
    block_end(lambda at, lanes: k.third[at, lanes].astype(f32) * box, k.totals2c, k.gain2c, k.bias2c, sum2c)
    sum2c.start()
    e2.wait()
    spread2.wait()
    d2.wait()
    moved2.wait()
    reduced2.wait()
    r2.wait()
    sum2c.relay()
    k.grads2c[...] = sum2c.finish()
    third_norm(k.totals2c, k.grads2c, k.gain2c)
    expanded1 = load(k.expanded1, k.expanded)
    through_expand()
    e1 = load(k.e1, k.e)
    sum2b = all_sum(False, 0)
    act_grad(k.spread, k.totals2b, k.gain2b, k.bias2b, k.low1, sum2b)
    sum2b.start()
    expand_weights()
    work_e2 = for_e()
    work_e2.s1()
    sum2b.relay()
    k.grads2b[...] = sum2b.finish()
    norm_grad(k.spread, k.totals2b, k.grads2b, k.gain2b, k.low2)
    spread1 = load(k.spread1, k.spread)
    work_e2.s2()

    area = pixels + 2 * rim
    k.spread_grad[:area, :] = jnp.zeros((area, mid), f32)
    for j in range(3):
        k.spread_grad[area : 2 * area, :] = jnp.zeros((area, mid), f32)

        def row_step(i, carry):
            at = pl.ds(pl.multiple_of(area + i * rim, 16), pixels)
            k.spread_grad[at, :] += mm_nt(k.low2[...], k.d[3 * i + j])
            return carry

        lax.fori_loop(0, 3, row_step, 0)

        def shift_back(r, carry):
            at = pl.ds(pl.multiple_of(r * columns, 16), columns)
            there = pl.ds(pl.multiple_of(area + r * columns, 16), columns)
            k.spread_grad[at, :] += column_shift(k.spread_grad[there, :], 2 - j, columns)
            return carry

        lax.fori_loop(0, geo.height + 4, shift_back, 0)
    d1 = load(k.d1, k.d)
    halo2 = rims_of(0, 0, pixels + rim, 0, rim, k.halo_sem.at[0])
    halo2.start()
    k.flow[...] = k.spread_grad[rim : pixels + rim, :]

    def plain_tap(tap, carry):
        first = lax.rem(tap, 3) * (pixels + 2 * rim) + lax.div(tap, 3) * rim
        cols = k.moved[pl.ds(pl.multiple_of(first, 16), pixels), :]
        stage_tap(tap, mm_nt(k.ident[...], cols).astype(bf))
        return carry

    work_d2 = for_d(k.four_d2, k.done_d2)
    for i in range(3):
        lax.fori_loop(3 * i, 3 * i + 3, plain_tap, 0)
        work_d2[i].s1()
    halo2.finish()
    add_rims(rim)
    sum2a = all_sum(False, 1)
    act_grad(k.reduced, k.totals2a, k.gain2a, k.bias2a, None, sum2a)
    sum2a.start()
    work_d2[0].s2()
    work_e2.s3()
    work_d2[1].s2()
    sum2a.relay()
    k.grads2a[...] = sum2a.finish()
    norm_grad(k.reduced, k.totals2a, k.grads2a, k.gain2a, k.low1)
    reduced1 = load(k.reduced1, k.reduced)
    through_reduce()
    r1 = load(k.r1, k.r)
    work_e2.s4()
    work_r2 = for_r(k.done_r2)
    reduce_weights(work_r2)
    features = load(k.features, k.inputs)

    expanded1.wait()
    features.wait()
    sum1c = all_sum(True, 1)
    block_end(lambda at, lanes: k.grad[at, lanes], k.totals1c, k.gain1c, k.bias1c, sum1c)
    sum1c.start()
    work_d2[2].s2()
    work_r2[0].s2()
    work_r2[1].s2()
    work_d2[0].s3()
    work_d2[1].s3()
    e1.wait()
    spread1.wait()
    d1.wait()
    reduced1.wait()
    r1.wait()
    ext1.wait()
    o1.wait()
    sum1c.relay()
    k.grads1c[...] = sum1c.finish()
    work_e2.s5()
    work_d2[0].s4()
    halo2.drain()
    third_norm(k.totals1c, k.grads1c, k.gain1c)
    through_expand()
    sum1b = all_sum(False, 2)
    act_grad(k.spread, k.totals1b, k.gain1b, k.bias1b, k.low1, sum1b)
    work_d2[2].s3_add()
    sum1b.start()
    work_r2[2].s2()
    work_r2[3].s2()
    work_e2.s6()
    work_d2[2].s3_send()
    expand_weights()
    work_r2[0].s3()
    work_r2[1].s3()
    work_e1 = for_e()
    sum1b.relay()
    work_e1.s1()
    work_e2.s7()
    e2_copy = deliver(work_e2, k.grad_e2)
    fetch(0, 0).start()
    k.grads1b[...] = sum1b.finish()
    work_d2[1].s4()
    work_d2[0].s5()
    norm_grad(k.spread, k.totals1b, k.grads1b, k.gain1b, k.low2)
    work_e1.s2()
    work_d1 = for_d(k.four_d, k.done_d, 0, 1)
    for i in range(3):
        lax.fori_loop(3 * i, 3 * i + 3, sampled_tap, 0)
        work_d1[i].s1()

    k.spread_grad[...] = jnp.zeros((3 * pixels, mid), f32)
    k.raw_grad[...] = jnp.zeros((32, pixels), f32)

    def tap_step(tap, carry):
        @pl.when(tap == 0)
        def _():
            work_d1[0].s2()
            work_d2[2].s4()
            work_d2[1].s5()
            work_d2[0].s6()

        @pl.when(tap == 3)
        def _():
            work_d1[1].s2()
            work_r2[0].s4()
            work_r2[1].s4()
            work_r2[2].s3()
            work_r2[3].s3()
            work_d2[2].s5()

        @pl.when(tap == 6)
        def _():
            work_e1.s3()
            work_r2[2].s4()
            work_r2[3].s4()

        i, j = lax.div(tap, 3), lax.rem(tap, 3)
        lane = iota((1, pixels), 1)
        row = (lax.div(lane, columns) + 6 + 2 * i).astype(f32) + REACH * k.bend[pl.ds(tap, 1), :]
        across = (lax.rem(lane, columns) - 2 + 2 * j).astype(f32) + REACH * k.bend[pl.ds(tap + 16, 1), :]
        cell = iota((columns, pixels), 0).astype(f32)
        k.col_weight[...] = cell_weights(across, cell)
        row_base = jnp.floor(row)
        row_part = row - row_base
        row_upper = smooth_rise(row_part)
        row_rate = 6.0 * row_part * (1.0 - row_part)
        for r in range(3 * geo.height):
            weight = jnp.where(row_base == r, 1.0 - row_upper, jnp.where(row_base == r - 1, row_upper, 0.0))
            cells[r * columns : (r + 1) * columns, :] = (k.col_weight[...] * weight).astype(bf)
        cols_grad_t[...] = mm_nt(k.d[tap], k.low2[...]).astype(bf)
        k.spread_grad[...] += mm_nt(cells[...], cols_grad_t[...])
        for part in range(3):
            rows_at = slice(part * pixels, (part + 1) * pixels)
            k.expanded[:, 512 * part : 512 * part + pixels] = mm(k.ext1[rows_at, :], cols_grad_t[...])
        for start in range(0, pixels, 128):
            lanes = slice(start, start + 128)
            base, upper, rate = row_base[:, lanes], row_upper[:, lanes], row_rate[:, lanes]
            along = jnp.zeros((columns, 128), f32)
            down = jnp.zeros((columns, 128), f32)
            for r in range(3 * geo.height):
                row_at, col_at = r % geo.height * columns, r // geo.height * 512 + start
                match = k.expanded[row_at : row_at + columns, col_at : col_at + 128]
                at, after = base == r, base == r - 1
                along += match * jnp.where(at, 1.0 - upper, jnp.where(after, upper, 0.0))
                down += match * jnp.where(at, -rate, jnp.where(after, rate, 0.0))
            place = across[:, lanes]
            col_base = jnp.floor(place)
            col_part = place - col_base
            col_rate = 6.0 * col_part * (1.0 - col_part)
            cell_at = cell[:, lanes]
            col_slope = jnp.where(cell_at == col_base, -col_rate, jnp.where(cell_at == col_base + 1.0, col_rate, 0.0))
            here = iota((16, 128), 0) == tap
            by_row = jnp.sum(down * k.col_weight[:, lanes], axis=0, keepdims=True)
            by_col = jnp.sum(along * col_slope, axis=0, keepdims=True)
            k.raw_grad[:16, lanes] = jnp.where(here, by_row, k.raw_grad[:16, lanes])
            k.raw_grad[16:, lanes] = jnp.where(here, by_col, k.raw_grad[16:, lanes])
        return carry

    lax.fori_loop(0, 9, tap_step, 0)
    rest = pixels - rim
    halo1_far = rims_of(0, 0, 2 * pixels + rim, rim, rest, k.halo_sem.at[2])
    halo1_far.start()

    window = slice(6 * columns, 18 * columns)
    inner = slice(2 * columns, 14 * columns)
    bend = k.bend[...]
    raw = k.raw_grad[...] * (REACH * (1.0 - bend * bend))
    col = lax.rem(iota((32, pixels), 1), columns)
    for tap in range(9):
        i, j = tap // 3, tap % 3
        offset = (2 + 2 * i) * columns + 2 * (j - 1)
        part = raw
        if j == 0:
            part = jnp.where(col < 2, 0.0, part)
        if j == 2:
            part = jnp.where(col >= columns - 2, 0.0, part)
        part = jnp.concatenate([part, jnp.zeros((32, 16 * columns - pixels), f32)], axis=1)
        placed[32 * tap : 32 * tap + 32, :] = pltpu.roll(part, offset, 1).astype(bf)
    for start in range(0, 16 * columns, 256):
        placed_t[start : start + 256, : 9 * 32] = mm_nt(k.ident[:256, :256], placed[:, start : start + 256]).astype(bf)
    for c in range(n_ch):
        k.spread_grad[window, c * wr : (c + 1) * wr] += mm(placed_t[inner, : 9 * 32], k.o1[c])
    halo1 = rims_of(rest, rest, 2 * pixels, 0, rim, k.halo_sem.at[1])
    halo1.start()
    k.flow[...] = k.spread_grad[pixels : 2 * pixels, :]
    product = mm(placed[...], k.ext1[4 * columns : 20 * columns, :])
    for c in range(n_ch):
        k.stage_o[(*place_of(c), pl.ds(0, 9 * 32))] = product[:, c * wr : (c + 1) * wr].astype(bf)
    work_o1 = reduction(k.stage_o, k.one_o, k.two_o, k.three_o, k.four_o, k.total_o, k.done_o)
    work_o1.s1()

    e2_copy.wait()
    work_e1.s4()
    work_d1[2].s2()
    for part in work_d2:
        part.freed()
    work_d1[0].s3()
    work_d1[1].s3()
    halo1_far.finish()
    halo1.finish()
    add_rims(pixels)
    sum1a = all_sum(False, 3)
    act_grad(k.reduced, k.totals1a, k.gain1a, k.bias1a, None, sum1a)
    sum1a.start()
    work_d2[1].s6()
    work_d2[2].s6()
    work_o1.s2()
    sum1a.relay()
    work_d1[0].s4()
    k.grads1a[...] = sum1a.finish()
    work_e1.s5()
    for part in work_r2:
        part.s5()
    norm_grad(k.reduced, k.totals1a, k.grads1a, k.gain1a, k.low1)
    work_r1 = for_r(k.done_r)
    reduce_weights(work_r1)
    for part in work_r1:
        part.s2()
    work_d1[2].s3()
    work_d1[1].s4()
    through_reduce()
    d_features = write_out(k.grad, k.d_features)
    for part in work_d2:
        part.s7_end()
    d2_copies = deliver_d(work_d2, k.grad_d2)
    work_o1.s3()
    work_e1.s6()
    for part in work_r2:
        part.freed()
    work_r1[0].s3()
    work_d1[0].s5()
    work_d1[1].s5()
    work_r2[0].s6()
    work_r2[1].s6()
    work_r1[1].s3()
    work_r1[0].s4()
    work_d1[2].s4()
    work_r2[2].s6()
    work_r2[3].s6()
    work_r1[2].s3()
    work_r1[1].s4()
    work_o1.s4()
    for part in work_r2:
        part.s7_end()
    r2_copies = deliver_r(work_r2, k.grad_r2)
    work_r1[0].s5()
    work_r1[3].s3()
    work_d1[0].s6()
    work_r1[2].s4()
    work_r1[1].s5()
    work_d1[2].s5()
    work_r1[0].s6()
    work_r1[3].s4()
    work_d1[1].s6()
    work_o1.s5()
    work_r1[2].s5()
    work_r1[1].s6()
    work_e1.s7()
    e1_copy = deliver(work_e1, k.grad_e1)
    work_r1[3].s5()
    work_r1[2].s6()
    work_o1.s6()
    work_d1[2].s6()
    work_r1[3].s6()
    for part in work_d1:
        part.s7()
    d1_copies = deliver_d(work_d1, k.grad_d1)
    work_o1.s7()
    o1_copy = deliver(work_o1, k.grad_o1)
    for part in work_r1:
        part.s7()
    wait_all(deliver_r(work_r1, k.grad_r1) + d1_copies + d2_copies + r2_copies)
    e1_copy.wait()
    o1_copy.wait()
    for task in (sum2c, sum2b, sum2a, sum1c, sum1b, sum1a, halo1, halo1_far):
        task.drain()
    d_features.wait()


def run_backward(geo, kept, features, cotangent, counts, norms):
    bf, f32 = jnp.bfloat16, jnp.float32
    n_ch, n_sp, mid, pixels, wr, we = geo.n_ch, geo.n_sp, geo.mid, geo.pixels, geo.wr, geo.we
    n_x, near, far = n_ch // 2, 2 * n_ch, n_sp // 2
    columns, c_in = geo.columns, geo.c_in
    rim = 2 * columns
    vmem = pl.BlockSpec(memory_space=pltpu.VMEM)
    anywhere = pl.BlockSpec(memory_space=pl.ANY)
    far_away = dict(
        features=features,
        cotangent=cotangent,
        expanded2=kept.expanded2,
        middle=kept.middle,
        e2=kept.e2_all,
        spread2=kept.spread2,
        d2=kept.d2_all,
        moved_in=kept.moved.reshape(-1, mid),
        reduced2=kept.reduced2,
        r2=kept.r2_all,
        expanded1=kept.expanded1,
        e1=kept.e1_all,
        spread1=kept.spread1,
        d1=kept.d1_all,
        cols1=kept.cols1_t,
        ext1_in=kept.ext1,
        reduced1=kept.reduced1,
        r1=kept.r1_all,
        o1_in=kept.o1_all,
    )
    close = dict(
        bend=kept.bend,
        counts=counts,
        totals1a=kept.totals1a,
        totals1b=kept.totals1b,
        totals1c=kept.totals1c,
        totals2a=kept.totals2a,
        totals2b=kept.totals2b,
        totals2c=kept.totals2c,
        **norms,
    )
    grads = dict(
        grad_e2=((mid, we), bf, anywhere),
        grad_d2=((geo.d_parts, 9 // geo.d_parts * wr * 4, 128), bf, anywhere),
        grad_r2=((4, 512, wr), bf, anywhere),
        grad_e1=((mid, we), bf, anywhere),
        grad_d1=((geo.d_parts, 9 // geo.d_parts * wr * 4, 128), bf, anywhere),
        grad_r1=((4, 512, wr), bf, anywhere),
        grad_o1=((9 * 32, wr), bf, anywhere),
        d_features=((pixels, c_in), f32, anywhere),
        grads2c=((2, c_in), f32, vmem),
        grads2b=((2, mid), f32, vmem),
        grads2a=((2, mid), f32, vmem),
        grads1c=((2, c_in), f32, vmem),
        grads1b=((2, mid), f32, vmem),
        grads1a=((2, mid), f32, vmem),
    )
    dma = pltpu.SemaphoreType.DMA
    v = pltpu.VMEM
    scratch = dict(
        e=v((n_ch, mid, we), bf),
        d=v((9, mid, mid), bf),
        r=v((n_ch, c_in, wr), bf),
        o1=v((n_ch, 9 * 32, wr), bf),
        expanded=v((pixels, c_in), f32),
        grad=v((pixels, c_in), f32),
        inputs=v((pixels, c_in), bf),
        third=v((pixels, c_in), bf),
        spread=v((pixels, mid), f32),
        reduced=v((pixels, mid), f32),
        flow=v((pixels, mid), f32),
        act_t=v((mid, pixels), bf),
        low1=v((pixels, mid), bf),
        low2=v((pixels, mid), bf),
        moved=v((3 * (pixels + 2 * rim), mid), bf),
        ext1=v((3 * pixels, mid), bf),
        cols_t=v((2, mid, pixels), bf),
        col_weight=v((columns, pixels), f32),
        spread_grad=v((3 * pixels, mid), f32),
        raw_grad=v((32, pixels), f32),
        ident=v((mid, mid), bf),
        rim_recv=v((2, pixels, mid), bf),
        slim_one=v((4, near, 2, mid), f32),
        slim_two=v((4, far, 2, mid), f32),
        slim_send=dma((4, near + far)),
        slim_recv_one=dma((4, near)),
        slim_recv_two=dma((4, far)),
        wide_one=v((2, near, 2, c_in), f32),
        wide_two=v((2, far, 2, c_in), f32),
        wide_send=dma((2, near + far)),
        wide_recv_one=dma((2, near)),
        wide_recv_two=dma((2, far)),
        halo_sem=dma((3, 4)),
        load_sem=dma((20,)),
        out_sem=dma((24,)),
        fetch_sem=dma((2,)),
        reduce_send=dma((17, Reduce.sems(n_sp, n_ch))),
        reduce_recv=dma((17, Reduce.sems(n_sp, n_ch))),
    )

    def staging(rows, lanes, *parts, both=1):
        return (
            v((*parts, 2, n_x, rows, lanes), bf),
            v((*parts, n_x, rows, lanes), bf),
            v((*parts, n_x - 1, rows, lanes), bf),
            v((*parts, rows // 2, lanes), bf),
            v((*parts, far, both * rows // n_sp, lanes), bf),
            v((*parts, rows, lanes), bf),
            v((*parts, rows, lanes), bf),
        )

    def padded(rows):
        return -(-rows // (32 * far)) * 32 * far

    d_rows = padded(9 // geo.d_parts * wr * mid // 128)
    e, d, r, o = staging(mid, we), staging(d_rows, 128, geo.d_parts, both=2 if geo.d_parts == 3 else 1), staging(512, wr, 4), staging(padded(9 * 32), wr)
    scratch |= dict(stage_e=e[0], one_e=e[1], two_e=e[2], three_e=e[3], four_e=e[4], total_e=e[5], done_e=e[6])
    scratch |= dict(stage_d=d[0], one_d=d[1], two_d=d[2], three_d=d[3], four_d=d[4], total_d=d[5], done_d=d[6], done_d2=d[6], four_d2=d[4])
    scratch |= dict(stage_r=r[0], one_r=r[1], two_r=r[2], three_r=r[3], four_r=r[4], total_r=r[5], done_r=r[6], done_r2=r[6])
    scratch |= dict(stage_o=o[0], one_o=o[1], two_o=o[2], three_o=o[3], four_o=o[4], total_o=o[5], done_o=o[6])
    results = pl.pallas_call(
        functools.partial(backward_kernel, geo, [*far_away, *close, *grads, *scratch]),
        out_shape=[jax.ShapeDtypeStruct(shape, dtype) for shape, dtype, _ in grads.values()],
        in_specs=[anywhere] * len(far_away) + [vmem] * len(close),
        out_specs=[spec for _, _, spec in grads.values()],
        scratch_shapes=list(scratch.values()),
        compiler_params=pltpu.CompilerParams(
            collective_id=1, has_side_effects=True, vmem_limit_bytes=63 * MIB
        ),
    )(*far_away.values(), *close.values())
    return types.SimpleNamespace(**dict(zip(grads, results, strict=True)))


def finish_kernel(geo, names, *refs):
    k = types.SimpleNamespace(**dict(zip(names, refs, strict=True)))
    f32 = jnp.float32
    wr = geo.wr
    for source, out in ((k.e2, k.e2_out), (k.e1, k.e1_out), (k.d_features, k.d_features_out), (k.last, k.last_out)):
        out[...] = source[...].astype(out.dtype)
    for source, out in ((k.r2, k.r2_out), (k.r1, k.r1_out)):
        out[...] = source[0].astype(f32)
    for source, out in ((k.d2, k.d2_out), (k.d1, k.d1_out)):
        rows = source.shape[2]
        for part in range(source.shape[0]):
            out[part * rows : (part + 1) * rows, :] = source[part, 0].astype(f32)

    @pl.when(pl.program_id(0) == 0)
    def _():
        row, offset = iota((18, 32), 1), iota((18, 32), 0)
        chosen = (lax.rem(row, 16) == lax.div(offset, 2)) & (lax.div(row, 16) == lax.rem(offset, 2))
        chosen = jnp.where(chosen, 1.0, 0.0).astype(jnp.bfloat16)
        for tap in range(9):
            part = k.o1[32 * tap : 32 * tap + 32, :]
            k.o1_out[tap] = mm(chosen, part)
        vectors = (
            (k.sums1a, k.gain1a, k.bias1a),
            (k.sums1b, k.gain1b, k.bias1b),
            (k.sums1c, k.gain1c, k.bias1c),
            (k.sums2a, k.gain2a, k.bias2a),
            (k.sums2b, k.gain2b, k.bias2b),
            (k.sums2c, k.gain2c, k.bias2c),
        )
        for sums, gain, bias in vectors:
            gain[...] = sums[1:2, :]
            bias[...] = sums[0:1, :]


def run_finish(geo, g, last):
    f32 = jnp.float32
    steps, wr, we, mid, c_in, pixels = 4, geo.wr, geo.we, geo.mid, geo.c_in, geo.pixels
    d_rows = 9 // geo.d_parts * wr

    def rows(height, width):
        return pl.BlockSpec((height // steps, width), lambda i: (i, 0))

    def whole(*shape):
        return pl.BlockSpec(shape, lambda i: (0,) * len(shape))

    d_in = pl.BlockSpec((geo.d_parts, 1, d_rows, 128), lambda i: (0, i, 0, 0))
    r_in = pl.BlockSpec((1, 512, wr), lambda i: (i, 0, 0))
    d_shape = (geo.d_parts, 4, d_rows, 128)
    ins = dict(
        e2=(g.grad_e2, rows(mid, we)),
        d2=(g.grad_d2.reshape(d_shape), d_in),
        r2=(g.grad_r2, r_in),
        e1=(g.grad_e1, rows(mid, we)),
        d1=(g.grad_d1.reshape(d_shape), d_in),
        r1=(g.grad_r1, r_in),
        o1=(g.grad_o1, whole(9 * 32, wr)),
        d_features=(g.d_features, rows(pixels, c_in)),
        last=(last, rows(pixels, c_in)),
        sums1a=(g.grads1a, whole(2, mid)),
        sums1b=(g.grads1b, whole(2, mid)),
        sums1c=(g.grads1c, whole(2, c_in)),
        sums2a=(g.grads2a, whole(2, mid)),
        sums2b=(g.grads2b, whole(2, mid)),
        sums2c=(g.grads2c, whole(2, c_in)),
    )
    slim, wide = ((1, mid), whole(1, mid)), ((1, c_in), whole(1, c_in))
    d_out = ((9 * wr, mid), pl.BlockSpec((9 * wr, 128), lambda i: (0, i)))
    outs = dict(
        e2_out=((mid, we), rows(mid, we)),
        d2_out=d_out,
        r2_out=((c_in, wr), rows(c_in, wr)),
        e1_out=((mid, we), rows(mid, we)),
        d1_out=d_out,
        r1_out=((c_in, wr), rows(c_in, wr)),
        o1_out=((9, 18, wr), whole(9, 18, wr)),
        d_features_out=((pixels, c_in), rows(pixels, c_in)),
        last_out=((pixels, c_in), rows(pixels, c_in)),
        gain1a=slim,
        bias1a=slim,
        gain1b=slim,
        bias1b=slim,
        gain1c=wide,
        bias1c=wide,
        gain2a=slim,
        bias2a=slim,
        gain2b=slim,
        bias2b=slim,
        gain2c=wide,
        bias2c=wide,
    )
    results = pl.pallas_call(
        functools.partial(finish_kernel, geo, [*ins, *outs]),
        grid=(steps,),
        out_shape=[
            jax.ShapeDtypeStruct(shape, last.dtype if name == "last_out" else f32) for name, (shape, _) in outs.items()
        ],
        in_specs=[spec for _, spec in ins.values()],
        out_specs=[spec for _, spec in outs.values()],
        compiler_params=pltpu.CompilerParams(vmem_limit_bytes=60 * MIB),
    )(*[array for array, _ in ins.values()])
    return types.SimpleNamespace(**dict(zip(outs, results, strict=True)))


def per_device(
    features,
    box_counts,
    b1_w_reduce,
    b1_gain1,
    b1_bias1,
    b1_w_offset,
    b1_w_deform,
    b1_gain2,
    b1_bias2,
    b1_w_expand,
    b1_gain3,
    b1_bias3,
    b2_w_reduce,
    b2_gain1,
    b2_bias1,
    b2_w_spatial,
    b2_gain2,
    b2_bias2,
    b2_w_expand,
    b2_gain3,
    b2_bias3,
    cotangent,
):
    images, height, columns, channels = features.shape
    n_sp, n_ch = lax.axis_size("sp"), lax.axis_size("ch")
    pixels = images * height * columns
    mid, wr = b1_w_deform.shape[2], b1_w_reduce.shape[1]
    geo = types.SimpleNamespace(
        n_sp=n_sp,
        n_ch=n_ch,
        pixels=pixels,
        height=height,
        columns=columns,
        mid=mid,
        c_in=channels,
        wr=wr,
        we=b1_w_expand.shape[1],
        pixel_total=pixels * n_sp * n_ch,
        d_parts=3 if 3 * wr * mid // 128 % (16 * n_sp) == 0 else 1,
    )
    shards = dict(
        r1=b1_w_reduce,
        d1=b1_w_deform,
        e1=b1_w_expand,
        r2=b2_w_reduce,
        d2=b2_w_spatial,
        e2=b2_w_expand,
    )
    norms = dict(
        gain1a=b1_gain1,
        bias1a=b1_bias1,
        gain1b=b1_gain2,
        bias1b=b1_bias2,
        gain1c=b1_gain3,
        bias1c=b1_bias3,
        gain2a=b2_gain1,
        bias2a=b2_bias1,
        gain2b=b2_gain2,
        bias2b=b2_bias2,
        gain2c=b2_gain3,
        bias2c=b2_bias3,
    )
    norms = {name: vector.reshape(1, -1) for name, vector in norms.items()}
    entry = features.reshape(pixels, channels)
    kept = run_forward(geo, entry, jnp.swapaxes(b1_w_offset, 1, 2), shards, norms)
    g = run_backward(geo, kept, entry, cotangent.reshape(pixels, channels), box_counts.reshape(1, -1), norms)
    done = run_finish(geo, g, kept.last)
    return (
        done.last_out.reshape(features.shape),
        done.d_features_out.reshape(features.shape),
        done.r1_out,
        done.gain1a.reshape(mid),
        done.bias1a.reshape(mid),
        jnp.swapaxes(done.o1_out, 1, 2),
        done.d1_out.reshape(9, wr, mid),
        done.gain1b.reshape(mid),
        done.bias1b.reshape(mid),
        done.e1_out,
        done.gain1c.reshape(channels),
        done.bias1c.reshape(channels),
        done.r2_out,
        done.gain2a.reshape(mid),
        done.bias2a.reshape(mid),
        done.d2_out.reshape(9, wr, mid),
        done.gain2b.reshape(mid),
        done.bias2b.reshape(mid),
        done.e2_out,
        done.gain2c.reshape(channels),
        done.bias2c.reshape(channels),
    )


def solution(mesh):
    return jax.shard_map(
        per_device,
        mesh=mesh,
        in_specs=(
            P("ch", "sp", None, None),
            P(),
            P(None, "ch"),
            P(),
            P(),
            P(None, "ch", None),
            P(None, "ch", None),
            P(),
            P(),
            P(None, "ch"),
            P(),
            P(),
            P(None, "ch"),
            P(),
            P(),
            P(None, "ch", None),
            P(),
            P(),
            P(None, "ch"),
            P(),
            P(),
            P("ch", "sp", None, None),
        ),
        out_specs=(
            P("ch", "sp", None, None),
            P("ch", "sp", None, None),
            P(None, "ch"),
            P(),
            P(),
            P(None, "ch", None),
            P(None, "ch", None),
            P(),
            P(),
            P(None, "ch"),
            P(),
            P(),
            P(None, "ch"),
            P(),
            P(),
            P(None, "ch", None),
            P(),
            P(),
            P(None, "ch"),
            P(),
            P(),
        ),
        check_vma=False,
    )
```

```python
import functools
import types

import jax
import jax.numpy as jnp
from jax import lax
from jax.experimental import pallas as pl
from jax.experimental.pallas import tpu as pltpu
from jax.sharding import PartitionSpec as P

EPS = 1e-05
REACH = 5.5
MESH = pl.DeviceIdType.MESH
MIB = 2**20


def mm(left, right):
    return jnp.dot(left, right, preferred_element_type=jnp.float32)


def mm_nt(left, right):
    return lax.dot_general(
        left, right, (((1,), (1,)), ((), ())), preferred_element_type=jnp.float32
    )


def smooth_rise(fraction):
    return fraction * fraction * (3.0 - 2.0 * fraction)


def sigmoid(v):
    return 1.0 / (1.0 + jnp.exp(-v))


class Place:
    def __init__(self, n_sp, n_ch):
        self.n_sp, self.n_ch, self.n_x = n_sp, n_ch, n_ch // 2
        self.s, self.c = lax.axis_index("sp"), lax.axis_index("ch")
        self.x, self.k = lax.div(self.c, 2), lax.rem(self.c, 2)
        self.y = lax.rem(self.s, 2)
        self.sib = self.c + 1 - 2 * self.k
        self.sibling = (self.s, self.sib)

    def other_x(self, d):
        return 2 * lax.rem(self.x + d, self.n_x) + self.k

    def near(self, d):
        q = lax.rem(self.y * self.n_ch + self.c + d, 2 * self.n_ch)
        return self.s - self.y + lax.div(q, self.n_ch), lax.rem(q, self.n_ch)

    def far(self, d):
        return lax.rem(self.s + 2 * d, self.n_sp), self.c

    def barrier(self):
        sem = pltpu.get_barrier_semaphore()

        def tell(device):
            pl.semaphore_signal(sem, inc=1, device_id=device, device_id_type=MESH)

        for d in range(1, 2 * self.n_ch):
            tell(self.near(d))
        for d in range(1, self.n_sp // 2):
            tell(self.far(d))
        diagonal = lax.rem(self.s + self.n_sp - 1 + 2 * self.y, self.n_sp)
        tell((diagonal, self.c))
        pl.semaphore_wait(sem, 2 * self.n_ch + self.n_sp // 2 - 1)


def remote(src, dst, send, recv, device):
    return pltpu.make_async_remote_copy(
        src_ref=src,
        dst_ref=dst,
        send_sem=send,
        recv_sem=recv,
        device_id=device,
        device_id_type=MESH,
    )


class AllSum:
    def __init__(self, place, first, second, send, recv_one, recv_two):
        self.p, self.first, self.second = place, first, second
        self.send, self.one, self.two = send, recv_one, recv_two
        self.me = place.y * place.n_ch + place.c
        self.row = lax.div(place.s, 2)

    def put(self, lanes, sums, squares):
        self.first[self.me, 0:1, lanes] = sums
        self.first[self.me, 1:2, lanes] = squares

    def _near(self, d):
        return remote(self.first.at[self.me], self.first.at[self.me], self.send.at[d], self.one.at[self.me], self.p.near(d))

    def _far(self, d):
        n = 2 * self.p.n_ch
        return remote(self.second.at[self.row], self.second.at[self.row], self.send.at[n + d], self.two.at[self.row], self.p.far(d))

    def start(self):
        for d in range(1, 2 * self.p.n_ch):
            self._near(d).start()

    def relay(self):
        n = 2 * self.p.n_ch
        for d in range(1, n):
            other = lax.rem(self.me + d, n)
            slot = self.first.at[other]
            remote(slot, slot, self.send.at[d], self.one.at[other], self.p.near(d)).wait_recv()
        total = self.first[0]
        for q in range(1, n):
            total = total + self.first[q]
        self.second[self.row] = total
        for d in range(1, self.p.n_sp // 2):
            self._far(d).start()

    def finish(self):
        n = self.p.n_sp // 2
        for d in range(1, n):
            other = lax.rem(self.row + d, n)
            slot = self.second.at[other]
            remote(slot, slot, self.send.at[d], self.two.at[other], self.p.far(d)).wait_recv()
        total = self.second[0]
        for q in range(1, n):
            total = total + self.second[q]
        return total

    def drain(self):
        for d in range(1, 2 * self.p.n_ch):
            self._near(d).wait_send()
        for d in range(1, self.p.n_sp // 2):
            self._far(d).wait_send()


class Gather:
    def __init__(self, place, src, slot, send, recv):
        self.p, self.src, self.slot, self.send, self.recv = place, src, slot, send, recv

    def _own(self):
        return pltpu.make_async_copy(self.src, self.slot(self.p.c), self.recv.at[self.p.c])

    def _sibling(self):
        c = self.p.c
        return remote(self.src, self.slot(c), self.send.at[0], self.recv.at[c], self.p.sibling)

    def _direct(self, d):
        c = self.p.c
        return remote(self.src, self.slot(c), self.send.at[d], self.recv.at[c], (self.p.s, self.p.other_x(d)))

    def _forward(self, d):
        o = self.p.other_x(d)
        return remote(self.slot(o), self.slot(o), self.send.at[self.p.n_x + d - 1], self.recv.at[o], self.p.sibling)

    def _arrived(self, o):
        remote(self.slot(o), self.slot(o), self.send.at[0], self.recv.at[o], self.p.sibling).wait_recv()

    def start(self):
        for d in range(1, self.p.n_x):
            self._direct(d).start()
        self._sibling().start()
        self._own().start()

    def pump(self):
        for d in range(1, self.p.n_x):
            self._arrived(self.p.other_x(d))
            self._forward(d).start()

    def finish(self):
        self._own().wait()
        self._arrived(self.p.sib)
        for d in range(1, self.p.n_x):
            self._arrived(self.p.other_x(d) + 1 - 2 * self.p.k)

    def drain(self):
        self._sibling().wait_send()
        for d in range(1, self.p.n_x):
            self._direct(d).wait_send()
            self._forward(d).wait_send()


class HalfGather:
    def __init__(self, place, src, slot, send, recv):
        self.p, self.src, self.slot, self.send, self.recv = place, src, slot, send, recv
        z = lax.div(place.s, 2)
        self.h = lax.rem(z, 2)
        self.beside = (place.s + 2 - 4 * self.h, place.c)

    def _own(self, h):
        c = self.p.c
        return pltpu.make_async_copy(self.src(h), self.slot(c, h), self.recv.at[2 * c + h])

    def _sibling(self, h):
        c = self.p.c
        return remote(self.src(h), self.slot(c, h), self.send.at[h], self.recv.at[2 * c + h], self.p.sibling)

    def _direct(self, d):
        c, h = self.p.c, self.h
        there = (self.p.s, self.p.other_x(d))
        return remote(self.src(h), self.slot(c, h), self.send.at[1 + d], self.recv.at[2 * c + h], there)

    def _pass(self, d, kind, h, device):
        o = self.p.other_x(d)
        sem = self.send.at[2 + (kind + 1) * (self.p.n_x - 1) + d - 1]
        return remote(self.slot(o, h), self.slot(o, h), sem, self.recv.at[2 * o + h], device)

    def _beside(self, d):
        return self._pass(d, 0, self.h, self.beside)

    def _forward(self, d):
        return self._pass(d, 1, self.h, self.p.sibling)

    def _second(self, d):
        return self._pass(d, 2, 1 - self.h, self.p.sibling)

    def _arrived(self, o, h):
        remote(self.slot(o, h), self.slot(o, h), self.send.at[0], self.recv.at[2 * o + h], self.p.sibling).wait_recv()

    def start(self):
        for d in range(1, self.p.n_x):
            self._direct(d).start()
        for h in range(2):
            self._sibling(h).start()
            self._own(h).start()

    def pump(self):
        for d in range(1, self.p.n_x):
            self._arrived(self.p.other_x(d), self.h)
            self._beside(d).start()
            self._forward(d).start()

    def pump_again(self):
        for d in range(1, self.p.n_x):
            self._arrived(self.p.other_x(d), 1 - self.h)
            self._second(d).start()

    def finish(self):
        for h in range(2):
            self._own(h).wait()
            self._arrived(self.p.sib, h)
            for d in range(1, self.p.n_x):
                self._arrived(self.p.other_x(d) + 1 - 2 * self.p.k, h)

    def drain(self):
        for h in range(2):
            self._sibling(h).wait_send()
        for d in range(1, self.p.n_x):
            for copy in (self._direct(d), self._beside(d), self._forward(d), self._second(d)):
                copy.wait_send()


class Halo:
    def __init__(self, place, up, down, sems):
        self.p, self.up, self.down, self.sems = place, up, down, sems

    def _up(self):
        return remote(*self.up, self.sems.at[0], self.sems.at[1], (self.p.s - 1, self.p.c))

    def _down(self):
        return remote(*self.down, self.sems.at[2], self.sems.at[3], (self.p.s + 1, self.p.c))

    def _each(self, act_up, act_down):
        pl.when(self.p.s > 0)(act_up)
        pl.when(self.p.s < self.p.n_sp - 1)(act_down)

    def start(self):
        self._each(lambda: self._up().start(), lambda: self._down().start())

    def finish(self):
        self._each(lambda: self._down().wait_recv(), lambda: self._up().wait_recv())

    def drain(self):
        self._each(lambda: self._up().wait_send(), lambda: self._down().wait_send())


def over_rows(rows, step, body, init):
    def one(i, carry):
        return body(pl.ds(pl.multiple_of(i * step, step), step), carry)

    return lax.fori_loop(0, rows // step, one, init, unroll=2)


def fold(v):
    return jnp.sum(v.reshape(-1, 8, v.shape[1]), axis=0)


def moments(ref, lanes, rows):
    width = lanes.size

    def body(at, carry):
        v = ref[at, lanes]
        return carry[0] + fold(v), carry[1] + fold(v * v)

    zero = jnp.zeros((8, width), jnp.float32)
    a, b = over_rows(rows, 16, body, (zero, zero))
    return jnp.sum(a, axis=0, keepdims=True), jnp.sum(b, axis=0, keepdims=True)


def center_inverse(sums, squares, pixel_total):
    center = sums / pixel_total
    return center, lax.rsqrt(squares / pixel_total - center * center + EPS)


def cell_weights(position, cells):
    base = jnp.floor(position)
    upper = smooth_rise(position - base)
    return jnp.where(cells == base, 1.0 - upper, jnp.where(cells == base + 1.0, upper, 0.0))


def iota(shape, axis):
    return lax.broadcasted_iota(jnp.int32, shape, axis)


def set_identity(ref):
    n = ref.shape[0]
    for r in range(0, n, 128):
        same = iota((128, n), 0) + r == iota((128, n), 1)
        ref[r : r + 128, :] = jnp.where(same, 1.0, 0.0).astype(jnp.bfloat16)


def column_shift(v, j, columns):
    if j == 1:
        return v
    col = lax.rem(iota(v.shape, 0), columns)
    if j == 0:
        return jnp.where(col < 2, 0.0, pltpu.roll(v, 2, 0))
    return jnp.where(col >= columns - 2, 0.0, pltpu.roll(v, v.shape[0] - 2, 0))


def forward_kernel(geo, names, *refs):
    k = types.SimpleNamespace(**dict(zip(names, refs, strict=True)))
    p = Place(geo.n_sp, geo.n_ch)
    s, pixels, columns, mid = p.s, geo.pixels, geo.columns, geo.mid
    n_ch, wr, we, total = p.n_ch, geo.wr, geo.we, geo.pixel_total
    bf, f32 = jnp.bfloat16, jnp.float32

    def rows_of(ref, width, first, taps):
        at = pl.ds(first, taps)
        return lambda c: ref.at[at, pl.ds(pl.multiple_of(c * width, width), width), :]

    def slots_of(ref):
        return lambda c: ref.at[c]

    def gather(i, src, slot):
        return Gather(p, src, slot, k.gather_send.at[i], k.gather_recv.at[i])

    o1 = gather(1, k.o1_own, slots_of(k.o1_all))
    d1a = gather(2, k.d1.at[pl.ds(0, 2)], rows_of(k.d1_all, wr, 0, 2))
    d1b = gather(3, k.d1.at[pl.ds(2, 7)], rows_of(k.d1_all, wr, 2, 7))
    e1 = gather(4, k.e1, slots_of(k.e1_all))

    def half_gather(i, src, slot):
        return HalfGather(p, src, slot, k.half_send.at[i], k.half_recv.at[i])

    def half_rows(ref, rows):
        return lambda h: ref.at[pl.ds(pl.multiple_of(h * rows, 16), rows)]

    def half_slots(ref, rows):
        return lambda c, h: ref.at[c, pl.ds(pl.multiple_of(h * rows, 16), rows)]

    def quarter(i):
        rows = geo.c_in // 8

        def at(h):
            return pl.ds(pl.multiple_of(2 * i * rows + h * rows, 16), rows)

        return half_gather(3 + i, lambda h: k.r1.at[at(h)], lambda c, h: k.r1_all.at[c, at(h)])

    r1 = [quarter(i) for i in range(4)]
    r2 = half_gather(0, half_rows(k.r2, geo.c_in // 2), half_slots(k.r2_all, geo.c_in // 2))
    d2 = half_gather(
        1,
        lambda h: k.d2.at[:, pl.ds(pl.multiple_of(h * (wr // 2), 16), wr // 2), :],
        lambda c, h: k.d2_all.at[:, pl.ds(pl.multiple_of(c * wr + h * (wr // 2), 16), wr // 2), :],
    )
    e2 = half_gather(2, half_rows(k.e2, mid // 2), half_slots(k.e2_all, mid // 2))

    def all_sum(wide, i):
        if wide:
            parts = (k.wide_one, k.wide_two, k.wide_send, k.wide_recv_one, k.wide_recv_two)
        else:
            parts = (k.slim_one, k.slim_two, k.slim_send, k.slim_recv_one, k.slim_recv_two)
        return AllSum(p, *[part.at[i] for part in parts])

    saves = []

    def save(src, dst):
        copy = pltpu.make_async_copy(src, dst, k.save_sem.at[len(saves)])
        copy.start()
        saves.append(copy)

    def run_sum(task, totals, *between):
        task.start()
        for one in between:
            one()
        task.relay()
        totals[...] = task.finish()

    def reduce_matmul(x, weights, out):
        for c in range(n_ch):
            out[:, c * wr : (c + 1) * wr] = mm(x[...], weights[c])

    def activate(values, totals, gain, bias, out, first_row):
        center, inverse = center_inverse(totals[0:1, :], totals[1:2, :], total)
        scale = gain[...] * inverse
        shift = bias[...]

        def body(at, carry):
            v = (values[at, :] - center) * scale + shift
            row = pl.ds(pl.multiple_of(at.start + first_row, 16), at.size)
            out[row, :] = (v * sigmoid(v)).astype(bf)
            return carry

        over_rows(pixels, 16, body, 0)

    def expand(x, weights, out, task):
        for c in range(n_ch):
            lanes = pl.ds(c * we, we)
            out[:, lanes] = mm(x[...], weights[c])
            task.put(lanes, *moments(out, lanes, pixels))

    def leave(values, totals, gain, bias, residual, out):
        for start in range(0, geo.c_in, 512):
            lanes = pl.ds(start, 512)
            center, inverse = center_inverse(totals[0:1, lanes], totals[1:2, lanes], total)
            scale = gain[:, lanes] * inverse
            shift = bias[:, lanes]

            def body(at, carry):
                v = (values[at, lanes] - center) * scale + shift + residual[at, lanes].astype(f32)
                out[at, lanes] = (v * sigmoid(v)).astype(bf)
                return carry

            over_rows(pixels, 16, body, 0)

    slim = pl.ds(0, mid)

    p.barrier()
    for part in r1:
        part.start()
    row, offset = iota((32, 18), 0), iota((32, 18), 1)
    chosen = (lax.rem(row, 16) == lax.div(offset, 2)) & (lax.div(row, 16) == lax.rem(offset, 2))
    chosen = jnp.where(chosen, 1.0, 0.0).astype(bf)
    for tap in range(9):
        k.o1_own[32 * tap : 32 * tap + 32, :] = mm(chosen, k.o1[tap]).astype(bf)
    o1.start()
    d1a.start()
    set_identity(k.ident)

    def reduce_quarter(i):
        r1[i].finish()
        at = slice(i * (geo.c_in // 4), (i + 1) * (geo.c_in // 4))
        for c in range(n_ch):
            part = mm(k.x[:, at], k.r1_all[c, at, :])
            if i == 0:
                k.reduced1[:, c * wr : (c + 1) * wr] = part
            else:
                k.reduced1[:, c * wr : (c + 1) * wr] += part

    r1[0].pump()
    r1[1].pump()
    r1[0].pump_again()
    r1[2].pump()
    r1[1].pump_again()
    r1[3].pump()
    reduce_quarter(0)
    r1[2].pump_again()
    reduce_quarter(1)
    r1[3].pump_again()
    reduce_quarter(2)
    reduce_quarter(3)
    task1 = all_sum(False, 0)
    task1.put(slim, *moments(k.reduced1, slim, pixels))
    run_sum(task1, k.totals1a, d1b.start, e1.start)
    o1.pump()
    activate(k.reduced1, k.totals1a, k.gain1a, k.bias1a, k.ext1, pixels)
    own = k.ext1.at[pixels : 2 * pixels]
    rim, rest = 2 * columns, pixels - 2 * columns

    def strip(start, size):
        return k.ext1.at[pl.ds(start, size)]

    halo1 = Halo(
        p,
        (strip(pixels, rim), strip(2 * pixels, rim)),
        (strip(2 * pixels - rim, rim), strip(rest, rim)),
        k.halo_sem.at[0],
    )
    halo1_far = Halo(
        p,
        (strip(pixels + rim, rest), strip(2 * pixels + rim, rest)),
        (strip(pixels, rest), strip(0, rest)),
        k.halo_sem.at[2],
    )
    halo1.start()
    halo1_far.start()
    save(k.reduced1, k.reduced1_out)

    @pl.when(s == 0)
    def _():
        k.ext1[:pixels, :] = jnp.zeros((pixels, mid), bf)

    @pl.when(s == p.n_sp - 1)
    def _():
        k.ext1[2 * pixels :, :] = jnp.zeros((pixels, mid), bf)

    d1a.pump()
    o1.finish()
    k.ext1_t[:, pixels : 2 * pixels] = mm_nt(k.ident[...], k.ext1[pixels : 2 * pixels, :]).astype(bf)
    edge = jnp.zeros((rim, mid), bf)
    k.window[:rim, :] = edge
    k.window[14 * columns :, :] = edge
    halo1.finish()
    k.window[rim : 14 * columns, :] = k.ext1[6 * columns : 18 * columns, :]
    raw_all = jnp.zeros((9 * 32, 16 * columns), f32)
    for c in range(n_ch):
        raw_all += mm_nt(k.o1_all[c], k.window[:, c * wr : (c + 1) * wr])
    k.raw_all[...] = raw_all
    lane = iota((32, pixels), 1)
    col = lax.rem(lane, columns)
    raw = jnp.zeros((32, pixels), f32)
    for tap in range(9):
        i, j = tap // 3, tap % 3
        offset = (2 + 2 * i) * columns + 2 * (j - 1)
        part = k.raw_all[32 * tap : 32 * tap + 32, :]
        part = pltpu.roll(part, 16 * columns - offset, 1)[:, :pixels]
        if j == 0:
            part = jnp.where(col < 2, 0.0, part)
        if j == 2:
            part = jnp.where(col >= columns - 2, 0.0, part)
        raw += part
    k.bend[...] = jnp.tanh(raw)
    save(k.bend, k.bend_out)

    halo1_far.finish()
    r2.start()
    d1b.pump()
    for part in (0, 2):
        at = slice(part * pixels, (part + 1) * pixels)
        k.ext1_t[:, at] = mm_nt(k.ident[...], k.ext1[at, :]).astype(bf)
    save(k.ext1, k.ext1_out)
    d1a.finish()
    d1b.finish()
    save(k.d1_all, k.d1_all_out)
    k.spread1[...] = jnp.zeros((pixels, mid), f32)

    def tap_step(tap, carry):
        i, j = lax.div(tap, 3), lax.rem(tap, 3)
        lane = iota((1, pixels), 1)
        row = (lax.div(lane, columns) + 6 + 2 * i).astype(f32) + REACH * k.bend[pl.ds(tap, 1), :]
        across = (lax.rem(lane, columns) - 2 + 2 * j).astype(f32) + REACH * k.bend[pl.ds(tap + 16, 1), :]
        k.col_weight[...] = cell_weights(across, iota((columns, pixels), 0).astype(f32))
        base = jnp.floor(row)
        upper = smooth_rise(row - base)
        for r in range(3 * geo.height):
            weight = jnp.where(base == r, 1.0 - upper, jnp.where(base == r - 1, upper, 0.0))
            k.cells[r * columns : (r + 1) * columns, :] = (k.col_weight[...] * weight).astype(bf)
        k.cols1_t[tap] = mm(k.ext1_t[...], k.cells[...]).astype(bf)
        cols = mm_nt(k.ident[:pixels, :pixels], k.cols1_t[tap]).astype(bf)
        k.spread1[...] += mm(cols, k.d1_all[tap])
        return carry

    lax.fori_loop(0, 9, tap_step, 0)
    save(k.cols1_t, k.cols1_t_out)
    task2 = all_sum(False, 1)
    task2.put(slim, *moments(k.spread1, slim, pixels))
    task2.start()
    d2.start()
    e1.pump()
    task2.relay()
    r2.pump()
    k.totals1b[...] = task2.finish()
    save(k.spread1, k.spread1_out)
    activate(k.spread1, k.totals1b, k.gain1b, k.bias1b, k.act, 0)
    e1.finish()
    save(k.e1_all, k.e1_all_out)
    task3 = all_sum(True, 0)
    expand(k.act, k.e1_all, k.expanded1, task3)
    task3.start()
    r2.pump_again()
    task3.relay()
    d2.pump()
    k.totals1c[...] = task3.finish()
    save(k.expanded1, k.expanded1_out)
    leave(k.expanded1, k.totals1c, k.gain1c, k.bias1c, k.x, k.middle)
    save(k.middle, k.middle_out)

    r2.finish()
    save(k.r1_all, k.r1_all_out)
    save(k.r2_all, k.r2_all_out)
    save(k.o1_all, k.o1_all_out)
    reduce_matmul(k.middle, k.r2_all, k.reduced2)
    task4 = all_sum(False, 2)
    task4.put(slim, *moments(k.reduced2, slim, pixels))
    task4.start()
    e2.start()
    task4.relay()
    k.totals2a[...] = task4.finish()
    d2.pump_again()
    save(k.reduced2, k.reduced2_out)
    activate(k.reduced2, k.totals2a, k.gain2a, k.bias2a, k.ext2, rim)
    halo2 = Halo(
        p,
        (k.ext2.at[rim : 2 * rim], k.ext2.at[pixels + rim :]),
        (k.ext2.at[pixels : pixels + rim], k.ext2.at[:rim]),
        k.halo_sem.at[1],
    )
    halo2.start()

    @pl.when(s == 0)
    def _():
        k.ext2[:rim, :] = jnp.zeros((rim, mid), bf)

    @pl.when(s == p.n_sp - 1)
    def _():
        k.ext2[pixels + rim :, :] = jnp.zeros((rim, mid), bf)

    e2.pump()
    d2.finish()
    save(k.d2_all, k.d2_all_out)
    halo2.finish()

    def shift_row(r, carry):
        at = pl.ds(pl.multiple_of(r * columns, columns), columns)
        v = k.ext2[at, :].astype(f32)
        k.moved[0, at, :] = column_shift(v, 0, columns).astype(bf)
        k.moved[1, at, :] = v.astype(bf)
        k.moved[2, at, :] = column_shift(v, 2, columns).astype(bf)
        return carry

    lax.fori_loop(0, geo.height + 4, shift_row, 0)
    save(k.moved, k.moved_out)
    k.spread2[...] = jnp.zeros((pixels, mid), f32)

    def plain_step(tap, carry):
        i, j = lax.div(tap, 3), lax.rem(tap, 3)
        cols = k.moved[j, pl.ds(pl.multiple_of(i * rim, rim), pixels), :]
        k.spread2[...] += mm(cols, k.d2_all[tap])
        return carry

    lax.fori_loop(0, 9, plain_step, 0)
    task5 = all_sum(False, 3)
    task5.put(slim, *moments(k.spread2, slim, pixels))
    run_sum(task5, k.totals2b, e2.pump_again)
    save(k.spread2, k.spread2_out)
    activate(k.spread2, k.totals2b, k.gain2b, k.bias2b, k.act, 0)
    e2.finish()
    save(k.e2_all, k.e2_all_out)
    task6 = all_sum(True, 1)
    expand(k.act, k.e2_all, k.expanded2, task6)
    run_sum(task6, k.totals2c)
    save(k.expanded2, k.expanded2_out)
    leave(k.expanded2, k.totals2c, k.gain2c, k.bias2c, k.middle, k.last)
    save(k.last, k.last_out)

    for task in (*r1, o1, d1a, d1b, e1, r2, d2, e2, task1, task2, task3, task4, task5, task6, halo1, halo1_far, halo2):
        task.drain()
    for copy in saves:
        copy.wait()


def run_forward(geo, features, offset_w, shards, norms):
    bf, f32 = jnp.bfloat16, jnp.float32
    n_ch, n_sp, mid, pixels, wr, we = geo.n_ch, geo.n_sp, geo.mid, geo.pixels, geo.wr, geo.we
    ext_rows = 3 * pixels
    rim_rows = pixels + 4 * geo.columns
    near, far = 2 * n_ch, n_sp // 2
    vmem = pl.BlockSpec(memory_space=pltpu.VMEM)
    anywhere = pl.BlockSpec(memory_space=pl.ANY)
    dma = pltpu.SemaphoreType.DMA
    v = pltpu.VMEM
    close = dict(x=features, o1=offset_w, **norms)
    kept = dict(
        r1_all=((n_ch, geo.c_in, wr), bf),
        o1_all=((n_ch, 9 * 32, wr), bf),
        d1_all=((9, mid, mid), bf),
        e1_all=((n_ch, mid, we), bf),
        r2_all=((n_ch, geo.c_in, wr), bf),
        d2_all=((9, mid, mid), bf),
        e2_all=((n_ch, mid, we), bf),
        reduced1=((pixels, mid), f32),
        ext1=((ext_rows, mid), bf),
        bend=((32, pixels), f32),
        cols1_t=((9, mid, pixels), bf),
        spread1=((pixels, mid), f32),
        expanded1=((pixels, geo.c_in), f32),
        middle=((pixels, geo.c_in), bf),
        reduced2=((pixels, mid), f32),
        moved=((3, rim_rows, mid), bf),
        spread2=((pixels, mid), f32),
        expanded2=((pixels, geo.c_in), f32),
        last=((pixels, geo.c_in), bf),
    )
    totals = dict(
        totals1a=(2, mid),
        totals1b=(2, mid),
        totals1c=(2, geo.c_in),
        totals2a=(2, mid),
        totals2b=(2, mid),
        totals2c=(2, geo.c_in),
    )
    scratch = dict(
        ident=v((mid, mid), bf),
        ext1_t=v((mid, ext_rows), bf),
        raw_all=v((9 * 32, 16 * geo.columns), f32),
        col_weight=v((geo.columns, pixels), f32),
        cells=v((ext_rows, pixels), bf),
        act=v((pixels, mid), bf),
        ext2=v((rim_rows, mid), bf),
        slim_one=v((4, near, 2, mid), f32),
        slim_two=v((4, far, 2, mid), f32),
        slim_send=dma((4, near + far)),
        slim_recv_one=dma((4, near)),
        slim_recv_two=dma((4, far)),
        wide_one=v((2, near, 2, geo.c_in), f32),
        wide_two=v((2, far, 2, geo.c_in), f32),
        wide_send=dma((2, near + far)),
        wide_recv_one=dma((2, near)),
        wide_recv_two=dma((2, far)),
        gather_send=dma((5, n_ch)),
        gather_recv=dma((5, n_ch)),
        half_send=dma((7, 2 + 4 * (n_ch // 2 - 1))),
        half_recv=dma((7, 2 * n_ch)),
        o1_own=v((9 * 32, wr), bf),
        window=v((16 * geo.columns, mid), bf),
        halo_sem=dma((3, 4)),
        save_sem=dma((len(kept),)),
    )
    scratch |= {name: v(*what) for name, what in kept.items()}
    out_names = [f"{name}_out" for name in kept]
    results = pl.pallas_call(
        functools.partial(forward_kernel, geo, [*close, *shards, *out_names, *totals, *scratch]),
        out_shape=[jax.ShapeDtypeStruct(*what) for what in kept.values()]
        + [jax.ShapeDtypeStruct(shape, f32) for shape in totals.values()],
        in_specs=[vmem] * len(close) + [anywhere] * len(shards),
        out_specs=[anywhere] * len(kept) + [vmem] * len(totals),
        scratch_shapes=list(scratch.values()),
        compiler_params=pltpu.CompilerParams(
            collective_id=0, has_side_effects=True, vmem_limit_bytes=60 * MIB
        ),
    )(*close.values(), *shards.values())
    return types.SimpleNamespace(**dict(zip([*kept, *totals], results, strict=True)))


class Reduce:
    def __init__(self, place, stage, one, two, three, four, total, done, send, recv, z_first=False):
        self.z_first = z_first
        self.p, self.stage, self.one, self.two, self.three, self.four = place, stage, one, two, three, four
        self.total, self.done = total, done
        self.send, self.recv = send, recv
        self.n_far = place.n_sp // 2
        self.half = stage.shape[2] // 2
        self.chunk = self.half // self.n_far
        self.row = lax.div(place.s, 2)
        self.pair = (place.s + 1 - 2 * place.y, place.c)
        self.mine = stage.at[place.k, place.x]
        self.at_x, self.at_out = 3, 3 + place.n_x
        self.at_back = self.at_out + 2 * self.n_far

    nothing = types.SimpleNamespace(**dict.fromkeys(["s1", "s2", "s3", "s3_add", "s3_send", "s4", "s5", "s6", "freed", "s7_end", "s7"], lambda: None))

    @staticmethod
    def sems(n_sp, n_ch):
        return 3 + n_ch // 2 + 3 * (n_sp // 2)

    def _half(self, ref, y):
        return ref.at[pl.ds(pl.multiple_of(y * self.half, 16), self.half)]

    def _chunk(self, ref, z, y=None):
        y = self.p.y if y is None else y
        return ref.at[pl.ds(pl.multiple_of(y * self.half + z * self.chunk, 16), self.chunk)]

    def _to_sibling(self):
        return remote(self.stage.at[1 - self.p.k], self.one, self.send.at[0], self.recv.at[0], self.p.sibling)

    def _to_x(self, d):
        other = lax.rem(self.p.x + d, self.p.n_x)
        return remote(
            self.stage.at[self.p.k, other],
            self.two.at[self.p.n_x - d - 1],
            self.send.at[self.at_x + d],
            self.recv.at[self.at_x + self.p.n_x - d],
            (self.p.s, 2 * other + self.p.k),
        )

    def _to_pair(self):
        if self.z_first:
            source, there = self._chunk(self.total, self.row, 1 - self.p.y), self.three.at[pl.ds(0, self.chunk)]
        else:
            source, there = self._half(self.total, 1 - self.p.y), self.three
        return remote(source, there, self.send.at[1], self.recv.at[1], self.pair)

    def _from(self, z, h):
        return self.four.at[z, pl.ds(h * self.chunk, self.chunk)]

    def _out(self, d, h):
        other = lax.rem(self.row + d, self.n_far)
        source = self._chunk(self.total, other, h if self.z_first else None)
        n = self.at_out + h * self.n_far
        return remote(source, self._from(self.row, h), self.send.at[n + d], self.recv.at[n + self.row], self.p.far(d))

    def _back(self, d):
        return remote(
            self._chunk(self.done, self.row), self._chunk(self.done, self.row), self.send.at[self.at_back + d], self.recv.at[self.at_back + self.row], self.p.far(d)
        )

    def _pair_back(self, y):
        return remote(self._half(self.done, y), self._half(self.done, y), self.send.at[2], self.recv.at[2], self.pair)

    def _await(self, ref, sem):
        remote(ref, ref, self.send.at[0], sem, self.p.sibling).wait_recv()

    def _add(self, source, start, rows, pieces, out):
        step = max(n for n in (16, 32, 48, 64) if rows % n == 0)

        def one(i, carry):
            at = pl.ds(pl.multiple_of(start + i * step, 16), step)
            there = pl.ds(pl.multiple_of(i * step, 16), step)
            total = source[at, :].astype(jnp.float32)
            for piece in pieces:
                total = total + piece[there, :].astype(jnp.float32)
            out[at, :] = total.astype(jnp.bfloat16)
            return carry

        lax.fori_loop(0, rows // step, one, 0)

    def s1(self):
        self._to_sibling().start()

    def s2(self):
        self._await(self.one, self.recv.at[0])
        rows = self.stage.shape[2]
        step = max(n for n in (16, 32, 48, 64) if rows % n == 0)
        for x in range(self.p.n_x):

            def one(i, carry):
                at = pl.ds(pl.multiple_of(i * step, 16), step)
                total = self.stage[self.p.k, x, at, :].astype(jnp.float32) + self.one[x, at, :].astype(jnp.float32)
                self.stage[self.p.k, x, at, :] = total.astype(jnp.bfloat16)
                return carry

            lax.fori_loop(0, rows // step, one, 0)
        for d in range(1, self.p.n_x):
            self._to_x(d).start()

    def s3_add(self):
        for d in range(1, self.p.n_x):
            self._await(self.two.at[d - 1], self.recv.at[self.at_x + d])
        pieces = [self.two.at[d - 1] for d in range(1, self.p.n_x)]
        self._add(self.mine, 0, self.stage.shape[2], pieces, self.total)
        self._to_sibling().wait_send()
        for d in range(1, self.p.n_x):
            self._to_x(d).wait_send()

    def _start_out(self):
        for d in range(1, self.n_far):
            for h in range(1 + self.z_first):
                self._out(d, h).start()

    def _add_far(self, h, y, out):
        others = [lax.rem(self.row + d, self.n_far) for d in range(1, self.n_far)]
        for other in others:
            self._await(self._from(other, h), self.recv.at[self.at_out + h * self.n_far + other])
        start = y * self.half + self.row * self.chunk
        self._add(self.total, start, self.chunk, [self._from(other, h) for other in others], out)

    def s3_send(self):
        if self.z_first:
            self._start_out()
        else:
            self._to_pair().start()

    def s3(self):
        self.s3_add()
        self.s3_send()

    def s4(self):
        if self.z_first:
            for h in range(2):
                self._add_far(h, h, self.total)
            self._to_pair().start()
        else:
            self._await(self.three, self.recv.at[1])
            self._add(self.total, self.p.y * self.half, self.half, [self.three], self.total)
            self._start_out()

    def s5(self):
        if self.z_first:
            there = self.three.at[pl.ds(0, self.chunk)]
            self._await(there, self.recv.at[1])
            start = self.p.y * self.half + self.row * self.chunk
            self._add(self.total, start, self.chunk, [there], self.done)
        else:
            self._add_far(0, self.p.y, self.done)
        for d in range(1, self.n_far):
            self._back(d).start()

    def s6(self):
        for d in range(1, self.n_far):
            other = lax.rem(self.row + d, self.n_far)
            self._await(self._chunk(self.done, other), self.recv.at[self.at_back + other])
        self._pair_back(self.p.y).start()

    def freed(self):
        self._to_pair().wait_send()
        for d in range(1, self.n_far):
            for h in range(1 + self.z_first):
                self._out(d, h).wait_send()

    def s7_end(self):
        self._await(self._half(self.done, 1 - self.p.y), self.recv.at[2])
        self._pair_back(self.p.y).wait_send()
        for d in range(1, self.n_far):
            self._back(d).wait_send()

    def s7(self):
        self.freed()
        self.s7_end()


def slope_of(v):
    sigma = sigmoid(v)
    return sigma, sigma * (1.0 + v * (1.0 - sigma))


def backward_kernel(geo, names, *refs):
    k = types.SimpleNamespace(**dict(zip(names, refs, strict=True)))
    p = Place(geo.n_sp, geo.n_ch)
    s, pixels, columns, mid = p.s, geo.pixels, geo.columns, geo.mid
    n_ch, wr, we, total = p.n_ch, geo.wr, geo.we, geo.pixel_total
    bf, f32 = jnp.bfloat16, jnp.float32
    rim = 2 * columns
    slim = pl.ds(0, mid)
    count = [0, 0, 0]

    cells = k.moved.at[pl.ds(0, 3 * pixels), pl.ds(0, pixels)]
    placed = k.third.at[pl.ds(0, 9 * 32), pl.ds(2 * mid, 16 * columns)]
    placed_t = k.moved.at[pl.ds(0, 16 * columns)]
    cols_grad_t = k.moved.at[pl.ds(3 * pixels, mid), pl.ds(0, pixels)]

    def load(src, dst):
        copy = pltpu.make_async_copy(src, dst, k.load_sem.at[count[0]])
        count[0] += 1
        copy.start()
        return copy

    def write_out(src, dst):
        copy = pltpu.make_async_copy(src, dst, k.out_sem.at[count[1]])
        count[1] += 1
        copy.start()
        return copy

    def reduction(*buffers, z_first=False):
        i = count[2]
        count[2] += 1
        return Reduce(p, *buffers, k.reduce_send.at[i], k.reduce_recv.at[i], z_first)

    def for_e():
        return reduction(k.stage_e, k.one_e, k.two_e, k.three_e, k.four_e, k.total_e, k.done_e)

    d_parts, tap_count = geo.d_parts, 9 // geo.d_parts

    def for_d(four, done, *z_first):
        buffers = (k.stage_d, k.one_d, k.two_d, k.three_d, four, k.total_d, done)
        parts = [reduction(*[b.at[i] for b in buffers], z_first=i in z_first and d_parts == 3) for i in range(d_parts)]
        return parts if d_parts == 3 else [Reduce.nothing, Reduce.nothing, parts[0]]

    def for_r(done):
        buffers = (k.stage_r, k.one_r, k.two_r, k.three_r, k.four_r, k.total_r, done)
        return [reduction(*[buffer.at[i] for buffer in buffers]) for i in range(4)]

    def all_sum(wide, i):
        if wide:
            parts = (k.wide_one, k.wide_two, k.wide_send, k.wide_recv_one, k.wide_recv_two)
        else:
            parts = (k.slim_one, k.slim_two, k.slim_send, k.slim_recv_one, k.slim_recv_two)
        return AllSum(p, *[part.at[i] for part in parts])

    def place_of(c):
        return c % 2, c // 2

    def norm_of(totals, lanes):
        return center_inverse(totals[0:1, lanes], totals[1:2, lanes], total)

    def block_end(upstream, totals, gain, bias, task):
        for start in range(0, geo.c_in, 512):
            lanes = pl.ds(start, 512)
            center, inverse = norm_of(totals, lanes)
            gain_row, bias_row = gain[:, lanes], bias[:, lanes]

            def body(at, carry):
                normed = (k.expanded[at, lanes] - center) * inverse
                joined = gain_row * normed + bias_row + k.inputs[at, lanes].astype(f32)
                grad = upstream(at, lanes) * slope_of(joined)[1]
                k.grad[at, lanes] = grad
                return carry[0] + fold(grad), carry[1] + fold(grad * normed)

            zero = jnp.zeros((8, 512), f32)
            a, b = over_rows(pixels, 16, body, (zero, zero))
            task.put(lanes, jnp.sum(a, axis=0, keepdims=True), jnp.sum(b, axis=0, keepdims=True))

    def third_norm(totals, grads, gain):
        for start in range(0, geo.c_in, 512):
            lanes = pl.ds(start, 512)
            center, inverse = norm_of(totals, lanes)
            scale = gain[:, lanes] * inverse
            bias_mean = grads[0:1, lanes] / total
            gain_mean = grads[1:2, lanes] / total

            def body(at, carry):
                normed = (k.expanded[at, lanes] - center) * inverse
                inner = k.grad[at, lanes] - bias_mean - normed * gain_mean
                k.third[at, lanes] = (scale * inner).astype(bf)
                return carry

            over_rows(pixels, 16, body, 0)

    def act_grad(values, totals, gain, bias, act, task):
        center, inverse = norm_of(totals, slim)
        gain_row, bias_row = gain[...], bias[...]

        def body(at, carry):
            normed = (values[at, :] - center) * inverse
            pre = gain_row * normed + bias_row
            sigma, slope = slope_of(pre)
            if act is not None:
                act[at, :] = (pre * sigma).astype(bf)
            grad = k.flow[at, :] * slope
            k.flow[at, :] = grad
            return carry[0] + fold(grad), carry[1] + fold(grad * normed)

        zero = jnp.zeros((8, mid), f32)
        a, b = over_rows(pixels, 16, body, (zero, zero))
        task.put(slim, jnp.sum(a, axis=0, keepdims=True), jnp.sum(b, axis=0, keepdims=True))

    def norm_grad(values, totals, grads, gain, out):
        center, inverse = norm_of(totals, slim)
        scale = gain[...] * inverse
        bias_mean = grads[0:1, :] / total
        gain_mean = grads[1:2, :] / total

        def body(at, carry):
            normed = (values[at, :] - center) * inverse
            out[at, :] = (scale * (k.flow[at, :] - bias_mean - normed * gain_mean)).astype(bf)
            return carry

        over_rows(pixels, 16, body, 0)

    def through_expand():
        for c in range(n_ch):
            part = mm_nt(k.third[:, c * we : (c + 1) * we], k.e[c])
            if c == 0:
                k.flow[...] = part
            else:
                k.flow[...] += part

    def expand_weights():
        k.act_t[...] = mm_nt(k.ident[...], k.low1[...]).astype(bf)
        for c in range(n_ch):
            k.stage_e[place_of(c)] = mm(k.act_t[...], k.third[:, c * we : (c + 1) * we]).astype(bf)

    def stage_tap(tap, cols_t):
        product = mm(cols_t, k.low2[...])
        part, inner = lax.div(tap, tap_count), lax.rem(tap, tap_count)
        for c in range(n_ch):
            for q in range(mid // 128):
                at = pl.ds(pl.multiple_of(inner * wr + q * tap_count * wr, 16), wr)
                piece = product[c * wr : (c + 1) * wr, q * 128 : (q + 1) * 128]
                k.stage_d[(part, *place_of(c), at)] = piece.astype(bf)

    def through_reduce():
        for start in range(0, geo.c_in, 512):
            rows = pl.ds(start, 512)
            for c in range(n_ch):
                k.grad[:, start : start + 512] += mm_nt(k.low1[:, c * wr : (c + 1) * wr], k.r[c, rows, :])

    def reduce_weights(work):
        for i, start in enumerate(range(0, geo.c_in, 512)):
            inputs_t = mm_nt(k.ident[...], k.inputs[:, start : start + 512]).astype(bf)
            product = mm(inputs_t, k.low1[...])
            for c in range(n_ch):
                k.stage_r[(i, *place_of(c))] = product[:, c * wr : (c + 1) * wr].astype(bf)
            work[i].s1()

    def deliver(task, out):
        return write_out(task.done.at[pl.ds(0, out.shape[0])], out)

    def deliver_d(parts, out):
        return [deliver(task, out.at[i]) for i, task in enumerate(parts[-d_parts:])]

    def deliver_r(parts, out):
        return [deliver(task, out.at[i]) for i, task in enumerate(parts)]

    def wait_all(copies):
        for copy in copies:
            copy.wait()

    def fetch(tap, slot):
        return pltpu.make_async_copy(k.cols1.at[tap], k.cols_t.at[slot], k.fetch_sem.at[slot])

    def sampled_tap(tap, carry):
        slot = lax.rem(tap, 2)

        @pl.when(tap < 8)
        def _():
            fetch(tap + 1, 1 - slot).start()

        fetch(tap, slot).wait()
        stage_tap(tap, k.cols_t[slot])
        return carry

    def rims_of(up, up_at, down, down_at, rows, sems):
        up_to, down_to = pl.ds(up_at, rows), pl.ds(down_at, rows)
        halo = Halo(
            p,
            (k.third.at[up_to, pl.ds(0, mid)], k.rim_recv.at[1, up_to]),
            (k.third.at[down_to, pl.ds(mid, mid)], k.rim_recv.at[0, down_to]),
            sems,
        )
        k.third[up_at : up_at + rows, :mid] = k.spread_grad[up : up + rows, :].astype(bf)
        k.third[down_at : down_at + rows, mid : 2 * mid] = k.spread_grad[down : down + rows, :].astype(bf)
        return halo

    def add_rims(rows):
        @pl.when(s > 0)
        def _():
            k.flow[:rows, :] += k.rim_recv[0, :rows, :].astype(f32)

        @pl.when(s < p.n_sp - 1)
        def _():
            k.flow[pixels - rows :, :] += k.rim_recv[1, :rows, :].astype(f32)

    expanded2 = load(k.expanded2, k.expanded)
    middle = load(k.middle, k.inputs)
    cotangent = load(k.cotangent, k.third)
    e2 = load(k.e2, k.e)
    spread2 = load(k.spread2, k.spread)
    d2 = load(k.d2, k.d)
    moved2 = load(k.moved_in, k.moved)
    reduced2 = load(k.reduced2, k.reduced)
    r2 = load(k.r2, k.r)
    ext1 = load(k.ext1_in, k.ext1)
    o1 = load(k.o1_in, k.o1)
    p.barrier()
    set_identity(k.ident)
    stages = [(k.stage_o, 9 * 32)] + [(k.stage_d.at[i], tap_count * wr * mid // 128) for i in range(d_parts)]
    for stage, rows in stages:
        if stage.shape[2] > rows:
            for q in range(n_ch):
                spare = (stage.shape[2] - rows, stage.shape[3])
                stage[(*place_of(q), pl.ds(rows, spare[0]))] = jnp.zeros(spare, bf)

    expanded2.wait()
    middle.wait()
    cotangent.wait()
    sum2c = all_sum(True, 0)
    counts = k.counts[...].astype(f32)
    mine = jnp.where(iota(counts.shape, 1) == p.c, counts, 0.0)
    box = jnp.sum(mine, axis=1, keepdims=True) * counts.shape[1] / jnp.sum(counts, axis=1, keepdims=True)
    block_end(lambda at, lanes: k.third[at, lanes].astype(f32) * box, k.totals2c, k.gain2c, k.bias2c, sum2c)
    sum2c.start()
    e2.wait()
    spread2.wait()
    d2.wait()
    moved2.wait()
    reduced2.wait()
    r2.wait()
    sum2c.relay()
    k.grads2c[...] = sum2c.finish()
    third_norm(k.totals2c, k.grads2c, k.gain2c)
    expanded1 = load(k.expanded1, k.expanded)
    through_expand()
    e1 = load(k.e1, k.e)
    sum2b = all_sum(False, 0)
    act_grad(k.spread, k.totals2b, k.gain2b, k.bias2b, k.low1, sum2b)
    sum2b.start()
    expand_weights()
    work_e2 = for_e()
    work_e2.s1()
    sum2b.relay()
    k.grads2b[...] = sum2b.finish()
    norm_grad(k.spread, k.totals2b, k.grads2b, k.gain2b, k.low2)
    spread1 = load(k.spread1, k.spread)
    work_e2.s2()

    area = pixels + 2 * rim
    k.spread_grad[:area, :] = jnp.zeros((area, mid), f32)
    for j in range(3):
        k.spread_grad[area : 2 * area, :] = jnp.zeros((area, mid), f32)

        def row_step(i, carry):
            at = pl.ds(pl.multiple_of(area + i * rim, 16), pixels)
            k.spread_grad[at, :] += mm_nt(k.low2[...], k.d[3 * i + j])
            return carry

        lax.fori_loop(0, 3, row_step, 0)

        def shift_back(r, carry):
            at = pl.ds(pl.multiple_of(r * columns, 16), columns)
            there = pl.ds(pl.multiple_of(area + r * columns, 16), columns)
            k.spread_grad[at, :] += column_shift(k.spread_grad[there, :], 2 - j, columns)
            return carry

        lax.fori_loop(0, geo.height + 4, shift_back, 0)
    d1 = load(k.d1, k.d)
    halo2 = rims_of(0, 0, pixels + rim, 0, rim, k.halo_sem.at[0])
    halo2.start()
    k.flow[...] = k.spread_grad[rim : pixels + rim, :]

    def plain_tap(tap, carry):
        first = lax.rem(tap, 3) * (pixels + 2 * rim) + lax.div(tap, 3) * rim
        cols = k.moved[pl.ds(pl.multiple_of(first, 16), pixels), :]
        stage_tap(tap, mm_nt(k.ident[...], cols).astype(bf))
        return carry

    work_d2 = for_d(k.four_d2, k.done_d2)
    for i in range(3):
        lax.fori_loop(3 * i, 3 * i + 3, plain_tap, 0)
        work_d2[i].s1()
    halo2.finish()
    add_rims(rim)
    sum2a = all_sum(False, 1)
    act_grad(k.reduced, k.totals2a, k.gain2a, k.bias2a, None, sum2a)
    sum2a.start()
    work_d2[0].s2()
    work_e2.s3()
    work_d2[1].s2()
    sum2a.relay()
    k.grads2a[...] = sum2a.finish()
    norm_grad(k.reduced, k.totals2a, k.grads2a, k.gain2a, k.low1)
    reduced1 = load(k.reduced1, k.reduced)
    through_reduce()
    r1 = load(k.r1, k.r)
    work_e2.s4()
    work_r2 = for_r(k.done_r2)
    reduce_weights(work_r2)
    features = load(k.features, k.inputs)

    expanded1.wait()
    features.wait()
    sum1c = all_sum(True, 1)
    block_end(lambda at, lanes: k.grad[at, lanes], k.totals1c, k.gain1c, k.bias1c, sum1c)
    sum1c.start()
    work_d2[2].s2()
    work_r2[0].s2()
    work_r2[1].s2()
    work_d2[0].s3()
    work_d2[1].s3()
    e1.wait()
    spread1.wait()
    d1.wait()
    reduced1.wait()
    r1.wait()
    ext1.wait()
    o1.wait()
    sum1c.relay()
    k.grads1c[...] = sum1c.finish()
    work_e2.s5()
    work_d2[0].s4()
    halo2.drain()
    third_norm(k.totals1c, k.grads1c, k.gain1c)
    through_expand()
    sum1b = all_sum(False, 2)
    act_grad(k.spread, k.totals1b, k.gain1b, k.bias1b, k.low1, sum1b)
    work_d2[2].s3_add()
    sum1b.start()
    work_r2[2].s2()
    work_r2[3].s2()
    work_e2.s6()
    work_d2[2].s3_send()
    expand_weights()
    work_r2[0].s3()
    work_r2[1].s3()
    work_e1 = for_e()
    sum1b.relay()
    work_e1.s1()
    work_e2.s7()
    e2_copy = deliver(work_e2, k.grad_e2)
    fetch(0, 0).start()
    k.grads1b[...] = sum1b.finish()
    work_d2[1].s4()
    work_d2[0].s5()
    norm_grad(k.spread, k.totals1b, k.grads1b, k.gain1b, k.low2)
    work_e1.s2()
    work_d1 = for_d(k.four_d, k.done_d, 0)
    for i in range(3):
        lax.fori_loop(3 * i, 3 * i + 3, sampled_tap, 0)
        work_d1[i].s1()

    k.spread_grad[...] = jnp.zeros((3 * pixels, mid), f32)
    k.raw_grad[...] = jnp.zeros((32, pixels), f32)

    def tap_step(tap, carry):
        @pl.when(tap == 0)
        def _():
            work_d1[0].s2()
            work_d2[2].s4()
            work_d2[1].s5()
            work_d2[0].s6()

        @pl.when(tap == 3)
        def _():
            work_d1[1].s2()
            work_r2[0].s4()
            work_r2[1].s4()
            work_r2[2].s3()
            work_r2[3].s3()
            work_d2[2].s5()

        @pl.when(tap == 6)
        def _():
            work_e1.s3()
            work_r2[2].s4()
            work_r2[3].s4()

        i, j = lax.div(tap, 3), lax.rem(tap, 3)
        lane = iota((1, pixels), 1)
        row = (lax.div(lane, columns) + 6 + 2 * i).astype(f32) + REACH * k.bend[pl.ds(tap, 1), :]
        across = (lax.rem(lane, columns) - 2 + 2 * j).astype(f32) + REACH * k.bend[pl.ds(tap + 16, 1), :]
        cell = iota((columns, pixels), 0).astype(f32)
        k.col_weight[...] = cell_weights(across, cell)
        row_base = jnp.floor(row)
        row_part = row - row_base
        row_upper = smooth_rise(row_part)
        row_rate = 6.0 * row_part * (1.0 - row_part)
        for r in range(3 * geo.height):
            weight = jnp.where(row_base == r, 1.0 - row_upper, jnp.where(row_base == r - 1, row_upper, 0.0))
            cells[r * columns : (r + 1) * columns, :] = (k.col_weight[...] * weight).astype(bf)
        cols_grad_t[...] = mm_nt(k.d[tap], k.low2[...]).astype(bf)
        k.spread_grad[...] += mm_nt(cells[...], cols_grad_t[...])
        for part in range(3):
            rows_at = slice(part * pixels, (part + 1) * pixels)
            k.expanded[:, 512 * part : 512 * part + pixels] = mm(k.ext1[rows_at, :], cols_grad_t[...])
        for start in range(0, pixels, 128):
            lanes = slice(start, start + 128)
            base, upper, rate = row_base[:, lanes], row_upper[:, lanes], row_rate[:, lanes]
            along = jnp.zeros((columns, 128), f32)
            down = jnp.zeros((columns, 128), f32)
            for r in range(3 * geo.height):
                row_at, col_at = r % geo.height * columns, r // geo.height * 512 + start
                match = k.expanded[row_at : row_at + columns, col_at : col_at + 128]
                at, after = base == r, base == r - 1
                along += match * jnp.where(at, 1.0 - upper, jnp.where(after, upper, 0.0))
                down += match * jnp.where(at, -rate, jnp.where(after, rate, 0.0))
            place = across[:, lanes]
            col_base = jnp.floor(place)
            col_part = place - col_base
            col_rate = 6.0 * col_part * (1.0 - col_part)
            cell_at = cell[:, lanes]
            col_slope = jnp.where(cell_at == col_base, -col_rate, jnp.where(cell_at == col_base + 1.0, col_rate, 0.0))
            here = iota((16, 128), 0) == tap
            by_row = jnp.sum(down * k.col_weight[:, lanes], axis=0, keepdims=True)
            by_col = jnp.sum(along * col_slope, axis=0, keepdims=True)
            k.raw_grad[:16, lanes] = jnp.where(here, by_row, k.raw_grad[:16, lanes])
            k.raw_grad[16:, lanes] = jnp.where(here, by_col, k.raw_grad[16:, lanes])
        return carry

    lax.fori_loop(0, 9, tap_step, 0)
    rest = pixels - rim
    halo1_far = rims_of(0, 0, 2 * pixels + rim, rim, rest, k.halo_sem.at[2])
    halo1_far.start()

    window = slice(6 * columns, 18 * columns)
    inner = slice(2 * columns, 14 * columns)
    bend = k.bend[...]
    raw = k.raw_grad[...] * (REACH * (1.0 - bend * bend))
    col = lax.rem(iota((32, pixels), 1), columns)
    for tap in range(9):
        i, j = tap // 3, tap % 3
        offset = (2 + 2 * i) * columns + 2 * (j - 1)
        part = raw
        if j == 0:
            part = jnp.where(col < 2, 0.0, part)
        if j == 2:
            part = jnp.where(col >= columns - 2, 0.0, part)
        part = jnp.concatenate([part, jnp.zeros((32, 16 * columns - pixels), f32)], axis=1)
        placed[32 * tap : 32 * tap + 32, :] = pltpu.roll(part, offset, 1).astype(bf)
    for start in range(0, 16 * columns, 256):
        placed_t[start : start + 256, : 9 * 32] = mm_nt(k.ident[:256, :256], placed[:, start : start + 256]).astype(bf)
    for c in range(n_ch):
        k.spread_grad[window, c * wr : (c + 1) * wr] += mm(placed_t[inner, : 9 * 32], k.o1[c])
    halo1 = rims_of(rest, rest, 2 * pixels, 0, rim, k.halo_sem.at[1])
    halo1.start()
    k.flow[...] = k.spread_grad[pixels : 2 * pixels, :]
    product = mm(placed[...], k.ext1[4 * columns : 20 * columns, :])
    for c in range(n_ch):
        k.stage_o[(*place_of(c), pl.ds(0, 9 * 32))] = product[:, c * wr : (c + 1) * wr].astype(bf)
    work_o1 = reduction(k.stage_o, k.one_o, k.two_o, k.three_o, k.four_o, k.total_o, k.done_o)
    work_o1.s1()

    e2_copy.wait()
    work_e1.s4()
    work_d1[2].s2()
    for part in work_d2:
        part.freed()
    work_d1[0].s3()
    halo1_far.finish()
    halo1.finish()
    add_rims(pixels)
    sum1a = all_sum(False, 3)
    act_grad(k.reduced, k.totals1a, k.gain1a, k.bias1a, None, sum1a)
    sum1a.start()
    work_d2[1].s6()
    work_d2[2].s6()
    work_o1.s2()
    sum1a.relay()
    work_d1[1].s3()
    work_d1[0].s4()
    k.grads1a[...] = sum1a.finish()
    work_e1.s5()
    for part in work_r2:
        part.s5()
    norm_grad(k.reduced, k.totals1a, k.grads1a, k.gain1a, k.low1)
    work_r1 = for_r(k.done_r)
    reduce_weights(work_r1)
    for part in work_r1:
        part.s2()
    work_d1[2].s3()
    work_d1[1].s4()
    through_reduce()
    d_features = write_out(k.grad, k.d_features)
    for part in work_d2:
        part.s7_end()
    d2_copies = deliver_d(work_d2, k.grad_d2)
    work_o1.s3()
    work_e1.s6()
    for part in work_r2:
        part.freed()
    work_r1[0].s3()
    work_d1[0].s5()
    work_d1[1].s5()
    work_r2[0].s6()
    work_r2[1].s6()
    work_r1[1].s3()
    work_r1[0].s4()
    work_d1[2].s4()
    work_r2[2].s6()
    work_r2[3].s6()
    work_r1[2].s3()
    work_r1[1].s4()
    work_o1.s4()
    for part in work_r2:
        part.s7_end()
    r2_copies = deliver_r(work_r2, k.grad_r2)
    work_r1[0].s5()
    work_r1[3].s3()
    work_d1[0].s6()
    work_r1[2].s4()
    work_r1[1].s5()
    work_d1[2].s5()
    work_r1[0].s6()
    work_r1[3].s4()
    work_d1[1].s6()
    work_o1.s5()
    work_r1[2].s5()
    work_r1[1].s6()
    work_e1.s7()
    e1_copy = deliver(work_e1, k.grad_e1)
    work_r1[3].s5()
    work_r1[2].s6()
    work_o1.s6()
    work_d1[2].s6()
    work_r1[3].s6()
    for part in work_d1:
        part.s7()
    d1_copies = deliver_d(work_d1, k.grad_d1)
    work_o1.s7()
    o1_copy = deliver(work_o1, k.grad_o1)
    for part in work_r1:
        part.s7()
    wait_all(deliver_r(work_r1, k.grad_r1) + d1_copies + d2_copies + r2_copies)
    e1_copy.wait()
    o1_copy.wait()
    for task in (sum2c, sum2b, sum2a, sum1c, sum1b, sum1a, halo1, halo1_far):
        task.drain()
    d_features.wait()


def run_backward(geo, kept, features, cotangent, counts, norms):
    bf, f32 = jnp.bfloat16, jnp.float32
    n_ch, n_sp, mid, pixels, wr, we = geo.n_ch, geo.n_sp, geo.mid, geo.pixels, geo.wr, geo.we
    n_x, near, far = n_ch // 2, 2 * n_ch, n_sp // 2
    columns, c_in = geo.columns, geo.c_in
    rim = 2 * columns
    vmem = pl.BlockSpec(memory_space=pltpu.VMEM)
    anywhere = pl.BlockSpec(memory_space=pl.ANY)
    far_away = dict(
        features=features,
        cotangent=cotangent,
        expanded2=kept.expanded2,
        middle=kept.middle,
        e2=kept.e2_all,
        spread2=kept.spread2,
        d2=kept.d2_all,
        moved_in=kept.moved.reshape(-1, mid),
        reduced2=kept.reduced2,
        r2=kept.r2_all,
        expanded1=kept.expanded1,
        e1=kept.e1_all,
        spread1=kept.spread1,
        d1=kept.d1_all,
        cols1=kept.cols1_t,
        ext1_in=kept.ext1,
        reduced1=kept.reduced1,
        r1=kept.r1_all,
        o1_in=kept.o1_all,
    )
    close = dict(
        bend=kept.bend,
        counts=counts,
        totals1a=kept.totals1a,
        totals1b=kept.totals1b,
        totals1c=kept.totals1c,
        totals2a=kept.totals2a,
        totals2b=kept.totals2b,
        totals2c=kept.totals2c,
        **norms,
    )
    grads = dict(
        grad_e2=((mid, we), bf, anywhere),
        grad_d2=((geo.d_parts, 9 // geo.d_parts * wr * 4, 128), bf, anywhere),
        grad_r2=((4, 512, wr), bf, anywhere),
        grad_e1=((mid, we), bf, anywhere),
        grad_d1=((geo.d_parts, 9 // geo.d_parts * wr * 4, 128), bf, anywhere),
        grad_r1=((4, 512, wr), bf, anywhere),
        grad_o1=((9 * 32, wr), bf, anywhere),
        d_features=((pixels, c_in), f32, anywhere),
        grads2c=((2, c_in), f32, vmem),
        grads2b=((2, mid), f32, vmem),
        grads2a=((2, mid), f32, vmem),
        grads1c=((2, c_in), f32, vmem),
        grads1b=((2, mid), f32, vmem),
        grads1a=((2, mid), f32, vmem),
    )
    dma = pltpu.SemaphoreType.DMA
    v = pltpu.VMEM
    scratch = dict(
        e=v((n_ch, mid, we), bf),
        d=v((9, mid, mid), bf),
        r=v((n_ch, c_in, wr), bf),
        o1=v((n_ch, 9 * 32, wr), bf),
        expanded=v((pixels, c_in), f32),
        grad=v((pixels, c_in), f32),
        inputs=v((pixels, c_in), bf),
        third=v((pixels, c_in), bf),
        spread=v((pixels, mid), f32),
        reduced=v((pixels, mid), f32),
        flow=v((pixels, mid), f32),
        act_t=v((mid, pixels), bf),
        low1=v((pixels, mid), bf),
        low2=v((pixels, mid), bf),
        moved=v((3 * (pixels + 2 * rim), mid), bf),
        ext1=v((3 * pixels, mid), bf),
        cols_t=v((2, mid, pixels), bf),
        col_weight=v((columns, pixels), f32),
        spread_grad=v((3 * pixels, mid), f32),
        raw_grad=v((32, pixels), f32),
        ident=v((mid, mid), bf),
        rim_recv=v((2, pixels, mid), bf),
        slim_one=v((4, near, 2, mid), f32),
        slim_two=v((4, far, 2, mid), f32),
        slim_send=dma((4, near + far)),
        slim_recv_one=dma((4, near)),
        slim_recv_two=dma((4, far)),
        wide_one=v((2, near, 2, c_in), f32),
        wide_two=v((2, far, 2, c_in), f32),
        wide_send=dma((2, near + far)),
        wide_recv_one=dma((2, near)),
        wide_recv_two=dma((2, far)),
        halo_sem=dma((3, 4)),
        load_sem=dma((20,)),
        out_sem=dma((24,)),
        fetch_sem=dma((2,)),
        reduce_send=dma((17, Reduce.sems(n_sp, n_ch))),
        reduce_recv=dma((17, Reduce.sems(n_sp, n_ch))),
    )

    def staging(rows, lanes, *parts, both=1):
        return (
            v((*parts, 2, n_x, rows, lanes), bf),
            v((*parts, n_x, rows, lanes), bf),
            v((*parts, n_x - 1, rows, lanes), bf),
            v((*parts, rows // 2, lanes), bf),
            v((*parts, far, both * rows // n_sp, lanes), bf),
            v((*parts, rows, lanes), bf),
            v((*parts, rows, lanes), bf),
        )

    def padded(rows):
        return -(-rows // (32 * far)) * 32 * far

    d_rows = padded(9 // geo.d_parts * wr * mid // 128)
    e, d, r, o = staging(mid, we), staging(d_rows, 128, geo.d_parts, both=2 if geo.d_parts == 3 else 1), staging(512, wr, 4), staging(padded(9 * 32), wr)
    scratch |= dict(stage_e=e[0], one_e=e[1], two_e=e[2], three_e=e[3], four_e=e[4], total_e=e[5], done_e=e[6])
    scratch |= dict(stage_d=d[0], one_d=d[1], two_d=d[2], three_d=d[3], four_d=d[4], total_d=d[5], done_d=d[6], done_d2=d[6], four_d2=d[4])
    scratch |= dict(stage_r=r[0], one_r=r[1], two_r=r[2], three_r=r[3], four_r=r[4], total_r=r[5], done_r=r[6], done_r2=r[6])
    scratch |= dict(stage_o=o[0], one_o=o[1], two_o=o[2], three_o=o[3], four_o=o[4], total_o=o[5], done_o=o[6])
    results = pl.pallas_call(
        functools.partial(backward_kernel, geo, [*far_away, *close, *grads, *scratch]),
        out_shape=[jax.ShapeDtypeStruct(shape, dtype) for shape, dtype, _ in grads.values()],
        in_specs=[anywhere] * len(far_away) + [vmem] * len(close),
        out_specs=[spec for _, _, spec in grads.values()],
        scratch_shapes=list(scratch.values()),
        compiler_params=pltpu.CompilerParams(
            collective_id=1, has_side_effects=True, vmem_limit_bytes=63 * MIB
        ),
    )(*far_away.values(), *close.values())
    return types.SimpleNamespace(**dict(zip(grads, results, strict=True)))


def finish_kernel(geo, names, *refs):
    k = types.SimpleNamespace(**dict(zip(names, refs, strict=True)))
    f32 = jnp.float32
    wr = geo.wr
    for source, out in ((k.e2, k.e2_out), (k.e1, k.e1_out), (k.d_features, k.d_features_out), (k.last, k.last_out)):
        out[...] = source[...].astype(out.dtype)
    for source, out in ((k.r2, k.r2_out), (k.r1, k.r1_out)):
        out[...] = source[0].astype(f32)
    for source, out in ((k.d2, k.d2_out), (k.d1, k.d1_out)):
        rows = source.shape[2]
        for part in range(source.shape[0]):
            out[part * rows : (part + 1) * rows, :] = source[part, 0].astype(f32)

    @pl.when(pl.program_id(0) == 0)
    def _():
        row, offset = iota((18, 32), 1), iota((18, 32), 0)
        chosen = (lax.rem(row, 16) == lax.div(offset, 2)) & (lax.div(row, 16) == lax.rem(offset, 2))
        chosen = jnp.where(chosen, 1.0, 0.0).astype(jnp.bfloat16)
        for tap in range(9):
            part = k.o1[32 * tap : 32 * tap + 32, :]
            k.o1_out[tap] = mm(chosen, part)
        vectors = (
            (k.sums1a, k.gain1a, k.bias1a),
            (k.sums1b, k.gain1b, k.bias1b),
            (k.sums1c, k.gain1c, k.bias1c),
            (k.sums2a, k.gain2a, k.bias2a),
            (k.sums2b, k.gain2b, k.bias2b),
            (k.sums2c, k.gain2c, k.bias2c),
        )
        for sums, gain, bias in vectors:
            gain[...] = sums[1:2, :]
            bias[...] = sums[0:1, :]


def run_finish(geo, g, last):
    f32 = jnp.float32
    steps, wr, we, mid, c_in, pixels = 4, geo.wr, geo.we, geo.mid, geo.c_in, geo.pixels
    d_rows = 9 // geo.d_parts * wr

    def rows(height, width):
        return pl.BlockSpec((height // steps, width), lambda i: (i, 0))

    def whole(*shape):
        return pl.BlockSpec(shape, lambda i: (0,) * len(shape))

    d_in = pl.BlockSpec((geo.d_parts, 1, d_rows, 128), lambda i: (0, i, 0, 0))
    r_in = pl.BlockSpec((1, 512, wr), lambda i: (i, 0, 0))
    d_shape = (geo.d_parts, 4, d_rows, 128)
    ins = dict(
        e2=(g.grad_e2, rows(mid, we)),
        d2=(g.grad_d2.reshape(d_shape), d_in),
        r2=(g.grad_r2, r_in),
        e1=(g.grad_e1, rows(mid, we)),
        d1=(g.grad_d1.reshape(d_shape), d_in),
        r1=(g.grad_r1, r_in),
        o1=(g.grad_o1, whole(9 * 32, wr)),
        d_features=(g.d_features, rows(pixels, c_in)),
        last=(last, rows(pixels, c_in)),
        sums1a=(g.grads1a, whole(2, mid)),
        sums1b=(g.grads1b, whole(2, mid)),
        sums1c=(g.grads1c, whole(2, c_in)),
        sums2a=(g.grads2a, whole(2, mid)),
        sums2b=(g.grads2b, whole(2, mid)),
        sums2c=(g.grads2c, whole(2, c_in)),
    )
    slim, wide = ((1, mid), whole(1, mid)), ((1, c_in), whole(1, c_in))
    d_out = ((9 * wr, mid), pl.BlockSpec((9 * wr, 128), lambda i: (0, i)))
    outs = dict(
        e2_out=((mid, we), rows(mid, we)),
        d2_out=d_out,
        r2_out=((c_in, wr), rows(c_in, wr)),
        e1_out=((mid, we), rows(mid, we)),
        d1_out=d_out,
        r1_out=((c_in, wr), rows(c_in, wr)),
        o1_out=((9, 18, wr), whole(9, 18, wr)),
        d_features_out=((pixels, c_in), rows(pixels, c_in)),
        last_out=((pixels, c_in), rows(pixels, c_in)),
        gain1a=slim,
        bias1a=slim,
        gain1b=slim,
        bias1b=slim,
        gain1c=wide,
        bias1c=wide,
        gain2a=slim,
        bias2a=slim,
        gain2b=slim,
        bias2b=slim,
        gain2c=wide,
        bias2c=wide,
    )
    results = pl.pallas_call(
        functools.partial(finish_kernel, geo, [*ins, *outs]),
        grid=(steps,),
        out_shape=[
            jax.ShapeDtypeStruct(shape, last.dtype if name == "last_out" else f32) for name, (shape, _) in outs.items()
        ],
        in_specs=[spec for _, spec in ins.values()],
        out_specs=[spec for _, spec in outs.values()],
        compiler_params=pltpu.CompilerParams(vmem_limit_bytes=60 * MIB),
    )(*[array for array, _ in ins.values()])
    return types.SimpleNamespace(**dict(zip(outs, results, strict=True)))


def per_device(
    features,
    box_counts,
    b1_w_reduce,
    b1_gain1,
    b1_bias1,
    b1_w_offset,
    b1_w_deform,
    b1_gain2,
    b1_bias2,
    b1_w_expand,
    b1_gain3,
    b1_bias3,
    b2_w_reduce,
    b2_gain1,
    b2_bias1,
    b2_w_spatial,
    b2_gain2,
    b2_bias2,
    b2_w_expand,
    b2_gain3,
    b2_bias3,
    cotangent,
):
    images, height, columns, channels = features.shape
    n_sp, n_ch = lax.axis_size("sp"), lax.axis_size("ch")
    pixels = images * height * columns
    mid, wr = b1_w_deform.shape[2], b1_w_reduce.shape[1]
    geo = types.SimpleNamespace(
        n_sp=n_sp,
        n_ch=n_ch,
        pixels=pixels,
        height=height,
        columns=columns,
        mid=mid,
        c_in=channels,
        wr=wr,
        we=b1_w_expand.shape[1],
        pixel_total=pixels * n_sp * n_ch,
        d_parts=3 if 3 * wr * mid // 128 % (16 * n_sp) == 0 else 1,
    )
    shards = dict(
        r1=b1_w_reduce,
        d1=b1_w_deform,
        e1=b1_w_expand,
        r2=b2_w_reduce,
        d2=b2_w_spatial,
        e2=b2_w_expand,
    )
    norms = dict(
        gain1a=b1_gain1,
        bias1a=b1_bias1,
        gain1b=b1_gain2,
        bias1b=b1_bias2,
        gain1c=b1_gain3,
        bias1c=b1_bias3,
        gain2a=b2_gain1,
        bias2a=b2_bias1,
        gain2b=b2_gain2,
        bias2b=b2_bias2,
        gain2c=b2_gain3,
        bias2c=b2_bias3,
    )
    norms = {name: vector.reshape(1, -1) for name, vector in norms.items()}
    entry = features.reshape(pixels, channels)
    kept = run_forward(geo, entry, jnp.swapaxes(b1_w_offset, 1, 2), shards, norms)
    g = run_backward(geo, kept, entry, cotangent.reshape(pixels, channels), box_counts.reshape(1, -1), norms)
    done = run_finish(geo, g, kept.last)
    return (
        done.last_out.reshape(features.shape),
        done.d_features_out.reshape(features.shape),
        done.r1_out,
        done.gain1a.reshape(mid),
        done.bias1a.reshape(mid),
        jnp.swapaxes(done.o1_out, 1, 2),
        done.d1_out.reshape(9, wr, mid),
        done.gain1b.reshape(mid),
        done.bias1b.reshape(mid),
        done.e1_out,
        done.gain1c.reshape(channels),
        done.bias1c.reshape(channels),
        done.r2_out,
        done.gain2a.reshape(mid),
        done.bias2a.reshape(mid),
        done.d2_out.reshape(9, wr, mid),
        done.gain2b.reshape(mid),
        done.bias2b.reshape(mid),
        done.e2_out,
        done.gain2c.reshape(channels),
        done.bias2c.reshape(channels),
    )


def solution(mesh):
    return jax.shard_map(
        per_device,
        mesh=mesh,
        in_specs=(
            P("ch", "sp", None, None),
            P(),
            P(None, "ch"),
            P(),
            P(),
            P(None, "ch", None),
            P(None, "ch", None),
            P(),
            P(),
            P(None, "ch"),
            P(),
            P(),
            P(None, "ch"),
            P(),
            P(),
            P(None, "ch", None),
            P(),
            P(),
            P(None, "ch"),
            P(),
            P(),
            P("ch", "sp", None, None),
        ),
        out_specs=(
            P("ch", "sp", None, None),
            P("ch", "sp", None, None),
            P(None, "ch"),
            P(),
            P(),
            P(None, "ch", None),
            P(None, "ch", None),
            P(),
            P(),
            P(None, "ch"),
            P(),
            P(),
            P(None, "ch"),
            P(),
            P(),
            P(None, "ch", None),
            P(),
            P(),
            P(None, "ch"),
            P(),
            P(),
        ),
        check_vma=False,
    )
```

```python
import functools
import types

import jax
import jax.numpy as jnp
from jax import lax
from jax.experimental import pallas as pl
from jax.experimental.pallas import tpu as pltpu
from jax.sharding import PartitionSpec as P

EPS = 1e-05
REACH = 5.5
MESH = pl.DeviceIdType.MESH
MIB = 2**20


def mm(left, right):
    return jnp.dot(left, right, preferred_element_type=jnp.float32)


def mm_nt(left, right):
    return lax.dot_general(
        left, right, (((1,), (1,)), ((), ())), preferred_element_type=jnp.float32
    )


def smooth_rise(fraction):
    return fraction * fraction * (3.0 - 2.0 * fraction)


def sigmoid(v):
    return 1.0 / (1.0 + jnp.exp(-v))


class Place:
    def __init__(self, n_sp, n_ch):
        self.n_sp, self.n_ch, self.n_x = n_sp, n_ch, n_ch // 2
        self.s, self.c = lax.axis_index("sp"), lax.axis_index("ch")
        self.x, self.k = lax.div(self.c, 2), lax.rem(self.c, 2)
        self.y = lax.rem(self.s, 2)
        self.sib = self.c + 1 - 2 * self.k
        self.sibling = (self.s, self.sib)

    def other_x(self, d):
        return 2 * lax.rem(self.x + d, self.n_x) + self.k

    def near(self, d):
        q = lax.rem(self.y * self.n_ch + self.c + d, 2 * self.n_ch)
        return self.s - self.y + lax.div(q, self.n_ch), lax.rem(q, self.n_ch)

    def far(self, d):
        return lax.rem(self.s + 2 * d, self.n_sp), self.c

    def barrier(self):
        sem = pltpu.get_barrier_semaphore()

        def tell(device):
            pl.semaphore_signal(sem, inc=1, device_id=device, device_id_type=MESH)

        for d in range(1, 2 * self.n_ch):
            tell(self.near(d))
        for d in range(1, self.n_sp // 2):
            tell(self.far(d))
        diagonal = lax.rem(self.s + self.n_sp - 1 + 2 * self.y, self.n_sp)
        tell((diagonal, self.c))
        pl.semaphore_wait(sem, 2 * self.n_ch + self.n_sp // 2 - 1)


def remote(src, dst, send, recv, device):
    return pltpu.make_async_remote_copy(
        src_ref=src,
        dst_ref=dst,
        send_sem=send,
        recv_sem=recv,
        device_id=device,
        device_id_type=MESH,
    )


class AllSum:
    def __init__(self, place, first, second, send, recv_one, recv_two):
        self.p, self.first, self.second = place, first, second
        self.send, self.one, self.two = send, recv_one, recv_two
        self.me = place.y * place.n_ch + place.c
        self.row = lax.div(place.s, 2)

    def put(self, lanes, sums, squares):
        self.first[self.me, 0:1, lanes] = sums
        self.first[self.me, 1:2, lanes] = squares

    def _near(self, d):
        return remote(self.first.at[self.me], self.first.at[self.me], self.send.at[d], self.one.at[self.me], self.p.near(d))

    def _far(self, d):
        n = 2 * self.p.n_ch
        return remote(self.second.at[self.row], self.second.at[self.row], self.send.at[n + d], self.two.at[self.row], self.p.far(d))

    def start(self):
        for d in range(1, 2 * self.p.n_ch):
            self._near(d).start()

    def relay(self):
        n = 2 * self.p.n_ch
        for d in range(1, n):
            other = lax.rem(self.me + d, n)
            slot = self.first.at[other]
            remote(slot, slot, self.send.at[d], self.one.at[other], self.p.near(d)).wait_recv()
        total = self.first[0]
        for q in range(1, n):
            total = total + self.first[q]
        self.second[self.row] = total
        for d in range(1, self.p.n_sp // 2):
            self._far(d).start()

    def finish(self):
        n = self.p.n_sp // 2
        for d in range(1, n):
            other = lax.rem(self.row + d, n)
            slot = self.second.at[other]
            remote(slot, slot, self.send.at[d], self.two.at[other], self.p.far(d)).wait_recv()
        total = self.second[0]
        for q in range(1, n):
            total = total + self.second[q]
        return total

    def drain(self):
        for d in range(1, 2 * self.p.n_ch):
            self._near(d).wait_send()
        for d in range(1, self.p.n_sp // 2):
            self._far(d).wait_send()


class Gather:
    def __init__(self, place, src, slot, send, recv):
        self.p, self.src, self.slot, self.send, self.recv = place, src, slot, send, recv

    def _own(self):
        return pltpu.make_async_copy(self.src, self.slot(self.p.c), self.recv.at[self.p.c])

    def _sibling(self):
        c = self.p.c
        return remote(self.src, self.slot(c), self.send.at[0], self.recv.at[c], self.p.sibling)

    def _direct(self, d):
        c = self.p.c
        return remote(self.src, self.slot(c), self.send.at[d], self.recv.at[c], (self.p.s, self.p.other_x(d)))

    def _forward(self, d):
        o = self.p.other_x(d)
        return remote(self.slot(o), self.slot(o), self.send.at[self.p.n_x + d - 1], self.recv.at[o], self.p.sibling)

    def _arrived(self, o):
        remote(self.slot(o), self.slot(o), self.send.at[0], self.recv.at[o], self.p.sibling).wait_recv()

    def start(self):
        for d in range(1, self.p.n_x):
            self._direct(d).start()
        self._sibling().start()
        self._own().start()

    def pump(self):
        for d in range(1, self.p.n_x):
            self._arrived(self.p.other_x(d))
            self._forward(d).start()

    def finish(self):
        self._own().wait()
        self._arrived(self.p.sib)
        for d in range(1, self.p.n_x):
            self._arrived(self.p.other_x(d) + 1 - 2 * self.p.k)

    def drain(self):
        self._sibling().wait_send()
        for d in range(1, self.p.n_x):
            self._direct(d).wait_send()
            self._forward(d).wait_send()


class HalfGather:
    def __init__(self, place, src, slot, send, recv):
        self.p, self.src, self.slot, self.send, self.recv = place, src, slot, send, recv
        z = lax.div(place.s, 2)
        self.h = lax.rem(z, 2)
        self.beside = (place.s + 2 - 4 * self.h, place.c)

    def _own(self, h):
        c = self.p.c
        return pltpu.make_async_copy(self.src(h), self.slot(c, h), self.recv.at[2 * c + h])

    def _sibling(self, h):
        c = self.p.c
        return remote(self.src(h), self.slot(c, h), self.send.at[h], self.recv.at[2 * c + h], self.p.sibling)

    def _direct(self, d):
        c, h = self.p.c, self.h
        there = (self.p.s, self.p.other_x(d))
        return remote(self.src(h), self.slot(c, h), self.send.at[1 + d], self.recv.at[2 * c + h], there)

    def _pass(self, d, kind, h, device):
        o = self.p.other_x(d)
        sem = self.send.at[2 + (kind + 1) * (self.p.n_x - 1) + d - 1]
        return remote(self.slot(o, h), self.slot(o, h), sem, self.recv.at[2 * o + h], device)

    def _beside(self, d):
        return self._pass(d, 0, self.h, self.beside)

    def _forward(self, d):
        return self._pass(d, 1, self.h, self.p.sibling)

    def _second(self, d):
        return self._pass(d, 2, 1 - self.h, self.p.sibling)

    def _arrived(self, o, h):
        remote(self.slot(o, h), self.slot(o, h), self.send.at[0], self.recv.at[2 * o + h], self.p.sibling).wait_recv()

    def start(self):
        for d in range(1, self.p.n_x):
            self._direct(d).start()
        for h in range(2):
            self._sibling(h).start()
            self._own(h).start()

    def pump(self):
        for d in range(1, self.p.n_x):
            self._arrived(self.p.other_x(d), self.h)
            self._beside(d).start()
            self._forward(d).start()

    def pump_again(self):
        for d in range(1, self.p.n_x):
            self._arrived(self.p.other_x(d), 1 - self.h)
            self._second(d).start()

    def finish(self):
        for h in range(2):
            self._own(h).wait()
            self._arrived(self.p.sib, h)
            for d in range(1, self.p.n_x):
                self._arrived(self.p.other_x(d) + 1 - 2 * self.p.k, h)

    def drain(self):
        for h in range(2):
            self._sibling(h).wait_send()
        for d in range(1, self.p.n_x):
            for copy in (self._direct(d), self._beside(d), self._forward(d), self._second(d)):
                copy.wait_send()


class Halo:
    def __init__(self, place, up, down, sems):
        self.p, self.up, self.down, self.sems = place, up, down, sems

    def _up(self):
        return remote(*self.up, self.sems.at[0], self.sems.at[1], (self.p.s - 1, self.p.c))

    def _down(self):
        return remote(*self.down, self.sems.at[2], self.sems.at[3], (self.p.s + 1, self.p.c))

    def _each(self, act_up, act_down):
        pl.when(self.p.s > 0)(act_up)
        pl.when(self.p.s < self.p.n_sp - 1)(act_down)

    def start(self):
        self._each(lambda: self._up().start(), lambda: self._down().start())

    def finish(self):
        self._each(lambda: self._down().wait_recv(), lambda: self._up().wait_recv())

    def drain(self):
        self._each(lambda: self._up().wait_send(), lambda: self._down().wait_send())


def over_rows(rows, step, body, init):
    def one(i, carry):
        return body(pl.ds(pl.multiple_of(i * step, step), step), carry)

    return lax.fori_loop(0, rows // step, one, init, unroll=2)


def fold(v):
    return jnp.sum(v.reshape(-1, 8, v.shape[1]), axis=0)


def moments(ref, lanes, rows):
    width = lanes.size

    def body(at, carry):
        v = ref[at, lanes]
        return carry[0] + fold(v), carry[1] + fold(v * v)

    zero = jnp.zeros((8, width), jnp.float32)
    a, b = over_rows(rows, 16, body, (zero, zero))
    return jnp.sum(a, axis=0, keepdims=True), jnp.sum(b, axis=0, keepdims=True)


def center_inverse(sums, squares, pixel_total):
    center = sums / pixel_total
    return center, lax.rsqrt(squares / pixel_total - center * center + EPS)


def cell_weights(position, cells):
    base = jnp.floor(position)
    upper = smooth_rise(position - base)
    return jnp.where(cells == base, 1.0 - upper, jnp.where(cells == base + 1.0, upper, 0.0))


def iota(shape, axis):
    return lax.broadcasted_iota(jnp.int32, shape, axis)


def set_identity(ref):
    n = ref.shape[0]
    for r in range(0, n, 128):
        same = iota((128, n), 0) + r == iota((128, n), 1)
        ref[r : r + 128, :] = jnp.where(same, 1.0, 0.0).astype(jnp.bfloat16)


def column_shift(v, j, columns):
    if j == 1:
        return v
    col = lax.rem(iota(v.shape, 0), columns)
    if j == 0:
        return jnp.where(col < 2, 0.0, pltpu.roll(v, 2, 0))
    return jnp.where(col >= columns - 2, 0.0, pltpu.roll(v, v.shape[0] - 2, 0))


def forward_kernel(geo, names, *refs):
    k = types.SimpleNamespace(**dict(zip(names, refs, strict=True)))
    p = Place(geo.n_sp, geo.n_ch)
    s, pixels, columns, mid = p.s, geo.pixels, geo.columns, geo.mid
    n_ch, wr, we, total = p.n_ch, geo.wr, geo.we, geo.pixel_total
    bf, f32 = jnp.bfloat16, jnp.float32

    def rows_of(ref, width, first, taps):
        at = pl.ds(first, taps)
        return lambda c: ref.at[at, pl.ds(pl.multiple_of(c * width, width), width), :]

    def slots_of(ref):
        return lambda c: ref.at[c]

    def gather(i, src, slot):
        return Gather(p, src, slot, k.gather_send.at[i], k.gather_recv.at[i])

    o1 = gather(1, k.o1_own, slots_of(k.o1_all))
    d1a = gather(2, k.d1.at[pl.ds(0, 2)], rows_of(k.d1_all, wr, 0, 2))
    d1b = gather(3, k.d1.at[pl.ds(2, 7)], rows_of(k.d1_all, wr, 2, 7))
    e1 = gather(4, k.e1, slots_of(k.e1_all))

    def half_gather(i, src, slot):
        return HalfGather(p, src, slot, k.half_send.at[i], k.half_recv.at[i])

    def half_rows(ref, rows):
        return lambda h: ref.at[pl.ds(pl.multiple_of(h * rows, 16), rows)]

    def half_slots(ref, rows):
        return lambda c, h: ref.at[c, pl.ds(pl.multiple_of(h * rows, 16), rows)]

    def quarter(i):
        rows = geo.c_in // 8

        def at(h):
            return pl.ds(pl.multiple_of(2 * i * rows + h * rows, 16), rows)

        return half_gather(3 + i, lambda h: k.r1.at[at(h)], lambda c, h: k.r1_all.at[c, at(h)])

    r1 = [quarter(i) for i in range(4)]
    r2 = half_gather(0, half_rows(k.r2, geo.c_in // 2), half_slots(k.r2_all, geo.c_in // 2))
    d2 = half_gather(
        1,
        lambda h: k.d2.at[:, pl.ds(pl.multiple_of(h * (wr // 2), 16), wr // 2), :],
        lambda c, h: k.d2_all.at[:, pl.ds(pl.multiple_of(c * wr + h * (wr // 2), 16), wr // 2), :],
    )
    e2 = half_gather(2, half_rows(k.e2, mid // 2), half_slots(k.e2_all, mid // 2))

    def all_sum(wide, i):
        if wide:
            parts = (k.wide_one, k.wide_two, k.wide_send, k.wide_recv_one, k.wide_recv_two)
        else:
            parts = (k.slim_one, k.slim_two, k.slim_send, k.slim_recv_one, k.slim_recv_two)
        return AllSum(p, *[part.at[i] for part in parts])

    saves = []

    def save(src, dst):
        copy = pltpu.make_async_copy(src, dst, k.save_sem.at[len(saves)])
        copy.start()
        saves.append(copy)

    def run_sum(task, totals, *between):
        task.start()
        for one in between:
            one()
        task.relay()
        totals[...] = task.finish()

    def reduce_matmul(x, weights, out):
        for c in range(n_ch):
            out[:, c * wr : (c + 1) * wr] = mm(x[...], weights[c])

    def activate(values, totals, gain, bias, out, first_row):
        center, inverse = center_inverse(totals[0:1, :], totals[1:2, :], total)
        scale = gain[...] * inverse
        shift = bias[...]

        def body(at, carry):
            v = (values[at, :] - center) * scale + shift
            row = pl.ds(pl.multiple_of(at.start + first_row, 16), at.size)
            out[row, :] = (v * sigmoid(v)).astype(bf)
            return carry

        over_rows(pixels, 16, body, 0)

    def expand(x, weights, out, task):
        for c in range(n_ch):
            lanes = pl.ds(c * we, we)
            out[:, lanes] = mm(x[...], weights[c])
            task.put(lanes, *moments(out, lanes, pixels))

    def leave(values, totals, gain, bias, residual, out):
        for start in range(0, geo.c_in, 512):
            lanes = pl.ds(start, 512)
            center, inverse = center_inverse(totals[0:1, lanes], totals[1:2, lanes], total)
            scale = gain[:, lanes] * inverse
            shift = bias[:, lanes]

            def body(at, carry):
                v = (values[at, lanes] - center) * scale + shift + residual[at, lanes].astype(f32)
                out[at, lanes] = (v * sigmoid(v)).astype(bf)
                return carry

            over_rows(pixels, 16, body, 0)

    slim = pl.ds(0, mid)

    p.barrier()
    for part in r1:
        part.start()
    row, offset = iota((32, 18), 0), iota((32, 18), 1)
    chosen = (lax.rem(row, 16) == lax.div(offset, 2)) & (lax.div(row, 16) == lax.rem(offset, 2))
    chosen = jnp.where(chosen, 1.0, 0.0).astype(bf)
    for tap in range(9):
        k.o1_own[32 * tap : 32 * tap + 32, :] = mm(chosen, k.o1[tap]).astype(bf)
    o1.start()
    d1a.start()
    set_identity(k.ident)

    def reduce_quarter(i):
        r1[i].finish()
        at = slice(i * (geo.c_in // 4), (i + 1) * (geo.c_in // 4))
        for c in range(n_ch):
            part = mm(k.x[:, at], k.r1_all[c, at, :])
            if i == 0:
                k.reduced1[:, c * wr : (c + 1) * wr] = part
            else:
                k.reduced1[:, c * wr : (c + 1) * wr] += part

    r1[0].pump()
    r1[1].pump()
    r1[0].pump_again()
    r1[2].pump()
    r1[1].pump_again()
    r1[3].pump()
    reduce_quarter(0)
    r1[2].pump_again()
    reduce_quarter(1)
    r1[3].pump_again()
    reduce_quarter(2)
    reduce_quarter(3)
    task1 = all_sum(False, 0)
    task1.put(slim, *moments(k.reduced1, slim, pixels))
    run_sum(task1, k.totals1a, d1b.start, e1.start)
    o1.pump()
    activate(k.reduced1, k.totals1a, k.gain1a, k.bias1a, k.ext1, pixels)
    own = k.ext1.at[pixels : 2 * pixels]
    rim, rest = 2 * columns, pixels - 2 * columns

    def strip(start, size):
        return k.ext1.at[pl.ds(start, size)]

    halo1 = Halo(
        p,
        (strip(pixels, rim), strip(2 * pixels, rim)),
        (strip(2 * pixels - rim, rim), strip(rest, rim)),
        k.halo_sem.at[0],
    )
    halo1_far = Halo(
        p,
        (strip(pixels + rim, rest), strip(2 * pixels + rim, rest)),
        (strip(pixels, rest), strip(0, rest)),
        k.halo_sem.at[2],
    )
    halo1.start()
    halo1_far.start()
    save(k.reduced1, k.reduced1_out)

    @pl.when(s == 0)
    def _():
        k.ext1[:pixels, :] = jnp.zeros((pixels, mid), bf)

    @pl.when(s == p.n_sp - 1)
    def _():
        k.ext1[2 * pixels :, :] = jnp.zeros((pixels, mid), bf)

    d1a.pump()
    o1.finish()
    k.ext1_t[:, pixels : 2 * pixels] = mm_nt(k.ident[...], k.ext1[pixels : 2 * pixels, :]).astype(bf)
    edge = jnp.zeros((rim, mid), bf)
    k.window[:rim, :] = edge
    k.window[14 * columns :, :] = edge
    halo1.finish()
    k.window[rim : 14 * columns, :] = k.ext1[6 * columns : 18 * columns, :]
    raw_all = jnp.zeros((9 * 32, 16 * columns), f32)
    for c in range(n_ch):
        raw_all += mm_nt(k.o1_all[c], k.window[:, c * wr : (c + 1) * wr])
    k.raw_all[...] = raw_all
    lane = iota((32, pixels), 1)
    col = lax.rem(lane, columns)
    raw = jnp.zeros((32, pixels), f32)
    for tap in range(9):
        i, j = tap // 3, tap % 3
        offset = (2 + 2 * i) * columns + 2 * (j - 1)
        part = k.raw_all[32 * tap : 32 * tap + 32, :]
        part = pltpu.roll(part, 16 * columns - offset, 1)[:, :pixels]
        if j == 0:
            part = jnp.where(col < 2, 0.0, part)
        if j == 2:
            part = jnp.where(col >= columns - 2, 0.0, part)
        raw += part
    k.bend[...] = jnp.tanh(raw)
    save(k.bend, k.bend_out)

    halo1_far.finish()
    r2.start()
    d1b.pump()
    for part in (0, 2):
        at = slice(part * pixels, (part + 1) * pixels)
        k.ext1_t[:, at] = mm_nt(k.ident[...], k.ext1[at, :]).astype(bf)
    save(k.ext1, k.ext1_out)
    d1a.finish()
    d1b.finish()
    save(k.d1_all, k.d1_all_out)
    k.spread1[...] = jnp.zeros((pixels, mid), f32)

    def tap_step(tap, carry):
        i, j = lax.div(tap, 3), lax.rem(tap, 3)
        lane = iota((1, pixels), 1)
        row = (lax.div(lane, columns) + 6 + 2 * i).astype(f32) + REACH * k.bend[pl.ds(tap, 1), :]
        across = (lax.rem(lane, columns) - 2 + 2 * j).astype(f32) + REACH * k.bend[pl.ds(tap + 16, 1), :]
        k.col_weight[...] = cell_weights(across, iota((columns, pixels), 0).astype(f32))
        base = jnp.floor(row)
        upper = smooth_rise(row - base)
        for r in range(3 * geo.height):
            weight = jnp.where(base == r, 1.0 - upper, jnp.where(base == r - 1, upper, 0.0))
            k.cells[r * columns : (r + 1) * columns, :] = (k.col_weight[...] * weight).astype(bf)
        k.cols1_t[tap] = mm(k.ext1_t[...], k.cells[...]).astype(bf)
        cols = mm_nt(k.ident[:pixels, :pixels], k.cols1_t[tap]).astype(bf)
        k.spread1[...] += mm(cols, k.d1_all[tap])
        return carry

    lax.fori_loop(0, 9, tap_step, 0)
    save(k.cols1_t, k.cols1_t_out)
    task2 = all_sum(False, 1)
    task2.put(slim, *moments(k.spread1, slim, pixels))
    task2.start()
    d2.start()
    e1.pump()
    task2.relay()
    r2.pump()
    k.totals1b[...] = task2.finish()
    save(k.spread1, k.spread1_out)
    activate(k.spread1, k.totals1b, k.gain1b, k.bias1b, k.act, 0)
    e1.finish()
    save(k.e1_all, k.e1_all_out)
    task3 = all_sum(True, 0)
    expand(k.act, k.e1_all, k.expanded1, task3)
    task3.start()
    r2.pump_again()
    task3.relay()
    d2.pump()
    k.totals1c[...] = task3.finish()
    save(k.expanded1, k.expanded1_out)
    leave(k.expanded1, k.totals1c, k.gain1c, k.bias1c, k.x, k.middle)
    save(k.middle, k.middle_out)

    r2.finish()
    save(k.r1_all, k.r1_all_out)
    save(k.r2_all, k.r2_all_out)
    save(k.o1_all, k.o1_all_out)
    reduce_matmul(k.middle, k.r2_all, k.reduced2)
    task4 = all_sum(False, 2)
    task4.put(slim, *moments(k.reduced2, slim, pixels))
    task4.start()
    e2.start()
    task4.relay()
    k.totals2a[...] = task4.finish()
    d2.pump_again()
    save(k.reduced2, k.reduced2_out)
    activate(k.reduced2, k.totals2a, k.gain2a, k.bias2a, k.ext2, rim)
    halo2 = Halo(
        p,
        (k.ext2.at[rim : 2 * rim], k.ext2.at[pixels + rim :]),
        (k.ext2.at[pixels : pixels + rim], k.ext2.at[:rim]),
        k.halo_sem.at[1],
    )
    halo2.start()

    @pl.when(s == 0)
    def _():
        k.ext2[:rim, :] = jnp.zeros((rim, mid), bf)

    @pl.when(s == p.n_sp - 1)
    def _():
        k.ext2[pixels + rim :, :] = jnp.zeros((rim, mid), bf)

    e2.pump()
    d2.finish()
    save(k.d2_all, k.d2_all_out)
    halo2.finish()

    def shift_row(r, carry):
        at = pl.ds(pl.multiple_of(r * columns, columns), columns)
        v = k.ext2[at, :].astype(f32)
        k.moved[0, at, :] = column_shift(v, 0, columns).astype(bf)
        k.moved[1, at, :] = v.astype(bf)
        k.moved[2, at, :] = column_shift(v, 2, columns).astype(bf)
        return carry

    lax.fori_loop(0, geo.height + 4, shift_row, 0)
    save(k.moved, k.moved_out)
    k.spread2[...] = jnp.zeros((pixels, mid), f32)

    def plain_step(tap, carry):
        i, j = lax.div(tap, 3), lax.rem(tap, 3)
        cols = k.moved[j, pl.ds(pl.multiple_of(i * rim, rim), pixels), :]
        k.spread2[...] += mm(cols, k.d2_all[tap])
        return carry

    lax.fori_loop(0, 9, plain_step, 0)
    task5 = all_sum(False, 3)
    task5.put(slim, *moments(k.spread2, slim, pixels))
    run_sum(task5, k.totals2b, e2.pump_again)
    save(k.spread2, k.spread2_out)
    activate(k.spread2, k.totals2b, k.gain2b, k.bias2b, k.act, 0)
    e2.finish()
    save(k.e2_all, k.e2_all_out)
    task6 = all_sum(True, 1)
    expand(k.act, k.e2_all, k.expanded2, task6)
    run_sum(task6, k.totals2c)
    save(k.expanded2, k.expanded2_out)
    leave(k.expanded2, k.totals2c, k.gain2c, k.bias2c, k.middle, k.last)
    save(k.last, k.last_out)

    for task in (*r1, o1, d1a, d1b, e1, r2, d2, e2, task1, task2, task3, task4, task5, task6, halo1, halo1_far, halo2):
        task.drain()
    for copy in saves:
        copy.wait()


def run_forward(geo, features, offset_w, shards, norms):
    bf, f32 = jnp.bfloat16, jnp.float32
    n_ch, n_sp, mid, pixels, wr, we = geo.n_ch, geo.n_sp, geo.mid, geo.pixels, geo.wr, geo.we
    ext_rows = 3 * pixels
    rim_rows = pixels + 4 * geo.columns
    near, far = 2 * n_ch, n_sp // 2
    vmem = pl.BlockSpec(memory_space=pltpu.VMEM)
    anywhere = pl.BlockSpec(memory_space=pl.ANY)
    dma = pltpu.SemaphoreType.DMA
    v = pltpu.VMEM
    close = dict(x=features, o1=offset_w, **norms)
    kept = dict(
        r1_all=((n_ch, geo.c_in, wr), bf),
        o1_all=((n_ch, 9 * 32, wr), bf),
        d1_all=((9, mid, mid), bf),
        e1_all=((n_ch, mid, we), bf),
        r2_all=((n_ch, geo.c_in, wr), bf),
        d2_all=((9, mid, mid), bf),
        e2_all=((n_ch, mid, we), bf),
        reduced1=((pixels, mid), f32),
        ext1=((ext_rows, mid), bf),
        bend=((32, pixels), f32),
        cols1_t=((9, mid, pixels), bf),
        spread1=((pixels, mid), f32),
        expanded1=((pixels, geo.c_in), f32),
        middle=((pixels, geo.c_in), bf),
        reduced2=((pixels, mid), f32),
        moved=((3, rim_rows, mid), bf),
        spread2=((pixels, mid), f32),
        expanded2=((pixels, geo.c_in), f32),
        last=((pixels, geo.c_in), bf),
    )
    totals = dict(
        totals1a=(2, mid),
        totals1b=(2, mid),
        totals1c=(2, geo.c_in),
        totals2a=(2, mid),
        totals2b=(2, mid),
        totals2c=(2, geo.c_in),
    )
    scratch = dict(
        ident=v((mid, mid), bf),
        ext1_t=v((mid, ext_rows), bf),
        raw_all=v((9 * 32, 16 * geo.columns), f32),
        col_weight=v((geo.columns, pixels), f32),
        cells=v((ext_rows, pixels), bf),
        act=v((pixels, mid), bf),
        ext2=v((rim_rows, mid), bf),
        slim_one=v((4, near, 2, mid), f32),
        slim_two=v((4, far, 2, mid), f32),
        slim_send=dma((4, near + far)),
        slim_recv_one=dma((4, near)),
        slim_recv_two=dma((4, far)),
        wide_one=v((2, near, 2, geo.c_in), f32),
        wide_two=v((2, far, 2, geo.c_in), f32),
        wide_send=dma((2, near + far)),
        wide_recv_one=dma((2, near)),
        wide_recv_two=dma((2, far)),
        gather_send=dma((5, n_ch)),
        gather_recv=dma((5, n_ch)),
        half_send=dma((7, 2 + 4 * (n_ch // 2 - 1))),
        half_recv=dma((7, 2 * n_ch)),
        o1_own=v((9 * 32, wr), bf),
        window=v((16 * geo.columns, mid), bf),
        halo_sem=dma((3, 4)),
        save_sem=dma((len(kept),)),
    )
    scratch |= {name: v(*what) for name, what in kept.items()}
    out_names = [f"{name}_out" for name in kept]
    results = pl.pallas_call(
        functools.partial(forward_kernel, geo, [*close, *shards, *out_names, *totals, *scratch]),
        out_shape=[jax.ShapeDtypeStruct(*what) for what in kept.values()]
        + [jax.ShapeDtypeStruct(shape, f32) for shape in totals.values()],
        in_specs=[vmem] * len(close) + [anywhere] * len(shards),
        out_specs=[anywhere] * len(kept) + [vmem] * len(totals),
        scratch_shapes=list(scratch.values()),
        compiler_params=pltpu.CompilerParams(
            collective_id=0, has_side_effects=True, vmem_limit_bytes=60 * MIB
        ),
    )(*close.values(), *shards.values())
    return types.SimpleNamespace(**dict(zip([*kept, *totals], results, strict=True)))


class Reduce:
    def __init__(self, place, stage, one, two, three, four, total, done, send, recv, z_first=False):
        self.z_first = z_first
        self.p, self.stage, self.one, self.two, self.three, self.four = place, stage, one, two, three, four
        self.total, self.done = total, done
        self.send, self.recv = send, recv
        self.n_far = place.n_sp // 2
        self.half = stage.shape[2] // 2
        self.chunk = self.half // self.n_far
        self.row = lax.div(place.s, 2)
        self.pair = (place.s + 1 - 2 * place.y, place.c)
        self.mine = stage.at[place.k, place.x]
        self.at_x, self.at_out = 3, 3 + place.n_x
        self.at_back = self.at_out + 2 * self.n_far

    nothing = types.SimpleNamespace(**dict.fromkeys(["s1", "s2", "s3", "s3_add", "s3_send", "s4", "s5", "s6", "freed", "s7_end", "s7"], lambda: None))

    @staticmethod
    def sems(n_sp, n_ch):
        return 3 + n_ch // 2 + 3 * (n_sp // 2)

    def _half(self, ref, y):
        return ref.at[pl.ds(pl.multiple_of(y * self.half, 16), self.half)]

    def _chunk(self, ref, z, y=None):
        y = self.p.y if y is None else y
        return ref.at[pl.ds(pl.multiple_of(y * self.half + z * self.chunk, 16), self.chunk)]

    def _to_sibling(self):
        return remote(self.stage.at[1 - self.p.k], self.one, self.send.at[0], self.recv.at[0], self.p.sibling)

    def _to_x(self, d):
        other = lax.rem(self.p.x + d, self.p.n_x)
        return remote(
            self.stage.at[self.p.k, other],
            self.two.at[self.p.n_x - d - 1],
            self.send.at[self.at_x + d],
            self.recv.at[self.at_x + self.p.n_x - d],
            (self.p.s, 2 * other + self.p.k),
        )

    def _to_pair(self):
        if self.z_first:
            source, there = self._chunk(self.total, self.row, 1 - self.p.y), self.three.at[pl.ds(0, self.chunk)]
        else:
            source, there = self._half(self.total, 1 - self.p.y), self.three
        return remote(source, there, self.send.at[1], self.recv.at[1], self.pair)

    def _from(self, z, h):
        return self.four.at[z, pl.ds(h * self.chunk, self.chunk)]

    def _out(self, d, h):
        other = lax.rem(self.row + d, self.n_far)
        source = self._chunk(self.total, other, h if self.z_first else None)
        n = self.at_out + h * self.n_far
        return remote(source, self._from(self.row, h), self.send.at[n + d], self.recv.at[n + self.row], self.p.far(d))

    def _back(self, d):
        return remote(
            self._chunk(self.done, self.row), self._chunk(self.done, self.row), self.send.at[self.at_back + d], self.recv.at[self.at_back + self.row], self.p.far(d)
        )

    def _pair_back(self, y):
        return remote(self._half(self.done, y), self._half(self.done, y), self.send.at[2], self.recv.at[2], self.pair)

    def _await(self, ref, sem):
        remote(ref, ref, self.send.at[0], sem, self.p.sibling).wait_recv()

    def _add(self, source, start, rows, pieces, out):
        step = max(n for n in (16, 32, 48, 64) if rows % n == 0)

        def one(i, carry):
            at = pl.ds(pl.multiple_of(start + i * step, 16), step)
            there = pl.ds(pl.multiple_of(i * step, 16), step)
            total = source[at, :].astype(jnp.float32)
            for piece in pieces:
                total = total + piece[there, :].astype(jnp.float32)
            out[at, :] = total.astype(jnp.bfloat16)
            return carry

        lax.fori_loop(0, rows // step, one, 0)

    def s1(self):
        self._to_sibling().start()

    def s2(self):
        self._await(self.one, self.recv.at[0])
        rows = self.stage.shape[2]
        step = max(n for n in (16, 32, 48, 64) if rows % n == 0)
        for x in range(self.p.n_x):

            def one(i, carry):
                at = pl.ds(pl.multiple_of(i * step, 16), step)
                total = self.stage[self.p.k, x, at, :].astype(jnp.float32) + self.one[x, at, :].astype(jnp.float32)
                self.stage[self.p.k, x, at, :] = total.astype(jnp.bfloat16)
                return carry

            lax.fori_loop(0, rows // step, one, 0)
        for d in range(1, self.p.n_x):
            self._to_x(d).start()

    def s3_add(self):
        for d in range(1, self.p.n_x):
            self._await(self.two.at[d - 1], self.recv.at[self.at_x + d])
        pieces = [self.two.at[d - 1] for d in range(1, self.p.n_x)]
        self._add(self.mine, 0, self.stage.shape[2], pieces, self.total)
        self._to_sibling().wait_send()
        for d in range(1, self.p.n_x):
            self._to_x(d).wait_send()

    def _start_out(self):
        for d in range(1, self.n_far):
            for h in range(1 + self.z_first):
                self._out(d, h).start()

    def _add_far(self, h, y, out):
        others = [lax.rem(self.row + d, self.n_far) for d in range(1, self.n_far)]
        for other in others:
            self._await(self._from(other, h), self.recv.at[self.at_out + h * self.n_far + other])
        start = y * self.half + self.row * self.chunk
        self._add(self.total, start, self.chunk, [self._from(other, h) for other in others], out)

    def s3_send(self):
        if self.z_first:
            self._start_out()
        else:
            self._to_pair().start()

    def s3(self):
        self.s3_add()
        self.s3_send()

    def s4(self):
        if self.z_first:
            for h in range(2):
                self._add_far(h, h, self.total)
            self._to_pair().start()
        else:
            self._await(self.three, self.recv.at[1])
            self._add(self.total, self.p.y * self.half, self.half, [self.three], self.total)
            self._start_out()

    def s5(self):
        if self.z_first:
            there = self.three.at[pl.ds(0, self.chunk)]
            self._await(there, self.recv.at[1])
            start = self.p.y * self.half + self.row * self.chunk
            self._add(self.total, start, self.chunk, [there], self.done)
        else:
            self._add_far(0, self.p.y, self.done)
        for d in range(1, self.n_far):
            self._back(d).start()

    def s6(self):
        for d in range(1, self.n_far):
            other = lax.rem(self.row + d, self.n_far)
            self._await(self._chunk(self.done, other), self.recv.at[self.at_back + other])
        self._pair_back(self.p.y).start()

    def freed(self):
        self._to_pair().wait_send()
        for d in range(1, self.n_far):
            for h in range(1 + self.z_first):
                self._out(d, h).wait_send()

    def s7_end(self):
        self._await(self._half(self.done, 1 - self.p.y), self.recv.at[2])
        self._pair_back(self.p.y).wait_send()
        for d in range(1, self.n_far):
            self._back(d).wait_send()

    def s7(self):
        self.freed()
        self.s7_end()


def slope_of(v):
    sigma = sigmoid(v)
    return sigma, sigma * (1.0 + v * (1.0 - sigma))


def backward_kernel(geo, names, *refs):
    k = types.SimpleNamespace(**dict(zip(names, refs, strict=True)))
    p = Place(geo.n_sp, geo.n_ch)
    s, pixels, columns, mid = p.s, geo.pixels, geo.columns, geo.mid
    n_ch, wr, we, total = p.n_ch, geo.wr, geo.we, geo.pixel_total
    bf, f32 = jnp.bfloat16, jnp.float32
    rim = 2 * columns
    slim = pl.ds(0, mid)
    count = [0, 0, 0]

    cells = k.moved.at[pl.ds(0, 3 * pixels), pl.ds(0, pixels)]
    placed = k.third.at[pl.ds(0, 9 * 32), pl.ds(2 * mid, 16 * columns)]
    placed_t = k.moved.at[pl.ds(0, 16 * columns)]
    cols_grad_t = k.moved.at[pl.ds(3 * pixels, mid), pl.ds(0, pixels)]

    def load(src, dst):
        copy = pltpu.make_async_copy(src, dst, k.load_sem.at[count[0]])
        count[0] += 1
        copy.start()
        return copy

    def write_out(src, dst):
        copy = pltpu.make_async_copy(src, dst, k.out_sem.at[count[1]])
        count[1] += 1
        copy.start()
        return copy

    def reduction(*buffers, z_first=False):
        i = count[2]
        count[2] += 1
        return Reduce(p, *buffers, k.reduce_send.at[i], k.reduce_recv.at[i], z_first)

    def for_e():
        return reduction(k.stage_e, k.one_e, k.two_e, k.three_e, k.four_e, k.total_e, k.done_e)

    d_parts, tap_count = geo.d_parts, 9 // geo.d_parts

    def for_d(four, done, *z_first):
        buffers = (k.stage_d, k.one_d, k.two_d, k.three_d, four, k.total_d, done)
        parts = [reduction(*[b.at[i] for b in buffers], z_first=i in z_first and d_parts == 3) for i in range(d_parts)]
        return parts if d_parts == 3 else [Reduce.nothing, Reduce.nothing, parts[0]]

    def for_r(done):
        buffers = (k.stage_r, k.one_r, k.two_r, k.three_r, k.four_r, k.total_r, done)
        return [reduction(*[buffer.at[i] for buffer in buffers]) for i in range(4)]

    def all_sum(wide, i):
        if wide:
            parts = (k.wide_one, k.wide_two, k.wide_send, k.wide_recv_one, k.wide_recv_two)
        else:
            parts = (k.slim_one, k.slim_two, k.slim_send, k.slim_recv_one, k.slim_recv_two)
        return AllSum(p, *[part.at[i] for part in parts])

    def place_of(c):
        return c % 2, c // 2

    def norm_of(totals, lanes):
        return center_inverse(totals[0:1, lanes], totals[1:2, lanes], total)

    def block_end(upstream, totals, gain, bias, task):
        for start in range(0, geo.c_in, 512):
            lanes = pl.ds(start, 512)
            center, inverse = norm_of(totals, lanes)
            gain_row, bias_row = gain[:, lanes], bias[:, lanes]

            def body(at, carry):
                normed = (k.expanded[at, lanes] - center) * inverse
                joined = gain_row * normed + bias_row + k.inputs[at, lanes].astype(f32)
                grad = upstream(at, lanes) * slope_of(joined)[1]
                k.grad[at, lanes] = grad
                return carry[0] + fold(grad), carry[1] + fold(grad * normed)

            zero = jnp.zeros((8, 512), f32)
            a, b = over_rows(pixels, 16, body, (zero, zero))
            task.put(lanes, jnp.sum(a, axis=0, keepdims=True), jnp.sum(b, axis=0, keepdims=True))

    def third_norm(totals, grads, gain):
        for start in range(0, geo.c_in, 512):
            lanes = pl.ds(start, 512)
            center, inverse = norm_of(totals, lanes)
            scale = gain[:, lanes] * inverse
            bias_mean = grads[0:1, lanes] / total
            gain_mean = grads[1:2, lanes] / total

            def body(at, carry):
                normed = (k.expanded[at, lanes] - center) * inverse
                inner = k.grad[at, lanes] - bias_mean - normed * gain_mean
                k.third[at, lanes] = (scale * inner).astype(bf)
                return carry

            over_rows(pixels, 16, body, 0)

    def act_grad(values, totals, gain, bias, act, task):
        center, inverse = norm_of(totals, slim)
        gain_row, bias_row = gain[...], bias[...]

        def body(at, carry):
            normed = (values[at, :] - center) * inverse
            pre = gain_row * normed + bias_row
            sigma, slope = slope_of(pre)
            if act is not None:
                act[at, :] = (pre * sigma).astype(bf)
            grad = k.flow[at, :] * slope
            k.flow[at, :] = grad
            return carry[0] + fold(grad), carry[1] + fold(grad * normed)

        zero = jnp.zeros((8, mid), f32)
        a, b = over_rows(pixels, 16, body, (zero, zero))
        task.put(slim, jnp.sum(a, axis=0, keepdims=True), jnp.sum(b, axis=0, keepdims=True))

    def norm_grad(values, totals, grads, gain, out):
        center, inverse = norm_of(totals, slim)
        scale = gain[...] * inverse
        bias_mean = grads[0:1, :] / total
        gain_mean = grads[1:2, :] / total

        def body(at, carry):
            normed = (values[at, :] - center) * inverse
            out[at, :] = (scale * (k.flow[at, :] - bias_mean - normed * gain_mean)).astype(bf)
            return carry

        over_rows(pixels, 16, body, 0)

    def through_expand():
        for c in range(n_ch):
            part = mm_nt(k.third[:, c * we : (c + 1) * we], k.e[c])
            if c == 0:
                k.flow[...] = part
            else:
                k.flow[...] += part

    def expand_weights():
        k.act_t[...] = mm_nt(k.ident[...], k.low1[...]).astype(bf)
        for c in range(n_ch):
            k.stage_e[place_of(c)] = mm(k.act_t[...], k.third[:, c * we : (c + 1) * we]).astype(bf)

    def stage_tap(tap, cols_t):
        product = mm(cols_t, k.low2[...])
        part, inner = lax.div(tap, tap_count), lax.rem(tap, tap_count)
        for c in range(n_ch):
            for q in range(mid // 128):
                at = pl.ds(pl.multiple_of(inner * wr + q * tap_count * wr, 16), wr)
                piece = product[c * wr : (c + 1) * wr, q * 128 : (q + 1) * 128]
                k.stage_d[(part, *place_of(c), at)] = piece.astype(bf)

    def through_reduce():
        for start in range(0, geo.c_in, 512):
            rows = pl.ds(start, 512)
            for c in range(n_ch):
                k.grad[:, start : start + 512] += mm_nt(k.low1[:, c * wr : (c + 1) * wr], k.r[c, rows, :])

    def reduce_weights(work):
        for i, start in enumerate(range(0, geo.c_in, 512)):
            inputs_t = mm_nt(k.ident[...], k.inputs[:, start : start + 512]).astype(bf)
            product = mm(inputs_t, k.low1[...])
            for c in range(n_ch):
                k.stage_r[(i, *place_of(c))] = product[:, c * wr : (c + 1) * wr].astype(bf)
            work[i].s1()

    def deliver(task, out):
        return write_out(task.done.at[pl.ds(0, out.shape[0])], out)

    def deliver_d(parts, out):
        return [deliver(task, out.at[i]) for i, task in enumerate(parts[-d_parts:])]

    def deliver_r(parts, out):
        return [deliver(task, out.at[i]) for i, task in enumerate(parts)]

    def wait_all(copies):
        for copy in copies:
            copy.wait()

    def fetch(tap, slot):
        return pltpu.make_async_copy(k.cols1.at[tap], k.cols_t.at[slot], k.fetch_sem.at[slot])

    def sampled_tap(tap, carry):
        slot = lax.rem(tap, 2)

        @pl.when(tap < 8)
        def _():
            fetch(tap + 1, 1 - slot).start()

        fetch(tap, slot).wait()
        stage_tap(tap, k.cols_t[slot])
        return carry

    def rims_of(up, up_at, down, down_at, rows, sems):
        up_to, down_to = pl.ds(up_at, rows), pl.ds(down_at, rows)
        halo = Halo(
            p,
            (k.third.at[up_to, pl.ds(0, mid)], k.rim_recv.at[1, up_to]),
            (k.third.at[down_to, pl.ds(mid, mid)], k.rim_recv.at[0, down_to]),
            sems,
        )
        k.third[up_at : up_at + rows, :mid] = k.spread_grad[up : up + rows, :].astype(bf)
        k.third[down_at : down_at + rows, mid : 2 * mid] = k.spread_grad[down : down + rows, :].astype(bf)
        return halo

    def add_rims(rows):
        @pl.when(s > 0)
        def _():
            k.flow[:rows, :] += k.rim_recv[0, :rows, :].astype(f32)

        @pl.when(s < p.n_sp - 1)
        def _():
            k.flow[pixels - rows :, :] += k.rim_recv[1, :rows, :].astype(f32)

    expanded2 = load(k.expanded2, k.expanded)
    middle = load(k.middle, k.inputs)
    cotangent = load(k.cotangent, k.third)
    e2 = load(k.e2, k.e)
    spread2 = load(k.spread2, k.spread)
    d2 = load(k.d2, k.d)
    moved2 = load(k.moved_in, k.moved)
    reduced2 = load(k.reduced2, k.reduced)
    r2 = load(k.r2, k.r)
    ext1 = load(k.ext1_in, k.ext1)
    o1 = load(k.o1_in, k.o1)
    p.barrier()
    set_identity(k.ident)
    stages = [(k.stage_o, 9 * 32)] + [(k.stage_d.at[i], tap_count * wr * mid // 128) for i in range(d_parts)]
    for stage, rows in stages:
        if stage.shape[2] > rows:
            for q in range(n_ch):
                spare = (stage.shape[2] - rows, stage.shape[3])
                stage[(*place_of(q), pl.ds(rows, spare[0]))] = jnp.zeros(spare, bf)

    expanded2.wait()
    middle.wait()
    cotangent.wait()
    sum2c = all_sum(True, 0)
    counts = k.counts[...].astype(f32)
    mine = jnp.where(iota(counts.shape, 1) == p.c, counts, 0.0)
    box = jnp.sum(mine, axis=1, keepdims=True) * counts.shape[1] / jnp.sum(counts, axis=1, keepdims=True)
    block_end(lambda at, lanes: k.third[at, lanes].astype(f32) * box, k.totals2c, k.gain2c, k.bias2c, sum2c)
    sum2c.start()
    e2.wait()
    spread2.wait()
    d2.wait()
    moved2.wait()
    reduced2.wait()
    r2.wait()
    sum2c.relay()
    k.grads2c[...] = sum2c.finish()
    third_norm(k.totals2c, k.grads2c, k.gain2c)
    expanded1 = load(k.expanded1, k.expanded)
    through_expand()
    e1 = load(k.e1, k.e)
    sum2b = all_sum(False, 0)
    act_grad(k.spread, k.totals2b, k.gain2b, k.bias2b, k.low1, sum2b)
    sum2b.start()
    expand_weights()
    work_e2 = for_e()
    work_e2.s1()
    sum2b.relay()
    k.grads2b[...] = sum2b.finish()
    norm_grad(k.spread, k.totals2b, k.grads2b, k.gain2b, k.low2)
    spread1 = load(k.spread1, k.spread)
    work_e2.s2()

    area = pixels + 2 * rim
    k.spread_grad[:area, :] = jnp.zeros((area, mid), f32)
    for j in range(3):
        k.spread_grad[area : 2 * area, :] = jnp.zeros((area, mid), f32)

        def row_step(i, carry):
            at = pl.ds(pl.multiple_of(area + i * rim, 16), pixels)
            k.spread_grad[at, :] += mm_nt(k.low2[...], k.d[3 * i + j])
            return carry

        lax.fori_loop(0, 3, row_step, 0)

        def shift_back(r, carry):
            at = pl.ds(pl.multiple_of(r * columns, 16), columns)
            there = pl.ds(pl.multiple_of(area + r * columns, 16), columns)
            k.spread_grad[at, :] += column_shift(k.spread_grad[there, :], 2 - j, columns)
            return carry

        lax.fori_loop(0, geo.height + 4, shift_back, 0)
    d1 = load(k.d1, k.d)
    halo2 = rims_of(0, 0, pixels + rim, 0, rim, k.halo_sem.at[0])
    halo2.start()
    k.flow[...] = k.spread_grad[rim : pixels + rim, :]

    def plain_tap(tap, carry):
        first = lax.rem(tap, 3) * (pixels + 2 * rim) + lax.div(tap, 3) * rim
        cols = k.moved[pl.ds(pl.multiple_of(first, 16), pixels), :]
        stage_tap(tap, mm_nt(k.ident[...], cols).astype(bf))
        return carry

    work_d2 = for_d(k.four_d2, k.done_d2)
    for i in range(3):
        lax.fori_loop(3 * i, 3 * i + 3, plain_tap, 0)
        work_d2[i].s1()
    halo2.finish()
    add_rims(rim)
    sum2a = all_sum(False, 1)
    act_grad(k.reduced, k.totals2a, k.gain2a, k.bias2a, None, sum2a)
    sum2a.start()
    work_d2[0].s2()
    work_e2.s3()
    work_d2[1].s2()
    sum2a.relay()
    k.grads2a[...] = sum2a.finish()
    norm_grad(k.reduced, k.totals2a, k.grads2a, k.gain2a, k.low1)
    reduced1 = load(k.reduced1, k.reduced)
    through_reduce()
    r1 = load(k.r1, k.r)
    work_e2.s4()
    work_r2 = for_r(k.done_r2)
    reduce_weights(work_r2)
    features = load(k.features, k.inputs)

    expanded1.wait()
    features.wait()
    sum1c = all_sum(True, 1)
    block_end(lambda at, lanes: k.grad[at, lanes], k.totals1c, k.gain1c, k.bias1c, sum1c)
    sum1c.start()
    work_d2[2].s2()
    work_r2[0].s2()
    work_r2[1].s2()
    work_d2[0].s3()
    work_d2[1].s3()
    e1.wait()
    spread1.wait()
    d1.wait()
    reduced1.wait()
    r1.wait()
    ext1.wait()
    o1.wait()
    sum1c.relay()
    k.grads1c[...] = sum1c.finish()
    work_e2.s5()
    work_d2[0].s4()
    halo2.drain()
    third_norm(k.totals1c, k.grads1c, k.gain1c)
    through_expand()
    sum1b = all_sum(False, 2)
    act_grad(k.spread, k.totals1b, k.gain1b, k.bias1b, k.low1, sum1b)
    work_d2[2].s3_add()
    sum1b.start()
    work_r2[2].s2()
    work_r2[3].s2()
    work_e2.s6()
    work_d2[2].s3_send()
    expand_weights()
    work_r2[0].s3()
    work_r2[1].s3()
    work_e1 = for_e()
    sum1b.relay()
    work_e1.s1()
    work_e2.s7()
    e2_copy = deliver(work_e2, k.grad_e2)
    fetch(0, 0).start()
    k.grads1b[...] = sum1b.finish()
    work_d2[1].s4()
    work_d2[0].s5()
    norm_grad(k.spread, k.totals1b, k.grads1b, k.gain1b, k.low2)
    work_e1.s2()
    work_d1 = for_d(k.four_d, k.done_d, 0)
    for i in range(3):
        lax.fori_loop(3 * i, 3 * i + 3, sampled_tap, 0)
        work_d1[i].s1()

    k.spread_grad[...] = jnp.zeros((3 * pixels, mid), f32)
    k.raw_grad[...] = jnp.zeros((32, pixels), f32)

    def tap_step(tap, carry):
        @pl.when(tap == 0)
        def _():
            work_d1[0].s2()
            work_d2[2].s4()
            work_d2[1].s5()
            work_d2[0].s6()

        @pl.when(tap == 3)
        def _():
            work_d1[1].s2()
            work_r2[0].s4()
            work_r2[1].s4()
            work_r2[2].s3()
            work_r2[3].s3()
            work_d2[2].s5()

        @pl.when(tap == 6)
        def _():
            work_e1.s3()
            work_r2[2].s4()
            work_r2[3].s4()

        i, j = lax.div(tap, 3), lax.rem(tap, 3)
        lane = iota((1, pixels), 1)
        row = (lax.div(lane, columns) + 6 + 2 * i).astype(f32) + REACH * k.bend[pl.ds(tap, 1), :]
        across = (lax.rem(lane, columns) - 2 + 2 * j).astype(f32) + REACH * k.bend[pl.ds(tap + 16, 1), :]
        cell = iota((columns, pixels), 0).astype(f32)
        k.col_weight[...] = cell_weights(across, cell)
        row_base = jnp.floor(row)
        row_part = row - row_base
        row_upper = smooth_rise(row_part)
        row_rate = 6.0 * row_part * (1.0 - row_part)
        for r in range(3 * geo.height):
            weight = jnp.where(row_base == r, 1.0 - row_upper, jnp.where(row_base == r - 1, row_upper, 0.0))
            cells[r * columns : (r + 1) * columns, :] = (k.col_weight[...] * weight).astype(bf)
        cols_grad_t[...] = mm_nt(k.d[tap], k.low2[...]).astype(bf)
        k.spread_grad[...] += mm_nt(cells[...], cols_grad_t[...])
        for part in range(3):
            rows_at = slice(part * pixels, (part + 1) * pixels)
            k.expanded[:, 512 * part : 512 * part + pixels] = mm(k.ext1[rows_at, :], cols_grad_t[...])
        for start in range(0, pixels, 128):
            lanes = slice(start, start + 128)
            base, upper, rate = row_base[:, lanes], row_upper[:, lanes], row_rate[:, lanes]
            along = jnp.zeros((columns, 128), f32)
            down = jnp.zeros((columns, 128), f32)
            for r in range(3 * geo.height):
                row_at, col_at = r % geo.height * columns, r // geo.height * 512 + start
                match = k.expanded[row_at : row_at + columns, col_at : col_at + 128]
                at, after = base == r, base == r - 1
                along += match * jnp.where(at, 1.0 - upper, jnp.where(after, upper, 0.0))
                down += match * jnp.where(at, -rate, jnp.where(after, rate, 0.0))
            place = across[:, lanes]
            col_base = jnp.floor(place)
            col_part = place - col_base
            col_rate = 6.0 * col_part * (1.0 - col_part)
            cell_at = cell[:, lanes]
            col_slope = jnp.where(cell_at == col_base, -col_rate, jnp.where(cell_at == col_base + 1.0, col_rate, 0.0))
            here = iota((16, 128), 0) == tap
            by_row = jnp.sum(down * k.col_weight[:, lanes], axis=0, keepdims=True)
            by_col = jnp.sum(along * col_slope, axis=0, keepdims=True)
            k.raw_grad[:16, lanes] = jnp.where(here, by_row, k.raw_grad[:16, lanes])
            k.raw_grad[16:, lanes] = jnp.where(here, by_col, k.raw_grad[16:, lanes])
        return carry

    lax.fori_loop(0, 9, tap_step, 0)
    rest = pixels - rim
    halo1_far = rims_of(0, 0, 2 * pixels + rim, rim, rest, k.halo_sem.at[2])
    halo1_far.start()

    window = slice(6 * columns, 18 * columns)
    inner = slice(2 * columns, 14 * columns)
    bend = k.bend[...]
    raw = k.raw_grad[...] * (REACH * (1.0 - bend * bend))
    col = lax.rem(iota((32, pixels), 1), columns)
    for tap in range(9):
        i, j = tap // 3, tap % 3
        offset = (2 + 2 * i) * columns + 2 * (j - 1)
        part = raw
        if j == 0:
            part = jnp.where(col < 2, 0.0, part)
        if j == 2:
            part = jnp.where(col >= columns - 2, 0.0, part)
        part = jnp.concatenate([part, jnp.zeros((32, 16 * columns - pixels), f32)], axis=1)
        placed[32 * tap : 32 * tap + 32, :] = pltpu.roll(part, offset, 1).astype(bf)
    for start in range(0, 16 * columns, 256):
        placed_t[start : start + 256, : 9 * 32] = mm_nt(k.ident[:256, :256], placed[:, start : start + 256]).astype(bf)
    for c in range(n_ch):
        k.spread_grad[window, c * wr : (c + 1) * wr] += mm(placed_t[inner, : 9 * 32], k.o1[c])
    halo1 = rims_of(rest, rest, 2 * pixels, 0, rim, k.halo_sem.at[1])
    halo1.start()
    k.flow[...] = k.spread_grad[pixels : 2 * pixels, :]
    product = mm(placed[...], k.ext1[4 * columns : 20 * columns, :])
    for c in range(n_ch):
        k.stage_o[(*place_of(c), pl.ds(0, 9 * 32))] = product[:, c * wr : (c + 1) * wr].astype(bf)
    work_o1 = reduction(k.stage_o, k.one_o, k.two_o, k.three_o, k.four_o, k.total_o, k.done_o)
    work_o1.s1()

    e2_copy.wait()
    work_e1.s4()
    work_d1[2].s2()
    for part in work_d2:
        part.freed()
    work_d1[0].s3()
    halo1_far.finish()
    halo1.finish()
    add_rims(pixels)
    sum1a = all_sum(False, 3)
    act_grad(k.reduced, k.totals1a, k.gain1a, k.bias1a, None, sum1a)
    sum1a.start()
    work_d2[1].s6()
    work_d2[2].s6()
    work_o1.s2()
    sum1a.relay()
    work_d1[1].s3()
    work_d1[0].s4()
    k.grads1a[...] = sum1a.finish()
    work_e1.s5()
    work_d1[1].s4()
    for part in work_r2:
        part.s5()
    norm_grad(k.reduced, k.totals1a, k.grads1a, k.gain1a, k.low1)
    work_r1 = for_r(k.done_r)
    reduce_weights(work_r1)
    for part in work_r1:
        part.s2()
    work_d1[2].s3()
    through_reduce()
    d_features = write_out(k.grad, k.d_features)
    for part in work_d2:
        part.s7_end()
    d2_copies = deliver_d(work_d2, k.grad_d2)
    work_o1.s3()
    work_e1.s6()
    for part in work_r2:
        part.freed()
    work_r1[0].s3()
    work_d1[0].s5()
    work_d1[1].s5()
    work_r2[0].s6()
    work_r2[1].s6()
    work_r1[1].s3()
    work_r1[0].s4()
    work_d1[2].s4()
    work_r2[2].s6()
    work_r2[3].s6()
    work_r1[2].s3()
    work_r1[1].s4()
    work_o1.s4()
    for part in work_r2:
        part.s7_end()
    r2_copies = deliver_r(work_r2, k.grad_r2)
    work_r1[0].s5()
    work_r1[3].s3()
    work_d1[0].s6()
    work_r1[2].s4()
    work_r1[1].s5()
    work_d1[2].s5()
    work_r1[0].s6()
    work_r1[3].s4()
    work_d1[1].s6()
    work_o1.s5()
    work_r1[2].s5()
    work_r1[1].s6()
    work_e1.s7()
    e1_copy = deliver(work_e1, k.grad_e1)
    work_r1[3].s5()
    work_r1[2].s6()
    work_o1.s6()
    work_d1[2].s6()
    work_r1[3].s6()
    for part in work_d1:
        part.s7()
    d1_copies = deliver_d(work_d1, k.grad_d1)
    work_o1.s7()
    o1_copy = deliver(work_o1, k.grad_o1)
    for part in work_r1:
        part.s7()
    wait_all(deliver_r(work_r1, k.grad_r1) + d1_copies + d2_copies + r2_copies)
    e1_copy.wait()
    o1_copy.wait()
    for task in (sum2c, sum2b, sum2a, sum1c, sum1b, sum1a, halo1, halo1_far):
        task.drain()
    d_features.wait()


def run_backward(geo, kept, features, cotangent, counts, norms):
    bf, f32 = jnp.bfloat16, jnp.float32
    n_ch, n_sp, mid, pixels, wr, we = geo.n_ch, geo.n_sp, geo.mid, geo.pixels, geo.wr, geo.we
    n_x, near, far = n_ch // 2, 2 * n_ch, n_sp // 2
    columns, c_in = geo.columns, geo.c_in
    rim = 2 * columns
    vmem = pl.BlockSpec(memory_space=pltpu.VMEM)
    anywhere = pl.BlockSpec(memory_space=pl.ANY)
    far_away = dict(
        features=features,
        cotangent=cotangent,
        expanded2=kept.expanded2,
        middle=kept.middle,
        e2=kept.e2_all,
        spread2=kept.spread2,
        d2=kept.d2_all,
        moved_in=kept.moved.reshape(-1, mid),
        reduced2=kept.reduced2,
        r2=kept.r2_all,
        expanded1=kept.expanded1,
        e1=kept.e1_all,
        spread1=kept.spread1,
        d1=kept.d1_all,
        cols1=kept.cols1_t,
        ext1_in=kept.ext1,
        reduced1=kept.reduced1,
        r1=kept.r1_all,
        o1_in=kept.o1_all,
    )
    close = dict(
        bend=kept.bend,
        counts=counts,
        totals1a=kept.totals1a,
        totals1b=kept.totals1b,
        totals1c=kept.totals1c,
        totals2a=kept.totals2a,
        totals2b=kept.totals2b,
        totals2c=kept.totals2c,
        **norms,
    )
    grads = dict(
        grad_e2=((mid, we), bf, anywhere),
        grad_d2=((geo.d_parts, 9 // geo.d_parts * wr * 4, 128), bf, anywhere),
        grad_r2=((4, 512, wr), bf, anywhere),
        grad_e1=((mid, we), bf, anywhere),
        grad_d1=((geo.d_parts, 9 // geo.d_parts * wr * 4, 128), bf, anywhere),
        grad_r1=((4, 512, wr), bf, anywhere),
        grad_o1=((9 * 32, wr), bf, anywhere),
        d_features=((pixels, c_in), f32, anywhere),
        grads2c=((2, c_in), f32, vmem),
        grads2b=((2, mid), f32, vmem),
        grads2a=((2, mid), f32, vmem),
        grads1c=((2, c_in), f32, vmem),
        grads1b=((2, mid), f32, vmem),
        grads1a=((2, mid), f32, vmem),
    )
    dma = pltpu.SemaphoreType.DMA
    v = pltpu.VMEM
    scratch = dict(
        e=v((n_ch, mid, we), bf),
        d=v((9, mid, mid), bf),
        r=v((n_ch, c_in, wr), bf),
        o1=v((n_ch, 9 * 32, wr), bf),
        expanded=v((pixels, c_in), f32),
        grad=v((pixels, c_in), f32),
        inputs=v((pixels, c_in), bf),
        third=v((pixels, c_in), bf),
        spread=v((pixels, mid), f32),
        reduced=v((pixels, mid), f32),
        flow=v((pixels, mid), f32),
        act_t=v((mid, pixels), bf),
        low1=v((pixels, mid), bf),
        low2=v((pixels, mid), bf),
        moved=v((3 * (pixels + 2 * rim), mid), bf),
        ext1=v((3 * pixels, mid), bf),
        cols_t=v((2, mid, pixels), bf),
        col_weight=v((columns, pixels), f32),
        spread_grad=v((3 * pixels, mid), f32),
        raw_grad=v((32, pixels), f32),
        ident=v((mid, mid), bf),
        rim_recv=v((2, pixels, mid), bf),
        slim_one=v((4, near, 2, mid), f32),
        slim_two=v((4, far, 2, mid), f32),
        slim_send=dma((4, near + far)),
        slim_recv_one=dma((4, near)),
        slim_recv_two=dma((4, far)),
        wide_one=v((2, near, 2, c_in), f32),
        wide_two=v((2, far, 2, c_in), f32),
        wide_send=dma((2, near + far)),
        wide_recv_one=dma((2, near)),
        wide_recv_two=dma((2, far)),
        halo_sem=dma((3, 4)),
        load_sem=dma((20,)),
        out_sem=dma((24,)),
        fetch_sem=dma((2,)),
        reduce_send=dma((17, Reduce.sems(n_sp, n_ch))),
        reduce_recv=dma((17, Reduce.sems(n_sp, n_ch))),
    )

    def staging(rows, lanes, *parts, both=1):
        return (
            v((*parts, 2, n_x, rows, lanes), bf),
            v((*parts, n_x, rows, lanes), bf),
            v((*parts, n_x - 1, rows, lanes), bf),
            v((*parts, rows // 2, lanes), bf),
            v((*parts, far, both * rows // n_sp, lanes), bf),
            v((*parts, rows, lanes), bf),
            v((*parts, rows, lanes), bf),
        )

    def padded(rows):
        return -(-rows // (32 * far)) * 32 * far

    d_rows = padded(9 // geo.d_parts * wr * mid // 128)
    e, d, r, o = staging(mid, we), staging(d_rows, 128, geo.d_parts, both=2 if geo.d_parts == 3 else 1), staging(512, wr, 4), staging(padded(9 * 32), wr)
    scratch |= dict(stage_e=e[0], one_e=e[1], two_e=e[2], three_e=e[3], four_e=e[4], total_e=e[5], done_e=e[6])
    scratch |= dict(stage_d=d[0], one_d=d[1], two_d=d[2], three_d=d[3], four_d=d[4], total_d=d[5], done_d=d[6], done_d2=d[6], four_d2=d[4])
    scratch |= dict(stage_r=r[0], one_r=r[1], two_r=r[2], three_r=r[3], four_r=r[4], total_r=r[5], done_r=r[6], done_r2=r[6])
    scratch |= dict(stage_o=o[0], one_o=o[1], two_o=o[2], three_o=o[3], four_o=o[4], total_o=o[5], done_o=o[6])
    results = pl.pallas_call(
        functools.partial(backward_kernel, geo, [*far_away, *close, *grads, *scratch]),
        out_shape=[jax.ShapeDtypeStruct(shape, dtype) for shape, dtype, _ in grads.values()],
        in_specs=[anywhere] * len(far_away) + [vmem] * len(close),
        out_specs=[spec for _, _, spec in grads.values()],
        scratch_shapes=list(scratch.values()),
        compiler_params=pltpu.CompilerParams(
            collective_id=1, has_side_effects=True, vmem_limit_bytes=63 * MIB
        ),
    )(*far_away.values(), *close.values())
    return types.SimpleNamespace(**dict(zip(grads, results, strict=True)))


def finish_kernel(geo, names, *refs):
    k = types.SimpleNamespace(**dict(zip(names, refs, strict=True)))
    f32 = jnp.float32
    wr = geo.wr
    for source, out in ((k.e2, k.e2_out), (k.e1, k.e1_out), (k.d_features, k.d_features_out), (k.last, k.last_out)):
        out[...] = source[...].astype(out.dtype)
    for source, out in ((k.r2, k.r2_out), (k.r1, k.r1_out)):
        out[...] = source[0].astype(f32)
    for source, out in ((k.d2, k.d2_out), (k.d1, k.d1_out)):
        rows = source.shape[2]
        for part in range(source.shape[0]):
            out[part * rows : (part + 1) * rows, :] = source[part, 0].astype(f32)

    @pl.when(pl.program_id(0) == 0)
    def _():
        row, offset = iota((18, 32), 1), iota((18, 32), 0)
        chosen = (lax.rem(row, 16) == lax.div(offset, 2)) & (lax.div(row, 16) == lax.rem(offset, 2))
        chosen = jnp.where(chosen, 1.0, 0.0).astype(jnp.bfloat16)
        for tap in range(9):
            part = k.o1[32 * tap : 32 * tap + 32, :]
            k.o1_out[tap] = mm(chosen, part)
        vectors = (
            (k.sums1a, k.gain1a, k.bias1a),
            (k.sums1b, k.gain1b, k.bias1b),
            (k.sums1c, k.gain1c, k.bias1c),
            (k.sums2a, k.gain2a, k.bias2a),
            (k.sums2b, k.gain2b, k.bias2b),
            (k.sums2c, k.gain2c, k.bias2c),
        )
        for sums, gain, bias in vectors:
            gain[...] = sums[1:2, :]
            bias[...] = sums[0:1, :]


def run_finish(geo, g, last):
    f32 = jnp.float32
    steps, wr, we, mid, c_in, pixels = 4, geo.wr, geo.we, geo.mid, geo.c_in, geo.pixels
    d_rows = 9 // geo.d_parts * wr

    def rows(height, width):
        return pl.BlockSpec((height // steps, width), lambda i: (i, 0))

    def whole(*shape):
        return pl.BlockSpec(shape, lambda i: (0,) * len(shape))

    d_in = pl.BlockSpec((geo.d_parts, 1, d_rows, 128), lambda i: (0, i, 0, 0))
    r_in = pl.BlockSpec((1, 512, wr), lambda i: (i, 0, 0))
    d_shape = (geo.d_parts, 4, d_rows, 128)
    ins = dict(
        e2=(g.grad_e2, rows(mid, we)),
        d2=(g.grad_d2.reshape(d_shape), d_in),
        r2=(g.grad_r2, r_in),
        e1=(g.grad_e1, rows(mid, we)),
        d1=(g.grad_d1.reshape(d_shape), d_in),
        r1=(g.grad_r1, r_in),
        o1=(g.grad_o1, whole(9 * 32, wr)),
        d_features=(g.d_features, rows(pixels, c_in)),
        last=(last, rows(pixels, c_in)),
        sums1a=(g.grads1a, whole(2, mid)),
        sums1b=(g.grads1b, whole(2, mid)),
        sums1c=(g.grads1c, whole(2, c_in)),
        sums2a=(g.grads2a, whole(2, mid)),
        sums2b=(g.grads2b, whole(2, mid)),
        sums2c=(g.grads2c, whole(2, c_in)),
    )
    slim, wide = ((1, mid), whole(1, mid)), ((1, c_in), whole(1, c_in))
    d_out = ((9 * wr, mid), pl.BlockSpec((9 * wr, 128), lambda i: (0, i)))
    outs = dict(
        e2_out=((mid, we), rows(mid, we)),
        d2_out=d_out,
        r2_out=((c_in, wr), rows(c_in, wr)),
        e1_out=((mid, we), rows(mid, we)),
        d1_out=d_out,
        r1_out=((c_in, wr), rows(c_in, wr)),
        o1_out=((9, 18, wr), whole(9, 18, wr)),
        d_features_out=((pixels, c_in), rows(pixels, c_in)),
        last_out=((pixels, c_in), rows(pixels, c_in)),
        gain1a=slim,
        bias1a=slim,
        gain1b=slim,
        bias1b=slim,
        gain1c=wide,
        bias1c=wide,
        gain2a=slim,
        bias2a=slim,
        gain2b=slim,
        bias2b=slim,
        gain2c=wide,
        bias2c=wide,
    )
    results = pl.pallas_call(
        functools.partial(finish_kernel, geo, [*ins, *outs]),
        grid=(steps,),
        out_shape=[
            jax.ShapeDtypeStruct(shape, last.dtype if name == "last_out" else f32) for name, (shape, _) in outs.items()
        ],
        in_specs=[spec for _, spec in ins.values()],
        out_specs=[spec for _, spec in outs.values()],
        compiler_params=pltpu.CompilerParams(vmem_limit_bytes=60 * MIB),
    )(*[array for array, _ in ins.values()])
    return types.SimpleNamespace(**dict(zip(outs, results, strict=True)))


def per_device(
    features,
    box_counts,
    b1_w_reduce,
    b1_gain1,
    b1_bias1,
    b1_w_offset,
    b1_w_deform,
    b1_gain2,
    b1_bias2,
    b1_w_expand,
    b1_gain3,
    b1_bias3,
    b2_w_reduce,
    b2_gain1,
    b2_bias1,
    b2_w_spatial,
    b2_gain2,
    b2_bias2,
    b2_w_expand,
    b2_gain3,
    b2_bias3,
    cotangent,
):
    images, height, columns, channels = features.shape
    n_sp, n_ch = lax.axis_size("sp"), lax.axis_size("ch")
    pixels = images * height * columns
    mid, wr = b1_w_deform.shape[2], b1_w_reduce.shape[1]
    geo = types.SimpleNamespace(
        n_sp=n_sp,
        n_ch=n_ch,
        pixels=pixels,
        height=height,
        columns=columns,
        mid=mid,
        c_in=channels,
        wr=wr,
        we=b1_w_expand.shape[1],
        pixel_total=pixels * n_sp * n_ch,
        d_parts=3 if 3 * wr * mid // 128 % (16 * n_sp) == 0 else 1,
    )
    shards = dict(
        r1=b1_w_reduce,
        d1=b1_w_deform,
        e1=b1_w_expand,
        r2=b2_w_reduce,
        d2=b2_w_spatial,
        e2=b2_w_expand,
    )
    norms = dict(
        gain1a=b1_gain1,
        bias1a=b1_bias1,
        gain1b=b1_gain2,
        bias1b=b1_bias2,
        gain1c=b1_gain3,
        bias1c=b1_bias3,
        gain2a=b2_gain1,
        bias2a=b2_bias1,
        gain2b=b2_gain2,
        bias2b=b2_bias2,
        gain2c=b2_gain3,
        bias2c=b2_bias3,
    )
    norms = {name: vector.reshape(1, -1) for name, vector in norms.items()}
    entry = features.reshape(pixels, channels)
    kept = run_forward(geo, entry, jnp.swapaxes(b1_w_offset, 1, 2), shards, norms)
    g = run_backward(geo, kept, entry, cotangent.reshape(pixels, channels), box_counts.reshape(1, -1), norms)
    done = run_finish(geo, g, kept.last)
    return (
        done.last_out.reshape(features.shape),
        done.d_features_out.reshape(features.shape),
        done.r1_out,
        done.gain1a.reshape(mid),
        done.bias1a.reshape(mid),
        jnp.swapaxes(done.o1_out, 1, 2),
        done.d1_out.reshape(9, wr, mid),
        done.gain1b.reshape(mid),
        done.bias1b.reshape(mid),
        done.e1_out,
        done.gain1c.reshape(channels),
        done.bias1c.reshape(channels),
        done.r2_out,
        done.gain2a.reshape(mid),
        done.bias2a.reshape(mid),
        done.d2_out.reshape(9, wr, mid),
        done.gain2b.reshape(mid),
        done.bias2b.reshape(mid),
        done.e2_out,
        done.gain2c.reshape(channels),
        done.bias2c.reshape(channels),
    )


def solution(mesh):
    return jax.shard_map(
        per_device,
        mesh=mesh,
        in_specs=(
            P("ch", "sp", None, None),
            P(),
            P(None, "ch"),
            P(),
            P(),
            P(None, "ch", None),
            P(None, "ch", None),
            P(),
            P(),
            P(None, "ch"),
            P(),
            P(),
            P(None, "ch"),
            P(),
            P(),
            P(None, "ch", None),
            P(),
            P(),
            P(None, "ch"),
            P(),
            P(),
            P("ch", "sp", None, None),
        ),
        out_specs=(
            P("ch", "sp", None, None),
            P("ch", "sp", None, None),
            P(None, "ch"),
            P(),
            P(),
            P(None, "ch", None),
            P(None, "ch", None),
            P(),
            P(),
            P(None, "ch"),
            P(),
            P(),
            P(None, "ch"),
            P(),
            P(),
            P(None, "ch", None),
            P(),
            P(),
            P(None, "ch"),
            P(),
            P(),
        ),
        check_vma=False,
    )
```
